32 devices in a mesh: groups: 2 (over y), gx: 4 (over z), gy: 2 (over x), gz: 2 (over core).
Axes of the slice: x: 2, y: 2, z: 4, core: 2. Of those that a mesh axis runs over, the one named last changes fastest.
Arguments:
- potential_cot: float32 [128, 64, 256], P(('groups', 'gx'), 'gy', 'gz'), parts along dimension 0, may hold values from -16 to 16
- damping: float32 [128, 64, 256], P(('groups', 'gx'), 'gy', 'gz'), parts along dimension 0, may hold values from 0.1 to 8
- tissue_label: int32 [128, 64, 256], P(('groups', 'gx'), 'gy', 'gz'), parts along dimension 0, may hold values from 0 to 1, as said below
- heart_index: int32 [8, 2, 2, 20480], P(('groups', 'gx'), 'gy', 'gz'), parts along dimension 0, may hold values from 0 to 65536, as said below
- voltage: float32 [8, 32768], P(('groups', 'gy', 'gz'), 'gx'), parts along dimension 0, may hold values from -4 to 4
- gates: float32 [20, 8, 32768], P(None, ('groups', 'gy', 'gz'), 'gx'), parts along dimension 1, may hold values from 0 to 1
- voltage_cot: float32 [8, 32768], P(('groups', 'gy', 'gz'), 'gx'), parts along dimension 0, may hold values from -6 to 6
- gates_cot: float32 [20, 8, 32768], P(None, ('groups', 'gy', 'gz'), 'gx'), parts along dimension 1, may hold values from -6 to 6
- half_voltage: float32 [20], replicated, may hold values from -0.8 to 0.8
- gate_slope: float32 [20], replicated, may hold values from 0.2 to 0.8
- tau_base: float32 [20], replicated, may hold values from 0.05 to 4
- conductance: float32 [20], replicated, may hold values from 0.01 to 0.1
- reversal: float32 [20], replicated, may hold values from -1.5 to 1.5
Outputs:
- potential_adjoint: float32 [128, 64, 256], P(('groups', 'gx'), 'gy', 'gz'), parts along dimension 0
- voltage_grad: float32 [8, 32768], P(('groups', 'gy', 'gz'), 'gx'), parts along dimension 0
- gate_grad: float32 [20, 8, 32768], P(None, ('groups', 'gy', 'gz'), 'gx'), parts along dimension 1
The draws below stay inside these ranges and needn't reach their ends.
There are 2 independent parts, one for each index of `groups`. The reference program is written for one: setup_inputs(seed, part) draws one part's arguments, and reference() takes and returns one part's arrays. A program takes and returns all parts, laid end to end along the dimension named above; an argument that names none is the same for every part. Nothing has to cross between parts.
Inputs may be any that keep to these rules, and one draw needn't show every extreme that they name: `tissue_label`: 1 marks a heart cell, 0 a torso cell. `heart_index`: for each tile, the local indices of its heart cells (tissue_label 1) in ascending order, then 16 * 32 * 128 in every remaining slot. Each column of tiles (same second and third index) holds exactly 32768 heart cells, each tile at most 20480, and in every column some tile holds exactly 20480.
All inputs are finite; a program needn't handle non-finite values.
Results may differ from the reference program's by a relative error of at most 0.0001.
Values sent between devices are 32-bit elements; how exact they have to be, the bound alone decides.
No kernel may reach another device: no remote copies, remote signals or barrier semaphores. Data moves between devices by JAX's collectives and lax.ppermute only.
A program may use at most 64 MiB of HBM per device.

```python
import math
import jax
import jax.numpy as jnp
from jax import lax

CX = 16
CY = 32
CZ = 128
GATES = 20
ITERS = 3
HB = 8192
HCAP = 20480
NX = 64
NY = 64
NZ = 256
COLUMNS = 4
COLHEART = 32768
N_GX = 4
N_GY = 2
N_GZ = 2


def heart_layout(key):
    tiles_x = NX // CX
    tiles_y = NY // CY
    tiles_z = NZ // CZ
    tile_size = CX * CY * CZ
    quarter = tiles_x // 4
    column_count = tiles_y * tiles_z
    key_start, key_heavy, key_light, key_rank = jax.random.split(key, 4)
    first_heavy = jax.random.randint(key_start, (column_count, 1), 0, tiles_x).astype(jnp.int32)
    heavy_cut = jax.random.randint(key_heavy, (column_count, quarter), 0, HB // 2 + 1).astype(jnp.int32)
    heavy_cut = heavy_cut * (jnp.arange(quarter, dtype=jnp.int32) > 0).astype(jnp.int32)[None, :]
    light_cut = jax.random.randint(key_light, (column_count, quarter), 0, HB // 4 + 1).astype(jnp.int32)
    half_block = HB // 2
    role_counts = jnp.concatenate([5 * half_block - heavy_cut, half_block + heavy_cut, half_block + light_cut, half_block - light_cut], axis=1)
    placed = (jnp.arange(tiles_x, dtype=jnp.int32)[None, :] - first_heavy) % tiles_x
    counts = jnp.take_along_axis(role_counts, placed, axis=1)
    counts = counts.T.reshape(tiles_x, tiles_y, tiles_z)
    sub_keys = jax.random.split(key_rank, tiles_x * tiles_y * tiles_z)
    cell_rank = jax.vmap(lambda sub_key: jax.random.permutation(sub_key, tile_size))(sub_keys)
    cell_rank = cell_rank.astype(jnp.int32).reshape(tiles_x, tiles_y, tiles_z, tile_size)
    return (cell_rank < counts[..., None]).astype(jnp.int32)


def draw_tissue_label(key, part):
    labels = heart_layout(key)
    tiles_x = NX // CX
    tiles_y = NY // CY
    tiles_z = NZ // CZ
    labels = labels.reshape(tiles_x, tiles_y, tiles_z, CX, CY, CZ).transpose(0, 3, 1, 4, 2, 5)
    return labels.reshape(NX, NY, NZ).astype(jnp.int32)


def draw_heart_index(key, part):
    labels = heart_layout(key)
    tile_size = CX * CY * CZ
    position = jnp.arange(tile_size, dtype=jnp.int32)
    order_key = jnp.where(labels > 0, position, position + tile_size)
    ordered = jnp.sort(order_key, axis=-1)[..., :HCAP]
    return jnp.where(ordered < tile_size, ordered, tile_size).astype(jnp.int32)


def block_levels(own_key, dims, pieces, least, top_value):
    def one(axis_at, shards_of):
        draws = jax.random.uniform(jax.random.fold_in(jax.random.fold_in(own_key, 6), axis_at), (shards_of,), jnp.float32, least / len(pieces), top_value / len(pieces))
        return jnp.repeat(jnp.exp(draws), dims[axis_at] // shards_of).reshape((-1,) + (1,) * (len(dims) - axis_at - 1))

    factor_of = one(*pieces[0])
    for cut in pieces[1:]:
        factor_of = factor_of * one(*cut)
    return factor_of


def noise(stream_key, shape, spread, bound, shards=(), held_as=jnp.bfloat16):
    entries = jax.random.normal(stream_key, shape, jnp.float32) * spread
    if len(shards) > 0:
        entries = block_levels(stream_key, shape, shards, -0.22, 0.18) * entries
    return jnp.clip(entries, min=-bound, max=bound).astype(held_as)


def setup_inputs(seed: int = 0, part: int = 0) -> dict:
    splits = jax.random.split(jax.random.key(seed), 14)
    part_keys = jax.random.split(jax.random.fold_in(splits[13], part), 14)
    potential_cot = noise(part_keys[0], (NX, NY, NZ), 4.0, 16.0, ((0, 4), (1, 2), (2, 2)), jnp.float32)
    damping = jnp.clip(jnp.exp(math.log(8.0) - 4.3820266 * jax.random.uniform(part_keys[1], (NX, NY, NZ), jnp.float32) ** block_levels(part_keys[1], (NX, NY, NZ), ((0, 4), (1, 2), (2, 2)), -0.2, 0.2)), 0.1, 8.0)
    tissue_label = draw_tissue_label(jax.random.fold_in(jax.random.fold_in(splits[13], part), 71), part)
    heart_index = draw_heart_index(jax.random.fold_in(jax.random.fold_in(splits[13], part), 71), part)
    voltage = noise(part_keys[4], (COLUMNS, COLHEART), 1.0, 4.0, ((0, 4), (1, 4)), jnp.float32)
    gates = jnp.clip(1.0 * jax.random.uniform(part_keys[5], (GATES, COLUMNS, COLHEART), jnp.float32) ** block_levels(part_keys[5], (GATES, COLUMNS, COLHEART), ((1, 4), (2, 4)), -0.2, 0.2), 0.0, 1.0)
    voltage_cot = noise(part_keys[6], (COLUMNS, COLHEART), 1.0, 6.0, ((0, 4), (1, 4)), jnp.float32)
    gates_cot = noise(part_keys[7], (GATES, COLUMNS, COLHEART), 1.0, 6.0, ((1, 4), (2, 4)), jnp.float32)
    half_voltage = jnp.clip(jax.random.uniform(splits[8], (GATES,), jnp.float32, -0.8, 0.8), -0.8, 0.8)
    gate_slope = jnp.clip(jnp.exp(jax.random.uniform(splits[9], (GATES,), jnp.float32, math.log(0.2), math.log(0.8))), 0.2, 0.8)
    tau_base = jnp.clip(jnp.exp(jax.random.uniform(splits[10], (GATES,), jnp.float32, math.log(0.05), math.log(4.0))), 0.05, 4.0)
    conductance = jnp.clip(jnp.exp(jax.random.uniform(splits[11], (GATES,), jnp.float32, math.log(0.01), math.log(0.1))), 0.01, 0.1)
    reversal = jnp.clip(jax.random.uniform(splits[12], (GATES,), jnp.float32, -1.5, 1.5), -1.5, 1.5)
    return {"potential_cot": potential_cot, "damping": damping, "tissue_label": tissue_label, "heart_index": heart_index, "voltage": voltage, "gates": gates, "voltage_cot": voltage_cot, "gates_cot": gates_cot, "half_voltage": half_voltage, "gate_slope": gate_slope, "tau_base": tau_base, "conductance": conductance, "reversal": reversal}


time_step = 0.5
face_moves = ((1, 0, 0), (-1, 0, 0), (0, 1, 0), (0, -1, 0), (0, 0, 1), (0, 0, -1))
edge_moves = ((1, 1, 0), (1, -1, 0), (-1, 1, 0), (-1, -1, 0), (1, 0, 1), (1, 0, -1), (-1, 0, 1), (-1, 0, -1), (0, 1, 1), (0, 1, -1), (0, -1, 1), (0, -1, -1))

def neighbour(padded, offset, extent):
    return padded[1 + offset[0]:1 + offset[0] + extent[0], 1 + offset[1]:1 + offset[1] + extent[1], 1 + offset[2]:1 + offset[2] + extent[2]]

def face_total(padded, extent):
    face_sum = neighbour(padded, face_moves[0], extent)
    for offset in face_moves[1:]:
        face_sum = face_sum + neighbour(padded, offset, extent)
    return face_sum

def apply_operator(padded, source, diagonal):
    extent = source.shape
    edge_sum = neighbour(padded, edge_moves[0], extent)
    for offset in edge_moves[1:]:
        edge_sum = edge_sum + neighbour(padded, offset, extent)
    return diagonal * source - face_total(padded, extent) - 0.5 * edge_sum

def membrane_step(voltage, gates, half_voltage, gate_slope, tau_base, conductance, reversal):
    param_shape = (-1,) + (1,) * voltage.ndim
    scaled = (voltage[None] - half_voltage.reshape(param_shape)) / gate_slope.reshape(param_shape)
    steady = 1.0 / (1.0 + jnp.exp(-scaled))
    time_const = tau_base.reshape(param_shape) * (0.5 + jnp.exp(-scaled * scaled))
    decay = jnp.exp(-time_step / time_const)
    new_gates = steady + (gates - steady) * decay
    current = lax.optimization_barrier(jnp.sum(conductance.reshape(param_shape) * gates * (voltage[None] - reversal.reshape(param_shape)), axis=0))
    return (voltage - time_step * current, new_gates)

def solve(right_side, diagonal):
    inverse = 1.0 / diagonal
    solution = jnp.zeros_like(right_side)
    residual = right_side
    precond = inverse * residual
    direction = precond
    norm_now = jnp.sum(residual * precond)
    for iteration in range(ITERS):
        applied = apply_operator(jnp.pad(direction, 1), direction, diagonal)
        step_size = norm_now / jnp.sum(direction * applied)
        solution = solution + step_size * direction
        residual = residual - step_size * applied
        if iteration + 1 < ITERS:
            precond = inverse * residual
            norm_next = jnp.sum(residual * precond)
            direction = precond + norm_next / norm_now * direction
            norm_now = norm_next
    return solution

def to_columns(coupling, heart_index):
    tile_size = CX * CY * CZ
    blocks = coupling.reshape(N_GX, CX, N_GY, CY, N_GZ, CZ).transpose(0, 2, 4, 1, 3, 5).reshape(N_GX, N_GY, N_GZ, tile_size)
    is_heart = heart_index < tile_size
    values = jnp.take_along_axis(blocks, jnp.minimum(heart_index, tile_size - 1).astype(jnp.int32), axis=3)
    counts = lax.optimization_barrier(jnp.sum(is_heart.astype(jnp.int32), axis=3)).astype(jnp.int32)
    before = (jnp.cumsum(counts, axis=0) - counts).astype(jnp.int32)
    rank_of = before[..., None] + jnp.arange(HCAP, dtype=jnp.int32)
    rank_of = jnp.where(is_heart, rank_of, COLHEART).astype(jnp.int32)
    column = jnp.arange(N_GY, dtype=jnp.int32)[:, None] * N_GZ + jnp.arange(N_GZ, dtype=jnp.int32)[None, :]
    column = jnp.broadcast_to(column[None, :, :, None], rank_of.shape).astype(jnp.int32)
    landed = jnp.zeros((COLUMNS, COLHEART), jnp.float32)
    return landed.at[column, rank_of].set(values, mode='drop')

def reference(potential_cot, damping, tissue_label, heart_index, voltage, gates, voltage_cot, gates_cot, half_voltage, gate_slope, tau_base, conductance, reversal):
    diagonal = 12.0 + damping * (1.0 + 3.0 * tissue_label.astype(jnp.float32))
    solution = solve(potential_cot, diagonal)
    coupling = face_total(jnp.pad(solution, 1), solution.shape) - 6.0 * solution
    landed = to_columns(coupling, heart_index)

    def per_column(column_data):
        column_volts, column_gates, column_vcot, column_gcot, column_land = column_data

        def local_step(volts_in, gates_in):
            return membrane_step(volts_in, gates_in, half_voltage, gate_slope, tau_base, conductance, reversal)
        outputs, pullback = jax.vjp(local_step, column_volts, column_gates)
        return pullback((column_vcot + column_land, column_gcot))
    volt_grads, gate_grads = lax.map(per_column, (voltage, jnp.transpose(gates, (1, 0, 2)), voltage_cot, jnp.transpose(gates_cot, (1, 0, 2)), landed))
    return (solution, volt_grads, jnp.transpose(gate_grads, (1, 0, 2)))
```

```python
import functools

import jax
import jax.numpy as jnp
from jax import lax
from jax.experimental import pallas as pl
from jax.experimental.pallas import tpu as pltpu
from jax.sharding import PartitionSpec as P

TIME_STEP = 0.5
LANES = 128
SIDES = (("gz", 2), ("gy", 1), ("gx", 0))


def exchange(pair, axis, dim):
    count = lax.axis_size(axis)
    here = lax.axis_index(axis)
    first = lax.slice_in_dim(pair, 0, 3, axis=dim)
    last = lax.slice_in_dim(pair, pair.shape[dim] - 3, None, axis=dim)
    if count == 2:
        got = lax.ppermute(jnp.where(here == 0, last, first), axis, [(0, 1), (1, 0)])
        low = jnp.where(here == 1, got, 0.0)
        high = jnp.where(here == 0, got, 0.0)
    else:
        forward = [(i, i + 1) for i in range(count - 1)]
        backward = [(i + 1, i) for i in range(count - 1)]
        low = lax.ppermute(last, axis, forward)
        high = lax.ppermute(first, axis, backward)
    return jnp.concatenate([low, pair, high], axis=dim)


def neighbour_sum(v):
    mid = v[:, :, 1:-1]
    along_z = v[:, :, 2:] + v[:, :, :-2]
    both = mid + 0.5 * along_z
    plane = along_z[:, 1:-1] + both[:, 2:] + both[:, :-2]
    wing = both[:, 1:-1] + 0.5 * (mid[:, 2:] + mid[:, :-2])
    return plane[1:-1] + wing[2:] + wing[:-2]


def core(v, width):
    return v[width:-width, width:-width, width:-width] if width else v


def face_sum(v):
    return (
        v[2:, 1:-1, 1:-1] + v[:-2, 1:-1, 1:-1]
        + v[1:-1, 2:, 1:-1] + v[1:-1, :-2, 1:-1]
        + v[1:-1, 1:-1, 2:] + v[1:-1, 1:-1, :-2]
    )


def galerkin(t):
    g00, g01, g02, g12, g22 = t[0] - t[1], t[1] - t[2], t[2] - t[3], t[3] - t[4], t[4] - t[5]
    g11 = g02
    l10, l20 = g01 / g00, g02 / g00
    d1 = g11 - l10 * g01
    m21 = g12 - l20 * g01
    ok1 = d1 > 1e-6 * g11
    d1 = jnp.where(ok1, d1, 1.0)
    l21 = jnp.where(ok1, m21 / d1, 0.0)
    d2 = g22 - l20 * g02 - l21 * m21
    ok2 = ok1 & (d2 > 1e-6 * g22)
    d2 = jnp.where(ok2, d2, 1.0)
    y1 = t[1] - l10 * t[0]
    y2 = t[2] - l20 * t[0] - l21 * y1
    c2 = jnp.where(ok2, y2 / d2, 0.0)
    c1 = jnp.where(ok1, y1 / d1 - l21 * c2, 0.0)
    c0 = t[0] / g00 - l10 * c1 - l20 * c2
    return c0, c1, c2


def shift_left(v, amount, lane):
    rows = v.shape[0]
    if amount < LANES:
        turned = pltpu.roll(v, LANES - amount, 1)
        below = pltpu.roll(turned, rows - 1, 0)
        return jnp.where(lane < LANES - amount, turned, below)
    return jnp.concatenate([v[amount // LANES :], v[: amount // LANES]], axis=0)


def compact_kernel(place_ref, label_ref, value_ref, out_ref):
    rows = label_ref.shape[0]
    label = label_ref[...]
    lane = lax.broadcasted_iota(jnp.int32, (rows, LANES), 1)
    row = lax.broadcasted_iota(jnp.int32, (rows, LANES), 0)
    heart = label == 1
    ones = heart.astype(jnp.bfloat16)
    upper = (
        lax.broadcasted_iota(jnp.int32, (LANES, LANES), 0) < lax.broadcasted_iota(jnp.int32, (LANES, LANES), 1)
    ).astype(jnp.bfloat16)
    in_row = jnp.dot(ones, upper, preferred_element_type=jnp.float32)
    totals = jnp.dot(ones, jnp.ones((LANES, LANES), jnp.bfloat16), preferred_element_type=jnp.float32)
    lower = (
        lax.broadcasted_iota(jnp.int32, (rows, rows), 0) > lax.broadcasted_iota(jnp.int32, (rows, rows), 1)
    ).astype(jnp.bfloat16)
    before = jnp.dot(lower, totals.astype(jnp.bfloat16), preferred_element_type=jnp.float32)
    rank = (in_row + before).astype(jnp.int32)
    way = jnp.where(heart, row * LANES + lane - rank, 0)
    value = value_ref[...]
    step = 1
    while step < rows * LANES:
        moving = jnp.where((way & step) != 0, way, 0)
        arriving = shift_left(moving, step, lane)
        value = jnp.where(arriving != 0, shift_left(value, step, lane), value)
        way = (way - moving) | arriving
        step *= 2
    offset = place_ref[0]
    count = place_ref[1]
    slots = value[:160]
    index = (row * LANES + lane)[:160]
    slots = jnp.where(index < count, slots, 0.0)
    slots = jnp.concatenate([slots, jnp.zeros((8, LANES), jnp.float32)], axis=0)
    inner = lax.rem(offset, LANES)
    turned = pltpu.roll(slots, inner, 1)
    above = pltpu.roll(turned, 1, 0)
    moved = jnp.where(lane[:168] >= inner, turned, above)
    out_ref[...] = jnp.zeros_like(out_ref)
    out_ref[pl.ds(offset // LANES, 168), :] = moved


def local(
    potential_cot, damping, tissue_label, heart_index, voltage, gates, voltage_cot, gates_cot,
    half_voltage, gate_slope, tau_base, conductance, reversal,
):
    shape = potential_cot.shape
    rows = shape[0] * shape[1]
    n_gx = lax.axis_size("gx")
    width_block = voltage.shape[1]
    block_rows = width_block // LANES

    diagonal = 12.0 + damping * (1.0 + 3.0 * tissue_label.astype(jnp.float32))
    inverse = 1.0 / diagonal
    w0 = inverse * potential_cot
    pair = jnp.stack([w0, inverse])
    for axis, dim in SIDES:
        pair = exchange(pair, axis, dim + 1)
    field, inverse = pair[0], core(pair[1], 1)
    w1 = neighbour_sum(field) * inverse
    w2 = neighbour_sum(w1) * core(inverse, 1)
    n2 = neighbour_sum(w2)
    in0, in1, in2 = core(field, 3), core(w1, 2), core(w2, 1)

    count = jnp.sum((tissue_label == 1).astype(jnp.float32))
    sums = jnp.stack([
        jnp.sum(potential_cot * in0),
        jnp.sum(potential_cot * in1),
        jnp.sum(diagonal * in1 * in1),
        jnp.sum(diagonal * in1 * in2),
        jnp.sum(diagonal * in2 * in2),
        jnp.sum(in2 * n2),
    ])
    here = (lax.axis_index("gx") * lax.axis_size("gy") + lax.axis_index("gy")) * lax.axis_size("gz") + lax.axis_index("gz")
    n_dev = n_gx * lax.axis_size("gy") * lax.axis_size("gz")
    counts = jnp.where(jnp.arange(n_dev) == here, count, 0.0)
    total = lax.psum(jnp.concatenate([sums, counts]), ("gx", "gy", "gz"))
    c0, c1, c2 = galerkin([total[i] for i in range(6)])
    wide = c0 * core(field, 2) + c1 * core(w1, 1) + c2 * w2
    solution = core(wide, 1)
    coupling = face_sum(wide) - 6.0 * solution

    column = total[6:].reshape(n_gx, -1)
    mine = lax.axis_index("gy") * lax.axis_size("gz") + lax.axis_index("gz")
    column = lax.dynamic_index_in_dim(column, mine, axis=1, keepdims=False)
    offset = jnp.sum(jnp.where(jnp.arange(n_gx) < lax.axis_index("gx"), column, 0.0))
    place = jnp.stack([offset, count]).astype(jnp.int32)
    placed = pl.pallas_call(
        compact_kernel,
        out_shape=jax.ShapeDtypeStruct((n_gx * block_rows + 168, LANES), jnp.float32),
        in_specs=[
            pl.BlockSpec(memory_space=pltpu.SMEM),
            pl.BlockSpec(memory_space=pltpu.VMEM),
            pl.BlockSpec(memory_space=pltpu.VMEM),
        ],
        out_specs=pl.BlockSpec(memory_space=pltpu.VMEM),
        compiler_params=pltpu.CompilerParams(vmem_limit_bytes=32 * 1024 * 1024),
    )(place, tissue_label.reshape(rows, LANES), coupling.reshape(rows, LANES))
    blocks = placed[: n_gx * block_rows].reshape(n_gx, block_rows, LANES)
    landed = jnp.sum(lax.all_to_all(blocks, "gx", 0, 0, tiled=True), axis=0)

    param = lambda a: a.reshape(-1, 1, 1)
    scaled = (voltage[None] - param(half_voltage)) / param(gate_slope)
    steady = 1.0 / (1.0 + jnp.exp(-scaled))
    bell = jnp.exp(-scaled * scaled)
    tau = param(tau_base) * (0.5 + bell)
    decay = jnp.exp(-TIME_STEP / tau)
    steady_slope = steady * (1.0 - steady) / param(gate_slope)
    tau_slope = param(tau_base) * bell * (-2.0 * scaled) / param(gate_slope)
    decay_slope = decay * TIME_STEP / (tau * tau) * tau_slope
    gate_slope_total = steady_slope * (1.0 - decay) + (gates - steady) * decay_slope
    cot = voltage_cot + landed.reshape(voltage.shape)
    volt_grad = (
        cot * (1.0 - TIME_STEP * jnp.sum(param(conductance) * gates, axis=0))
        + jnp.sum(gates_cot * gate_slope_total, axis=0)
    )
    gate_grad = gates_cot * decay - TIME_STEP * param(conductance) * (voltage[None] - param(reversal)) * cot[None]
    return solution, volt_grad, gate_grad


def solution(mesh):
    grid = P(("groups", "gx"), "gy", "gz")
    cells = P(("groups", "gy", "gz"), "gx")
    states = P(None, ("groups", "gy", "gz"), "gx")
    in_specs = (
        grid, grid, grid, P(("groups", "gx"), "gy", "gz", None), cells, states, cells, states,
        P(), P(), P(), P(), P(),
    )
    return jax.shard_map(
        local, mesh=mesh, in_specs=in_specs, out_specs=(grid, cells, states), check_vma=False
    )
```

```python
import functools

import jax
import jax.numpy as jnp
from jax import lax
from jax.experimental import pallas as pl
from jax.experimental.pallas import tpu as pltpu
from jax.sharding import PartitionSpec as P

TIME_STEP = 0.5
LANES = 128
SUB = 8
PACK = 8
F32 = jnp.float32

VMEM = pl.BlockSpec(memory_space=pltpu.VMEM)
SMEM = pl.BlockSpec(memory_space=pltpu.SMEM)


def shape_of(*dims):
    return jax.ShapeDtypeStruct(dims, F32)


def call(kernel, out_shape, n_in, specs=None, scratch=(), cost=2_000_000, limit=32):
    return pl.pallas_call(
        kernel,
        out_shape=out_shape,
        in_specs=specs if specs is not None else [VMEM] * n_in,
        out_specs=jax.tree.map(lambda _: VMEM, out_shape),
        scratch_shapes=list(scratch),
        compiler_params=pltpu.CompilerParams(vmem_limit_bytes=limit * 1024 * 1024),
        cost_estimate=pl.CostEstimate(flops=cost, bytes_accessed=cost, transcendentals=0),
    )


def lanes_of(shape):
    return lax.broadcasted_iota(jnp.int32, shape, len(shape) - 1)


def subs_of(shape):
    return lax.broadcasted_iota(jnp.int32, shape, len(shape) - 2)


def start_kernel(right_ref, damping_ref, label_ref, w0_ref, inv_ref, pack_ref, stat_ref):
    nx, ny, nz = right_ref.shape
    gz = lax.axis_index("gz")
    lane = lanes_of((ny, nz))
    packed_w = jnp.zeros((ny, nz), F32)
    packed_i = jnp.zeros((ny, nz), F32)
    energy = jnp.zeros((ny, nz), F32)
    cells = jnp.zeros((ny, nz), F32)
    for x in range(nx):
        label = label_ref[x].astype(F32)
        right = right_ref[x]
        inv = 1.0 / (12.0 + damping_ref[x] * (1.0 + 3.0 * label))
        w0 = right * inv
        w0_ref[x] = w0
        inv_ref[x] = inv
        energy = energy + right * w0
        cells = cells + label
        turn = (PACK * x + 3) % nz
        begin = PACK * x + 3 * gz
        chosen = (lane >= begin) & (lane < begin + 3)
        packed_w = jnp.where(chosen, pltpu.roll(w0, turn, 1), packed_w)
        packed_i = jnp.where(chosen, pltpu.roll(inv, turn, 1), packed_i)
    pack_ref[0] = packed_w
    pack_ref[1] = packed_i
    stat_ref[0] = jnp.broadcast_to(jnp.sum(energy, axis=0, keepdims=True), (SUB, nz))
    stat_ref[1] = jnp.broadcast_to(jnp.sum(cells, axis=0, keepdims=True), (SUB, nz))


def y_faces_kernel(w0_ref, inv_ref, own_ref, got_ref, slab_ref, up_ref, down_ref):
    nx, ny, nz = w0_ref.shape
    sub = subs_of((SUB, nz))
    slab_ref[...] = own_ref[...] + got_ref[...]
    for x in range(nx + 1):
        if x < nx:
            w_last, w_first = w0_ref[x, ny - SUB :], w0_ref[x, :SUB]
            i_last, i_first = inv_ref[x, ny - SUB :], inv_ref[x, :SUB]
        else:
            w_last, w_first = slab_ref[0, ny - SUB :], slab_ref[0, :SUB]
            i_last, i_first = slab_ref[1, ny - SUB :], slab_ref[1, :SUB]
        up_ref[x] = jnp.where(sub >= 5, w_last, pltpu.roll(i_last, 4, 0))
        down_ref[x] = jnp.where(sub <= 2, w_first, pltpu.roll(i_first, 4, 0))


def y_face_one_kernel(w0_ref, inv_ref, own_ref, got_ref, slab_ref, face_ref):
    nx, ny, nz = w0_ref.shape
    sub = subs_of((SUB, nz))
    up = lax.axis_index("gy") == 0
    keep_w = jnp.where(up, sub, SUB - 1 - sub) >= 5
    slab_ref[...] = own_ref[...] + got_ref[...]
    for x in range(nx + 1):
        if x < nx:
            w_last, w_first = w0_ref[x, ny - SUB :], w0_ref[x, :SUB]
            i_last, i_first = inv_ref[x, ny - SUB :], inv_ref[x, :SUB]
        else:
            w_last, w_first = slab_ref[0, ny - SUB :], slab_ref[0, :SUB]
            i_last, i_first = slab_ref[1, ny - SUB :], slab_ref[1, :SUB]
        w_face = jnp.where(up, w_last, w_first)
        i_face = jnp.where(up, i_last, i_first)
        face_ref[x] = jnp.where(keep_w, w_face, pltpu.roll(i_face, 4, 0))


def x_faces_kernel(one, w0_ref, inv_ref, slab_ref, *refs):
    if one:
        got_ref, w_ref, i_ref, ring_ref, up_ref, down_ref = refs
    else:
        low_ref, high_ref, w_ref, i_ref, ring_ref, up_ref, down_ref = refs
    nx, ny, nz = w0_ref.shape
    sub = subs_of((SUB, nz))
    lane = lanes_of((ny + SUB, nz))
    if one:
        gy = lax.axis_index("gy")
        from_low = (gy == 1) & (sub >= 5)
        from_high = (gy == 0) & (sub <= 2)
        inv_low = (gy == 1) & (sub >= 6)
        inv_high = (gy == 0) & (sub <= 1)
    for x in range(nx + 1):
        if one:
            got = got_ref[x]
            turned = pltpu.roll(got, 4, 0)
            w_halo = jnp.where(from_low | from_high, got, 0.0)
            i_halo = jnp.where(inv_low | inv_high, turned, 0.0)
        else:
            low, high = low_ref[x], high_ref[x]
            w_halo = jnp.where(sub >= 5, low, jnp.where(sub <= 2, high, 0.0))
            i_halo = jnp.where(
                sub >= 6, pltpu.roll(low, 4, 0), jnp.where(sub <= 1, pltpu.roll(high, 4, 0), 0.0)
            )
        if x < nx:
            w_ref[x, :ny] = w0_ref[x]
            w_ref[x, ny:] = w_halo
            i_ref[x, :ny] = inv_ref[x]
            i_ref[x, ny:] = i_halo
        else:
            ring_ref[0, :ny] = slab_ref[0]
            ring_ref[0, ny:] = w_halo
            ring_ref[1, :ny] = slab_ref[1]
            ring_ref[1, ny:] = i_halo
    for k in range(3):
        up_ref[k] = w_ref[nx - 3 + k]
        down_ref[k] = w_ref[k]
    for k in range(2):
        up_ref[3 + k] = i_ref[nx - 2 + k]
        down_ref[3 + k] = i_ref[k]
    half = pltpu.roll(ring_ref[1], nz // 2, 1)
    up_ref[5] = jnp.where(lane >= nz - 3 * PACK, ring_ref[0], half)
    down_ref[5] = jnp.where(lane < 3 * PACK, ring_ref[0], half)


def around(v):
    rows = v.shape[0]
    return pltpu.roll(v, 1, 0) + pltpu.roll(v, rows - 1, 0)


def stencil_kernel(
    w_ref, i_ref, ring_ref, low_ref, high_ref, stat_ref,
    w1_ref, w2_ref, f0_ref, f1_ref, f2_ref, total_ref,
    a_ref, b_ref, sw_ref,
):
    nx, ring, nz = w_ref.shape
    ny = ring - SUB
    gz = lax.axis_index("gz")
    lane = lanes_of((ring, nz))
    entry = (nz - 1) * gz
    at_entry = lane == entry
    lane_first = lane == 0
    lane_last = lane == nz - 1

    def w0_plane(x):
        if x < 0:
            return low_ref[3 + x]
        if x >= nx:
            return high_ref[x - nx]
        return w_ref[x]

    def inv_plane(x):
        if x < 0:
            return low_ref[5 + x]
        if x >= nx:
            return high_ref[3 + x - nx]
        return i_ref[x]

    lo5, hi5 = low_ref[5], high_ref[5]
    slab_w = jnp.where(lane < 3 * PACK, hi5, 0.0) + jnp.where(lane >= nz - 3 * PACK, lo5, 0.0)
    lo5, hi5 = pltpu.roll(lo5, nz // 2, 1), pltpu.roll(hi5, nz // 2, 1)
    slab_i = jnp.where(lane < 2 * PACK, hi5, 0.0) + jnp.where(lane >= nz - 2 * PACK, lo5, 0.0)
    slab = jnp.concatenate([ring_ref[0], slab_w], axis=1)
    slab_inv = jnp.concatenate([ring_ref[1], slab_i], axis=1)

    def slab_step(s):
        width = s.shape[1]
        along = pltpu.roll(s, 1, 1) + pltpu.roll(s, width - 1, 1)
        both = s + 0.5 * along
        wing = both + 0.5 * around(s)
        total = along + around(both) + pltpu.roll(wing, PACK, 1) + pltpu.roll(wing, width - PACK, 1)
        return total * slab_inv

    def sweep(source, margin, face_ref, store):
        wing_before = wing_here = rest_here = None
        v_before = v_here = face_here = None
        for x in range(-margin - 1, nx + margin + 1):
            v = source(x)
            place = (PACK * x) % (2 * nz)
            half = sw_ref[:, nz * (place // nz) : nz * (place // nz) + nz]
            turn = lax.rem(entry - (place % nz + 3 - gz) + 2 * nz, nz)
            edge = jnp.where(at_entry, pltpu.roll(half, turn, 1), 0.0)
            along = pltpu.roll(jnp.where(lane_first, edge, v), nz - 1, 1) + pltpu.roll(
                jnp.where(lane_last, edge, v), 1, 1
            )
            both = v + 0.5 * along
            beside = around(v)
            wing = both + 0.5 * beside
            rest = along + around(both)
            done = x - 1
            if done >= -margin:
                store(done, rest_here + wing_before + wing, v_here)
                if 0 <= done < nx:
                    face_ref[done] = face_here + (v_before + v)[:ny]
            wing_before, wing_here, rest_here = wing_here, wing, rest
            v_before, v_here = v_here, v
            if 0 <= x < nx:
                face_here = (along + beside - 6.0 * v)[:ny]

    sums = {}

    def add(name, value):
        part = jnp.sum(value[:ny].reshape(ny // SUB, SUB, nz), axis=0)
        sums[name] = part if name not in sums else sums[name] + part

    def store0(x, total, v):
        w1 = total * inv_plane(x)
        a_ref[x + 2] = w1
        if 0 <= x < nx:
            w1_ref[x] = w1[:ny]
            add(1, v * total)
            add(2, w1 * total)

    def store1(x, total, v):
        w2 = total * inv_plane(x)
        b_ref[x + 1] = w2
        if 0 <= x < nx:
            w2_ref[x] = w2[:ny]
            add(3, v * total)
            add(4, w2 * total)

    def store2(x, total, v):
        add(5, v * total)

    sw_ref[...] = slab
    sweep(w0_plane, 2, f0_ref, store0)
    slab = slab_step(slab)
    sw_ref[...] = slab
    sweep(lambda x: a_ref[x + 2], 1, f1_ref, store1)
    slab = slab_step(slab)
    sw_ref[...] = slab
    sweep(lambda x: b_ref[x + 1], 0, f2_ref, store2)

    total_ref[0:1] = stat_ref[0, 0:1]
    for k in range(1, 6):
        total_ref[k : k + 1] = jnp.sum(sums[k], axis=0, keepdims=True)
    total_ref[6:8] = jnp.zeros((2, nz), F32)
    here = (lax.axis_index("gx") * lax.axis_size("gy") + lax.axis_index("gy")) * lax.axis_size("gz") + gz
    count = jnp.sum(stat_ref[1], axis=1, keepdims=True)
    total_ref[8:16] = jnp.where(lanes_of((SUB, nz)) == here, count, 0.0)


def shift_left(v, amount, lane):
    rows = v.shape[0]
    if amount < LANES:
        turned = pltpu.roll(v, LANES - amount, 1)
        below = pltpu.roll(turned, rows - 1, 0)
        return jnp.where(lane < LANES - amount, turned, below)
    return jnp.concatenate([v[amount // LANES :], v[: amount // LANES]], axis=0)


def plan_kernel(label_ref, plan_ref):
    rows = label_ref.shape[0]
    lane = lanes_of((rows, LANES))
    row = subs_of((rows, LANES))
    heart = label_ref[...] == 1
    ones = heart.astype(jnp.bfloat16)
    upper = (subs_of((LANES, LANES)) < lanes_of((LANES, LANES))).astype(jnp.bfloat16)
    in_row = jnp.dot(ones, upper, preferred_element_type=F32)
    totals = jnp.dot(ones, jnp.ones((LANES, LANES), jnp.bfloat16), preferred_element_type=F32)
    lower = (subs_of((rows, rows)) > lanes_of((rows, rows))).astype(jnp.bfloat16)
    before = jnp.dot(lower, totals.astype(jnp.bfloat16), preferred_element_type=F32)
    rank = (in_row + before).astype(jnp.int32)
    way = jnp.where(heart, row * LANES + lane - rank, 0)
    plan = jnp.zeros((rows, LANES), jnp.int32)
    step = 1
    while step < rows * LANES:
        moving = jnp.where((way & step) != 0, way, 0)
        arriving = shift_left(moving, step, lane)
        plan = plan | (arriving & step)
        way = (way - moving) | arriving
        step *= 2
    plan_ref[...] = plan


def galerkin(t):
    g00, g01, g02, g12, g22 = t[0] - t[1], t[1] - t[2], t[2] - t[3], t[3] - t[4], t[4] - t[5]
    g11 = g02
    l10, l20 = g01 / g00, g02 / g00
    d1 = g11 - l10 * g01
    m21 = g12 - l20 * g01
    ok1 = d1 > 1e-6 * g11
    d1 = jnp.where(ok1, d1, 1.0)
    l21 = jnp.where(ok1, m21 / d1, 0.0)
    d2 = g22 - l20 * g02 - l21 * m21
    ok2 = ok1 & (d2 > 1e-6 * g22)
    d2 = jnp.where(ok2, d2, 1.0)
    y1 = t[1] - l10 * t[0]
    y2 = t[2] - l20 * t[0] - l21 * y1
    c2 = jnp.where(ok2, y2 / d2, 0.0)
    c1 = jnp.where(ok1, y1 / d1 - l21 * c2, 0.0)
    c0 = t[0] / g00 - l10 * c1 - l20 * c2
    return c0, c1, c2


def combine_kernel(
    slot_rows, total_ref, w0_ref, w1_ref, w2_ref, f0_ref, f1_ref, f2_ref, plan_ref, x_ref, out_ref, buf_ref
):
    rows = w0_ref.shape[0]
    lane = lanes_of((rows, LANES))
    row = subs_of((rows, LANES))
    sums = jnp.sum(total_ref[0:8], axis=1, keepdims=True)
    t = [jnp.broadcast_to(sums[k : k + 1], (1, LANES)) for k in range(6)]
    c0, c1, c2 = galerkin(t)
    x_ref[...] = c0 * w0_ref[...] + c1 * w1_ref[...] + c2 * w2_ref[...]
    value = c0 * f0_ref[...] + c1 * f1_ref[...] + c2 * f2_ref[...]
    plan = plan_ref[...]
    step = 1
    while step < rows * LANES:
        value = jnp.where((plan & step) != 0, shift_left(value, step, lane), value)
        step *= 2
    ny, nz = lax.axis_size("gy"), lax.axis_size("gz")
    counts = total_ref[8:16]
    dev = lanes_of((SUB, LANES))
    column = lax.axis_index("gy") * nz + lax.axis_index("gz")
    mine = lax.rem(dev, ny * nz) == column
    gx = lax.axis_index("gx")
    first = subs_of((SUB, LANES)) == 0
    offset = jnp.sum(jnp.where(first & mine & (dev < gx * ny * nz), counts, 0.0)).astype(jnp.int32)
    count = jnp.sum(jnp.where(first & mine & (dev // (ny * nz) == gx), counts, 0.0)).astype(jnp.int32)
    slots = value[:slot_rows]
    index = (row * LANES + lane)[:slot_rows]
    slots = jnp.where(index < count, slots, 0.0)
    slots = jnp.concatenate([slots, jnp.zeros((SUB, LANES), F32)], axis=0)
    inner = lax.rem(offset, LANES)
    turned = pltpu.roll(slots, inner, 1)
    above = pltpu.roll(turned, 1, 0)
    moved = jnp.where(lane[: slot_rows + SUB] >= inner, turned, above)
    buf_ref[...] = jnp.zeros_like(buf_ref)
    buf_ref[pl.ds(offset // LANES, slot_rows + SUB), :] = moved
    out_ref[...] = buf_ref[: out_ref.shape[0]]


def membrane_kernel(
    half_ref, slope_ref, tau_ref, cond_ref, v_ref, gates_ref, cot_ref, base_ref, sum_ref, factor_ref
):
    n_states = gates_ref.shape[0]
    v = v_ref[...]
    rows = v.shape[0]

    def state(g, carry):
        total, current = carry
        inv_slope = 1.0 / slope_ref[g]
        tau_base = tau_ref[g]
        scaled = (v - half_ref[g]) * inv_slope
        gate = gates_ref[g]
        cot = cot_ref[g]
        steady = 1.0 / (1.0 + jnp.exp(-scaled))
        bell = jnp.exp(-scaled * scaled)
        rate = TIME_STEP / (tau_base * (0.5 + bell))
        decay = jnp.exp(-rate)
        steady_slope = steady * (1.0 - steady)
        decay_slope = decay * rate * rate * ((tau_base / TIME_STEP) * bell * (-2.0 * scaled))
        change = (steady_slope * (1.0 - decay) + (gate - steady) * decay_slope) * inv_slope
        base_ref[g] = cot * decay
        return total + cot * change, current + cond_ref[g] * gate

    zero = jnp.zeros((rows, LANES), F32)
    total, current = lax.fori_loop(0, n_states, state, (zero, zero), unroll=2)
    sum_ref[...] = total
    factor_ref[...] = 1.0 - TIME_STEP * current


def finish_kernel(
    cond_ref, rev_ref, landed_ref, vcot_ref, v_ref, sum_ref, factor_ref, base_ref, volt_ref, gate_ref
):
    landed = landed_ref[0]
    for k in range(1, landed_ref.shape[0]):
        landed = landed + landed_ref[k]
    cot = vcot_ref[...] + landed
    v = v_ref[...]
    volt_ref[...] = cot * factor_ref[...] + sum_ref[...]
    half = TIME_STEP * cot
    for g in range(base_ref.shape[0]):
        gate_ref[g] = base_ref[g] - (cond_ref[g] * half) * (v - rev_ref[g])


def both_ways(up, down, axis):
    count = lax.axis_size(axis)
    low = lax.ppermute(up, axis, [(i, i + 1) for i in range(count - 1)])
    high = lax.ppermute(down, axis, [(i + 1, i) for i in range(count - 1)])
    return low, high


def reduce_over(value, axis):
    count = lax.axis_size(axis)
    step = 1
    while step < count:
        value = value + lax.ppermute(value, axis, [(i, i ^ step) for i in range(count)])
        step *= 2
    return value


def local(
    potential_cot, damping, tissue_label, heart_index, voltage, gates, voltage_cot, gates_cot,
    half_voltage, gate_slope, tau_base, conductance, reversal,
):
    nx, ny, nz = potential_cot.shape
    rows = nx * ny
    ring = ny + SUB
    n_gx, n_gy = lax.axis_size("gx"), lax.axis_size("gy")
    n_states = gates.shape[0]
    block_rows = voltage.shape[1] // LANES
    slot_rows = heart_index.shape[3] // LANES
    block = shape_of(nx, ny, nz)
    flat = lambda a: a.reshape(rows, LANES)
    cells = lambda a: a.reshape(block_rows, LANES)
    states = lambda a: a.reshape(n_states, block_rows, LANES)

    w0, inv, packed, stat = call(
        start_kernel, (block, block, shape_of(2, ny, nz), shape_of(2, SUB, nz)), 3
    )(potential_cot, damping, tissue_label)

    got = lax.ppermute(packed, "gz", [(0, 1), (1, 0)])
    base, total_change, factor = call(
        membrane_kernel,
        (shape_of(n_states, block_rows, LANES), shape_of(block_rows, LANES), shape_of(block_rows, LANES)),
        7,
        specs=[SMEM] * 4 + [VMEM] * 3,
        cost=6_000_000,
    )(half_voltage, gate_slope, tau_base, conductance, cells(voltage), states(gates), states(gates_cot))
    plan = call(plan_kernel, jax.ShapeDtypeStruct((rows, LANES), jnp.int32), 1, cost=6_000_000)(flat(tissue_label))

    face = shape_of(nx + 1, SUB, nz)
    slab_shape = shape_of(2, ny, nz)
    ring_shapes = (shape_of(nx, ring, nz), shape_of(nx, ring, nz), shape_of(2, ring, nz))
    x_shapes = ring_shapes + (shape_of(6, ring, nz), shape_of(6, ring, nz))
    if n_gy == 2:
        slab, mine = call(y_face_one_kernel, (slab_shape, face), 4)(w0, inv, packed, got)
        halo = (lax.ppermute(mine, "gy", [(0, 1), (1, 0)]),)
    else:
        slab, up, down = call(y_faces_kernel, (slab_shape, face, face), 4)(w0, inv, packed, got)
        halo = both_ways(up, down, "gy")
    wide, wide_inv, ring_slab, up, down = call(
        functools.partial(x_faces_kernel, n_gy == 2), x_shapes, 3 + len(halo)
    )(w0, inv, slab, *halo)
    low, high = both_ways(up, down, "gx")

    w1, w2, f0, f1, f2, sums = call(
        stencil_kernel,
        (block,) * 5 + (shape_of(16, nz),),
        6,
        scratch=[
            pltpu.VMEM((nx + 4, ring, nz), F32),
            pltpu.VMEM((nx + 2, ring, nz), F32),
            pltpu.VMEM((ring, 2 * nz), F32),
        ],
    )(wide, wide_inv, ring_slab, low, high, stat)
    for axis in ("gz", "gy", "gx"):
        sums = reduce_over(sums, axis)

    solution, placed = call(
        functools.partial(combine_kernel, slot_rows),
        (shape_of(rows, LANES), shape_of(n_gx * block_rows, LANES)),
        8,
        scratch=[pltpu.VMEM((n_gx * block_rows + slot_rows + SUB, LANES), F32)],
    )(sums, flat(w0), flat(w1), flat(w2), flat(f0), flat(f1), flat(f2), plan)
    landed = lax.all_to_all(placed.reshape(n_gx, block_rows, LANES), "gx", 0, 0, tiled=True)

    volt_grad, gate_grad = call(
        finish_kernel,
        (shape_of(block_rows, LANES), shape_of(n_states, block_rows, LANES)),
        8,
        specs=[SMEM] * 2 + [VMEM] * 6,
    )(conductance, reversal, landed, cells(voltage_cot), cells(voltage), total_change, factor, base)
    return solution.reshape(nx, ny, nz), volt_grad.reshape(voltage.shape), gate_grad.reshape(gates.shape)


def solution(mesh):
    grid = P(("groups", "gx"), "gy", "gz")
    cells = P(("groups", "gy", "gz"), "gx")
    states = P(None, ("groups", "gy", "gz"), "gx")
    in_specs = (
        grid, grid, grid, P(("groups", "gx"), "gy", "gz", None), cells, states, cells, states,
        P(), P(), P(), P(), P(),
    )
    return jax.shard_map(
        local, mesh=mesh, in_specs=in_specs, out_specs=(grid, cells, states), check_vma=False
    )
```

```python
import functools

import jax
import jax.numpy as jnp
from jax import lax
from jax.experimental import pallas as pl
from jax.experimental.pallas import tpu as pltpu
from jax.sharding import PartitionSpec as P

TIME_STEP = 0.5
LANES = 128
SUB = 8
PACK = 8
F32 = jnp.float32

VMEM = pl.BlockSpec(memory_space=pltpu.VMEM)
SMEM = pl.BlockSpec(memory_space=pltpu.SMEM)
HBM = pl.BlockSpec(memory_space=pltpu.HBM)


def shape_of(*dims):
    return jax.ShapeDtypeStruct(dims, F32)


def call(kernel, out_shape, n_in, specs=None, scratch=(), cost=2_000_000, limit=32):
    return pl.pallas_call(
        kernel,
        out_shape=out_shape,
        in_specs=specs if specs is not None else [VMEM] * n_in,
        out_specs=jax.tree.map(lambda _: VMEM, out_shape),
        scratch_shapes=list(scratch),
        compiler_params=pltpu.CompilerParams(vmem_limit_bytes=limit * 1024 * 1024),
        cost_estimate=pl.CostEstimate(flops=cost, bytes_accessed=cost, transcendentals=0),
    )


def lanes_of(shape):
    return lax.broadcasted_iota(jnp.int32, shape, len(shape) - 1)


def subs_of(shape):
    return lax.broadcasted_iota(jnp.int32, shape, len(shape) - 2)


def start_kernel(
    right_hbm, damping_hbm, label_hbm, w0_ref, inv_ref, pack_ref, stat_ref, right_ref, damping_ref, label_ref, sems
):
    nx, ny, nz = right_ref.shape
    parts = sems.shape[1]
    size = nx // parts
    copies = []
    for part in range(parts):
        here = pl.ds(part * size, size)
        for k, (source, target) in enumerate(
            ((right_hbm, right_ref), (damping_hbm, damping_ref), (label_hbm, label_ref))
        ):
            copies.append(pltpu.make_async_copy(source.at[here], target.at[here], sems.at[k, part]))
            copies[-1].start()
    gz = lax.axis_index("gz")
    lane = lanes_of((ny, nz))
    packed_w = jnp.zeros((ny, nz), F32)
    packed_i = jnp.zeros((ny, nz), F32)
    energy = jnp.zeros((ny, nz), F32)
    cells = jnp.zeros((ny, nz), F32)
    for x in range(nx):
        if x % size == 0:
            for k in range(3):
                copies[3 * (x // size) + k].wait()
        label = label_ref[x].astype(F32)
        right = right_ref[x]
        inv = 1.0 / (12.0 + damping_ref[x] * (1.0 + 3.0 * label))
        w0 = right * inv
        w0_ref[x] = w0
        inv_ref[x] = inv
        energy = energy + right * w0
        cells = cells + label
        turn = (PACK * x + 3) % nz
        begin = PACK * x + 3 * gz
        chosen = (lane >= begin) & (lane < begin + 3)
        packed_w = jnp.where(chosen, pltpu.roll(w0, turn, 1), packed_w)
        packed_i = jnp.where(chosen, pltpu.roll(inv, turn, 1), packed_i)
    pack_ref[0] = packed_w
    pack_ref[1] = packed_i
    stat_ref[0] = jnp.broadcast_to(jnp.sum(energy, axis=0, keepdims=True), (SUB, nz))
    stat_ref[1] = jnp.broadcast_to(jnp.sum(cells, axis=0, keepdims=True), (SUB, nz))


def y_faces_kernel(w0_ref, inv_ref, own_ref, got_ref, slab_ref, up_ref, down_ref):
    nx, ny, nz = w0_ref.shape
    sub = subs_of((SUB, nz))
    slab_ref[...] = own_ref[...] + got_ref[...]
    for x in range(nx + 1):
        if x < nx:
            w_last, w_first = w0_ref[x, ny - SUB :], w0_ref[x, :SUB]
            i_last, i_first = inv_ref[x, ny - SUB :], inv_ref[x, :SUB]
        else:
            w_last, w_first = slab_ref[0, ny - SUB :], slab_ref[0, :SUB]
            i_last, i_first = slab_ref[1, ny - SUB :], slab_ref[1, :SUB]
        up_ref[x] = jnp.where(sub >= 5, w_last, pltpu.roll(i_last, 4, 0))
        down_ref[x] = jnp.where(sub <= 2, w_first, pltpu.roll(i_first, 4, 0))


def y_face_one_kernel(w0_ref, inv_ref, own_ref, got_ref, slab_ref, face_ref):
    nx, ny, nz = w0_ref.shape
    sub = subs_of((SUB, nz))
    up = lax.axis_index("gy") == 0
    keep_w = jnp.where(up, sub, SUB - 1 - sub) >= 5
    slab_ref[...] = own_ref[...] + got_ref[...]
    for x in range(nx + 1):
        if x < nx:
            w_last, w_first = w0_ref[x, ny - SUB :], w0_ref[x, :SUB]
            i_last, i_first = inv_ref[x, ny - SUB :], inv_ref[x, :SUB]
        else:
            w_last, w_first = slab_ref[0, ny - SUB :], slab_ref[0, :SUB]
            i_last, i_first = slab_ref[1, ny - SUB :], slab_ref[1, :SUB]
        w_face = jnp.where(up, w_last, w_first)
        i_face = jnp.where(up, i_last, i_first)
        face_ref[x] = jnp.where(keep_w, w_face, pltpu.roll(i_face, 4, 0))


def x_faces_kernel(one, w0_ref, inv_ref, slab_ref, *refs):
    if one:
        got_ref, w_ref, i_ref, ring_ref, first_ref, second_ref = refs
    else:
        low_ref, high_ref, w_ref, i_ref, ring_ref, first_ref, second_ref = refs
    nx, ny, nz = w0_ref.shape
    sub = subs_of((SUB, nz))
    lane = lanes_of((ny + SUB, nz))
    if one:
        gy = lax.axis_index("gy")
        from_low = (gy == 1) & (sub >= 5)
        from_high = (gy == 0) & (sub <= 2)
        inv_low = (gy == 1) & (sub >= 6)
        inv_high = (gy == 0) & (sub <= 1)
    for x in range(nx + 1):
        if one:
            got = got_ref[x]
            turned = pltpu.roll(got, 4, 0)
            w_halo = jnp.where(from_low | from_high, got, 0.0)
            i_halo = jnp.where(inv_low | inv_high, turned, 0.0)
        else:
            low, high = low_ref[x], high_ref[x]
            w_halo = jnp.where(sub >= 5, low, jnp.where(sub <= 2, high, 0.0))
            i_halo = jnp.where(
                sub >= 6, pltpu.roll(low, 4, 0), jnp.where(sub <= 1, pltpu.roll(high, 4, 0), 0.0)
            )
        if x < nx:
            w_ref[x, :ny] = w0_ref[x]
            w_ref[x, ny:] = w_halo
            i_ref[x, :ny] = inv_ref[x]
            i_ref[x, ny:] = i_halo
        else:
            ring_ref[0, :ny] = slab_ref[0]
            ring_ref[0, ny:] = w_halo
            ring_ref[1, :ny] = slab_ref[1]
            ring_ref[1, ny:] = i_halo
    odd = lax.rem(lax.axis_index("gx"), 2)
    half = pltpu.roll(ring_ref[1], nz // 2, 1)
    up = jnp.where(lane >= nz - 3 * PACK, ring_ref[0], half)
    down = jnp.where(lane < 3 * PACK, ring_ref[0], half)
    for face_ref, lower in ((first_ref, odd), (second_ref, 1 - odd)):
        for k in range(3):
            face_ref[k] = w_ref[(1 - lower) * (nx - 3) + k]
        for k in range(2):
            face_ref[3 + k] = i_ref[(1 - lower) * (nx - 2) + k]
        face_ref[5] = jnp.where(lower == 1, down, up)


def around(v):
    rows = v.shape[0]
    return pltpu.roll(v, 1, 0) + pltpu.roll(v, rows - 1, 0)


def stencil_kernel(
    w_ref, i_ref, ring_ref, first_ref, second_ref, stat_ref,
    w1_ref, w2_ref, f0_ref, f1_ref, f2_ref, total_ref,
    a_ref, b_ref, sw_ref,
):
    nx, ring, nz = w_ref.shape
    ny = ring - SUB
    gz = lax.axis_index("gz")
    lane = lanes_of((ring, nz))
    entry = (nz - 1) * gz
    at_entry = lane == entry
    lane_first = lane == 0
    lane_last = lane == nz - 1

    odd = lax.rem(lax.axis_index("gx"), 2) == 1

    def low(k):
        return jnp.where(odd, first_ref[k], second_ref[k])

    def high(k):
        return jnp.where(odd, second_ref[k], first_ref[k])

    def w0_plane(x):
        if x < 0:
            return low(3 + x)
        if x >= nx:
            return high(x - nx)
        return w_ref[x]

    def inv_plane(x):
        if x < 0:
            return low(5 + x)
        if x >= nx:
            return high(3 + x - nx)
        return i_ref[x]

    lo5, hi5 = low(5), high(5)
    slab_w = jnp.where(lane < 3 * PACK, hi5, 0.0) + jnp.where(lane >= nz - 3 * PACK, lo5, 0.0)
    lo5, hi5 = pltpu.roll(lo5, nz // 2, 1), pltpu.roll(hi5, nz // 2, 1)
    slab_i = jnp.where(lane < 2 * PACK, hi5, 0.0) + jnp.where(lane >= nz - 2 * PACK, lo5, 0.0)
    slab = jnp.concatenate([ring_ref[0], slab_w], axis=1)
    slab_inv = jnp.concatenate([ring_ref[1], slab_i], axis=1)

    def slab_step(s):
        width = s.shape[1]
        along = pltpu.roll(s, 1, 1) + pltpu.roll(s, width - 1, 1)
        both = s + 0.5 * along
        wing = both + 0.5 * around(s)
        total = along + around(both) + pltpu.roll(wing, PACK, 1) + pltpu.roll(wing, width - PACK, 1)
        return total * slab_inv

    def sweep(source, margin, face_ref, store):
        wing_before = wing_here = rest_here = None
        v_before = v_here = face_here = None
        for x in range(-margin - 1, nx + margin + 1):
            v = source(x)
            place = (PACK * x) % (2 * nz)
            half = sw_ref[:, nz * (place // nz) : nz * (place // nz) + nz]
            turn = lax.rem(entry - (place % nz + 3 - gz) + 2 * nz, nz)
            edge = jnp.where(at_entry, pltpu.roll(half, turn, 1), 0.0)
            along = pltpu.roll(jnp.where(lane_first, edge, v), nz - 1, 1) + pltpu.roll(
                jnp.where(lane_last, edge, v), 1, 1
            )
            both = v + 0.5 * along
            beside = around(v)
            wing = both + 0.5 * beside
            rest = along + around(both)
            done = x - 1
            if done >= -margin:
                store(done, rest_here + wing_before + wing, v_here)
                if 0 <= done < nx:
                    face_ref[done] = face_here + (v_before + v)[:ny]
            wing_before, wing_here, rest_here = wing_here, wing, rest
            v_before, v_here = v_here, v
            if 0 <= x < nx:
                face_here = (along + beside - 6.0 * v)[:ny]

    sums = {}

    def add(name, value):
        part = jnp.sum(value[:ny].reshape(ny // SUB, SUB, nz), axis=0)
        sums[name] = part if name not in sums else sums[name] + part

    def store0(x, total, v):
        w1 = total * inv_plane(x)
        a_ref[x + 2] = w1
        if 0 <= x < nx:
            w1_ref[x] = w1[:ny]
            add(1, v * total)
            add(2, w1 * total)

    def store1(x, total, v):
        w2 = total * inv_plane(x)
        b_ref[x + 1] = w2
        if 0 <= x < nx:
            w2_ref[x] = w2[:ny]
            add(3, v * total)
            add(4, w2 * total)

    def store2(x, total, v):
        add(5, v * total)

    sw_ref[...] = slab
    sweep(w0_plane, 2, f0_ref, store0)
    slab = slab_step(slab)
    sw_ref[...] = slab
    sweep(lambda x: a_ref[x + 2], 1, f1_ref, store1)
    slab = slab_step(slab)
    sw_ref[...] = slab
    sweep(lambda x: b_ref[x + 1], 0, f2_ref, store2)

    total_ref[0:1] = stat_ref[0, 0:1]
    for k in range(1, 6):
        total_ref[k : k + 1] = jnp.sum(sums[k], axis=0, keepdims=True)
    total_ref[6:8] = jnp.zeros((2, nz), F32)
    here = (lax.axis_index("gx") * lax.axis_size("gy") + lax.axis_index("gy")) * lax.axis_size("gz") + gz
    count = jnp.sum(stat_ref[1], axis=1, keepdims=True)
    total_ref[8:16] = jnp.where(lanes_of((SUB, nz)) == here, count, 0.0)


def shift_left(v, amount, lane):
    rows = v.shape[0]
    if amount < LANES:
        turned = pltpu.roll(v, LANES - amount, 1)
        below = pltpu.roll(turned, rows - 1, 0)
        return jnp.where(lane < LANES - amount, turned, below)
    return jnp.concatenate([v[amount // LANES :], v[: amount // LANES]], axis=0)


def plan_kernel(label_ref, plan_ref):
    rows = label_ref.shape[0]
    lane = lanes_of((rows, LANES))
    row = subs_of((rows, LANES))
    heart = label_ref[...] == 1
    ones = heart.astype(jnp.bfloat16)
    upper = (subs_of((LANES, LANES)) < lanes_of((LANES, LANES))).astype(jnp.bfloat16)
    in_row = jnp.dot(ones, upper, preferred_element_type=F32)
    totals = jnp.dot(ones, jnp.ones((LANES, LANES), jnp.bfloat16), preferred_element_type=F32)
    lower = (subs_of((rows, rows)) > lanes_of((rows, rows))).astype(jnp.bfloat16)
    before = jnp.dot(lower, totals.astype(jnp.bfloat16), preferred_element_type=F32)
    rank = (in_row + before).astype(jnp.int32)
    way = jnp.where(heart, row * LANES + lane - rank, 0)
    plan = jnp.zeros((rows, LANES), jnp.int32)
    step = 1
    while step < rows * LANES:
        moving = jnp.where((way & step) != 0, way, 0)
        arriving = shift_left(moving, step, lane)
        plan = plan | (arriving & step)
        way = (way - moving) | arriving
        step *= 2
    plan_ref[...] = plan


def galerkin(t):
    g00, g01, g02, g12, g22 = t[0] - t[1], t[1] - t[2], t[2] - t[3], t[3] - t[4], t[4] - t[5]
    g11 = g02
    l10, l20 = g01 / g00, g02 / g00
    d1 = g11 - l10 * g01
    m21 = g12 - l20 * g01
    ok1 = d1 > 1e-6 * g11
    d1 = jnp.where(ok1, d1, 1.0)
    l21 = jnp.where(ok1, m21 / d1, 0.0)
    d2 = g22 - l20 * g02 - l21 * m21
    ok2 = ok1 & (d2 > 1e-6 * g22)
    d2 = jnp.where(ok2, d2, 1.0)
    y1 = t[1] - l10 * t[0]
    y2 = t[2] - l20 * t[0] - l21 * y1
    c2 = jnp.where(ok2, y2 / d2, 0.0)
    c1 = jnp.where(ok1, y1 / d1 - l21 * c2, 0.0)
    c0 = t[0] / g00 - l10 * c1 - l20 * c2
    return c0, c1, c2


def combine_kernel(
    slot_rows, total_ref, w0_ref, w1_ref, w2_ref, f0_ref, f1_ref, f2_ref, plan_ref, x_ref, *out_refs
):
    rows = w0_ref.shape[0]
    lane = lanes_of((rows, LANES))
    row = subs_of((rows, LANES))
    sums = jnp.sum(total_ref[0:8], axis=1, keepdims=True)
    t = [jnp.broadcast_to(sums[k : k + 1], (1, LANES)) for k in range(6)]
    c0, c1, c2 = galerkin(t)
    x_ref[...] = c0 * w0_ref[...] + c1 * w1_ref[...] + c2 * w2_ref[...]
    value = c0 * f0_ref[...] + c1 * f1_ref[...] + c2 * f2_ref[...]
    plan = plan_ref[...]
    step = 1
    while step < rows * LANES:
        value = jnp.where((plan & step) != 0, shift_left(value, step, lane), value)
        step *= 2
    ny, nz = lax.axis_size("gy"), lax.axis_size("gz")
    counts = total_ref[8:16]
    dev = lanes_of((SUB, LANES))
    column = lax.axis_index("gy") * nz + lax.axis_index("gz")
    mine = lax.rem(dev, ny * nz) == column
    gx = lax.axis_index("gx")
    first = subs_of((SUB, LANES)) == 0
    offset = jnp.sum(jnp.where(first & mine & (dev < gx * ny * nz), counts, 0.0)).astype(jnp.int32)
    count = jnp.sum(jnp.where(first & mine & (dev // (ny * nz) == gx), counts, 0.0)).astype(jnp.int32)
    slots = value[:slot_rows]
    index = (row * LANES + lane)[:slot_rows]
    slots = jnp.where(index < count, slots, 0.0)
    slots = jnp.concatenate([slots, jnp.zeros((SUB, LANES), F32)], axis=0)
    inner = lax.rem(offset, LANES)
    turned = pltpu.roll(slots, inner, 1)
    above = pltpu.roll(turned, 1, 0)
    moved = jnp.where(lane[: slot_rows + SUB] >= inner, turned, above)
    *out_refs, buf_ref = out_refs
    buf_ref[...] = jnp.zeros_like(buf_ref)
    buf_ref[pl.ds(offset // LANES, slot_rows + SUB), :] = moved
    for k, out_ref in enumerate(out_refs):
        size = out_ref.shape[0]
        out_ref[...] = buf_ref[pl.ds(pl.multiple_of((gx ^ k) * size, SUB), size), :]


def membrane_kernel(
    half_ref, slope_ref, tau_ref, cond_ref, rev_ref, v_ref, gates_ref, cot_ref,
    base_ref, sum_ref, factor_ref, coef_ref,
):
    n_states = gates_ref.shape[0]
    v = v_ref[...]
    rows = v.shape[0]

    def state(g, carry):
        total, current = carry
        inv_slope = 1.0 / slope_ref[g]
        tau_base = tau_ref[g]
        scaled = (v - half_ref[g]) * inv_slope
        gate = gates_ref[g]
        cot = cot_ref[g]
        steady = 1.0 / (1.0 + jnp.exp(-scaled))
        bell = jnp.exp(-scaled * scaled)
        rate = TIME_STEP / (tau_base * (0.5 + bell))
        decay = jnp.exp(-rate)
        steady_slope = steady * (1.0 - steady)
        decay_slope = decay * rate * rate * ((tau_base / TIME_STEP) * bell * (-2.0 * scaled))
        change = (steady_slope * (1.0 - decay) + (gate - steady) * decay_slope) * inv_slope
        base_ref[g] = cot * decay
        coef_ref[0, pl.ds(g, 1)] = jnp.full((1, LANES), TIME_STEP * cond_ref[g])
        coef_ref[1, pl.ds(g, 1)] = jnp.full((1, LANES), rev_ref[g])
        return total + cot * change, current + cond_ref[g] * gate

    zero = jnp.zeros((rows, LANES), F32)
    total, current = lax.fori_loop(0, n_states, state, (zero, zero), unroll=2)
    sum_ref[...] = total
    factor_ref[...] = 1.0 - TIME_STEP * current


def finish_kernel(coef_ref, vcot_ref, v_ref, sum_ref, factor_ref, base_ref, *refs):
    *landed_refs, volt_ref, gate_ref = refs
    landed = landed_refs[0][...]
    for ref in landed_refs[1:]:
        landed = landed + ref[...]
    cot = vcot_ref[...] + landed
    v = v_ref[...]
    volt_ref[...] = cot * factor_ref[...] + sum_ref[...]
    for g in range(base_ref.shape[0]):
        gate_ref[g] = base_ref[g] - (coef_ref[0, g : g + 1] * cot) * (v - coef_ref[1, g : g + 1])


def both_ways(up, down, axis):
    count = lax.axis_size(axis)
    low = lax.ppermute(up, axis, [(i, i + 1) for i in range(count - 1)])
    high = lax.ppermute(down, axis, [(i + 1, i) for i in range(count - 1)])
    return low, high


def pair_swaps(first, second, axis):
    count = lax.axis_size(axis)
    even = [(i, i ^ 1) for i in range(count)]
    between = [(i, i + 1) for i in range(1, count - 1, 2)]
    between = between + [(j, i) for i, j in between]
    return lax.ppermute(first, axis, even), lax.ppermute(second, axis, between)


def reduce_over(value, axis):
    count = lax.axis_size(axis)
    step = 1
    while step < count:
        value = value + lax.ppermute(value, axis, [(i, i ^ step) for i in range(count)])
        step *= 2
    return value


def local(
    potential_cot, damping, tissue_label, heart_index, voltage, gates, voltage_cot, gates_cot,
    half_voltage, gate_slope, tau_base, conductance, reversal,
):
    nx, ny, nz = potential_cot.shape
    rows = nx * ny
    ring = ny + SUB
    n_gx, n_gy = lax.axis_size("gx"), lax.axis_size("gy")
    n_states = gates.shape[0]
    block_rows = voltage.shape[1] // LANES
    slot_rows = heart_index.shape[3] // LANES
    block = shape_of(nx, ny, nz)
    flat = lambda a: a.reshape(rows, LANES)
    cells = lambda a: a.reshape(block_rows, LANES)
    states = lambda a: a.reshape(n_states, block_rows, LANES)

    w0, inv, packed, stat = call(
        start_kernel, (block, block, shape_of(2, ny, nz), shape_of(2, SUB, nz)), 3,
        specs=[HBM] * 3,
        scratch=[
            pltpu.VMEM((nx, ny, nz), F32), pltpu.VMEM((nx, ny, nz), F32), pltpu.VMEM((nx, ny, nz), jnp.int32),
            pltpu.SemaphoreType.DMA((3, 4)),
        ],
    )(*[pltpu.with_memory_space_constraint(a, pltpu.HBM) for a in (potential_cot, damping, tissue_label)])

    got = lax.ppermute(packed, "gz", [(0, 1), (1, 0)])
    base, total_change, factor, coefs = call(
        membrane_kernel,
        (
            shape_of(n_states, block_rows, LANES), shape_of(block_rows, LANES), shape_of(block_rows, LANES),
            shape_of(2, n_states, LANES),
        ),
        8,
        specs=[SMEM] * 5 + [VMEM] * 3,
        cost=6_000_000,
    )(half_voltage, gate_slope, tau_base, conductance, reversal, cells(voltage), states(gates), states(gates_cot))
    plan = call(plan_kernel, jax.ShapeDtypeStruct((rows, LANES), jnp.int32), 1, cost=6_000_000)(flat(tissue_label))

    face = shape_of(nx + 1, SUB, nz)
    slab_shape = shape_of(2, ny, nz)
    ring_shapes = (shape_of(nx, ring, nz), shape_of(nx, ring, nz), shape_of(2, ring, nz))
    x_shapes = ring_shapes + (shape_of(6, ring, nz), shape_of(6, ring, nz))
    if n_gy == 2:
        slab, mine = call(y_face_one_kernel, (slab_shape, face), 4)(w0, inv, packed, got)
        halo = (lax.ppermute(mine, "gy", [(0, 1), (1, 0)]),)
    else:
        slab, up, down = call(y_faces_kernel, (slab_shape, face, face), 4)(w0, inv, packed, got)
        halo = both_ways(up, down, "gy")
    wide, wide_inv, ring_slab, first, second = call(
        functools.partial(x_faces_kernel, n_gy == 2), x_shapes, 3 + len(halo)
    )(w0, inv, slab, *halo)
    first, second = pair_swaps(first, second, "gx")

    w1, w2, f0, f1, f2, sums = call(
        stencil_kernel,
        (block,) * 5 + (shape_of(16, nz),),
        6,
        scratch=[
            pltpu.VMEM((nx + 4, ring, nz), F32),
            pltpu.VMEM((nx + 2, ring, nz), F32),
            pltpu.VMEM((ring, 2 * nz), F32),
        ],
    )(wide, wide_inv, ring_slab, first, second, stat)
    for axis in ("gz", "gy", "gx"):
        sums = reduce_over(sums, axis)

    solution, *blocks = call(
        functools.partial(combine_kernel, slot_rows),
        (shape_of(rows, LANES),) + (shape_of(block_rows, LANES),) * n_gx,
        8,
        scratch=[pltpu.VMEM((n_gx * block_rows + slot_rows + SUB, LANES), F32)],
    )(sums, flat(w0), flat(w1), flat(w2), flat(f0), flat(f1), flat(f2), plan)
    landed = blocks[:1] + [
        lax.ppermute(blocks[k], "gx", [(i, i ^ k) for i in range(n_gx)]) for k in range(1, n_gx)
    ]

    volt_grad, gate_grad = call(
        finish_kernel,
        (shape_of(block_rows, LANES), shape_of(n_states, block_rows, LANES)),
        6 + n_gx,
    )(coefs, cells(voltage_cot), cells(voltage), total_change, factor, base, *landed)
    return solution.reshape(nx, ny, nz), volt_grad.reshape(voltage.shape), gate_grad.reshape(gates.shape)


def solution(mesh):
    grid = P(("groups", "gx"), "gy", "gz")
    cells = P(("groups", "gy", "gz"), "gx")
    states = P(None, ("groups", "gy", "gz"), "gx")
    in_specs = (
        grid, grid, grid, P(("groups", "gx"), "gy", "gz", None), cells, states, cells, states,
        P(), P(), P(), P(), P(),
    )
    return jax.shard_map(
        local, mesh=mesh, in_specs=in_specs, out_specs=(grid, cells, states), check_vma=False
    )
```

```python
import functools

import jax
import jax.numpy as jnp
from jax import lax
from jax.experimental import pallas as pl
from jax.experimental.pallas import tpu as pltpu
from jax.sharding import PartitionSpec as P

TIME_STEP = 0.5
LANES = 128
SUB = 8
PACK = 8
F32 = jnp.float32

VMEM = pl.BlockSpec(memory_space=pltpu.VMEM)
SMEM = pl.BlockSpec(memory_space=pltpu.SMEM)
HBM = pl.BlockSpec(memory_space=pltpu.HBM)


def shape_of(*dims):
    return jax.ShapeDtypeStruct(dims, F32)


def call(kernel, out_shape, n_in, specs=None, outs=None, scratch=(), cost=2_000_000, limit=32):
    return pl.pallas_call(
        kernel,
        out_shape=out_shape,
        in_specs=specs if specs is not None else [VMEM] * n_in,
        out_specs=outs if outs is not None else jax.tree.map(lambda _: VMEM, out_shape),
        scratch_shapes=list(scratch),
        compiler_params=pltpu.CompilerParams(vmem_limit_bytes=limit * 1024 * 1024),
        cost_estimate=pl.CostEstimate(flops=cost, bytes_accessed=cost, transcendentals=0),
    )


def in_hbm(array):
    return pltpu.with_memory_space_constraint(array, pltpu.HBM)


def lanes_of(shape):
    return lax.broadcasted_iota(jnp.int32, shape, len(shape) - 1)


def subs_of(shape):
    return lax.broadcasted_iota(jnp.int32, shape, len(shape) - 2)


def start_kernel(
    right_hbm, damping_hbm, label_hbm, w0_ref, inv_ref, pack_ref, stat_ref, right_ref, damping_ref, label_ref, sems
):
    nx, ny, nz = right_ref.shape
    parts = sems.shape[1]
    size = nx // parts
    copies = []
    for part in range(parts):
        here = pl.ds(part * size, size)
        for k, (source, target) in enumerate(
            ((right_hbm, right_ref), (damping_hbm, damping_ref), (label_hbm, label_ref))
        ):
            copies.append(pltpu.make_async_copy(source.at[here], target.at[here], sems.at[k, part]))
            copies[-1].start()
    gz = lax.axis_index("gz")
    lane = lanes_of((ny, nz))
    packed_w = jnp.zeros((ny, nz), F32)
    packed_i = jnp.zeros((ny, nz), F32)
    energy = jnp.zeros((ny, nz), F32)
    cells = jnp.zeros((ny, nz), F32)
    for x in range(nx):
        if x % size == 0:
            for k in range(3):
                copies[3 * (x // size) + k].wait()
        label = label_ref[x].astype(F32)
        right = right_ref[x]
        inv = 1.0 / (12.0 + damping_ref[x] * (1.0 + 3.0 * label))
        w0 = right * inv
        w0_ref[x] = w0
        inv_ref[x] = inv
        energy = energy + right * w0
        cells = cells + label
        turn = (PACK * x + 3) % nz
        begin = PACK * x + 3 * gz
        chosen = (lane >= begin) & (lane < begin + 3)
        packed_w = jnp.where(chosen, pltpu.roll(w0, turn, 1), packed_w)
        packed_i = jnp.where(chosen, pltpu.roll(inv, turn, 1), packed_i)
    pack_ref[0] = packed_w
    pack_ref[1] = packed_i
    stat_ref[0] = jnp.broadcast_to(jnp.sum(energy, axis=0, keepdims=True), (SUB, nz))
    stat_ref[1] = jnp.broadcast_to(jnp.sum(cells, axis=0, keepdims=True), (SUB, nz))


def y_faces_kernel(w0_ref, inv_ref, own_ref, got_ref, slab_ref, up_ref, down_ref):
    nx, ny, nz = w0_ref.shape
    sub = subs_of((SUB, nz))
    slab_ref[...] = own_ref[...] + got_ref[...]
    for x in range(nx + 1):
        if x < nx:
            w_last, w_first = w0_ref[x, ny - SUB :], w0_ref[x, :SUB]
            i_last, i_first = inv_ref[x, ny - SUB :], inv_ref[x, :SUB]
        else:
            w_last, w_first = slab_ref[0, ny - SUB :], slab_ref[0, :SUB]
            i_last, i_first = slab_ref[1, ny - SUB :], slab_ref[1, :SUB]
        up_ref[x] = jnp.where(sub >= 5, w_last, pltpu.roll(i_last, 4, 0))
        down_ref[x] = jnp.where(sub <= 2, w_first, pltpu.roll(i_first, 4, 0))


def y_face_one_kernel(w0_ref, inv_ref, own_ref, got_ref, slab_ref, face_ref):
    nx, ny, nz = w0_ref.shape
    sub = subs_of((SUB, nz))
    up = lax.axis_index("gy") == 0
    keep_w = jnp.where(up, sub, SUB - 1 - sub) >= 5
    slab_ref[...] = own_ref[...] + got_ref[...]
    for x in range(nx + 1):
        if x < nx:
            w_last, w_first = w0_ref[x, ny - SUB :], w0_ref[x, :SUB]
            i_last, i_first = inv_ref[x, ny - SUB :], inv_ref[x, :SUB]
        else:
            w_last, w_first = slab_ref[0, ny - SUB :], slab_ref[0, :SUB]
            i_last, i_first = slab_ref[1, ny - SUB :], slab_ref[1, :SUB]
        w_face = jnp.where(up, w_last, w_first)
        i_face = jnp.where(up, i_last, i_first)
        face_ref[x] = jnp.where(keep_w, w_face, pltpu.roll(i_face, 4, 0))


def x_faces_kernel(one, w0_ref, inv_ref, slab_ref, *refs):
    if one:
        got_ref, halo_ref, first_ref, second_ref = refs
    else:
        low_ref, high_ref, halo_ref, first_ref, second_ref = refs
    nx, ny, nz = w0_ref.shape
    sub = subs_of((SUB, nz))
    lane = lanes_of((ny + SUB, nz))
    if one:
        gy = lax.axis_index("gy")
        w_rows = ((gy == 1) & (sub >= 5)) | ((gy == 0) & (sub <= 2))
        i_rows = ((gy == 1) & (sub >= 6)) | ((gy == 0) & (sub <= 1))
    for x in range(nx + 1):
        if one:
            got = got_ref[x]
            halo_ref[0, x] = jnp.where(w_rows, got, 0.0)
            halo_ref[1, x] = jnp.where(i_rows, pltpu.roll(got, 4, 0), 0.0)
        else:
            low, high = low_ref[x], high_ref[x]
            halo_ref[0, x] = jnp.where(sub >= 5, low, jnp.where(sub <= 2, high, 0.0))
            halo_ref[1, x] = jnp.where(
                sub >= 6, pltpu.roll(low, 4, 0), jnp.where(sub <= 1, pltpu.roll(high, 4, 0), 0.0)
            )
    odd = lax.rem(lax.axis_index("gx"), 2)
    slab_w = jnp.concatenate([slab_ref[0], halo_ref[0, nx]], axis=0)
    slab_i = jnp.concatenate([slab_ref[1], halo_ref[1, nx]], axis=0)
    half = pltpu.roll(slab_i, nz // 2, 1)
    up = jnp.where(lane >= nz - 3 * PACK, slab_w, half)
    down = jnp.where(lane < 3 * PACK, slab_w, half)
    for face_ref, lower in ((first_ref, odd), (second_ref, 1 - odd)):
        for k in range(5):
            field, source = (0, w0_ref) if k < 3 else (1, inv_ref)
            place = (1 - lower) * (nx - 3 + field) + k - 3 * field
            face_ref[k, :ny] = source[place]
            face_ref[k, ny:] = halo_ref[field, place]
        face_ref[5] = jnp.where(lower == 1, down, up)


def stencil_kernel(
    w0_ref, inv_ref, slab_ref, halo_ref, first_ref, second_ref, stat_ref,
    a_ref, b_ref, c_ref, slabs_ref, total_ref,
    i_ref, si_ref,
):
    nx, ny, nz = w0_ref.shape
    ring = ny + SUB
    gz = lax.axis_index("gz")
    odd = lax.rem(lax.axis_index("gx"), 2) == 1

    def low(k):
        return jnp.where(odd, first_ref[k], second_ref[k])

    def high(k):
        return jnp.where(odd, second_ref[k], first_ref[k])

    def place(ref, x, own, halo):
        ref[x, SUB : SUB + ny] = own
        ref[x, :SUB] = halo
        ref[x, SUB + ny :] = halo

    for x in range(nx):
        place(a_ref, 3 + x, w0_ref[x], halo_ref[0, x])
        place(i_ref, 2 + x, inv_ref[x], halo_ref[1, x])
    for k in range(3):
        for x, plane in ((k, low(k)), (nx + 3 + k, high(k))):
            place(a_ref, x, plane[:ny], plane[ny:])
    for k in range(2):
        for x, plane in ((k, low(3 + k)), (nx + 2 + k, high(3 + k))):
            place(i_ref, x, plane[:ny], plane[ny:])

    lane = lanes_of((ring, nz))
    lo5, hi5 = low(5), high(5)
    slab_w = jnp.where(lane < 3 * PACK, hi5, 0.0) + jnp.where(lane >= nz - 3 * PACK, lo5, 0.0)
    lo5, hi5 = pltpu.roll(lo5, nz // 2, 1), pltpu.roll(hi5, nz // 2, 1)
    slab_i = jnp.where(lane < 2 * PACK, hi5, 0.0) + jnp.where(lane >= nz - 2 * PACK, lo5, 0.0)
    for ref, at, k, beyond in ((slabs_ref, 0, 0, slab_w), (si_ref, 0, 1, slab_i)):
        ref[at, SUB : SUB + ny, :nz] = slab_ref[k]
        ref[at, SUB : SUB + ny, nz:] = beyond[:ny]
        for rows in (slice(0, SUB), slice(SUB + ny, SUB + ring)):
            ref[at, rows, :nz] = halo_ref[k, nx]
            ref[at, rows, nz:] = beyond[ny:]

    sums = {}

    def add(name, value, skip):
        value = value[skip : skip + ny]
        part = value[:SUB]
        for k in range(SUB, ny, SUB):
            part = part + value[k : k + SUB]
        sums[name] = part if name not in sums else sums[name] + part

    def rows_of(ref, x, start, size):
        return ref[x, start : start + size]

    for stage in range(3):
        source = (a_ref, b_ref, c_ref)[stage]
        target = (b_ref, c_ref, None)[stage]
        margin = 2 - stage
        start = SUB - margin
        size = ny if margin == 0 else ring
        lane = lanes_of((size, nz))
        entry = (nz - 1) * gz
        at_entry, lane_first, lane_last = lane == entry, lane == 0, lane == nz - 1

        width = 2 * nz
        v = slabs_ref[stage, start : start + size]
        s = slabs_ref[stage, start - 1 : start - 1 + size] + slabs_ref[stage, start + 1 : start + 1 + size]
        across = pltpu.roll(v, PACK, 1) + pltpu.roll(v, width - PACK, 1)
        slab_q = v + 0.5 * (s + across)
        if stage < 2:
            total = (
                pltpu.roll(slab_q, 1, 1) + pltpu.roll(slab_q, width - 1, 1) + s + across
                + 0.5 * (pltpu.roll(s, PACK, 1) + pltpu.roll(s, width - PACK, 1))
            )
            slabs_ref[stage + 1, start : start + size] = total * si_ref[0, start : start + size]

        def beside(x):
            return rows_of(source, x, start - 1, size) + rows_of(source, x, start + 1, size)

        s_low, s_mid = beside(0), beside(1)
        v_low, v_mid = rows_of(source, 0, start, size), rows_of(source, 1, start, size)
        for x in range(-margin, nx + margin):
            at = x + margin + 1
            v_high, s_high = rows_of(source, at + 1, start, size), beside(at + 1)
            across = v_low + v_high
            q = v_mid + 0.5 * (s_mid + across)
            column = (PACK * x) % width
            half = slab_q[:, column // nz * nz : column // nz * nz + nz]
            turn = lax.rem(entry - (column % nz + 3 - gz) + 2 * nz, nz)
            edge = jnp.where(at_entry, pltpu.roll(half, turn, 1), 0.0)
            along = pltpu.roll(jnp.where(lane_first, edge, q), nz - 1, 1) + pltpu.roll(
                jnp.where(lane_last, edge, q), 1, 1
            )
            total = along + s_mid + across + 0.5 * (s_low + s_high)
            if target is not None:
                after = total * rows_of(i_ref, x + 2, start, size)
                target[x + margin, start : start + size] = after
            if 0 <= x < nx:
                add(2 * stage + 1, v_mid * total, margin)
                if target is not None:
                    add(2 * stage + 2, after * total, margin)
            v_low, v_mid, s_low, s_mid = v_mid, v_high, s_mid, s_high

    total_ref[0:1] = stat_ref[0, 0:1]
    for k in range(1, 6):
        total_ref[k : k + 1] = jnp.sum(sums[k], axis=0, keepdims=True)
    total_ref[6:8] = jnp.zeros((2, nz), F32)
    here = (lax.axis_index("gx") * lax.axis_size("gy") + lax.axis_index("gy")) * lax.axis_size("gz") + gz
    count = jnp.sum(stat_ref[1], axis=1, keepdims=True)
    total_ref[8:16] = jnp.where(lanes_of((SUB, nz)) == here, count, 0.0)


def shift_left(v, amount, lane):
    rows = v.shape[0]
    if amount < LANES:
        turned = pltpu.roll(v, LANES - amount, 1)
        below = pltpu.roll(turned, rows - 1, 0)
        return jnp.where(lane < LANES - amount, turned, below)
    return jnp.concatenate([v[amount // LANES :], v[: amount // LANES]], axis=0)


def plan_kernel(label_ref, plan_ref):
    rows = label_ref.shape[0]
    lane = lanes_of((rows, LANES))
    row = subs_of((rows, LANES))
    heart = label_ref[...] == 1
    ones = heart.astype(jnp.bfloat16)
    upper = (subs_of((LANES, LANES)) < lanes_of((LANES, LANES))).astype(jnp.bfloat16)
    in_row = jnp.dot(ones, upper, preferred_element_type=F32)
    totals = jnp.dot(ones, jnp.ones((LANES, LANES), jnp.bfloat16), preferred_element_type=F32)
    lower = (subs_of((rows, rows)) > lanes_of((rows, rows))).astype(jnp.bfloat16)
    before = jnp.dot(lower, totals.astype(jnp.bfloat16), preferred_element_type=F32)
    rank = (in_row + before).astype(jnp.int32)
    way = jnp.where(heart, row * LANES + lane - rank, 0)
    plan = jnp.zeros((rows, LANES), jnp.int32)
    step = 1
    while step < rows * LANES:
        moving = jnp.where((way & step) != 0, way, 0)
        arriving = shift_left(moving, step, lane)
        plan = plan | (arriving & step)
        way = (way - moving) | arriving
        step *= 2
    plan_ref[...] = plan


def galerkin(t):
    g00, g01, g02, g12, g22 = t[0] - t[1], t[1] - t[2], t[2] - t[3], t[3] - t[4], t[4] - t[5]
    g11 = g02
    l10, l20 = g01 / g00, g02 / g00
    d1 = g11 - l10 * g01
    m21 = g12 - l20 * g01
    ok1 = d1 > 1e-6 * g11
    d1 = jnp.where(ok1, d1, 1.0)
    l21 = jnp.where(ok1, m21 / d1, 0.0)
    d2 = g22 - l20 * g02 - l21 * m21
    ok2 = ok1 & (d2 > 1e-6 * g22)
    d2 = jnp.where(ok2, d2, 1.0)
    y1 = t[1] - l10 * t[0]
    y2 = t[2] - l20 * t[0] - l21 * y1
    c2 = jnp.where(ok2, y2 / d2, 0.0)
    c1 = jnp.where(ok1, y1 / d1 - l21 * c2, 0.0)
    c0 = t[0] / g00 - l10 * c1 - l20 * c2
    return c0, c1, c2


def combine_kernel(slot_rows, total_ref, w0_ref, w1_ref, w2_ref, slabs_ref, plan_ref, x_hbm, *refs):
    *out_refs, wide_ref, x_ref, value_ref, buf_ref, sem = refs
    nx, ny, nz = x_ref.shape
    rows = nx * ny
    lane = lanes_of((rows, LANES))
    row = subs_of((rows, LANES))
    sums = jnp.sum(total_ref[0:8], axis=1, keepdims=True)
    t = [jnp.broadcast_to(sums[k : k + 1], (1, LANES)) for k in range(6)]
    c0, c1, c2 = galerkin(t)
    for x in range(nx + 2):
        wide_ref[x] = c0 * w0_ref[x + 2] + c1 * w1_ref[x + 1] + c2 * w2_ref[x]
    for x in range(nx):
        x_ref[x] = wide_ref[x + 1, SUB : SUB + ny]
    leave = pltpu.make_async_copy(x_ref, x_hbm, sem)
    leave.start()

    gz = lax.axis_index("gz")
    own = slice(SUB, SUB + ny)
    slab = c0 * slabs_ref[0, own, :nz] + c1 * slabs_ref[1, own, :nz] + c2 * slabs_ref[2, own, :nz]
    column = lanes_of((ny, nz))
    entry = (nz - 1) * gz
    at_entry, lane_first, lane_last = column == entry, column == 0, column == nz - 1
    for x in range(nx):
        v = wide_ref[x + 1, own]
        turn = lax.rem(entry - (PACK * x + 3 - gz) + 2 * nz, nz)
        edge = jnp.where(at_entry, pltpu.roll(slab, turn, 1), 0.0)
        along = pltpu.roll(jnp.where(lane_first, edge, v), nz - 1, 1) + pltpu.roll(
            jnp.where(lane_last, edge, v), 1, 1
        )
        beside = wide_ref[x + 1, SUB - 1 : SUB - 1 + ny] + wide_ref[x + 1, SUB + 1 : SUB + 1 + ny]
        across = wide_ref[x, own] + wide_ref[x + 2, own]
        value_ref[ny * x : ny * x + ny] = along + beside + across - 6.0 * v

    value = value_ref[...]
    plan = plan_ref[...]
    step = 1
    while step < rows * LANES:
        value = jnp.where((plan & step) != 0, shift_left(value, step, lane), value)
        step *= 2
    n_y, n_z = lax.axis_size("gy"), lax.axis_size("gz")
    counts = total_ref[8:16]
    dev = lanes_of((SUB, LANES))
    mine = lax.rem(dev, n_y * n_z) == lax.axis_index("gy") * n_z + gz
    gx = lax.axis_index("gx")
    first = subs_of((SUB, LANES)) == 0
    offset = jnp.sum(jnp.where(first & mine & (dev < gx * n_y * n_z), counts, 0.0)).astype(jnp.int32)
    count = jnp.sum(jnp.where(first & mine & (dev // (n_y * n_z) == gx), counts, 0.0)).astype(jnp.int32)
    slots = value[:slot_rows]
    index = (row * LANES + lane)[:slot_rows]
    slots = jnp.where(index < count, slots, 0.0)
    slots = jnp.concatenate([slots, jnp.zeros((SUB, LANES), F32)], axis=0)
    inner = lax.rem(offset, LANES)
    turned = pltpu.roll(slots, inner, 1)
    above = pltpu.roll(turned, 1, 0)
    moved = jnp.where(lane[: slot_rows + SUB] >= inner, turned, above)
    buf_ref[...] = jnp.zeros_like(buf_ref)
    buf_ref[pl.ds(offset // LANES, slot_rows + SUB), :] = moved
    for k, out_ref in enumerate(out_refs):
        size = out_ref.shape[0]
        out_ref[...] = buf_ref[pl.ds(pl.multiple_of((gx ^ k) * size, SUB), size), :]
    leave.wait()


def chunks_of(n_states, parts):
    size = -(-n_states // parts)
    return [(k, min(size, n_states - k)) for k in range(0, n_states, size)]


def membrane_kernel(
    half_ref, slope_ref, tau_ref, cond_ref, rev_ref, v_ref, gates_hbm, cot_hbm,
    base_ref, sum_ref, factor_ref, coef_ref,
    gates_ref, cot_ref, sems,
):
    n_states, rows = gates_ref.shape[:2]
    chunks = chunks_of(n_states, sems.shape[1])
    copies = []
    for part, (begin, size) in enumerate(chunks):
        for k, (source, target) in enumerate(((gates_hbm, gates_ref), (cot_hbm, cot_ref))):
            here = pl.ds(begin, size)
            copies.append(pltpu.make_async_copy(source.at[here], target.at[here], sems.at[k, part]))
            copies[-1].start()
    v = v_ref[...]

    def state(g, carry):
        total, current = carry
        inv_slope = 1.0 / slope_ref[g]
        tau_base = tau_ref[g]
        scaled = (v - half_ref[g]) * inv_slope
        gate = gates_ref[g]
        cot = cot_ref[g]
        steady = 1.0 / (1.0 + jnp.exp(-scaled))
        bell = jnp.exp(-scaled * scaled)
        rate = TIME_STEP / (tau_base * (0.5 + bell))
        decay = jnp.exp(-rate)
        steady_slope = steady * (1.0 - steady)
        decay_slope = decay * rate * rate * ((tau_base / TIME_STEP) * bell * (-2.0 * scaled))
        change = (steady_slope * (1.0 - decay) + (gate - steady) * decay_slope) * inv_slope
        base_ref[g] = cot * decay
        coef_ref[0, pl.ds(g, 1)] = jnp.full((1, LANES), TIME_STEP * cond_ref[g])
        coef_ref[1, pl.ds(g, 1)] = jnp.full((1, LANES), rev_ref[g])
        return total + cot * change, current + cond_ref[g] * gate

    carry = (jnp.zeros((rows, LANES), F32),) * 2
    for part, (begin, size) in enumerate(chunks):
        copies[2 * part].wait()
        copies[2 * part + 1].wait()
        carry = lax.fori_loop(begin, begin + size, state, carry, unroll=True)
    sum_ref[...] = carry[0]
    factor_ref[...] = 1.0 - TIME_STEP * carry[1]


def finish_kernel(coef_ref, vcot_ref, v_ref, sum_ref, factor_ref, base_ref, *refs):
    *landed_refs, volt_ref, gate_hbm, gate_ref, sems = refs
    landed = landed_refs[0][...]
    for ref in landed_refs[1:]:
        landed = landed + ref[...]
    cot = vcot_ref[...] + landed
    v = v_ref[...]
    copies = []
    for part, (begin, size) in enumerate(chunks_of(base_ref.shape[0], sems.shape[0])):
        for g in range(begin, begin + size):
            gate_ref[g] = base_ref[g] - (coef_ref[0, g : g + 1] * cot) * (v - coef_ref[1, g : g + 1])
        here = pl.ds(begin, size)
        copies.append(pltpu.make_async_copy(gate_ref.at[here], gate_hbm.at[here], sems.at[part]))
        copies[-1].start()
    volt_ref[...] = cot * factor_ref[...] + sum_ref[...]
    for copy in copies:
        copy.wait()


def both_ways(up, down, axis):
    count = lax.axis_size(axis)
    low = lax.ppermute(up, axis, [(i, i + 1) for i in range(count - 1)])
    high = lax.ppermute(down, axis, [(i + 1, i) for i in range(count - 1)])
    return low, high


def pair_swaps(first, second, axis):
    count = lax.axis_size(axis)
    even = [(i, i ^ 1) for i in range(count)]
    between = [(i, i + 1) for i in range(1, count - 1, 2)]
    between = between + [(j, i) for i, j in between]
    return lax.ppermute(first, axis, even), lax.ppermute(second, axis, between)


def reduce_over(value, axis):
    count = lax.axis_size(axis)
    step = 1
    while step < count:
        value = value + lax.ppermute(value, axis, [(i, i ^ step) for i in range(count)])
        step *= 2
    return value


def local(
    potential_cot, damping, tissue_label, heart_index, voltage, gates, voltage_cot, gates_cot,
    half_voltage, gate_slope, tau_base, conductance, reversal,
):
    nx, ny, nz = potential_cot.shape
    rows = nx * ny
    ring = ny + SUB
    n_gx, n_gy = lax.axis_size("gx"), lax.axis_size("gy")
    n_states = gates.shape[0]
    block_rows = voltage.shape[1] // LANES
    slot_rows = heart_index.shape[3] // LANES
    block = shape_of(nx, ny, nz)
    flat = lambda a: a.reshape(rows, LANES)
    cells = lambda a: a.reshape(block_rows, LANES)
    states = lambda a: a.reshape(n_states, block_rows, LANES)

    w0, inv, packed, stat = call(
        start_kernel, (block, block, shape_of(2, ny, nz), shape_of(2, SUB, nz)), 3,
        specs=[HBM] * 3,
        scratch=[
            pltpu.VMEM((nx, ny, nz), F32), pltpu.VMEM((nx, ny, nz), F32), pltpu.VMEM((nx, ny, nz), jnp.int32),
            pltpu.SemaphoreType.DMA((3, 4)),
        ],
    )(in_hbm(potential_cot), in_hbm(damping), in_hbm(tissue_label))

    got = lax.ppermute(packed, "gz", [(0, 1), (1, 0)])
    base, total_change, factor, coefs = call(
        membrane_kernel,
        (
            shape_of(n_states, block_rows, LANES), shape_of(block_rows, LANES), shape_of(block_rows, LANES),
            shape_of(2, n_states, LANES),
        ),
        8,
        specs=[SMEM] * 5 + [VMEM] + [HBM] * 2,
        scratch=[pltpu.VMEM((n_states, block_rows, LANES), F32)] * 2 + [pltpu.SemaphoreType.DMA((2, 4))],
        cost=6_000_000,
    )(
        half_voltage, gate_slope, tau_base, conductance, reversal,
        cells(voltage), in_hbm(states(gates)), in_hbm(states(gates_cot)),
    )
    plan = call(plan_kernel, jax.ShapeDtypeStruct((rows, LANES), jnp.int32), 1, cost=6_000_000)(flat(tissue_label))

    face = shape_of(nx + 1, SUB, nz)
    slab_shape = shape_of(2, ny, nz)
    x_shapes = (shape_of(2, nx + 1, SUB, nz), shape_of(6, ring, nz), shape_of(6, ring, nz))
    if n_gy == 2:
        slab, mine = call(y_face_one_kernel, (slab_shape, face), 4)(w0, inv, packed, got)
        halo = (lax.ppermute(mine, "gy", [(0, 1), (1, 0)]),)
    else:
        slab, up, down = call(y_faces_kernel, (slab_shape, face, face), 4)(w0, inv, packed, got)
        halo = both_ways(up, down, "gy")
    edge_rows, first, second = call(
        functools.partial(x_faces_kernel, n_gy == 2), x_shapes, 3 + len(halo)
    )(w0, inv, slab, *halo)
    first, second = pair_swaps(first, second, "gx")

    tall = ring + SUB
    basis = [shape_of(nx + 2 * k, tall, nz) for k in (3, 2, 1)]
    wide0, wide1, wide2, slabs, sums = call(
        stencil_kernel,
        (*basis, shape_of(3, tall, 2 * nz), shape_of(16, nz)),
        7,
        scratch=[pltpu.VMEM((nx + 4, tall, nz), F32), pltpu.VMEM((1, tall, 2 * nz), F32)],
    )(w0, inv, slab, edge_rows, first, second, stat)
    for axis in ("gz", "gy", "gx"):
        sums = reduce_over(sums, axis)

    solution, *blocks = call(
        functools.partial(combine_kernel, slot_rows),
        (block,) + (shape_of(block_rows, LANES),) * n_gx,
        6,
        outs=(HBM,) + (VMEM,) * n_gx,
        scratch=[
            pltpu.VMEM((nx + 2, tall, nz), F32),
            pltpu.VMEM((nx, ny, nz), F32),
            pltpu.VMEM((rows, LANES), F32),
            pltpu.VMEM((n_gx * block_rows + slot_rows + SUB, LANES), F32),
            pltpu.SemaphoreType.DMA(()),
        ],
    )(sums, wide0, wide1, wide2, slabs, plan)
    landed = blocks[:1] + [
        lax.ppermute(blocks[k], "gx", [(i, i ^ k) for i in range(n_gx)]) for k in range(1, n_gx)
    ]

    volt_grad, gate_grad = call(
        finish_kernel,
        (shape_of(block_rows, LANES), shape_of(n_states, block_rows, LANES)),
        6 + n_gx,
        outs=(VMEM, HBM),
        scratch=[pltpu.VMEM((n_states, block_rows, LANES), F32), pltpu.SemaphoreType.DMA((4,))],
    )(coefs, cells(voltage_cot), cells(voltage), total_change, factor, base, *landed)
    return solution, volt_grad.reshape(voltage.shape), gate_grad.reshape(gates.shape)


def solution(mesh):
    grid = P(("groups", "gx"), "gy", "gz")
    cells = P(("groups", "gy", "gz"), "gx")
    states = P(None, ("groups", "gy", "gz"), "gx")
    in_specs = (
        grid, grid, grid, P(("groups", "gx"), "gy", "gz", None), cells, states, cells, states,
        P(), P(), P(), P(), P(),
    )
    return jax.shard_map(
        local, mesh=mesh, in_specs=in_specs, out_specs=(grid, cells, states), check_vma=False
    )
```

```python
import functools

import jax
import jax.numpy as jnp
from jax import lax
from jax.experimental import pallas as pl
from jax.experimental.pallas import tpu as pltpu
from jax.sharding import PartitionSpec as P

TIME_STEP = 0.5
LANES = 128
SUB = 8
PACK = 8
F32 = jnp.float32

VMEM = pl.BlockSpec(memory_space=pltpu.VMEM)
SMEM = pl.BlockSpec(memory_space=pltpu.SMEM)
HBM = pl.BlockSpec(memory_space=pltpu.HBM)


def shape_of(*dims):
    return jax.ShapeDtypeStruct(dims, F32)


def call(kernel, out_shape, n_in, specs=None, outs=None, scratch=(), cost=2_000_000, limit=32):
    return pl.pallas_call(
        kernel,
        out_shape=out_shape,
        in_specs=specs if specs is not None else [VMEM] * n_in,
        out_specs=outs if outs is not None else jax.tree.map(lambda _: VMEM, out_shape),
        scratch_shapes=list(scratch),
        compiler_params=pltpu.CompilerParams(vmem_limit_bytes=limit * 1024 * 1024),
        cost_estimate=pl.CostEstimate(flops=cost, bytes_accessed=cost, transcendentals=0),
    )


def in_hbm(array):
    return pltpu.with_memory_space_constraint(array, pltpu.HBM)


def lanes_of(shape):
    return lax.broadcasted_iota(jnp.int32, shape, len(shape) - 1)


def subs_of(shape):
    return lax.broadcasted_iota(jnp.int32, shape, len(shape) - 2)


def start_kernel(
    right_hbm, damping_hbm, label_hbm, w0_ref, inv_ref, pack_ref, stat_ref, right_ref, damping_ref, label_ref, sems
):
    nx, ny, nz = right_ref.shape
    parts = sems.shape[1]
    size = nx // parts
    copies = []
    for part in range(parts):
        here = pl.ds(part * size, size)
        for k, (source, target) in enumerate(
            ((right_hbm, right_ref), (damping_hbm, damping_ref), (label_hbm, label_ref))
        ):
            copies.append(pltpu.make_async_copy(source.at[here], target.at[here], sems.at[k, part]))
            copies[-1].start()
    gz = lax.axis_index("gz")
    lane = lanes_of((ny, nz))
    packed_w = jnp.zeros((ny, nz), F32)
    packed_i = jnp.zeros((ny, nz), F32)
    energy = jnp.zeros((ny, nz), F32)
    cells = jnp.zeros((ny, nz), F32)
    for x in range(nx):
        if x % size == 0:
            for k in range(3):
                copies[3 * (x // size) + k].wait()
        label = label_ref[x].astype(F32)
        right = right_ref[x]
        inv = 1.0 / (12.0 + damping_ref[x] * (1.0 + 3.0 * label))
        w0 = right * inv
        w0_ref[x] = w0
        inv_ref[x] = inv
        energy = energy + right * w0
        cells = cells + label
        turn = (PACK * x + 3) % nz
        begin = PACK * x + 3 * gz
        chosen = (lane >= begin) & (lane < begin + 3)
        packed_w = jnp.where(chosen, pltpu.roll(w0, turn, 1), packed_w)
        packed_i = jnp.where(chosen, pltpu.roll(inv, turn, 1), packed_i)
    pack_ref[0] = packed_w
    pack_ref[1] = packed_i
    stat_ref[0] = jnp.broadcast_to(jnp.sum(energy, axis=0, keepdims=True), (SUB, nz))
    stat_ref[1] = jnp.broadcast_to(jnp.sum(cells, axis=0, keepdims=True), (SUB, nz))


def y_faces_kernel(w0_ref, inv_ref, own_ref, got_ref, slab_ref, up_ref, down_ref):
    nx, ny, nz = w0_ref.shape
    sub = subs_of((SUB, nz))
    slab_ref[...] = own_ref[...] + got_ref[...]
    for x in range(nx + 1):
        if x < nx:
            w_last, w_first = w0_ref[x, ny - SUB :], w0_ref[x, :SUB]
            i_last, i_first = inv_ref[x, ny - SUB :], inv_ref[x, :SUB]
        else:
            w_last, w_first = slab_ref[0, ny - SUB :], slab_ref[0, :SUB]
            i_last, i_first = slab_ref[1, ny - SUB :], slab_ref[1, :SUB]
        up_ref[x] = jnp.where(sub >= 5, w_last, pltpu.roll(i_last, 4, 0))
        down_ref[x] = jnp.where(sub <= 2, w_first, pltpu.roll(i_first, 4, 0))


def y_face_one_kernel(w0_ref, inv_ref, own_ref, got_ref, slab_ref, face_ref):
    nx, ny, nz = w0_ref.shape
    sub = subs_of((SUB, nz))
    up = lax.axis_index("gy") == 0
    keep_w = jnp.where(up, sub, SUB - 1 - sub) >= 5
    slab_ref[...] = own_ref[...] + got_ref[...]
    for x in range(nx + 1):
        if x < nx:
            w_last, w_first = w0_ref[x, ny - SUB :], w0_ref[x, :SUB]
            i_last, i_first = inv_ref[x, ny - SUB :], inv_ref[x, :SUB]
        else:
            w_last, w_first = slab_ref[0, ny - SUB :], slab_ref[0, :SUB]
            i_last, i_first = slab_ref[1, ny - SUB :], slab_ref[1, :SUB]
        w_face = jnp.where(up, w_last, w_first)
        i_face = jnp.where(up, i_last, i_first)
        face_ref[x] = jnp.where(keep_w, w_face, pltpu.roll(i_face, 4, 0))


def x_faces_kernel(one, after_ref, w0_ref, inv_ref, slab_ref, *refs):
    if one:
        got_ref, halo_ref, first_ref, second_ref = refs
    else:
        low_ref, high_ref, halo_ref, first_ref, second_ref = refs
    nx, ny, nz = w0_ref.shape
    sub = subs_of((SUB, nz))
    lane = lanes_of((ny + SUB, nz))
    if one:
        gy = lax.axis_index("gy")
        w_rows = ((gy == 1) & (sub >= 5)) | ((gy == 0) & (sub <= 2))
        i_rows = ((gy == 1) & (sub >= 6)) | ((gy == 0) & (sub <= 1))
    for x in range(nx + 1):
        if one:
            got = got_ref[x]
            halo_ref[0, x] = jnp.where(w_rows, got, 0.0)
            halo_ref[1, x] = jnp.where(i_rows, pltpu.roll(got, 4, 0), 0.0)
        else:
            low, high = low_ref[x], high_ref[x]
            halo_ref[0, x] = jnp.where(sub >= 5, low, jnp.where(sub <= 2, high, 0.0))
            halo_ref[1, x] = jnp.where(
                sub >= 6, pltpu.roll(low, 4, 0), jnp.where(sub <= 1, pltpu.roll(high, 4, 0), 0.0)
            )
    odd = lax.rem(lax.axis_index("gx"), 2)
    slab_w = jnp.concatenate([slab_ref[0], halo_ref[0, nx]], axis=0)
    slab_i = jnp.concatenate([slab_ref[1], halo_ref[1, nx]], axis=0)
    half = pltpu.roll(slab_i, nz // 2, 1)
    up = jnp.where(lane >= nz - 3 * PACK, slab_w, half)
    down = jnp.where(lane < 3 * PACK, slab_w, half)
    for face_ref, lower in ((first_ref, odd), (second_ref, 1 - odd)):
        for k in range(5):
            field, source = (0, w0_ref) if k < 3 else (1, inv_ref)
            place = (1 - lower) * (nx - 3 + field) + k - 3 * field
            face_ref[k, :ny] = source[place]
            face_ref[k, ny:] = halo_ref[field, place]
        face_ref[5] = jnp.where(lower == 1, down, up)


def stencil_kernel(
    w0_ref, inv_ref, slab_ref, halo_ref, first_ref, second_ref, stat_ref,
    a_ref, b_ref, c_ref, slabs_ref, total_ref,
    i_ref, si_ref,
):
    nx, ny, nz = w0_ref.shape
    ring = ny + SUB
    gz = lax.axis_index("gz")
    odd = lax.rem(lax.axis_index("gx"), 2) == 1

    def low(k):
        return jnp.where(odd, first_ref[k], second_ref[k])

    def high(k):
        return jnp.where(odd, second_ref[k], first_ref[k])

    def place(ref, x, own, halo):
        ref[x, SUB : SUB + ny] = own
        ref[x, :SUB] = halo
        ref[x, SUB + ny :] = halo

    for x in range(nx):
        place(a_ref, 3 + x, w0_ref[x], halo_ref[0, x])
        place(i_ref, 2 + x, inv_ref[x], halo_ref[1, x])
    for k in range(3):
        for x, plane in ((k, low(k)), (nx + 3 + k, high(k))):
            place(a_ref, x, plane[:ny], plane[ny:])
    for k in range(2):
        for x, plane in ((k, low(3 + k)), (nx + 2 + k, high(3 + k))):
            place(i_ref, x, plane[:ny], plane[ny:])

    lane = lanes_of((ring, nz))
    lo5, hi5 = low(5), high(5)
    slab_w = jnp.where(lane < 3 * PACK, hi5, 0.0) + jnp.where(lane >= nz - 3 * PACK, lo5, 0.0)
    lo5, hi5 = pltpu.roll(lo5, nz // 2, 1), pltpu.roll(hi5, nz // 2, 1)
    slab_i = jnp.where(lane < 2 * PACK, hi5, 0.0) + jnp.where(lane >= nz - 2 * PACK, lo5, 0.0)
    for ref, at, k, beyond in ((slabs_ref, 0, 0, slab_w), (si_ref, 0, 1, slab_i)):
        ref[at, SUB : SUB + ny, :nz] = slab_ref[k]
        ref[at, SUB : SUB + ny, nz:] = beyond[:ny]
        for rows in (slice(0, SUB), slice(SUB + ny, SUB + ring)):
            ref[at, rows, :nz] = halo_ref[k, nx]
            ref[at, rows, nz:] = beyond[ny:]

    sums = {}

    def add(name, value, skip):
        value = value[skip : skip + ny]
        part = value[:SUB]
        for k in range(SUB, ny, SUB):
            part = part + value[k : k + SUB]
        sums[name] = part if name not in sums else sums[name] + part

    def rows_of(ref, x, start, size):
        return ref[x, start : start + size]

    for stage in range(3):
        source = (a_ref, b_ref, c_ref)[stage]
        target = (b_ref, c_ref, None)[stage]
        margin = 2 - stage
        start = SUB - margin
        size = ny if margin == 0 else ring
        lane = lanes_of((size, nz))
        entry = (nz - 1) * gz
        at_entry, lane_first, lane_last = lane == entry, lane == 0, lane == nz - 1

        width = 2 * nz
        v = slabs_ref[stage, start : start + size]
        s = slabs_ref[stage, start - 1 : start - 1 + size] + slabs_ref[stage, start + 1 : start + 1 + size]
        across = pltpu.roll(v, PACK, 1) + pltpu.roll(v, width - PACK, 1)
        slab_q = v + 0.5 * (s + across)
        if stage < 2:
            total = (
                pltpu.roll(slab_q, 1, 1) + pltpu.roll(slab_q, width - 1, 1) + s + across
                + 0.5 * (pltpu.roll(s, PACK, 1) + pltpu.roll(s, width - PACK, 1))
            )
            slabs_ref[stage + 1, start : start + size] = total * si_ref[0, start : start + size]

        def beside(x):
            return rows_of(source, x, start - 1, size) + rows_of(source, x, start + 1, size)

        s_low, s_mid = beside(0), beside(1)
        v_low, v_mid = rows_of(source, 0, start, size), rows_of(source, 1, start, size)
        for x in range(-margin, nx + margin):
            at = x + margin + 1
            v_high, s_high = rows_of(source, at + 1, start, size), beside(at + 1)
            across = v_low + v_high
            q = v_mid + 0.5 * (s_mid + across)
            column = (PACK * x) % width
            half = slab_q[:, column // nz * nz : column // nz * nz + nz]
            turn = lax.rem(entry - (column % nz + 3 - gz) + 2 * nz, nz)
            edge = jnp.where(at_entry, pltpu.roll(half, turn, 1), 0.0)
            along = pltpu.roll(jnp.where(lane_first, edge, q), nz - 1, 1) + pltpu.roll(
                jnp.where(lane_last, edge, q), 1, 1
            )
            total = along + s_mid + across + 0.5 * (s_low + s_high)
            if target is not None:
                after = total * rows_of(i_ref, x + 2, start, size)
                target[x + margin, start : start + size] = after
            if 0 <= x < nx:
                add(2 * stage + 1, v_mid * total, margin)
                if target is not None:
                    add(2 * stage + 2, after * total, margin)
            v_low, v_mid, s_low, s_mid = v_mid, v_high, s_mid, s_high

    total_ref[0:1] = stat_ref[0, 0:1]
    for k in range(1, 6):
        total_ref[k : k + 1] = jnp.sum(sums[k], axis=0, keepdims=True)
    total_ref[6:8] = jnp.zeros((2, nz), F32)
    here = (lax.axis_index("gx") * lax.axis_size("gy") + lax.axis_index("gy")) * lax.axis_size("gz") + gz
    count = jnp.sum(stat_ref[1], axis=1, keepdims=True)
    total_ref[8:16] = jnp.where(lanes_of((SUB, nz)) == here, count, 0.0)


def shift_left(v, amount, lane):
    rows = v.shape[0]
    if amount < LANES:
        turned = pltpu.roll(v, LANES - amount, 1)
        below = pltpu.roll(turned, rows - 1, 0)
        return jnp.where(lane < LANES - amount, turned, below)
    return jnp.concatenate([v[amount // LANES :], v[: amount // LANES]], axis=0)


def plan_kernel(label_ref, plan_ref):
    rows = label_ref.shape[0]
    lane = lanes_of((rows, LANES))
    row = subs_of((rows, LANES))
    heart = label_ref[...] == 1
    ones = heart.astype(jnp.bfloat16)
    upper = (subs_of((LANES, LANES)) < lanes_of((LANES, LANES))).astype(jnp.bfloat16)
    in_row = jnp.dot(ones, upper, preferred_element_type=F32)
    totals = jnp.dot(ones, jnp.ones((LANES, LANES), jnp.bfloat16), preferred_element_type=F32)
    lower = (subs_of((rows, rows)) > lanes_of((rows, rows))).astype(jnp.bfloat16)
    before = jnp.dot(lower, totals.astype(jnp.bfloat16), preferred_element_type=F32)
    rank = (in_row + before).astype(jnp.int32)
    way = jnp.where(heart, row * LANES + lane - rank, 0)
    plan = jnp.zeros((rows, LANES), jnp.int32)
    step = 1
    while step < rows * LANES:
        moving = jnp.where((way & step) != 0, way, 0)
        arriving = shift_left(moving, step, lane)
        plan = plan | (arriving & step)
        way = (way - moving) | arriving
        step *= 2
    plan_ref[...] = plan


def galerkin(t):
    g00, g01, g02, g12, g22 = t[0] - t[1], t[1] - t[2], t[2] - t[3], t[3] - t[4], t[4] - t[5]
    g11 = g02
    l10, l20 = g01 / g00, g02 / g00
    d1 = g11 - l10 * g01
    m21 = g12 - l20 * g01
    ok1 = d1 > 1e-6 * g11
    d1 = jnp.where(ok1, d1, 1.0)
    l21 = jnp.where(ok1, m21 / d1, 0.0)
    d2 = g22 - l20 * g02 - l21 * m21
    ok2 = ok1 & (d2 > 1e-6 * g22)
    d2 = jnp.where(ok2, d2, 1.0)
    y1 = t[1] - l10 * t[0]
    y2 = t[2] - l20 * t[0] - l21 * y1
    c2 = jnp.where(ok2, y2 / d2, 0.0)
    c1 = jnp.where(ok1, y1 / d1 - l21 * c2, 0.0)
    c0 = t[0] / g00 - l10 * c1 - l20 * c2
    return c0, c1, c2


def combine_kernel(slot_rows, total_ref, w0_ref, w1_ref, w2_ref, slabs_ref, plan_ref, x_hbm, *refs):
    *out_refs, wide_ref, x_ref, value_ref, buf_ref, sem = refs
    nx, ny, nz = x_ref.shape
    rows = nx * ny
    lane = lanes_of((rows, LANES))
    row = subs_of((rows, LANES))
    sums = jnp.sum(total_ref[0:8], axis=1, keepdims=True)
    t = [jnp.broadcast_to(sums[k : k + 1], (1, LANES)) for k in range(6)]
    c0, c1, c2 = galerkin(t)
    for x in range(nx + 2):
        wide_ref[x] = c0 * w0_ref[x + 2] + c1 * w1_ref[x + 1] + c2 * w2_ref[x]
    for x in range(nx):
        x_ref[x] = wide_ref[x + 1, SUB : SUB + ny]
    leave = pltpu.make_async_copy(x_ref, x_hbm, sem)
    leave.start()

    gz = lax.axis_index("gz")
    own = slice(SUB, SUB + ny)
    slab = c0 * slabs_ref[0, own, :nz] + c1 * slabs_ref[1, own, :nz] + c2 * slabs_ref[2, own, :nz]
    column = lanes_of((ny, nz))
    entry = (nz - 1) * gz
    at_entry, lane_first, lane_last = column == entry, column == 0, column == nz - 1
    for x in range(nx):
        v = wide_ref[x + 1, own]
        turn = lax.rem(entry - (PACK * x + 3 - gz) + 2 * nz, nz)
        edge = jnp.where(at_entry, pltpu.roll(slab, turn, 1), 0.0)
        along = pltpu.roll(jnp.where(lane_first, edge, v), nz - 1, 1) + pltpu.roll(
            jnp.where(lane_last, edge, v), 1, 1
        )
        beside = wide_ref[x + 1, SUB - 1 : SUB - 1 + ny] + wide_ref[x + 1, SUB + 1 : SUB + 1 + ny]
        across = wide_ref[x, own] + wide_ref[x + 2, own]
        value_ref[ny * x : ny * x + ny] = along + beside + across - 6.0 * v

    value = value_ref[...]
    plan = plan_ref[...]
    step = 1
    while step < rows * LANES:
        value = jnp.where((plan & step) != 0, shift_left(value, step, lane), value)
        step *= 2
    n_y, n_z = lax.axis_size("gy"), lax.axis_size("gz")
    counts = total_ref[8:16]
    dev = lanes_of((SUB, LANES))
    mine = lax.rem(dev, n_y * n_z) == lax.axis_index("gy") * n_z + gz
    gx = lax.axis_index("gx")
    first = subs_of((SUB, LANES)) == 0
    offset = jnp.sum(jnp.where(first & mine & (dev < gx * n_y * n_z), counts, 0.0)).astype(jnp.int32)
    count = jnp.sum(jnp.where(first & mine & (dev // (n_y * n_z) == gx), counts, 0.0)).astype(jnp.int32)
    slots = value[:slot_rows]
    index = (row * LANES + lane)[:slot_rows]
    slots = jnp.where(index < count, slots, 0.0)
    slots = jnp.concatenate([slots, jnp.zeros((SUB, LANES), F32)], axis=0)
    inner = lax.rem(offset, LANES)
    turned = pltpu.roll(slots, inner, 1)
    above = pltpu.roll(turned, 1, 0)
    moved = jnp.where(lane[: slot_rows + SUB] >= inner, turned, above)
    buf_ref[...] = jnp.zeros_like(buf_ref)
    buf_ref[pl.ds(offset // LANES, slot_rows + SUB), :] = moved
    for k, out_ref in enumerate(out_refs):
        size = out_ref.shape[0]
        out_ref[...] = buf_ref[pl.ds(pl.multiple_of((gx ^ k) * size, SUB), size), :]
    leave.wait()


def membrane_kernel(
    half_ref, slope_ref, tau_ref, cond_ref, rev_ref, after_ref, v_ref, gates_ref, cot_ref,
    base_ref, sum_ref, factor_ref, coef_ref,
):
    n_states, rows = gates_ref.shape[:2]
    v = v_ref[...]

    def state(g, carry):
        total, current = carry
        inv_slope = 1.0 / slope_ref[g]
        tau_base = tau_ref[g]
        scaled = (v - half_ref[g]) * inv_slope
        gate = gates_ref[g]
        cot = cot_ref[g]
        steady = 1.0 / (1.0 + jnp.exp(-scaled))
        bell = jnp.exp(-scaled * scaled)
        rate = TIME_STEP / (tau_base * (0.5 + bell))
        decay = jnp.exp(-rate)
        steady_slope = steady * (1.0 - steady)
        decay_slope = decay * rate * rate * ((tau_base / TIME_STEP) * bell * (-2.0 * scaled))
        change = (steady_slope * (1.0 - decay) + (gate - steady) * decay_slope) * inv_slope
        base_ref[g] = cot * decay
        coef_ref[0, pl.ds(g, 1)] = jnp.full((1, LANES), TIME_STEP * cond_ref[g])
        coef_ref[1, pl.ds(g, 1)] = jnp.full((1, LANES), rev_ref[g])
        return total + cot * change, current + cond_ref[g] * gate

    zero = jnp.zeros((rows, LANES), F32)
    total, current = lax.fori_loop(0, n_states, state, (zero, zero), unroll=2)
    sum_ref[...] = total
    factor_ref[...] = 1.0 - TIME_STEP * current


def finish_kernel(coef_ref, vcot_ref, v_ref, sum_ref, factor_ref, base_ref, *refs):
    *landed_refs, volt_ref, gate_ref = refs
    landed = landed_refs[0][...]
    for ref in landed_refs[1:]:
        landed = landed + ref[...]
    cot = vcot_ref[...] + landed
    v = v_ref[...]
    volt_ref[...] = cot * factor_ref[...] + sum_ref[...]
    for g in range(base_ref.shape[0]):
        gate_ref[g] = base_ref[g] - (coef_ref[0, g : g + 1] * cot) * (v - coef_ref[1, g : g + 1])


def both_ways(up, down, axis):
    count = lax.axis_size(axis)
    low = lax.ppermute(up, axis, [(i, i + 1) for i in range(count - 1)])
    high = lax.ppermute(down, axis, [(i + 1, i) for i in range(count - 1)])
    return low, high


def pair_swaps(first, second, axis):
    count = lax.axis_size(axis)
    even = [(i, i ^ 1) for i in range(count)]
    between = [(i, i + 1) for i in range(1, count - 1, 2)]
    between = between + [(j, i) for i, j in between]
    return lax.ppermute(first, axis, even), lax.ppermute(second, axis, between)


def reduce_over(value, axis):
    count = lax.axis_size(axis)
    step = 1
    while step < count:
        value = value + lax.ppermute(value, axis, [(i, i ^ step) for i in range(count)])
        step *= 2
    return value


def local(
    potential_cot, damping, tissue_label, heart_index, voltage, gates, voltage_cot, gates_cot,
    half_voltage, gate_slope, tau_base, conductance, reversal,
):
    nx, ny, nz = potential_cot.shape
    rows = nx * ny
    ring = ny + SUB
    n_gx, n_gy = lax.axis_size("gx"), lax.axis_size("gy")
    n_states = gates.shape[0]
    block_rows = voltage.shape[1] // LANES
    slot_rows = heart_index.shape[3] // LANES
    block = shape_of(nx, ny, nz)
    flat = lambda a: a.reshape(rows, LANES)
    cells = lambda a: a.reshape(block_rows, LANES)
    states = lambda a: a.reshape(n_states, block_rows, LANES)

    w0, inv, packed, stat = call(
        start_kernel, (block, block, shape_of(2, ny, nz), shape_of(2, SUB, nz)), 3,
        specs=[HBM] * 3,
        scratch=[
            pltpu.VMEM((nx, ny, nz), F32), pltpu.VMEM((nx, ny, nz), F32), pltpu.VMEM((nx, ny, nz), jnp.int32),
            pltpu.SemaphoreType.DMA((3, 4)),
        ],
    )(in_hbm(potential_cot), in_hbm(damping), in_hbm(tissue_label))

    got = lax.ppermute(packed, "gz", [(0, 1), (1, 0)])
    base, total_change, factor, coefs = call(
        membrane_kernel,
        (
            shape_of(n_states, block_rows, LANES), shape_of(block_rows, LANES), shape_of(block_rows, LANES),
            shape_of(2, n_states, LANES),
        ),
        9,
        specs=[SMEM] * 5 + [VMEM] * 4,
        cost=6_000_000,
    )(
        half_voltage, gate_slope, tau_base, conductance, reversal,
        stat, cells(voltage), states(gates), states(gates_cot),
    )
    plan = call(plan_kernel, jax.ShapeDtypeStruct((rows, LANES), jnp.int32), 1, cost=6_000_000)(flat(tissue_label))

    face = shape_of(nx + 1, SUB, nz)
    slab_shape = shape_of(2, ny, nz)
    x_shapes = (shape_of(2, nx + 1, SUB, nz), shape_of(6, ring, nz), shape_of(6, ring, nz))
    if n_gy == 2:
        slab, mine = call(y_face_one_kernel, (slab_shape, face), 4)(w0, inv, packed, got)
        halo = (lax.ppermute(mine, "gy", [(0, 1), (1, 0)]),)
    else:
        slab, up, down = call(y_faces_kernel, (slab_shape, face, face), 4)(w0, inv, packed, got)
        halo = both_ways(up, down, "gy")
    edge_rows, first, second = call(
        functools.partial(x_faces_kernel, n_gy == 2), x_shapes, 4 + len(halo)
    )(coefs, w0, inv, slab, *halo)
    first, second = pair_swaps(first, second, "gx")

    tall = ring + SUB
    basis = [shape_of(nx + 2 * k, tall, nz) for k in (3, 2, 1)]
    wide0, wide1, wide2, slabs, sums = call(
        stencil_kernel,
        (*basis, shape_of(3, tall, 2 * nz), shape_of(16, nz)),
        7,
        scratch=[pltpu.VMEM((nx + 4, tall, nz), F32), pltpu.VMEM((1, tall, 2 * nz), F32)],
    )(w0, inv, slab, edge_rows, first, second, stat)
    for axis in ("gz", "gy"):
        sums = reduce_over(sums, axis)
    sums = lax.psum(sums, "gx")

    solution, *blocks = call(
        functools.partial(combine_kernel, slot_rows),
        (block,) + (shape_of(block_rows, LANES),) * n_gx,
        6,
        outs=(HBM,) + (VMEM,) * n_gx,
        scratch=[
            pltpu.VMEM((nx + 2, tall, nz), F32),
            pltpu.VMEM((nx, ny, nz), F32),
            pltpu.VMEM((rows, LANES), F32),
            pltpu.VMEM((n_gx * block_rows + slot_rows + SUB, LANES), F32),
            pltpu.SemaphoreType.DMA(()),
        ],
    )(sums, wide0, wide1, wide2, slabs, plan)
    landed = blocks[:1] + [
        lax.ppermute(blocks[k], "gx", [(i, i ^ k) for i in range(n_gx)]) for k in range(1, n_gx)
    ]

    volt_grad, gate_grad = call(
        finish_kernel,
        (shape_of(block_rows, LANES), shape_of(n_states, block_rows, LANES)),
        6 + n_gx,
    )(coefs, cells(voltage_cot), cells(voltage), total_change, factor, base, *landed)
    return solution, volt_grad.reshape(voltage.shape), gate_grad.reshape(gates.shape)


def solution(mesh):
    grid = P(("groups", "gx"), "gy", "gz")
    cells = P(("groups", "gy", "gz"), "gx")
    states = P(None, ("groups", "gy", "gz"), "gx")
    in_specs = (
        grid, grid, grid, P(("groups", "gx"), "gy", "gz", None), cells, states, cells, states,
        P(), P(), P(), P(), P(),
    )
    return jax.shard_map(
        local, mesh=mesh, in_specs=in_specs, out_specs=(grid, cells, states), check_vma=False
    )
```

```python
import functools

import jax
import jax.numpy as jnp
from jax import lax
from jax.experimental import pallas as pl
from jax.experimental.pallas import tpu as pltpu
from jax.sharding import PartitionSpec as P

TIME_STEP = 0.5
LANES = 128
SUB = 8
PACK = 8
F32 = jnp.float32

VMEM = pl.BlockSpec(memory_space=pltpu.VMEM)
SMEM = pl.BlockSpec(memory_space=pltpu.SMEM)
HBM = pl.BlockSpec(memory_space=pltpu.HBM)


def shape_of(*dims):
    return jax.ShapeDtypeStruct(dims, F32)


def call(kernel, out_shape, n_in, specs=None, outs=None, scratch=(), cost=2_000_000, limit=32):
    return pl.pallas_call(
        kernel,
        out_shape=out_shape,
        in_specs=specs if specs is not None else [VMEM] * n_in,
        out_specs=outs if outs is not None else jax.tree.map(lambda _: VMEM, out_shape),
        scratch_shapes=list(scratch),
        compiler_params=pltpu.CompilerParams(vmem_limit_bytes=limit * 1024 * 1024),
        cost_estimate=pl.CostEstimate(flops=cost, bytes_accessed=cost, transcendentals=0),
    )


def in_hbm(array):
    return pltpu.with_memory_space_constraint(array, pltpu.HBM)


def lanes_of(shape):
    return lax.broadcasted_iota(jnp.int32, shape, len(shape) - 1)


def subs_of(shape):
    return lax.broadcasted_iota(jnp.int32, shape, len(shape) - 2)


def start_kernel(
    right_hbm, damping_hbm, label_hbm, w0_ref, inv_ref, pack_ref, stat_ref, right_ref, damping_ref, label_ref, sems
):
    nx, ny, nz = right_ref.shape
    parts = sems.shape[1]
    size = nx // parts
    copies = []
    for part in range(parts):
        here = pl.ds(part * size, size)
        for k, (source, target) in enumerate(
            ((right_hbm, right_ref), (damping_hbm, damping_ref), (label_hbm, label_ref))
        ):
            copies.append(pltpu.make_async_copy(source.at[here], target.at[here], sems.at[k, part]))
            copies[-1].start()
    gz = lax.axis_index("gz")
    lane = lanes_of((ny, nz))
    packed_w = jnp.zeros((ny, nz), F32)
    packed_i = jnp.zeros((ny, nz), F32)
    energy = jnp.zeros((ny, nz), F32)
    cells = jnp.zeros((ny, nz), F32)
    for x in range(nx):
        if x % size == 0:
            for k in range(3):
                copies[3 * (x // size) + k].wait()
        label = label_ref[x].astype(F32)
        right = right_ref[x]
        inv = 1.0 / (12.0 + damping_ref[x] * (1.0 + 3.0 * label))
        w0 = right * inv
        w0_ref[x] = w0
        inv_ref[x] = inv
        energy = energy + right * w0
        cells = cells + label
        turn = (PACK * x + 3) % nz
        begin = PACK * x + 3 * gz
        chosen = (lane >= begin) & (lane < begin + 3)
        packed_w = jnp.where(chosen, pltpu.roll(w0, turn, 1), packed_w)
        packed_i = jnp.where(chosen, pltpu.roll(inv, turn, 1), packed_i)
    pack_ref[0] = packed_w
    pack_ref[1] = packed_i
    stat_ref[0] = jnp.broadcast_to(jnp.sum(energy, axis=0, keepdims=True), (SUB, nz))
    stat_ref[1] = jnp.broadcast_to(jnp.sum(cells, axis=0, keepdims=True), (SUB, nz))


def y_faces_kernel(w0_ref, inv_ref, own_ref, got_ref, slab_ref, up_ref, down_ref):
    nx, ny, nz = w0_ref.shape
    sub = subs_of((SUB, nz))
    slab_ref[...] = own_ref[...] + got_ref[...]
    for x in range(nx + 1):
        if x < nx:
            w_last, w_first = w0_ref[x, ny - SUB :], w0_ref[x, :SUB]
            i_last, i_first = inv_ref[x, ny - SUB :], inv_ref[x, :SUB]
        else:
            w_last, w_first = slab_ref[0, ny - SUB :], slab_ref[0, :SUB]
            i_last, i_first = slab_ref[1, ny - SUB :], slab_ref[1, :SUB]
        up_ref[x] = jnp.where(sub >= 5, w_last, pltpu.roll(i_last, 4, 0))
        down_ref[x] = jnp.where(sub <= 2, w_first, pltpu.roll(i_first, 4, 0))


def y_face_one_kernel(w0_ref, inv_ref, own_ref, got_ref, slab_ref, face_ref):
    nx, ny, nz = w0_ref.shape
    sub = subs_of((SUB, nz))
    up = lax.axis_index("gy") == 0
    keep_w = jnp.where(up, sub, SUB - 1 - sub) >= 5
    slab_ref[...] = own_ref[...] + got_ref[...]
    for x in range(nx + 1):
        if x < nx:
            w_last, w_first = w0_ref[x, ny - SUB :], w0_ref[x, :SUB]
            i_last, i_first = inv_ref[x, ny - SUB :], inv_ref[x, :SUB]
        else:
            w_last, w_first = slab_ref[0, ny - SUB :], slab_ref[0, :SUB]
            i_last, i_first = slab_ref[1, ny - SUB :], slab_ref[1, :SUB]
        w_face = jnp.where(up, w_last, w_first)
        i_face = jnp.where(up, i_last, i_first)
        face_ref[x] = jnp.where(keep_w, w_face, pltpu.roll(i_face, 4, 0))


def x_faces_kernel(one, after_ref, w0_ref, inv_ref, slab_ref, *refs):
    if one:
        got_ref, halo_ref, first_ref, second_ref = refs
    else:
        low_ref, high_ref, halo_ref, first_ref, second_ref = refs
    nx, ny, nz = w0_ref.shape
    sub = subs_of((SUB, nz))
    lane = lanes_of((ny + SUB, nz))
    if one:
        gy = lax.axis_index("gy")
        w_rows = ((gy == 1) & (sub >= 5)) | ((gy == 0) & (sub <= 2))
        i_rows = ((gy == 1) & (sub >= 6)) | ((gy == 0) & (sub <= 1))
    for x in range(nx + 1):
        if one:
            got = got_ref[x]
            halo_ref[0, x] = jnp.where(w_rows, got, 0.0)
            halo_ref[1, x] = jnp.where(i_rows, pltpu.roll(got, 4, 0), 0.0)
        else:
            low, high = low_ref[x], high_ref[x]
            halo_ref[0, x] = jnp.where(sub >= 5, low, jnp.where(sub <= 2, high, 0.0))
            halo_ref[1, x] = jnp.where(
                sub >= 6, pltpu.roll(low, 4, 0), jnp.where(sub <= 1, pltpu.roll(high, 4, 0), 0.0)
            )
    odd = lax.rem(lax.axis_index("gx"), 2)
    slab_w = jnp.concatenate([slab_ref[0], halo_ref[0, nx]], axis=0)
    slab_i = jnp.concatenate([slab_ref[1], halo_ref[1, nx]], axis=0)
    half = pltpu.roll(slab_i, nz // 2, 1)
    up = jnp.where(lane >= nz - 3 * PACK, slab_w, half)
    down = jnp.where(lane < 3 * PACK, slab_w, half)
    for face_ref, lower in ((first_ref, odd), (second_ref, 1 - odd)):
        for k in range(5):
            field, source = (0, w0_ref) if k < 3 else (1, inv_ref)
            place = (1 - lower) * (nx - 3 + field) + k - 3 * field
            face_ref[k, :ny] = source[place]
            face_ref[k, ny:] = halo_ref[field, place]
        face_ref[5] = jnp.where(lower == 1, down, up)


def slab_step(v, s, inv):
    width = v.shape[1]
    across = pltpu.roll(v, PACK, 1) + pltpu.roll(v, width - PACK, 1)
    q = v + 0.5 * (s + across)
    if inv is None:
        return q, None
    total = (
        pltpu.roll(q, 1, 1) + pltpu.roll(q, width - 1, 1) + s + across
        + 0.5 * (pltpu.roll(s, PACK, 1) + pltpu.roll(s, width - PACK, 1))
    )
    return q, total * inv


def along_z(q, half, column, gz):
    nz = q.shape[1]
    lane = lanes_of(q.shape)
    entry = (nz - 1) * (1 - gz)
    turn = lax.rem(entry - (column + 3 - gz) + 2 * nz, nz)
    up = jnp.where(lane == nz - 1, 0.0, pltpu.roll(q, nz - 1, 1))
    down = jnp.where(lane == 0, 0.0, pltpu.roll(q, 1, 1))
    return up + down + jnp.where(lane == entry, pltpu.roll(half, turn, 1), 0.0)


def sweep(stage, spans, nx, ny, nz, gz, get, get_inv, put, slab_q, sums):
    margin = 2 - stage
    start = SUB - margin
    tiles = ny // SUB + (margin > 0)
    own = subs_of((SUB, nz)) >= margin
    parts = [[], []]
    for tile in range(tiles):
        row = start + SUB * tile
        q_rows = slab_q[SUB * tile : SUB * tile + SUB]
        acc = [jnp.zeros((SUB, nz), F32) for _ in range(2)]

        def beside(x):
            return get(x, row - 1) + get(x, row + 1)

        for first, last in spans:
            s_low, s_mid = beside(first - 1), beside(first)
            v_low, v_mid = get(first - 1, row), get(first, row)
            for x in range(first, last):
                v_high, s_high = get(x + 1, row), beside(x + 1)
                across = v_low + v_high
                column = (PACK * x) % (2 * nz)
                half = q_rows[:, column // nz * nz : column // nz * nz + nz]
                rest = s_mid + across
                total = along_z(v_mid + 0.5 * rest, half, column % nz, gz) + rest + 0.5 * (s_low + s_high)
                if stage < 2:
                    after = total * get_inv(x, row)
                    put(x, row, after)
                if 0 <= x < nx:
                    acc[0] = acc[0] + v_mid * total
                    if stage < 2:
                        acc[1] = acc[1] + after * total
                v_low, v_mid, s_low, s_mid = v_mid, v_high, s_mid, s_high
        for k in range(2):
            parts[k].append(acc[k])
    for k in range(2 if stage < 2 else 1):
        part = parts[k]
        total = part[1]
        for other in part[2 : ny // SUB]:
            total = total + other
        total = total + (jnp.where(own, part[0], part[-1]) if margin else part[0])
        sums[2 * stage + k] = total


def inner_kernel(
    w0_ref, inv_ref, slab_ref, halo_ref, a_ref, i_ref, b_ref, c_ref, sum_ref, slabs_ref,
):
    nx, ny, nz = w0_ref.shape
    gz = lax.axis_index("gz")
    for x in range(nx):
        for ref, own, halo in ((a_ref, w0_ref[x], halo_ref[0, x]), (i_ref, inv_ref[x], halo_ref[1, x])):
            ref[x, :SUB] = halo
            ref[x, SUB : SUB + ny] = own
            ref[x, SUB + ny :] = halo
    for k in range(2):
        slabs_ref[3 * k, :SUB] = halo_ref[k, nx]
        slabs_ref[3 * k, SUB : SUB + ny] = slab_ref[k]
        slabs_ref[3 * k, SUB + ny :] = halo_ref[k, nx]
    sums = {}
    for stage in range(3):
        source, target = (a_ref, b_ref, c_ref)[stage], (b_ref, c_ref, None)[stage]
        start, size = SUB - 2 + stage, ny if stage == 2 else ny + SUB
        v = slabs_ref[stage, start : start + size]
        s = slabs_ref[stage, start - 1 : start - 1 + size] + slabs_ref[stage, start + 1 : start + 1 + size]
        q, after = slab_step(v, s, slabs_ref[3, start : start + size] if stage < 2 else None)
        if stage < 2:
            slabs_ref[stage + 1, start : start + size] = after

        def put(x, row, value):
            target[x, row : row + SUB] = value

        sweep(
            stage, [(1 + stage, nx - 1 - stage)], nx, ny, nz, gz,
            lambda x, row: source[x, row : row + SUB], lambda x, row: i_ref[x, row : row + SUB],
            put, q, sums,
        )
    for k in range(5):
        sum_ref[k] = sums[k]


def outer_kernel(
    a_ref, i_ref, b_ref, c_ref, slab_ref, halo_ref, sum_ref, first_ref, second_ref, stat_ref,
    ea_ref, eb_ref, ec_ref, slabs_ref, total_ref, ei_ref, si_ref,
):
    nx, ny, nz = a_ref.shape[0], a_ref.shape[1] - 2 * SUB, a_ref.shape[2]
    ring = ny + SUB
    gz = lax.axis_index("gz")
    odd = lax.rem(lax.axis_index("gx"), 2) == 1

    def low(k):
        return jnp.where(odd, first_ref[k], second_ref[k])

    def high(k):
        return jnp.where(odd, second_ref[k], first_ref[k])

    for ref, at, plane in (
        [(ea_ref, k, low(k)) for k in range(3)] + [(ea_ref, 3 + k, high(k)) for k in range(3)]
        + [(ei_ref, k, low(3 + k)) for k in range(2)] + [(ei_ref, 2 + k, high(3 + k)) for k in range(2)]
    ):
        ref[at, :SUB] = plane[ny:]
        ref[at, SUB : SUB + ny] = plane[:ny]
        ref[at, SUB + ny :] = plane[ny:]

    lane = lanes_of((ring, nz))
    lo5, hi5 = low(5), high(5)
    slab_w = jnp.where(lane < 3 * PACK, hi5, 0.0) + jnp.where(lane >= nz - 3 * PACK, lo5, 0.0)
    lo5, hi5 = pltpu.roll(lo5, nz // 2, 1), pltpu.roll(hi5, nz // 2, 1)
    slab_i = jnp.where(lane < 2 * PACK, hi5, 0.0) + jnp.where(lane >= nz - 2 * PACK, lo5, 0.0)
    for ref, k, beyond in ((slabs_ref, 0, slab_w), (si_ref, 1, slab_i)):
        ref[0, SUB : SUB + ny, :nz] = slab_ref[k]
        ref[0, SUB : SUB + ny, nz:] = beyond[:ny]
        for rows in (slice(0, SUB), slice(SUB + ny, SUB + ring)):
            ref[0, rows, :nz] = halo_ref[k, nx]
            ref[0, rows, nz:] = beyond[ny:]

    def reader(inside_ref, edge_ref, first, count):
        def get(x, row):
            if first <= x < nx - first:
                return inside_ref[x, row : row + SUB]
            at = x - (first - count) if x < first else x - (nx - first) + count
            return edge_ref[at, row : row + SUB]

        return get

    sums = {}
    for stage in range(3):
        get = reader((a_ref, b_ref, c_ref)[stage], (ea_ref, eb_ref, ec_ref)[stage], stage, 3)
        start, size = SUB - 2 + stage, ny if stage == 2 else ring
        v = slabs_ref[stage, start : start + size]
        s = slabs_ref[stage, start - 1 : start - 1 + size] + slabs_ref[stage, start + 1 : start + 1 + size]
        q, after = slab_step(v, s, si_ref[0, start : start + size] if stage < 2 else None)
        if stage < 2:
            slabs_ref[stage + 1, start : start + size] = after

        def put(x, row, value):
            edge_ref = (eb_ref, ec_ref)[stage]
            at = x - (stage - 2) if x < nx // 2 else x - (nx - 1 - stage) + 3
            edge_ref[at, row : row + SUB] = value

        sweep(
            stage, [(stage - 2, stage + 1), (nx - 1 - stage, nx + 2 - stage)], nx, ny, nz, gz,
            get, reader(i_ref, ei_ref, 0, 2), put, q, sums,
        )

    total_ref[0:1] = stat_ref[0, 0:1]
    for k in range(5):
        total_ref[k + 1 : k + 2] = jnp.sum(sums[k] + sum_ref[k], axis=0, keepdims=True)
    total_ref[6:8] = jnp.zeros((2, nz), F32)
    here = (lax.axis_index("gx") * lax.axis_size("gy") + lax.axis_index("gy")) * lax.axis_size("gz") + gz
    count = jnp.sum(stat_ref[1], axis=1, keepdims=True)
    total_ref[8:16] = jnp.where(lanes_of((SUB, nz)) == here, count, 0.0)


def shift_left(v, amount, lane):
    rows = v.shape[0]
    if amount < LANES:
        turned = pltpu.roll(v, LANES - amount, 1)
        below = pltpu.roll(turned, rows - 1, 0)
        return jnp.where(lane < LANES - amount, turned, below)
    return jnp.concatenate([v[amount // LANES :], v[: amount // LANES]], axis=0)


def plan_kernel(after_ref, label_ref, plan_ref):
    rows = label_ref.shape[0]
    lane = lanes_of((rows, LANES))
    row = subs_of((rows, LANES))
    heart = label_ref[...] == 1
    ones = heart.astype(jnp.bfloat16)
    upper = (subs_of((LANES, LANES)) < lanes_of((LANES, LANES))).astype(jnp.bfloat16)
    in_row = jnp.dot(ones, upper, preferred_element_type=F32)
    totals = jnp.dot(ones, jnp.ones((LANES, LANES), jnp.bfloat16), preferred_element_type=F32)
    lower = (subs_of((rows, rows)) > lanes_of((rows, rows))).astype(jnp.bfloat16)
    before = jnp.dot(lower, totals.astype(jnp.bfloat16), preferred_element_type=F32)
    rank = (in_row + before).astype(jnp.int32)
    way = jnp.where(heart, row * LANES + lane - rank, 0)
    plan = jnp.zeros((rows, LANES), jnp.int32)
    step = 1
    while step < rows * LANES:
        moving = jnp.where((way & step) != 0, way, 0)
        arriving = shift_left(moving, step, lane)
        plan = plan | (arriving & step)
        way = (way - moving) | arriving
        step *= 2
    plan_ref[...] = plan


def galerkin(t):
    g00, g01, g02, g12, g22 = t[0] - t[1], t[1] - t[2], t[2] - t[3], t[3] - t[4], t[4] - t[5]
    g11 = g02
    l10, l20 = g01 / g00, g02 / g00
    d1 = g11 - l10 * g01
    m21 = g12 - l20 * g01
    ok1 = d1 > 1e-6 * g11
    d1 = jnp.where(ok1, d1, 1.0)
    l21 = jnp.where(ok1, m21 / d1, 0.0)
    d2 = g22 - l20 * g02 - l21 * m21
    ok2 = ok1 & (d2 > 1e-6 * g22)
    d2 = jnp.where(ok2, d2, 1.0)
    y1 = t[1] - l10 * t[0]
    y2 = t[2] - l20 * t[0] - l21 * y1
    c2 = jnp.where(ok2, y2 / d2, 0.0)
    c1 = jnp.where(ok1, y1 / d1 - l21 * c2, 0.0)
    c0 = t[0] / g00 - l10 * c1 - l20 * c2
    return c0, c1, c2


def couple_kernel(stage, slot_rows, after_ref, inside_ref, edge_ref, slabs_ref, plan_ref, list_ref, value_ref):
    nx, nz = inside_ref.shape[0], inside_ref.shape[2]
    ny = inside_ref.shape[1] - 2 * SUB
    rows = nx * ny
    gz = lax.axis_index("gz")

    def get(x, row):
        if stage <= x < nx - stage:
            return inside_ref[x, row : row + SUB]
        return edge_ref[x - (stage - 3) if x < stage else x - (nx - stage) + 3, row : row + SUB]

    for tile in range(ny // SUB):
        row = SUB + SUB * tile
        slab = slabs_ref[stage, row : row + SUB, :nz]
        v_low, v_mid = get(-1, row), get(0, row)
        for x in range(nx):
            v_high = get(x + 1, row)
            beside = get(x, row - 1) + get(x, row + 1)
            at = ny * x + SUB * tile
            value_ref[at : at + SUB] = (
                along_z(v_mid, slab, PACK * x, gz) + beside + (v_low + v_high) - 6.0 * v_mid
            )
            v_low, v_mid = v_mid, v_high
    lane = lanes_of((rows, LANES))
    value = value_ref[...]
    plan = plan_ref[...]
    step = 1
    while step < rows * LANES:
        value = jnp.where((plan & step) != 0, shift_left(value, step, lane), value)
        step *= 2
    list_ref[...] = value[:slot_rows]


def add_kernel(a_ref, b_ref, after_ref, out_ref):
    out_ref[...] = a_ref[...] + b_ref[...]


def place_kernel(n_sums, *refs):
    sum_refs, refs = refs[:n_sums], refs[n_sums:]
    list_refs, refs = refs[:3], refs[3:]
    coef_ref, *out_refs, buf_ref = refs
    total = sum_refs[0][...]
    for ref in sum_refs[1:]:
        total = total + ref[...]
    sums = jnp.sum(total[0:8], axis=1, keepdims=True)
    t = [jnp.broadcast_to(sums[k : k + 1], (1, LANES)) for k in range(6)]
    coefs = galerkin(t)
    for k in range(3):
        coef_ref[k : k + 1] = coefs[k]
    value = coefs[0] * list_refs[0][...] + coefs[1] * list_refs[1][...] + coefs[2] * list_refs[2][...]
    slot_rows = value.shape[0]
    n_y, n_z = lax.axis_size("gy"), lax.axis_size("gz")
    counts = total[8:16]
    dev = lanes_of((SUB, LANES))
    mine = lax.rem(dev, n_y * n_z) == lax.axis_index("gy") * n_z + lax.axis_index("gz")
    gx = lax.axis_index("gx")
    first = subs_of((SUB, LANES)) == 0
    offset = jnp.sum(jnp.where(first & mine & (dev < gx * n_y * n_z), counts, 0.0)).astype(jnp.int32)
    count = jnp.sum(jnp.where(first & mine & (dev // (n_y * n_z) == gx), counts, 0.0)).astype(jnp.int32)
    shape = (slot_rows, LANES)
    slots = jnp.where(subs_of(shape) * LANES + lanes_of(shape) < count, value, 0.0)
    slots = jnp.concatenate([slots, jnp.zeros((SUB, LANES), F32)], axis=0)
    inner = lax.rem(offset, LANES)
    turned = pltpu.roll(slots, inner, 1)
    above = pltpu.roll(turned, 1, 0)
    moved = jnp.where(lanes_of((slot_rows + SUB, LANES)) >= inner, turned, above)
    buf_ref[...] = jnp.zeros_like(buf_ref)
    buf_ref[pl.ds(offset // LANES, slot_rows + SUB), :] = moved
    for k, out_ref in enumerate(out_refs):
        size = out_ref.shape[0]
        out_ref[...] = buf_ref[pl.ds(pl.multiple_of((gx ^ k) * size, SUB), size), :]


def potential_kernel(coef_ref, a_ref, b_ref, c_ref, eb_ref, ec_ref, x_ref):
    nx, ny, nz = x_ref.shape
    own = slice(SUB, SUB + ny)
    c0, c1, c2 = [coef_ref[k : k + 1] for k in range(3)]
    for x in range(nx):
        w1 = b_ref[x, own] if 1 <= x < nx - 1 else eb_ref[2 if x == 0 else 3, own]
        w2 = c_ref[x, own] if 2 <= x < nx - 2 else ec_ref[x + 1 if x < 2 else x - (nx - 2) + 3, own]
        x_ref[x] = c0 * a_ref[x, own] + c1 * w1 + c2 * w2


def membrane_kernel(
    half_ref, slope_ref, tau_ref, cond_ref, rev_ref, after_ref, v_ref, gates_ref, cot_ref,
    base_ref, sum_ref, factor_ref, coef_ref,
):
    n_states, rows = gates_ref.shape[:2]
    v = v_ref[...]

    def state(g, carry):
        total, current = carry
        inv_slope = 1.0 / slope_ref[g]
        tau_base = tau_ref[g]
        scaled = (v - half_ref[g]) * inv_slope
        gate = gates_ref[g]
        cot = cot_ref[g]
        steady = 1.0 / (1.0 + jnp.exp(-scaled))
        bell = jnp.exp(-scaled * scaled)
        rate = TIME_STEP / (tau_base * (0.5 + bell))
        decay = jnp.exp(-rate)
        steady_slope = steady * (1.0 - steady)
        decay_slope = decay * rate * rate * ((tau_base / TIME_STEP) * bell * (-2.0 * scaled))
        change = (steady_slope * (1.0 - decay) + (gate - steady) * decay_slope) * inv_slope
        base_ref[g] = cot * decay
        coef_ref[0, pl.ds(g, 1)] = jnp.full((1, LANES), TIME_STEP * cond_ref[g])
        coef_ref[1, pl.ds(g, 1)] = jnp.full((1, LANES), rev_ref[g])
        return total + cot * change, current + cond_ref[g] * gate

    zero = jnp.zeros((rows, LANES), F32)
    total, current = lax.fori_loop(0, n_states, state, (zero, zero), unroll=2)
    sum_ref[...] = total
    factor_ref[...] = 1.0 - TIME_STEP * current


def finish_kernel(coef_ref, vcot_ref, v_ref, sum_ref, factor_ref, base_ref, *refs):
    *landed_refs, volt_ref, gate_ref = refs
    landed = landed_refs[0][...]
    for ref in landed_refs[1:]:
        landed = landed + ref[...]
    cot = vcot_ref[...] + landed
    v = v_ref[...]
    volt_ref[...] = cot * factor_ref[...] + sum_ref[...]
    for g in range(base_ref.shape[0]):
        gate_ref[g] = base_ref[g] - (coef_ref[0, g : g + 1] * cot) * (v - coef_ref[1, g : g + 1])


def both_ways(up, down, axis):
    count = lax.axis_size(axis)
    low = lax.ppermute(up, axis, [(i, i + 1) for i in range(count - 1)])
    high = lax.ppermute(down, axis, [(i + 1, i) for i in range(count - 1)])
    return low, high


def pair_swaps(first, second, axis):
    count = lax.axis_size(axis)
    even = [(i, i ^ 1) for i in range(count)]
    between = [(i, i + 1) for i in range(1, count - 1, 2)]
    between = between + [(j, i) for i, j in between]
    return lax.ppermute(first, axis, even), lax.ppermute(second, axis, between)


def reduce_over(value, axis):
    count = lax.axis_size(axis)
    step = 1
    while step < count:
        value = value + lax.ppermute(value, axis, [(i, i ^ step) for i in range(count)])
        step *= 2
    return value


def local(
    potential_cot, damping, tissue_label, heart_index, voltage, gates, voltage_cot, gates_cot,
    half_voltage, gate_slope, tau_base, conductance, reversal,
):
    nx, ny, nz = potential_cot.shape
    rows = nx * ny
    ring = ny + SUB
    n_gx, n_gy = lax.axis_size("gx"), lax.axis_size("gy")
    n_states = gates.shape[0]
    block_rows = voltage.shape[1] // LANES
    slot_rows = heart_index.shape[3] // LANES
    block = shape_of(nx, ny, nz)
    flat = lambda a: a.reshape(rows, LANES)
    cells = lambda a: a.reshape(block_rows, LANES)
    states = lambda a: a.reshape(n_states, block_rows, LANES)

    w0, inv, packed, stat = call(
        start_kernel, (block, block, shape_of(2, ny, nz), shape_of(2, SUB, nz)), 3,
        specs=[HBM] * 3,
        scratch=[
            pltpu.VMEM((nx, ny, nz), F32), pltpu.VMEM((nx, ny, nz), F32), pltpu.VMEM((nx, ny, nz), jnp.int32),
            pltpu.SemaphoreType.DMA((3, 4)),
        ],
    )(in_hbm(potential_cot), in_hbm(damping), in_hbm(tissue_label))

    got = lax.ppermute(packed, "gz", [(0, 1), (1, 0)])
    plan = call(plan_kernel, jax.ShapeDtypeStruct((rows, LANES), jnp.int32), 2, cost=6_000_000)(
        stat, flat(tissue_label)
    )

    face = shape_of(nx + 1, SUB, nz)
    slab_shape = shape_of(2, ny, nz)
    x_shapes = (shape_of(2, nx + 1, SUB, nz), shape_of(6, ring, nz), shape_of(6, ring, nz))
    if n_gy == 2:
        slab, mine = call(y_face_one_kernel, (slab_shape, face), 4)(w0, inv, packed, got)
        halo = (lax.ppermute(mine, "gy", [(0, 1), (1, 0)]),)
    else:
        slab, up, down = call(y_faces_kernel, (slab_shape, face, face), 4)(w0, inv, packed, got)
        halo = both_ways(up, down, "gy")
    edge_rows, first, second = call(
        functools.partial(x_faces_kernel, n_gy == 2), x_shapes, 4 + len(halo)
    )(plan, w0, inv, slab, *halo)
    first, second = pair_swaps(first, second, "gx")

    tall = ring + SUB
    planes = shape_of(nx, tall, nz)
    edges = shape_of(6, tall, nz)
    in0, in_inv, in1, in2, in_sums = call(
        inner_kernel,
        (planes,) * 4 + (shape_of(5, SUB, nz),),
        4,
        scratch=[pltpu.VMEM((4, tall, nz), F32)],
        cost=6_000_000,
    )(w0, inv, slab, edge_rows)
    ends0, ends1, ends2, slabs, sums = call(
        outer_kernel,
        (edges,) * 3 + (shape_of(3, tall, 2 * nz), shape_of(16, nz)),
        10,
        scratch=[pltpu.VMEM((4, tall, nz), F32), pltpu.VMEM((1, tall, 2 * nz), F32)],
    )(in0, in_inv, in1, in2, slab, edge_rows, in_sums, first, second, stat)

    def couple(stage, after, inside, ends):
        return call(
            functools.partial(couple_kernel, stage, slot_rows),
            shape_of(slot_rows, LANES),
            5,
            scratch=[pltpu.VMEM((rows, LANES), F32)],
            cost=6_000_000,
        )(after, inside, ends, slabs, plan)

    def add(value, axis, step, after):
        got = lax.ppermute(value, axis, [(i, i ^ step) for i in range(lax.axis_size(axis))])
        return call(add_kernel, shape_of(16, nz), 3)(value, got, after)

    list0 = couple(0, sums, in0, ends0)
    sums = add(sums, "gz", 1, list0)
    list1 = couple(1, sums, in1, ends1)
    sums = add(sums, "gy", 1, list1)
    for step in [2**k for k in range(1, n_gy.bit_length() - 1)]:
        sums = add(sums, "gy", step, list1)
    list2 = couple(2, sums, in2, ends2)
    if n_gx <= 4:
        sums = [sums] + [lax.ppermute(sums, "gx", [(i, i ^ k) for i in range(n_gx)]) for k in range(1, n_gx)]
    else:
        sums = [reduce_over(sums, "gx")]

    coefs, *blocks = call(
        functools.partial(place_kernel, len(sums)),
        (shape_of(SUB, LANES),) + (shape_of(block_rows, LANES),) * n_gx,
        len(sums) + 3,
        scratch=[pltpu.VMEM((n_gx * block_rows + slot_rows + SUB, LANES), F32)],
    )(*sums, list0, list1, list2)
    landed = blocks[:1] + [
        lax.ppermute(blocks[k], "gx", [(i, i ^ k) for i in range(n_gx)]) for k in range(1, n_gx)
    ]

    solution = call(potential_kernel, block, 6)(coefs, in0, in1, in2, ends1, ends2)
    base, total_change, factor, state_coefs = call(
        membrane_kernel,
        (
            shape_of(n_states, block_rows, LANES), shape_of(block_rows, LANES), shape_of(block_rows, LANES),
            shape_of(2, n_states, LANES),
        ),
        9,
        specs=[SMEM] * 5 + [VMEM] * 4,
        cost=6_000_000,
    )(
        half_voltage, gate_slope, tau_base, conductance, reversal,
        coefs, cells(voltage), states(gates), states(gates_cot),
    )
    volt_grad, gate_grad = call(
        finish_kernel,
        (shape_of(block_rows, LANES), shape_of(n_states, block_rows, LANES)),
        6 + n_gx,
    )(state_coefs, cells(voltage_cot), cells(voltage), total_change, factor, base, *landed)
    return solution, volt_grad.reshape(voltage.shape), gate_grad.reshape(gates.shape)


def solution(mesh):
    grid = P(("groups", "gx"), "gy", "gz")
    cells = P(("groups", "gy", "gz"), "gx")
    states = P(None, ("groups", "gy", "gz"), "gx")
    in_specs = (
        grid, grid, grid, P(("groups", "gx"), "gy", "gz", None), cells, states, cells, states,
        P(), P(), P(), P(), P(),
    )
    return jax.shard_map(
        local, mesh=mesh, in_specs=in_specs, out_specs=(grid, cells, states), check_vma=False
    )
```

```python
import functools

import jax
import jax.numpy as jnp
from jax import lax
from jax.experimental import pallas as pl
from jax.experimental.pallas import tpu as pltpu
from jax.sharding import PartitionSpec as P

TIME_STEP = 0.5
LANES = 128
SUB = 8
PACK = 8
F32 = jnp.float32

VMEM = pl.BlockSpec(memory_space=pltpu.VMEM)
SMEM = pl.BlockSpec(memory_space=pltpu.SMEM)
HBM = pl.BlockSpec(memory_space=pltpu.HBM)


def shape_of(*dims):
    return jax.ShapeDtypeStruct(dims, F32)


def call(kernel, out_shape, n_in, specs=None, outs=None, scratch=(), cost=2_000_000, limit=32):
    return pl.pallas_call(
        kernel,
        out_shape=out_shape,
        in_specs=specs if specs is not None else [VMEM] * n_in,
        out_specs=outs if outs is not None else jax.tree.map(lambda _: VMEM, out_shape),
        scratch_shapes=list(scratch),
        compiler_params=pltpu.CompilerParams(vmem_limit_bytes=limit * 1024 * 1024),
        cost_estimate=pl.CostEstimate(flops=cost, bytes_accessed=cost, transcendentals=0),
    )


def in_hbm(array):
    return pltpu.with_memory_space_constraint(array, pltpu.HBM)


def lanes_of(shape):
    return lax.broadcasted_iota(jnp.int32, shape, len(shape) - 1)


def subs_of(shape):
    return lax.broadcasted_iota(jnp.int32, shape, len(shape) - 2)


def start_kernel(
    right_hbm, damping_hbm, label_hbm, w0_ref, inv_ref, pack_ref, stat_ref, right_ref, damping_ref, label_ref, sems
):
    nx, ny, nz = right_ref.shape
    parts = sems.shape[1]
    size = nx // parts
    copies = []
    for part in range(parts):
        here = pl.ds(part * size, size)
        for k, (source, target) in enumerate(
            ((right_hbm, right_ref), (damping_hbm, damping_ref), (label_hbm, label_ref))
        ):
            copies.append(pltpu.make_async_copy(source.at[here], target.at[here], sems.at[k, part]))
            copies[-1].start()
    gz = lax.axis_index("gz")
    lane = lanes_of((ny, nz))
    packed_w = jnp.zeros((ny, nz), F32)
    packed_i = jnp.zeros((ny, nz), F32)
    energy = jnp.zeros((ny, nz), F32)
    cells = jnp.zeros((ny, nz), F32)
    for x in range(nx):
        if x % size == 0:
            for k in range(3):
                copies[3 * (x // size) + k].wait()
        label = label_ref[x].astype(F32)
        right = right_ref[x]
        inv = 1.0 / (12.0 + damping_ref[x] * (1.0 + 3.0 * label))
        w0 = right * inv
        w0_ref[x] = w0
        inv_ref[x] = inv
        energy = energy + right * w0
        cells = cells + label
        turn = (PACK * x + 3) % nz
        begin = PACK * x + 3 * gz
        chosen = (lane >= begin) & (lane < begin + 3)
        packed_w = jnp.where(chosen, pltpu.roll(w0, turn, 1), packed_w)
        packed_i = jnp.where(chosen, pltpu.roll(inv, turn, 1), packed_i)
    pack_ref[0] = packed_w
    pack_ref[1] = packed_i
    stat_ref[0] = jnp.broadcast_to(jnp.sum(energy, axis=0, keepdims=True), (SUB, nz))
    stat_ref[1] = jnp.broadcast_to(jnp.sum(cells, axis=0, keepdims=True), (SUB, nz))


def y_faces_kernel(w0_ref, inv_ref, own_ref, got_ref, slab_ref, up_ref, down_ref):
    nx, ny, nz = w0_ref.shape
    sub = subs_of((SUB, nz))
    slab_ref[...] = own_ref[...] + got_ref[...]
    for x in range(nx + 1):
        if x < nx:
            w_last, w_first = w0_ref[x, ny - SUB :], w0_ref[x, :SUB]
            i_last, i_first = inv_ref[x, ny - SUB :], inv_ref[x, :SUB]
        else:
            w_last, w_first = slab_ref[0, ny - SUB :], slab_ref[0, :SUB]
            i_last, i_first = slab_ref[1, ny - SUB :], slab_ref[1, :SUB]
        up_ref[x] = jnp.where(sub >= 5, w_last, pltpu.roll(i_last, 4, 0))
        down_ref[x] = jnp.where(sub <= 2, w_first, pltpu.roll(i_first, 4, 0))


def y_face_one_kernel(w0_ref, inv_ref, own_ref, got_ref, slab_ref, face_ref):
    nx, ny, nz = w0_ref.shape
    sub = subs_of((SUB, nz))
    up = lax.axis_index("gy") == 0
    keep_w = jnp.where(up, sub, SUB - 1 - sub) >= 5
    slab_ref[...] = own_ref[...] + got_ref[...]
    for x in range(nx + 1):
        if x < nx:
            w_last, w_first = w0_ref[x, ny - SUB :], w0_ref[x, :SUB]
            i_last, i_first = inv_ref[x, ny - SUB :], inv_ref[x, :SUB]
        else:
            w_last, w_first = slab_ref[0, ny - SUB :], slab_ref[0, :SUB]
            i_last, i_first = slab_ref[1, ny - SUB :], slab_ref[1, :SUB]
        w_face = jnp.where(up, w_last, w_first)
        i_face = jnp.where(up, i_last, i_first)
        face_ref[x] = jnp.where(keep_w, w_face, pltpu.roll(i_face, 4, 0))


def x_faces_kernel(one, after_ref, w0_ref, inv_ref, slab_ref, *refs):
    if one:
        got_ref, halo_ref, first_ref, second_ref = refs
    else:
        low_ref, high_ref, halo_ref, first_ref, second_ref = refs
    nx, ny, nz = w0_ref.shape
    sub = subs_of((SUB, nz))
    lane = lanes_of((ny + SUB, nz))
    if one:
        gy = lax.axis_index("gy")
        w_rows = ((gy == 1) & (sub >= 5)) | ((gy == 0) & (sub <= 2))
        i_rows = ((gy == 1) & (sub >= 6)) | ((gy == 0) & (sub <= 1))
    for x in range(nx + 1):
        if one:
            got = got_ref[x]
            halo_ref[0, x] = jnp.where(w_rows, got, 0.0)
            halo_ref[1, x] = jnp.where(i_rows, pltpu.roll(got, 4, 0), 0.0)
        else:
            low, high = low_ref[x], high_ref[x]
            halo_ref[0, x] = jnp.where(sub >= 5, low, jnp.where(sub <= 2, high, 0.0))
            halo_ref[1, x] = jnp.where(
                sub >= 6, pltpu.roll(low, 4, 0), jnp.where(sub <= 1, pltpu.roll(high, 4, 0), 0.0)
            )
    odd = lax.rem(lax.axis_index("gx"), 2)
    slab_w = jnp.concatenate([slab_ref[0], halo_ref[0, nx]], axis=0)
    slab_i = jnp.concatenate([slab_ref[1], halo_ref[1, nx]], axis=0)
    half = pltpu.roll(slab_i, nz // 2, 1)
    up = jnp.where(lane >= nz - 3 * PACK, slab_w, half)
    down = jnp.where(lane < 3 * PACK, slab_w, half)
    for face_ref, lower in ((first_ref, odd), (second_ref, 1 - odd)):
        for k in range(5):
            field, source = (0, w0_ref) if k < 3 else (1, inv_ref)
            place = (1 - lower) * (nx - 3 + field) + k - 3 * field
            face_ref[k, :ny] = source[place]
            face_ref[k, ny:] = halo_ref[field, place]
        face_ref[5] = jnp.where(lower == 1, down, up)


def slab_step(v, s, inv):
    width = v.shape[1]
    across = pltpu.roll(v, PACK, 1) + pltpu.roll(v, width - PACK, 1)
    q = v + 0.5 * (s + across)
    if inv is None:
        return q, None
    total = (
        pltpu.roll(q, 1, 1) + pltpu.roll(q, width - 1, 1) + s + across
        + 0.5 * (pltpu.roll(s, PACK, 1) + pltpu.roll(s, width - PACK, 1))
    )
    return q, total * inv


def along_z(q, half, column, gz):
    nz = q.shape[1]
    lane = lanes_of(q.shape)
    entry = (nz - 1) * (1 - gz)
    turn = lax.rem(entry - (column + 3 - gz) + 2 * nz, nz)
    up = jnp.where(lane == nz - 1, 0.0, pltpu.roll(q, nz - 1, 1))
    down = jnp.where(lane == 0, 0.0, pltpu.roll(q, 1, 1))
    return up + down + jnp.where(lane == entry, pltpu.roll(half, turn, 1), 0.0)


def sweep(stage, spans, nx, ny, nz, gz, get, get_inv, put, slab_q, sums):
    margin = 2 - stage
    start = SUB - margin
    tiles = ny // SUB + (margin > 0)
    own = subs_of((SUB, nz)) >= margin
    parts = [[], []]
    for tile in range(tiles):
        row = start + SUB * tile
        q_rows = slab_q[SUB * tile : SUB * tile + SUB]
        acc = [jnp.zeros((SUB, nz), F32) for _ in range(2)]

        def beside(x):
            return get(x, row - 1) + get(x, row + 1)

        for first, last in spans:
            s_low, s_mid = beside(first - 1), beside(first)
            v_low, v_mid = get(first - 1, row), get(first, row)
            for x in range(first, last):
                v_high, s_high = get(x + 1, row), beside(x + 1)
                across = v_low + v_high
                column = (PACK * x) % (2 * nz)
                half = q_rows[:, column // nz * nz : column // nz * nz + nz]
                rest = s_mid + across
                total = along_z(v_mid + 0.5 * rest, half, column % nz, gz) + rest + 0.5 * (s_low + s_high)
                if stage < 2:
                    after = total * get_inv(x, row)
                    put(x, row, after)
                if 0 <= x < nx:
                    acc[0] = acc[0] + v_mid * total
                    if stage < 2:
                        acc[1] = acc[1] + after * total
                v_low, v_mid, s_low, s_mid = v_mid, v_high, s_mid, s_high
        for k in range(2):
            parts[k].append(acc[k])
    for k in range(2 if stage < 2 else 1):
        part = parts[k]
        total = part[1]
        for other in part[2 : ny // SUB]:
            total = total + other
        total = total + (jnp.where(own, part[0], part[-1]) if margin else part[0])
        sums[2 * stage + k] = total


def inner_kernel(
    w0_ref, inv_ref, slab_ref, halo_ref, a_ref, i_ref, b_ref, c_ref, sum_ref, slabs_ref,
):
    nx, ny, nz = w0_ref.shape
    gz = lax.axis_index("gz")
    for x in range(nx):
        for ref, own, halo in ((a_ref, w0_ref[x], halo_ref[0, x]), (i_ref, inv_ref[x], halo_ref[1, x])):
            ref[x, :SUB] = halo
            ref[x, SUB : SUB + ny] = own
            ref[x, SUB + ny :] = halo
    for k in range(2):
        slabs_ref[3 * k, :SUB] = halo_ref[k, nx]
        slabs_ref[3 * k, SUB : SUB + ny] = slab_ref[k]
        slabs_ref[3 * k, SUB + ny :] = halo_ref[k, nx]
    sums = {}
    for stage in range(3):
        source, target = (a_ref, b_ref, c_ref)[stage], (b_ref, c_ref, None)[stage]
        start, size = SUB - 2 + stage, ny if stage == 2 else ny + SUB
        v = slabs_ref[stage, start : start + size]
        s = slabs_ref[stage, start - 1 : start - 1 + size] + slabs_ref[stage, start + 1 : start + 1 + size]
        q, after = slab_step(v, s, slabs_ref[3, start : start + size] if stage < 2 else None)
        if stage < 2:
            slabs_ref[stage + 1, start : start + size] = after

        def put(x, row, value):
            target[x, row : row + SUB] = value

        sweep(
            stage, [(1 + stage, nx - 1 - stage)], nx, ny, nz, gz,
            lambda x, row: source[x, row : row + SUB], lambda x, row: i_ref[x, row : row + SUB],
            put, q, sums,
        )
    for k in range(5):
        sum_ref[k] = sums[k]


def outer_kernel(
    after_ref, a_ref, i_ref, b_ref, c_ref, slab_ref, halo_ref, sum_ref, first_ref, second_ref, stat_ref,
    ea_ref, eb_ref, ec_ref, slabs_ref, total_ref, ei_ref, si_ref,
):
    nx, ny, nz = a_ref.shape[0], a_ref.shape[1] - 2 * SUB, a_ref.shape[2]
    ring = ny + SUB
    gz = lax.axis_index("gz")
    gx = lax.axis_index("gx")
    odd = lax.rem(gx, 2) == 1
    inside = jnp.where((gx > 0) & (gx < lax.axis_size("gx") - 1), 1.0, 0.0).astype(F32)

    def low(k):
        return jnp.where(odd, first_ref[k], second_ref[k] * inside)

    def high(k):
        return jnp.where(odd, second_ref[k] * inside, first_ref[k])

    for ref, at, plane in (
        [(ea_ref, k, low(k)) for k in range(3)] + [(ea_ref, 3 + k, high(k)) for k in range(3)]
        + [(ei_ref, k, low(3 + k)) for k in range(2)] + [(ei_ref, 2 + k, high(3 + k)) for k in range(2)]
    ):
        ref[at, :SUB] = plane[ny:]
        ref[at, SUB : SUB + ny] = plane[:ny]
        ref[at, SUB + ny :] = plane[ny:]

    lane = lanes_of((ring, nz))
    lo5, hi5 = low(5), high(5)
    slab_w = jnp.where(lane < 3 * PACK, hi5, 0.0) + jnp.where(lane >= nz - 3 * PACK, lo5, 0.0)
    lo5, hi5 = pltpu.roll(lo5, nz // 2, 1), pltpu.roll(hi5, nz // 2, 1)
    slab_i = jnp.where(lane < 2 * PACK, hi5, 0.0) + jnp.where(lane >= nz - 2 * PACK, lo5, 0.0)
    for ref, k, beyond in ((slabs_ref, 0, slab_w), (si_ref, 1, slab_i)):
        ref[0, SUB : SUB + ny, :nz] = slab_ref[k]
        ref[0, SUB : SUB + ny, nz:] = beyond[:ny]
        for rows in (slice(0, SUB), slice(SUB + ny, SUB + ring)):
            ref[0, rows, :nz] = halo_ref[k, nx]
            ref[0, rows, nz:] = beyond[ny:]

    def reader(inside_ref, edge_ref, first, count):
        def get(x, row):
            if first <= x < nx - first:
                return inside_ref[x, row : row + SUB]
            at = x - (first - count) if x < first else x - (nx - first) + count
            return edge_ref[at, row : row + SUB]

        return get

    sums = {}
    for stage in range(3):
        get = reader((a_ref, b_ref, c_ref)[stage], (ea_ref, eb_ref, ec_ref)[stage], stage, 3)
        start, size = SUB - 2 + stage, ny if stage == 2 else ring
        v = slabs_ref[stage, start : start + size]
        s = slabs_ref[stage, start - 1 : start - 1 + size] + slabs_ref[stage, start + 1 : start + 1 + size]
        q, after = slab_step(v, s, si_ref[0, start : start + size] if stage < 2 else None)
        if stage < 2:
            slabs_ref[stage + 1, start : start + size] = after

        def put(x, row, value):
            edge_ref = (eb_ref, ec_ref)[stage]
            at = x - (stage - 2) if x < nx // 2 else x - (nx - 1 - stage) + 3
            edge_ref[at, row : row + SUB] = value

        sweep(
            stage, [(stage - 2, stage + 1), (nx - 1 - stage, nx + 2 - stage)], nx, ny, nz, gz,
            get, reader(i_ref, ei_ref, 0, 2), put, q, sums,
        )

    total_ref[0:1] = stat_ref[0, 0:1]
    for k in range(5):
        total_ref[k + 1 : k + 2] = jnp.sum(sums[k] + sum_ref[k], axis=0, keepdims=True)
    total_ref[6:8] = jnp.zeros((2, nz), F32)
    here = (lax.axis_index("gx") * lax.axis_size("gy") + lax.axis_index("gy")) * lax.axis_size("gz") + gz
    count = jnp.sum(stat_ref[1], axis=1, keepdims=True)
    total_ref[8:16] = jnp.where(lanes_of((SUB, nz)) == here, count, 0.0)


def shift_left(v, amount, lane):
    rows = v.shape[0]
    if amount < LANES:
        turned = pltpu.roll(v, LANES - amount, 1)
        below = pltpu.roll(turned, rows - 1, 0)
        return jnp.where(lane < LANES - amount, turned, below)
    return jnp.concatenate([v[amount // LANES :], v[: amount // LANES]], axis=0)


def plan_kernel(after_ref, label_ref, plan_ref):
    rows = label_ref.shape[0]
    lane = lanes_of((rows, LANES))
    row = subs_of((rows, LANES))
    heart = label_ref[...] == 1
    ones = heart.astype(jnp.bfloat16)
    upper = (subs_of((LANES, LANES)) < lanes_of((LANES, LANES))).astype(jnp.bfloat16)
    in_row = jnp.dot(ones, upper, preferred_element_type=F32)
    totals = jnp.dot(ones, jnp.ones((LANES, LANES), jnp.bfloat16), preferred_element_type=F32)
    lower = (subs_of((rows, rows)) > lanes_of((rows, rows))).astype(jnp.bfloat16)
    before = jnp.dot(lower, totals.astype(jnp.bfloat16), preferred_element_type=F32)
    rank = (in_row + before).astype(jnp.int32)
    way = jnp.where(heart, row * LANES + lane - rank, 0)
    plan = jnp.zeros((rows, LANES), jnp.int32)
    step = 1
    while step < rows * LANES:
        moving = jnp.where((way & step) != 0, way, 0)
        arriving = shift_left(moving, step, lane)
        plan = plan | (arriving & step)
        way = (way - moving) | arriving
        step *= 2
    plan_ref[...] = plan


def galerkin(t):
    g00, g01, g02, g12, g22 = t[0] - t[1], t[1] - t[2], t[2] - t[3], t[3] - t[4], t[4] - t[5]
    g11 = g02
    l10, l20 = g01 / g00, g02 / g00
    d1 = g11 - l10 * g01
    m21 = g12 - l20 * g01
    ok1 = d1 > 1e-6 * g11
    d1 = jnp.where(ok1, d1, 1.0)
    l21 = jnp.where(ok1, m21 / d1, 0.0)
    d2 = g22 - l20 * g02 - l21 * m21
    ok2 = ok1 & (d2 > 1e-6 * g22)
    d2 = jnp.where(ok2, d2, 1.0)
    y1 = t[1] - l10 * t[0]
    y2 = t[2] - l20 * t[0] - l21 * y1
    c2 = jnp.where(ok2, y2 / d2, 0.0)
    c1 = jnp.where(ok1, y1 / d1 - l21 * c2, 0.0)
    c0 = t[0] / g00 - l10 * c1 - l20 * c2
    return c0, c1, c2


def couple_kernel(stage, slot_rows, after_ref, inside_ref, edge_ref, slabs_ref, plan_ref, list_ref, value_ref):
    nx, nz = inside_ref.shape[0], inside_ref.shape[2]
    ny = inside_ref.shape[1] - 2 * SUB
    rows = nx * ny
    gz = lax.axis_index("gz")

    def get(x, row):
        if stage <= x < nx - stage:
            return inside_ref[x, row : row + SUB]
        return edge_ref[x - (stage - 3) if x < stage else x - (nx - stage) + 3, row : row + SUB]

    for tile in range(ny // SUB):
        row = SUB + SUB * tile
        slab = slabs_ref[stage, row : row + SUB, :nz]
        v_low, v_mid = get(-1, row), get(0, row)
        for x in range(nx):
            v_high = get(x + 1, row)
            beside = get(x, row - 1) + get(x, row + 1)
            at = ny * x + SUB * tile
            value_ref[at : at + SUB] = (
                along_z(v_mid, slab, PACK * x, gz) + beside + (v_low + v_high) - 6.0 * v_mid
            )
            v_low, v_mid = v_mid, v_high
    lane = lanes_of((rows, LANES))
    value = value_ref[...]
    plan = plan_ref[...]
    step = 1
    while step < rows * LANES:
        value = jnp.where((plan & step) != 0, shift_left(value, step, lane), value)
        step *= 2
    list_ref[...] = value[:slot_rows]


def add_kernel(a_ref, b_ref, after_ref, out_ref):
    out_ref[...] = a_ref[...] + b_ref[...]


def place_kernel(n_sums, *refs):
    sum_refs, refs = refs[:n_sums], refs[n_sums:]
    list_refs, refs = refs[:3], refs[3:]
    coef_ref, *out_refs, buf_ref = refs
    total = sum_refs[0][...]
    for ref in sum_refs[1:]:
        total = total + ref[...]
    sums = jnp.sum(total[0:8], axis=1, keepdims=True)
    t = [jnp.broadcast_to(sums[k : k + 1], (1, LANES)) for k in range(6)]
    coefs = galerkin(t)
    for k in range(3):
        coef_ref[k : k + 1] = coefs[k]
    value = coefs[0] * list_refs[0][...] + coefs[1] * list_refs[1][...] + coefs[2] * list_refs[2][...]
    slot_rows = value.shape[0]
    n_y, n_z = lax.axis_size("gy"), lax.axis_size("gz")
    counts = total[8:16]
    dev = lanes_of((SUB, LANES))
    mine = lax.rem(dev, n_y * n_z) == lax.axis_index("gy") * n_z + lax.axis_index("gz")
    gx = lax.axis_index("gx")
    first = subs_of((SUB, LANES)) == 0
    offset = jnp.sum(jnp.where(first & mine & (dev < gx * n_y * n_z), counts, 0.0)).astype(jnp.int32)
    count = jnp.sum(jnp.where(first & mine & (dev // (n_y * n_z) == gx), counts, 0.0)).astype(jnp.int32)
    shape = (slot_rows, LANES)
    slots = jnp.where(subs_of(shape) * LANES + lanes_of(shape) < count, value, 0.0)
    slots = jnp.concatenate([slots, jnp.zeros((SUB, LANES), F32)], axis=0)
    inner = lax.rem(offset, LANES)
    turned = pltpu.roll(slots, inner, 1)
    above = pltpu.roll(turned, 1, 0)
    moved = jnp.where(lanes_of((slot_rows + SUB, LANES)) >= inner, turned, above)
    buf_ref[...] = jnp.zeros_like(buf_ref)
    buf_ref[pl.ds(offset // LANES, slot_rows + SUB), :] = moved
    for k, out_ref in enumerate(out_refs):
        size = out_ref.shape[0]
        out_ref[...] = buf_ref[pl.ds(pl.multiple_of((gx ^ k) * size, SUB), size), :]


def potential_kernel(coef_ref, a_ref, b_ref, c_ref, eb_ref, ec_ref, x_ref):
    nx, ny, nz = x_ref.shape
    own = slice(SUB, SUB + ny)
    c0, c1, c2 = [coef_ref[k : k + 1] for k in range(3)]
    for x in range(nx):
        w1 = b_ref[x, own] if 1 <= x < nx - 1 else eb_ref[2 if x == 0 else 3, own]
        w2 = c_ref[x, own] if 2 <= x < nx - 2 else ec_ref[x + 1 if x < 2 else x - (nx - 2) + 3, own]
        x_ref[x] = c0 * a_ref[x, own] + c1 * w1 + c2 * w2


def membrane_kernel(
    half_ref, slope_ref, tau_ref, cond_ref, rev_ref, after_ref, v_ref, gates_ref, cot_ref,
    base_ref, sum_ref, factor_ref, coef_ref,
):
    n_states, rows = gates_ref.shape[:2]
    v = v_ref[...]

    def state(g, carry):
        total, current = carry
        inv_slope = 1.0 / slope_ref[g]
        tau_base = tau_ref[g]
        scaled = (v - half_ref[g]) * inv_slope
        gate = gates_ref[g]
        cot = cot_ref[g]
        steady = 1.0 / (1.0 + jnp.exp(-scaled))
        bell = jnp.exp(-scaled * scaled)
        rate = TIME_STEP / (tau_base * (0.5 + bell))
        decay = jnp.exp(-rate)
        steady_slope = steady * (1.0 - steady)
        decay_slope = decay * rate * rate * ((tau_base / TIME_STEP) * bell * (-2.0 * scaled))
        change = (steady_slope * (1.0 - decay) + (gate - steady) * decay_slope) * inv_slope
        base_ref[g] = cot * decay
        coef_ref[0, pl.ds(g, 1)] = jnp.full((1, LANES), TIME_STEP * cond_ref[g])
        coef_ref[1, pl.ds(g, 1)] = jnp.full((1, LANES), rev_ref[g])
        return total + cot * change, current + cond_ref[g] * gate

    zero = jnp.zeros((rows, LANES), F32)
    total, current = lax.fori_loop(0, n_states, state, (zero, zero), unroll=2)
    sum_ref[...] = total
    factor_ref[...] = 1.0 - TIME_STEP * current


def finish_kernel(coef_ref, vcot_ref, v_ref, sum_ref, factor_ref, base_ref, *refs):
    *landed_refs, volt_ref, gate_ref = refs
    landed = landed_refs[0][...]
    for ref in landed_refs[1:]:
        landed = landed + ref[...]
    cot = vcot_ref[...] + landed
    v = v_ref[...]
    volt_ref[...] = cot * factor_ref[...] + sum_ref[...]
    for g in range(base_ref.shape[0]):
        gate_ref[g] = base_ref[g] - (coef_ref[0, g : g + 1] * cot) * (v - coef_ref[1, g : g + 1])


def both_ways(up, down, axis):
    count = lax.axis_size(axis)
    low = lax.ppermute(up, axis, [(i, i + 1) for i in range(count - 1)])
    high = lax.ppermute(down, axis, [(i + 1, i) for i in range(count - 1)])
    return low, high


def pair_swaps(first, second, axis):
    count = lax.axis_size(axis)
    even = [(i, i ^ 1) for i in range(count)]
    between = [(0, 0), (count - 1, count - 1)]
    for i in range(1, count - 1, 2):
        between += [(i, i + 1), (i + 1, i)]
    return lax.ppermute(first, axis, even), lax.ppermute(second, axis, between)


def block_pairs(count, k, slots, block):
    def apart(tile, owner):
        return owner * block >= (tile + 1) * slots or (owner + 1) * block <= count * block - (count - tile) * slots

    return [(i, i if apart(i, i ^ k) and apart(i ^ k, i) else i ^ k) for i in range(count)]


def reduce_over(value, axis):
    count = lax.axis_size(axis)
    step = 1
    while step < count:
        value = value + lax.ppermute(value, axis, [(i, i ^ step) for i in range(count)])
        step *= 2
    return value


def local(
    potential_cot, damping, tissue_label, heart_index, voltage, gates, voltage_cot, gates_cot,
    half_voltage, gate_slope, tau_base, conductance, reversal,
):
    nx, ny, nz = potential_cot.shape
    rows = nx * ny
    ring = ny + SUB
    n_gx, n_gy = lax.axis_size("gx"), lax.axis_size("gy")
    n_states = gates.shape[0]
    block_rows = voltage.shape[1] // LANES
    slot_rows = heart_index.shape[3] // LANES
    block = shape_of(nx, ny, nz)
    flat = lambda a: a.reshape(rows, LANES)
    cells = lambda a: a.reshape(block_rows, LANES)
    states = lambda a: a.reshape(n_states, block_rows, LANES)

    w0, inv, packed, stat = call(
        start_kernel, (block, block, shape_of(2, ny, nz), shape_of(2, SUB, nz)), 3,
        specs=[HBM] * 3,
        scratch=[
            pltpu.VMEM((nx, ny, nz), F32), pltpu.VMEM((nx, ny, nz), F32), pltpu.VMEM((nx, ny, nz), jnp.int32),
            pltpu.SemaphoreType.DMA((3, 4)),
        ],
    )(in_hbm(potential_cot), in_hbm(damping), in_hbm(tissue_label))

    got = lax.ppermute(packed, "gz", [(0, 1), (1, 0)])
    plan = call(plan_kernel, jax.ShapeDtypeStruct((rows, LANES), jnp.int32), 2, cost=6_000_000)(
        stat, flat(tissue_label)
    )

    face = shape_of(nx + 1, SUB, nz)
    slab_shape = shape_of(2, ny, nz)
    x_shapes = (shape_of(2, nx + 1, SUB, nz), shape_of(6, ring, nz), shape_of(6, ring, nz))
    if n_gy == 2:
        slab, mine = call(y_face_one_kernel, (slab_shape, face), 4)(w0, inv, packed, got)
        halo = (lax.ppermute(mine, "gy", [(0, 1), (1, 0)]),)
    else:
        slab, up, down = call(y_faces_kernel, (slab_shape, face, face), 4)(w0, inv, packed, got)
        halo = both_ways(up, down, "gy")
    edge_rows, first, second = call(
        functools.partial(x_faces_kernel, n_gy == 2), x_shapes, 4 + len(halo)
    )(plan, w0, inv, slab, *halo)
    first, second = pair_swaps(first, second, "gx")

    tall = ring + SUB
    planes = shape_of(nx, tall, nz)
    edges = shape_of(6, tall, nz)
    in0, in_inv, in1, in2, in_sums = call(
        inner_kernel,
        (planes,) * 4 + (shape_of(5, SUB, nz),),
        4,
        scratch=[pltpu.VMEM((4, tall, nz), F32)],
        cost=6_000_000,
    )(w0, inv, slab, edge_rows)
    base, total_change, factor, state_coefs = call(
        membrane_kernel,
        (
            shape_of(n_states, block_rows, LANES), shape_of(block_rows, LANES), shape_of(block_rows, LANES),
            shape_of(2, n_states, LANES),
        ),
        9,
        specs=[SMEM] * 5 + [VMEM] * 4,
        cost=6_000_000,
    )(
        half_voltage, gate_slope, tau_base, conductance, reversal,
        in_sums, cells(voltage), states(gates), states(gates_cot),
    )
    ends0, ends1, ends2, slabs, sums = call(
        outer_kernel,
        (edges,) * 3 + (shape_of(3, tall, 2 * nz), shape_of(16, nz)),
        11,
        scratch=[pltpu.VMEM((4, tall, nz), F32), pltpu.VMEM((1, tall, 2 * nz), F32)],
    )(state_coefs, in0, in_inv, in1, in2, slab, edge_rows, in_sums, first, second, stat)

    def couple(stage, after, inside, ends):
        return call(
            functools.partial(couple_kernel, stage, slot_rows),
            shape_of(slot_rows, LANES),
            5,
            scratch=[pltpu.VMEM((rows, LANES), F32)],
            cost=6_000_000,
        )(after, inside, ends, slabs, plan)

    def add(value, axis, step, after):
        got = lax.ppermute(value, axis, [(i, i ^ step) for i in range(lax.axis_size(axis))])
        return call(add_kernel, shape_of(16, nz), 3)(value, got, after)

    list0 = couple(0, sums, in0, ends0)
    sums = add(sums, "gz", 1, list0)
    list1 = couple(1, sums, in1, ends1)
    sums = add(sums, "gy", 1, list1)
    for step in [2**k for k in range(1, n_gy.bit_length() - 1)]:
        sums = add(sums, "gy", step, list1)
    list2 = couple(2, sums, in2, ends2)
    if n_gx <= 4:
        sums = [sums] + [lax.ppermute(sums, "gx", [(i, i ^ k) for i in range(n_gx)]) for k in range(1, n_gx)]
    else:
        sums = [reduce_over(sums, "gx")]

    coefs, *blocks = call(
        functools.partial(place_kernel, len(sums)),
        (shape_of(SUB, LANES),) + (shape_of(block_rows, LANES),) * n_gx,
        len(sums) + 3,
        scratch=[pltpu.VMEM((n_gx * block_rows + slot_rows + SUB, LANES), F32)],
    )(*sums, list0, list1, list2)
    landed = blocks[:1] + [
        lax.ppermute(blocks[k], "gx", block_pairs(n_gx, k, slot_rows, block_rows)) for k in range(1, n_gx)
    ]

    solution = call(potential_kernel, block, 6)(coefs, in0, in1, in2, ends1, ends2)
    volt_grad, gate_grad = call(
        finish_kernel,
        (shape_of(block_rows, LANES), shape_of(n_states, block_rows, LANES)),
        6 + n_gx,
    )(state_coefs, cells(voltage_cot), cells(voltage), total_change, factor, base, *landed)
    return solution, volt_grad.reshape(voltage.shape), gate_grad.reshape(gates.shape)


def solution(mesh):
    grid = P(("groups", "gx"), "gy", "gz")
    cells = P(("groups", "gy", "gz"), "gx")
    states = P(None, ("groups", "gy", "gz"), "gx")
    in_specs = (
        grid, grid, grid, P(("groups", "gx"), "gy", "gz", None), cells, states, cells, states,
        P(), P(), P(), P(), P(),
    )
    return jax.shard_map(
        local, mesh=mesh, in_specs=in_specs, out_specs=(grid, cells, states), check_vma=False
    )
```

```python
import functools

import jax
import jax.numpy as jnp
from jax import lax
from jax.experimental import pallas as pl
from jax.experimental.pallas import tpu as pltpu
from jax.sharding import PartitionSpec as P

TIME_STEP = 0.5
LANES = 128
SUB = 8
PACK = 8
F32 = jnp.float32

VMEM = pl.BlockSpec(memory_space=pltpu.VMEM)
SMEM = pl.BlockSpec(memory_space=pltpu.SMEM)
HBM = pl.BlockSpec(memory_space=pltpu.HBM)


def shape_of(*dims):
    return jax.ShapeDtypeStruct(dims, F32)


def call(kernel, out_shape, n_in, specs=None, outs=None, scratch=(), cost=2_000_000, limit=32):
    return pl.pallas_call(
        kernel,
        out_shape=out_shape,
        in_specs=specs if specs is not None else [VMEM] * n_in,
        out_specs=outs if outs is not None else jax.tree.map(lambda _: VMEM, out_shape),
        scratch_shapes=list(scratch),
        compiler_params=pltpu.CompilerParams(vmem_limit_bytes=limit * 1024 * 1024),
        cost_estimate=pl.CostEstimate(flops=cost, bytes_accessed=cost, transcendentals=0),
    )


def in_hbm(array):
    return pltpu.with_memory_space_constraint(array, pltpu.HBM)


def lanes_of(shape):
    return lax.broadcasted_iota(jnp.int32, shape, len(shape) - 1)


def subs_of(shape):
    return lax.broadcasted_iota(jnp.int32, shape, len(shape) - 2)


def start_kernel(
    right_hbm, damping_hbm, label_hbm, w0_ref, inv_ref, pack_ref, stat_ref, right_ref, damping_ref, label_ref, sems
):
    nx, ny, nz = right_ref.shape
    parts = sems.shape[1]
    size = nx // parts
    copies = []
    for part in range(parts):
        here = pl.ds(part * size, size)
        for k, (source, target) in enumerate(
            ((right_hbm, right_ref), (damping_hbm, damping_ref), (label_hbm, label_ref))
        ):
            copies.append(pltpu.make_async_copy(source.at[here], target.at[here], sems.at[k, part]))
            copies[-1].start()
    gz = lax.axis_index("gz")
    lane = lanes_of((ny, nz))
    packed_w = jnp.zeros((ny, nz), F32)
    packed_i = jnp.zeros((ny, nz), F32)
    energy = jnp.zeros((ny, nz), F32)
    cells = jnp.zeros((ny, nz), F32)
    for x in range(nx):
        if x % size == 0:
            for k in range(3):
                copies[3 * (x // size) + k].wait()
        label = label_ref[x].astype(F32)
        right = right_ref[x]
        inv = 1.0 / (12.0 + damping_ref[x] * (1.0 + 3.0 * label))
        w0 = right * inv
        w0_ref[x] = w0
        inv_ref[x] = inv
        energy = energy + right * w0
        cells = cells + label
        turn = (PACK * x + 3) % nz
        begin = PACK * x + 3 * gz
        chosen = (lane >= begin) & (lane < begin + 3)
        packed_w = jnp.where(chosen, pltpu.roll(w0, turn, 1), packed_w)
        packed_i = jnp.where(chosen, pltpu.roll(inv, turn, 1), packed_i)
    pack_ref[0] = packed_w
    pack_ref[1] = packed_i
    stat_ref[0] = jnp.broadcast_to(jnp.sum(energy, axis=0, keepdims=True), (SUB, nz))
    stat_ref[1] = jnp.broadcast_to(jnp.sum(cells, axis=0, keepdims=True), (SUB, nz))


def y_faces_kernel(w0_ref, inv_ref, own_ref, got_ref, slab_ref, up_ref, down_ref):
    nx, ny, nz = w0_ref.shape
    sub = subs_of((SUB, nz))
    slab_ref[...] = own_ref[...] + got_ref[...]
    for x in range(nx + 1):
        if x < nx:
            w_last, w_first = w0_ref[x, ny - SUB :], w0_ref[x, :SUB]
            i_last, i_first = inv_ref[x, ny - SUB :], inv_ref[x, :SUB]
        else:
            w_last, w_first = slab_ref[0, ny - SUB :], slab_ref[0, :SUB]
            i_last, i_first = slab_ref[1, ny - SUB :], slab_ref[1, :SUB]
        up_ref[x] = jnp.where(sub >= 5, w_last, pltpu.roll(i_last, 4, 0))
        down_ref[x] = jnp.where(sub <= 2, w_first, pltpu.roll(i_first, 4, 0))


def y_face_one_kernel(w0_ref, inv_ref, own_ref, got_ref, slab_ref, face_ref):
    nx, ny, nz = w0_ref.shape
    sub = subs_of((SUB, nz))
    up = lax.axis_index("gy") == 0
    keep_w = jnp.where(up, sub, SUB - 1 - sub) >= 5
    slab_ref[...] = own_ref[...] + got_ref[...]
    for x in range(nx + 1):
        if x < nx:
            w_last, w_first = w0_ref[x, ny - SUB :], w0_ref[x, :SUB]
            i_last, i_first = inv_ref[x, ny - SUB :], inv_ref[x, :SUB]
        else:
            w_last, w_first = slab_ref[0, ny - SUB :], slab_ref[0, :SUB]
            i_last, i_first = slab_ref[1, ny - SUB :], slab_ref[1, :SUB]
        w_face = jnp.where(up, w_last, w_first)
        i_face = jnp.where(up, i_last, i_first)
        face_ref[x] = jnp.where(keep_w, w_face, pltpu.roll(i_face, 4, 0))


def x_faces_kernel(one, after_ref, w0_ref, inv_ref, slab_ref, *refs):
    if one:
        got_ref, halo_ref, first_ref, second_ref = refs
    else:
        low_ref, high_ref, halo_ref, first_ref, second_ref = refs
    nx, ny, nz = w0_ref.shape
    sub = subs_of((SUB, nz))
    lane = lanes_of((ny + SUB, nz))
    if one:
        gy = lax.axis_index("gy")
        w_rows = ((gy == 1) & (sub >= 5)) | ((gy == 0) & (sub <= 2))
        i_rows = ((gy == 1) & (sub >= 6)) | ((gy == 0) & (sub <= 1))
    for x in range(nx + 1):
        if one:
            got = got_ref[x]
            halo_ref[0, x] = jnp.where(w_rows, got, 0.0)
            halo_ref[1, x] = jnp.where(i_rows, pltpu.roll(got, 4, 0), 0.0)
        else:
            low, high = low_ref[x], high_ref[x]
            halo_ref[0, x] = jnp.where(sub >= 5, low, jnp.where(sub <= 2, high, 0.0))
            halo_ref[1, x] = jnp.where(
                sub >= 6, pltpu.roll(low, 4, 0), jnp.where(sub <= 1, pltpu.roll(high, 4, 0), 0.0)
            )
    odd = lax.rem(lax.axis_index("gx") + lax.axis_index("gz"), 2)
    slab_w = jnp.concatenate([slab_ref[0], halo_ref[0, nx]], axis=0)
    slab_i = jnp.concatenate([slab_ref[1], halo_ref[1, nx]], axis=0)
    half = pltpu.roll(slab_i, nz // 2, 1)
    up = jnp.where(lane >= nz - 3 * PACK, slab_w, half)
    down = jnp.where(lane < 3 * PACK, slab_w, half)
    for face_ref, lower in ((first_ref, odd), (second_ref, 1 - odd)):
        for k in range(5):
            field, source = (0, w0_ref) if k < 3 else (1, inv_ref)
            place = (1 - lower) * (nx - 3 + field) + k - 3 * field
            face_ref[k, :ny] = source[place]
            face_ref[k, ny:] = halo_ref[field, place]
        face_ref[5] = jnp.where(lower == 1, down, up)


def slab_step(v, s, inv):
    width = v.shape[1]
    across = pltpu.roll(v, PACK, 1) + pltpu.roll(v, width - PACK, 1)
    q = v + 0.5 * (s + across)
    if inv is None:
        return q, None
    total = (
        pltpu.roll(q, 1, 1) + pltpu.roll(q, width - 1, 1) + s + across
        + 0.5 * (pltpu.roll(s, PACK, 1) + pltpu.roll(s, width - PACK, 1))
    )
    return q, total * inv


def along_z(q, half, column, gz):
    nz = q.shape[1]
    lane = lanes_of(q.shape)
    entry = (nz - 1) * (1 - gz)
    turn = lax.rem(entry - (column + 3 - gz) + 2 * nz, nz)
    up = jnp.where(lane == nz - 1, 0.0, pltpu.roll(q, nz - 1, 1))
    down = jnp.where(lane == 0, 0.0, pltpu.roll(q, 1, 1))
    return up + down + jnp.where(lane == entry, pltpu.roll(half, turn, 1), 0.0)


def sweep(stage, spans, nx, ny, nz, gz, get, get_inv, put, slab_q, sums):
    margin = 2 - stage
    start = SUB - margin
    tiles = ny // SUB + (margin > 0)
    own = subs_of((SUB, nz)) >= margin
    parts = [[], []]
    for tile in range(tiles):
        row = start + SUB * tile
        q_rows = slab_q[SUB * tile : SUB * tile + SUB]
        acc = [jnp.zeros((SUB, nz), F32) for _ in range(2)]

        def beside(x):
            return get(x, row - 1) + get(x, row + 1)

        for first, last in spans:
            s_low, s_mid = beside(first - 1), beside(first)
            v_low, v_mid = get(first - 1, row), get(first, row)
            for x in range(first, last):
                v_high, s_high = get(x + 1, row), beside(x + 1)
                across = v_low + v_high
                column = (PACK * x) % (2 * nz)
                half = q_rows[:, column // nz * nz : column // nz * nz + nz]
                rest = s_mid + across
                total = along_z(v_mid + 0.5 * rest, half, column % nz, gz) + rest + 0.5 * (s_low + s_high)
                if stage < 2:
                    after = total * get_inv(x, row)
                    put(x, row, after)
                if 0 <= x < nx:
                    acc[0] = acc[0] + v_mid * total
                    if stage < 2:
                        acc[1] = acc[1] + after * total
                v_low, v_mid, s_low, s_mid = v_mid, v_high, s_mid, s_high
        for k in range(2):
            parts[k].append(acc[k])
    for k in range(2 if stage < 2 else 1):
        part = parts[k]
        total = part[1]
        for other in part[2 : ny // SUB]:
            total = total + other
        total = total + (jnp.where(own, part[0], part[-1]) if margin else part[0])
        sums[2 * stage + k] = total


def inner_kernel(
    w0_ref, inv_ref, slab_ref, halo_ref, a_ref, i_ref, b_ref, c_ref, sum_ref, slabs_ref,
):
    nx, ny, nz = w0_ref.shape
    gz = lax.axis_index("gz")
    for x in range(nx):
        for ref, own, halo in ((a_ref, w0_ref[x], halo_ref[0, x]), (i_ref, inv_ref[x], halo_ref[1, x])):
            ref[x, :SUB] = halo
            ref[x, SUB : SUB + ny] = own
            ref[x, SUB + ny :] = halo
    for k in range(2):
        slabs_ref[3 * k, :SUB] = halo_ref[k, nx]
        slabs_ref[3 * k, SUB : SUB + ny] = slab_ref[k]
        slabs_ref[3 * k, SUB + ny :] = halo_ref[k, nx]
    sums = {}
    for stage in range(3):
        source, target = (a_ref, b_ref, c_ref)[stage], (b_ref, c_ref, None)[stage]
        start, size = SUB - 2 + stage, ny if stage == 2 else ny + SUB
        v = slabs_ref[stage, start : start + size]
        s = slabs_ref[stage, start - 1 : start - 1 + size] + slabs_ref[stage, start + 1 : start + 1 + size]
        q, after = slab_step(v, s, slabs_ref[3, start : start + size] if stage < 2 else None)
        if stage < 2:
            slabs_ref[stage + 1, start : start + size] = after

        def put(x, row, value):
            target[x, row : row + SUB] = value

        sweep(
            stage, [(1 + stage, nx - 1 - stage)], nx, ny, nz, gz,
            lambda x, row: source[x, row : row + SUB], lambda x, row: i_ref[x, row : row + SUB],
            put, q, sums,
        )
    for k in range(5):
        sum_ref[k] = sums[k]


def outer_kernel(
    after_ref, a_ref, i_ref, b_ref, c_ref, slab_ref, halo_ref, sum_ref, first_ref, second_ref, stat_ref,
    ea_ref, eb_ref, ec_ref, slabs_ref, total_ref, ei_ref, si_ref,
):
    nx, ny, nz = a_ref.shape[0], a_ref.shape[1] - 2 * SUB, a_ref.shape[2]
    ring = ny + SUB
    gz = lax.axis_index("gz")
    gx = lax.axis_index("gx")
    odd = lax.rem(gx + gz, 2) == 1
    has_low, has_high = gx > 0, gx < lax.axis_size("gx") - 1

    def low(k):
        return jnp.where(has_low, jnp.where(odd, first_ref[k], second_ref[k]), 0.0)

    def high(k):
        return jnp.where(has_high, jnp.where(odd, second_ref[k], first_ref[k]), 0.0)

    for ref, at, plane in (
        [(ea_ref, k, low(k)) for k in range(3)] + [(ea_ref, 3 + k, high(k)) for k in range(3)]
        + [(ei_ref, k, low(3 + k)) for k in range(2)] + [(ei_ref, 2 + k, high(3 + k)) for k in range(2)]
    ):
        ref[at, :SUB] = plane[ny:]
        ref[at, SUB : SUB + ny] = plane[:ny]
        ref[at, SUB + ny :] = plane[ny:]

    lane = lanes_of((ring, nz))
    lo5, hi5 = low(5), high(5)
    slab_w = jnp.where(lane < 3 * PACK, hi5, 0.0) + jnp.where(lane >= nz - 3 * PACK, lo5, 0.0)
    lo5, hi5 = pltpu.roll(lo5, nz // 2, 1), pltpu.roll(hi5, nz // 2, 1)
    slab_i = jnp.where(lane < 2 * PACK, hi5, 0.0) + jnp.where(lane >= nz - 2 * PACK, lo5, 0.0)
    for ref, k, beyond in ((slabs_ref, 0, slab_w), (si_ref, 1, slab_i)):
        ref[0, SUB : SUB + ny, :nz] = slab_ref[k]
        ref[0, SUB : SUB + ny, nz:] = beyond[:ny]
        for rows in (slice(0, SUB), slice(SUB + ny, SUB + ring)):
            ref[0, rows, :nz] = halo_ref[k, nx]
            ref[0, rows, nz:] = beyond[ny:]

    def reader(inside_ref, edge_ref, first, count):
        def get(x, row):
            if first <= x < nx - first:
                return inside_ref[x, row : row + SUB]
            at = x - (first - count) if x < first else x - (nx - first) + count
            return edge_ref[at, row : row + SUB]

        return get

    sums = {}
    for stage in range(3):
        get = reader((a_ref, b_ref, c_ref)[stage], (ea_ref, eb_ref, ec_ref)[stage], stage, 3)
        start, size = SUB - 2 + stage, ny if stage == 2 else ring
        v = slabs_ref[stage, start : start + size]
        s = slabs_ref[stage, start - 1 : start - 1 + size] + slabs_ref[stage, start + 1 : start + 1 + size]
        q, after = slab_step(v, s, si_ref[0, start : start + size] if stage < 2 else None)
        if stage < 2:
            slabs_ref[stage + 1, start : start + size] = after

        def put(x, row, value):
            edge_ref = (eb_ref, ec_ref)[stage]
            at = x - (stage - 2) if x < nx // 2 else x - (nx - 1 - stage) + 3
            edge_ref[at, row : row + SUB] = value

        sweep(
            stage, [(stage - 2, stage + 1), (nx - 1 - stage, nx + 2 - stage)], nx, ny, nz, gz,
            get, reader(i_ref, ei_ref, 0, 2), put, q, sums,
        )

    total_ref[0:1] = stat_ref[0, 0:1]
    for k in range(5):
        total_ref[k + 1 : k + 2] = jnp.sum(sums[k] + sum_ref[k], axis=0, keepdims=True)
    total_ref[6:8] = jnp.zeros((2, nz), F32)
    here = (lax.axis_index("gx") * lax.axis_size("gy") + lax.axis_index("gy")) * lax.axis_size("gz") + gz
    count = jnp.sum(stat_ref[1], axis=1, keepdims=True)
    total_ref[8:16] = jnp.where(lanes_of((SUB, nz)) == here, count, 0.0)


def shift_left(v, amount, lane):
    rows = v.shape[0]
    if amount < LANES:
        turned = pltpu.roll(v, LANES - amount, 1)
        below = pltpu.roll(turned, rows - 1, 0)
        return jnp.where(lane < LANES - amount, turned, below)
    return jnp.concatenate([v[amount // LANES :], v[: amount // LANES]], axis=0)


def plan_kernel(after_ref, label_ref, plan_ref):
    rows = label_ref.shape[0]
    lane = lanes_of((rows, LANES))
    row = subs_of((rows, LANES))
    heart = label_ref[...] == 1
    ones = heart.astype(jnp.bfloat16)
    upper = (subs_of((LANES, LANES)) < lanes_of((LANES, LANES))).astype(jnp.bfloat16)
    in_row = jnp.dot(ones, upper, preferred_element_type=F32)
    totals = jnp.dot(ones, jnp.ones((LANES, LANES), jnp.bfloat16), preferred_element_type=F32)
    lower = (subs_of((rows, rows)) > lanes_of((rows, rows))).astype(jnp.bfloat16)
    before = jnp.dot(lower, totals.astype(jnp.bfloat16), preferred_element_type=F32)
    rank = (in_row + before).astype(jnp.int32)
    way = jnp.where(heart, row * LANES + lane - rank, 0)
    plan = jnp.zeros((rows, LANES), jnp.int32)
    step = 1
    while step < rows * LANES:
        moving = jnp.where((way & step) != 0, way, 0)
        arriving = shift_left(moving, step, lane)
        plan = plan | (arriving & step)
        way = (way - moving) | arriving
        step *= 2
    plan_ref[...] = plan


def galerkin(t):
    g00, g01, g02, g12, g22 = t[0] - t[1], t[1] - t[2], t[2] - t[3], t[3] - t[4], t[4] - t[5]
    g11 = g02
    l10, l20 = g01 / g00, g02 / g00
    d1 = g11 - l10 * g01
    m21 = g12 - l20 * g01
    ok1 = d1 > 1e-6 * g11
    d1 = jnp.where(ok1, d1, 1.0)
    l21 = jnp.where(ok1, m21 / d1, 0.0)
    d2 = g22 - l20 * g02 - l21 * m21
    ok2 = ok1 & (d2 > 1e-6 * g22)
    d2 = jnp.where(ok2, d2, 1.0)
    y1 = t[1] - l10 * t[0]
    y2 = t[2] - l20 * t[0] - l21 * y1
    c2 = jnp.where(ok2, y2 / d2, 0.0)
    c1 = jnp.where(ok1, y1 / d1 - l21 * c2, 0.0)
    c0 = t[0] / g00 - l10 * c1 - l20 * c2
    return c0, c1, c2


def couple_kernel(stage, slot_rows, after_ref, inside_ref, edge_ref, slabs_ref, plan_ref, list_ref, value_ref):
    nx, nz = inside_ref.shape[0], inside_ref.shape[2]
    ny = inside_ref.shape[1] - 2 * SUB
    rows = nx * ny
    gz = lax.axis_index("gz")

    def get(x, row):
        if stage <= x < nx - stage:
            return inside_ref[x, row : row + SUB]
        return edge_ref[x - (stage - 3) if x < stage else x - (nx - stage) + 3, row : row + SUB]

    for tile in range(ny // SUB):
        row = SUB + SUB * tile
        slab = slabs_ref[stage, row : row + SUB, :nz]
        v_low, v_mid = get(-1, row), get(0, row)
        for x in range(nx):
            v_high = get(x + 1, row)
            beside = get(x, row - 1) + get(x, row + 1)
            at = ny * x + SUB * tile
            value_ref[at : at + SUB] = (
                along_z(v_mid, slab, PACK * x, gz) + beside + (v_low + v_high) - 6.0 * v_mid
            )
            v_low, v_mid = v_mid, v_high
    lane = lanes_of((rows, LANES))
    value = value_ref[...]
    plan = plan_ref[...]
    step = 1
    while step < rows * LANES:
        value = jnp.where((plan & step) != 0, shift_left(value, step, lane), value)
        step *= 2
    list_ref[...] = value[:slot_rows]


def add_kernel(a_ref, b_ref, after_ref, out_ref):
    out_ref[...] = a_ref[...] + b_ref[...]


def place_kernel(n_sums, *refs):
    sum_refs, refs = refs[:n_sums], refs[n_sums:]
    list_refs, refs = refs[:3], refs[3:]
    coef_ref, *out_refs, buf_ref = refs
    total = sum_refs[0][...]
    for ref in sum_refs[1:]:
        total = total + ref[...]
    sums = jnp.sum(total[0:8], axis=1, keepdims=True)
    t = [jnp.broadcast_to(sums[k : k + 1], (1, LANES)) for k in range(6)]
    coefs = galerkin(t)
    for k in range(3):
        coef_ref[k : k + 1] = coefs[k]
    value = coefs[0] * list_refs[0][...] + coefs[1] * list_refs[1][...] + coefs[2] * list_refs[2][...]
    slot_rows = value.shape[0]
    n_y, n_z = lax.axis_size("gy"), lax.axis_size("gz")
    counts = total[8:16]
    dev = lanes_of((SUB, LANES))
    mine = lax.rem(dev, n_y * n_z) == lax.axis_index("gy") * n_z + lax.axis_index("gz")
    gx = lax.axis_index("gx")
    first = subs_of((SUB, LANES)) == 0
    offset = jnp.sum(jnp.where(first & mine & (dev < gx * n_y * n_z), counts, 0.0)).astype(jnp.int32)
    count = jnp.sum(jnp.where(first & mine & (dev // (n_y * n_z) == gx), counts, 0.0)).astype(jnp.int32)
    shape = (slot_rows, LANES)
    slots = jnp.where(subs_of(shape) * LANES + lanes_of(shape) < count, value, 0.0)
    slots = jnp.concatenate([slots, jnp.zeros((SUB, LANES), F32)], axis=0)
    inner = lax.rem(offset, LANES)
    turned = pltpu.roll(slots, inner, 1)
    above = pltpu.roll(turned, 1, 0)
    moved = jnp.where(lanes_of((slot_rows + SUB, LANES)) >= inner, turned, above)
    buf_ref[...] = jnp.zeros_like(buf_ref)
    buf_ref[pl.ds(offset // LANES, slot_rows + SUB), :] = moved
    for k, out_ref in enumerate(out_refs):
        size = out_ref.shape[0]
        out_ref[...] = buf_ref[pl.ds(pl.multiple_of((gx ^ k) * size, SUB), size), :]


def potential_kernel(coef_ref, a_ref, b_ref, c_ref, eb_ref, ec_ref, x_ref):
    nx, ny, nz = x_ref.shape
    own = slice(SUB, SUB + ny)
    c0, c1, c2 = [coef_ref[k : k + 1] for k in range(3)]
    for x in range(nx):
        w1 = b_ref[x, own] if 1 <= x < nx - 1 else eb_ref[2 if x == 0 else 3, own]
        w2 = c_ref[x, own] if 2 <= x < nx - 2 else ec_ref[x + 1 if x < 2 else x - (nx - 2) + 3, own]
        x_ref[x] = c0 * a_ref[x, own] + c1 * w1 + c2 * w2


def membrane_kernel(
    half_ref, slope_ref, tau_ref, cond_ref, rev_ref, after_ref, v_ref, gates_ref, cot_ref,
    base_ref, sum_ref, factor_ref, coef_ref,
):
    n_states, rows = gates_ref.shape[:2]
    v = v_ref[...]

    def state(g, carry):
        total, current = carry
        inv_slope = 1.0 / slope_ref[g]
        tau_base = tau_ref[g]
        scaled = (v - half_ref[g]) * inv_slope
        gate = gates_ref[g]
        cot = cot_ref[g]
        steady = 1.0 / (1.0 + jnp.exp(-scaled))
        bell = jnp.exp(-scaled * scaled)
        rate = TIME_STEP / (tau_base * (0.5 + bell))
        decay = jnp.exp(-rate)
        steady_slope = steady * (1.0 - steady)
        decay_slope = decay * rate * rate * ((tau_base / TIME_STEP) * bell * (-2.0 * scaled))
        change = (steady_slope * (1.0 - decay) + (gate - steady) * decay_slope) * inv_slope
        base_ref[g] = cot * decay
        coef_ref[0, pl.ds(g, 1)] = jnp.full((1, LANES), TIME_STEP * cond_ref[g])
        coef_ref[1, pl.ds(g, 1)] = jnp.full((1, LANES), rev_ref[g])
        return total + cot * change, current + cond_ref[g] * gate

    zero = jnp.zeros((rows, LANES), F32)
    total, current = lax.fori_loop(0, n_states, state, (zero, zero), unroll=2)
    sum_ref[...] = total
    factor_ref[...] = 1.0 - TIME_STEP * current


def finish_kernel(coef_ref, vcot_ref, v_ref, sum_ref, factor_ref, base_ref, *refs):
    *landed_refs, volt_ref, gate_ref = refs
    landed = landed_refs[0][...]
    for ref in landed_refs[1:]:
        landed = landed + ref[...]
    cot = vcot_ref[...] + landed
    v = v_ref[...]
    volt_ref[...] = cot * factor_ref[...] + sum_ref[...]
    for g in range(base_ref.shape[0]):
        gate_ref[g] = base_ref[g] - (coef_ref[0, g : g + 1] * cot) * (v - coef_ref[1, g : g + 1])


def both_ways(up, down, axis):
    count = lax.axis_size(axis)
    low = lax.ppermute(up, axis, [(i, i + 1) for i in range(count - 1)])
    high = lax.ppermute(down, axis, [(i + 1, i) for i in range(count - 1)])
    return low, high


def pair_swaps(first, second):
    n_gx, n_gz = lax.axis_size("gx"), lax.axis_size("gz")
    even = [i ^ 1 for i in range(n_gx)]
    between = [0] + [i + 1 if i % 2 else i - 1 for i in range(1, n_gx - 1)] + [n_gx - 1]

    def pairs(orders):
        return [(x * n_gz + z, orders[z % 2][x] * n_gz + z) for x in range(n_gx) for z in range(n_gz)]

    return (
        lax.ppermute(first, ("gx", "gz"), pairs((even, between))),
        lax.ppermute(second, ("gx", "gz"), pairs((between, even))),
    )


def block_pairs(count, k, slots, block):
    def apart(tile, owner):
        return owner * block >= (tile + 1) * slots or (owner + 1) * block <= count * block - (count - tile) * slots

    return [(i, i if apart(i, i ^ k) and apart(i ^ k, i) else i ^ k) for i in range(count)]


def reduce_over(value, axis):
    count = lax.axis_size(axis)
    step = 1
    while step < count:
        value = value + lax.ppermute(value, axis, [(i, i ^ step) for i in range(count)])
        step *= 2
    return value


def local(
    potential_cot, damping, tissue_label, heart_index, voltage, gates, voltage_cot, gates_cot,
    half_voltage, gate_slope, tau_base, conductance, reversal,
):
    nx, ny, nz = potential_cot.shape
    rows = nx * ny
    ring = ny + SUB
    n_gx, n_gy = lax.axis_size("gx"), lax.axis_size("gy")
    n_states = gates.shape[0]
    block_rows = voltage.shape[1] // LANES
    slot_rows = heart_index.shape[3] // LANES
    block = shape_of(nx, ny, nz)
    flat = lambda a: a.reshape(rows, LANES)
    cells = lambda a: a.reshape(block_rows, LANES)
    states = lambda a: a.reshape(n_states, block_rows, LANES)

    w0, inv, packed, stat = call(
        start_kernel, (block, block, shape_of(2, ny, nz), shape_of(2, SUB, nz)), 3,
        specs=[HBM] * 3,
        scratch=[
            pltpu.VMEM((nx, ny, nz), F32), pltpu.VMEM((nx, ny, nz), F32), pltpu.VMEM((nx, ny, nz), jnp.int32),
            pltpu.SemaphoreType.DMA((3, 8)),
        ],
    )(in_hbm(potential_cot), in_hbm(damping), in_hbm(tissue_label))

    got = lax.ppermute(packed, "gz", [(0, 1), (1, 0)])
    plan = call(plan_kernel, jax.ShapeDtypeStruct((rows, LANES), jnp.int32), 2, cost=6_000_000)(
        stat, flat(tissue_label)
    )

    face = shape_of(nx + 1, SUB, nz)
    slab_shape = shape_of(2, ny, nz)
    x_shapes = (shape_of(2, nx + 1, SUB, nz), shape_of(6, ring, nz), shape_of(6, ring, nz))
    if n_gy == 2:
        slab, mine = call(y_face_one_kernel, (slab_shape, face), 4)(w0, inv, packed, got)
        halo = (lax.ppermute(mine, "gy", [(0, 1), (1, 0)]),)
    else:
        slab, up, down = call(y_faces_kernel, (slab_shape, face, face), 4)(w0, inv, packed, got)
        halo = both_ways(up, down, "gy")
    edge_rows, first, second = call(
        functools.partial(x_faces_kernel, n_gy == 2), x_shapes, 4 + len(halo)
    )(plan, w0, inv, slab, *halo)
    first, second = pair_swaps(first, second)

    tall = ring + SUB
    planes = shape_of(nx, tall, nz)
    edges = shape_of(6, tall, nz)
    in0, in_inv, in1, in2, in_sums = call(
        inner_kernel,
        (planes,) * 4 + (shape_of(5, SUB, nz),),
        4,
        scratch=[pltpu.VMEM((4, tall, nz), F32)],
        cost=6_000_000,
    )(w0, inv, slab, edge_rows)
    base, total_change, factor, state_coefs = call(
        membrane_kernel,
        (
            shape_of(n_states, block_rows, LANES), shape_of(block_rows, LANES), shape_of(block_rows, LANES),
            shape_of(2, n_states, LANES),
        ),
        9,
        specs=[SMEM] * 5 + [VMEM] * 4,
        cost=6_000_000,
    )(
        half_voltage, gate_slope, tau_base, conductance, reversal,
        in_sums, cells(voltage), states(gates), states(gates_cot),
    )
    ends0, ends1, ends2, slabs, sums = call(
        outer_kernel,
        (edges,) * 3 + (shape_of(3, tall, 2 * nz), shape_of(16, nz)),
        11,
        scratch=[pltpu.VMEM((4, tall, nz), F32), pltpu.VMEM((1, tall, 2 * nz), F32)],
    )(state_coefs, in0, in_inv, in1, in2, slab, edge_rows, in_sums, first, second, stat)

    def couple(stage, after, inside, ends):
        return call(
            functools.partial(couple_kernel, stage, slot_rows),
            shape_of(slot_rows, LANES),
            5,
            scratch=[pltpu.VMEM((rows, LANES), F32)],
            cost=6_000_000,
        )(after, inside, ends, slabs, plan)

    def add(value, axis, step, after):
        got = lax.ppermute(value, axis, [(i, i ^ step) for i in range(lax.axis_size(axis))])
        return call(add_kernel, shape_of(16, nz), 3)(value, got, after)

    list0 = couple(0, sums, in0, ends0)
    sums = add(sums, "gz", 1, list0)
    list1 = couple(1, sums, in1, ends1)
    sums = add(sums, "gy", 1, list1)
    for step in [2**k for k in range(1, n_gy.bit_length() - 1)]:
        sums = add(sums, "gy", step, list1)
    list2 = couple(2, sums, in2, ends2)
    if n_gx <= 4:
        sums = [sums] + [lax.ppermute(sums, "gx", [(i, i ^ k) for i in range(n_gx)]) for k in range(1, n_gx)]
    else:
        sums = [reduce_over(sums, "gx")]

    coefs, *blocks = call(
        functools.partial(place_kernel, len(sums)),
        (shape_of(SUB, LANES),) + (shape_of(block_rows, LANES),) * n_gx,
        len(sums) + 3,
        scratch=[pltpu.VMEM((n_gx * block_rows + slot_rows + SUB, LANES), F32)],
    )(*sums, list0, list1, list2)
    landed = blocks[:1] + [
        lax.ppermute(blocks[k], "gx", block_pairs(n_gx, k, slot_rows, block_rows)) for k in range(n_gx - 1, 0, -1)
    ]

    solution = call(potential_kernel, block, 6)(coefs, in0, in1, in2, ends1, ends2)
    volt_grad, gate_grad = call(
        finish_kernel,
        (shape_of(block_rows, LANES), shape_of(n_states, block_rows, LANES)),
        6 + n_gx,
    )(state_coefs, cells(voltage_cot), cells(voltage), total_change, factor, base, *landed)
    return solution, volt_grad.reshape(voltage.shape), gate_grad.reshape(gates.shape)


def solution(mesh):
    grid = P(("groups", "gx"), "gy", "gz")
    cells = P(("groups", "gy", "gz"), "gx")
    states = P(None, ("groups", "gy", "gz"), "gx")
    in_specs = (
        grid, grid, grid, P(("groups", "gx"), "gy", "gz", None), cells, states, cells, states,
        P(), P(), P(), P(), P(),
    )
    return jax.shard_map(
        local, mesh=mesh, in_specs=in_specs, out_specs=(grid, cells, states), check_vma=False
    )
```

```python
import functools

import jax
import jax.numpy as jnp
from jax import lax
from jax.experimental import pallas as pl
from jax.experimental.pallas import tpu as pltpu
from jax.sharding import PartitionSpec as P

TIME_STEP = 0.5
LANES = 128
SUB = 8
PACK = 8
F32 = jnp.float32

VMEM = pl.BlockSpec(memory_space=pltpu.VMEM)
SMEM = pl.BlockSpec(memory_space=pltpu.SMEM)
HBM = pl.BlockSpec(memory_space=pltpu.HBM)


def shape_of(*dims):
    return jax.ShapeDtypeStruct(dims, F32)


def call(kernel, out_shape, n_in, specs=None, outs=None, scratch=(), cost=2_000_000, limit=32):
    return pl.pallas_call(
        kernel,
        out_shape=out_shape,
        in_specs=specs if specs is not None else [VMEM] * n_in,
        out_specs=outs if outs is not None else jax.tree.map(lambda _: VMEM, out_shape),
        scratch_shapes=list(scratch),
        compiler_params=pltpu.CompilerParams(vmem_limit_bytes=limit * 1024 * 1024),
        cost_estimate=pl.CostEstimate(flops=cost, bytes_accessed=cost, transcendentals=0),
    )


def in_hbm(array):
    return pltpu.with_memory_space_constraint(array, pltpu.HBM)


def lanes_of(shape):
    return lax.broadcasted_iota(jnp.int32, shape, len(shape) - 1)


def subs_of(shape):
    return lax.broadcasted_iota(jnp.int32, shape, len(shape) - 2)


def start_kernel(
    right_hbm, damping_hbm, label_hbm, w0_ref, inv_ref, pack_ref, stat_ref, right_ref, damping_ref, label_ref, sems
):
    nx, ny, nz = right_ref.shape
    parts = sems.shape[1]
    size = nx // parts
    copies = []
    for part in range(parts):
        here = pl.ds(part * size, size)
        for k, (source, target) in enumerate(
            ((right_hbm, right_ref), (damping_hbm, damping_ref), (label_hbm, label_ref))
        ):
            copies.append(pltpu.make_async_copy(source.at[here], target.at[here], sems.at[k, part]))
            copies[-1].start()
    gz = lax.axis_index("gz")
    lane = lanes_of((ny, nz))
    packed_w = jnp.zeros((ny, nz), F32)
    packed_i = jnp.zeros((ny, nz), F32)
    energy = jnp.zeros((ny, nz), F32)
    cells = jnp.zeros((ny, nz), F32)
    for x in range(nx):
        if x % size == 0:
            for k in range(3):
                copies[3 * (x // size) + k].wait()
        label = label_ref[x].astype(F32)
        right = right_ref[x]
        inv = 1.0 / (12.0 + damping_ref[x] * (1.0 + 3.0 * label))
        w0 = right * inv
        w0_ref[x] = w0
        inv_ref[x] = inv
        energy = energy + right * w0
        cells = cells + label
        turn = (PACK * x + 3) % nz
        begin = PACK * x + 3 * gz
        chosen = (lane >= begin) & (lane < begin + 3)
        packed_w = jnp.where(chosen, pltpu.roll(w0, turn, 1), packed_w)
        packed_i = jnp.where(chosen, pltpu.roll(inv, turn, 1), packed_i)
    pack_ref[0] = packed_w
    pack_ref[1] = packed_i
    stat_ref[0] = jnp.broadcast_to(jnp.sum(energy, axis=0, keepdims=True), (SUB, nz))
    stat_ref[1] = jnp.broadcast_to(jnp.sum(cells, axis=0, keepdims=True), (SUB, nz))


def y_faces_kernel(w0_ref, inv_ref, own_ref, got_ref, slab_ref, up_ref, down_ref):
    nx, ny, nz = w0_ref.shape
    sub = subs_of((SUB, nz))
    slab_ref[...] = own_ref[...] + got_ref[...]
    for x in range(nx + 1):
        if x < nx:
            w_last, w_first = w0_ref[x, ny - SUB :], w0_ref[x, :SUB]
            i_last, i_first = inv_ref[x, ny - SUB :], inv_ref[x, :SUB]
        else:
            w_last, w_first = slab_ref[0, ny - SUB :], slab_ref[0, :SUB]
            i_last, i_first = slab_ref[1, ny - SUB :], slab_ref[1, :SUB]
        up_ref[x] = jnp.where(sub >= 5, w_last, pltpu.roll(i_last, 4, 0))
        down_ref[x] = jnp.where(sub <= 2, w_first, pltpu.roll(i_first, 4, 0))


def y_face_one_kernel(w0_ref, inv_ref, own_ref, got_ref, slab_ref, face_ref):
    nx, ny, nz = w0_ref.shape
    sub = subs_of((SUB, nz))
    up = lax.axis_index("gy") == 0
    keep_w = jnp.where(up, sub, SUB - 1 - sub) >= 5
    slab_ref[...] = own_ref[...] + got_ref[...]
    for x in range(nx + 1):
        if x < nx:
            w_last, w_first = w0_ref[x, ny - SUB :], w0_ref[x, :SUB]
            i_last, i_first = inv_ref[x, ny - SUB :], inv_ref[x, :SUB]
        else:
            w_last, w_first = slab_ref[0, ny - SUB :], slab_ref[0, :SUB]
            i_last, i_first = slab_ref[1, ny - SUB :], slab_ref[1, :SUB]
        w_face = jnp.where(up, w_last, w_first)
        i_face = jnp.where(up, i_last, i_first)
        face_ref[x] = jnp.where(keep_w, w_face, pltpu.roll(i_face, 4, 0))


def x_faces_kernel(one, after_ref, w0_ref, inv_ref, slab_ref, *refs):
    if one:
        got_ref, halo_ref, first_ref, second_ref = refs
    else:
        low_ref, high_ref, halo_ref, first_ref, second_ref = refs
    nx, ny, nz = w0_ref.shape
    sub = subs_of((SUB, nz))
    lane = lanes_of((ny + SUB, nz))
    if one:
        gy = lax.axis_index("gy")
        w_rows = ((gy == 1) & (sub >= 5)) | ((gy == 0) & (sub <= 2))
        i_rows = ((gy == 1) & (sub >= 6)) | ((gy == 0) & (sub <= 1))
    for x in range(nx + 1):
        if one:
            got = got_ref[x]
            halo_ref[0, x] = jnp.where(w_rows, got, 0.0)
            halo_ref[1, x] = jnp.where(i_rows, pltpu.roll(got, 4, 0), 0.0)
        else:
            low, high = low_ref[x], high_ref[x]
            halo_ref[0, x] = jnp.where(sub >= 5, low, jnp.where(sub <= 2, high, 0.0))
            halo_ref[1, x] = jnp.where(
                sub >= 6, pltpu.roll(low, 4, 0), jnp.where(sub <= 1, pltpu.roll(high, 4, 0), 0.0)
            )
    odd = lax.rem(lax.axis_index("gx"), 2)
    slab_w = jnp.concatenate([slab_ref[0], halo_ref[0, nx]], axis=0)
    slab_i = jnp.concatenate([slab_ref[1], halo_ref[1, nx]], axis=0)
    half = pltpu.roll(slab_i, nz // 2, 1)
    up = jnp.where(lane >= nz - 3 * PACK, slab_w, half)
    down = jnp.where(lane < 3 * PACK, slab_w, half)
    for face_ref, lower in ((first_ref, odd), (second_ref, 1 - odd)):
        for k in range(5):
            field, source = (0, w0_ref) if k < 3 else (1, inv_ref)
            place = (1 - lower) * (nx - 3 + field) + k - 3 * field
            face_ref[k, :ny] = source[place]
            face_ref[k, ny:] = halo_ref[field, place]
        face_ref[5] = jnp.where(lower == 1, down, up)


def slab_step(v, s, inv):
    width = v.shape[1]
    across = pltpu.roll(v, PACK, 1) + pltpu.roll(v, width - PACK, 1)
    q = v + 0.5 * (s + across)
    if inv is None:
        return q, None
    total = (
        pltpu.roll(q, 1, 1) + pltpu.roll(q, width - 1, 1) + s + across
        + 0.5 * (pltpu.roll(s, PACK, 1) + pltpu.roll(s, width - PACK, 1))
    )
    return q, total * inv


def along_z(q, half, column, gz):
    nz = q.shape[1]
    lane = lanes_of(q.shape)
    entry = (nz - 1) * (1 - gz)
    turn = lax.rem(entry - (column + 3 - gz) + 2 * nz, nz)
    up = jnp.where(lane == nz - 1, 0.0, pltpu.roll(q, nz - 1, 1))
    down = jnp.where(lane == 0, 0.0, pltpu.roll(q, 1, 1))
    return up + down + jnp.where(lane == entry, pltpu.roll(half, turn, 1), 0.0)


def sweep(stage, spans, nx, ny, nz, gz, get, get_inv, put, slab_q, sums):
    margin = 2 - stage
    start = SUB - margin
    tiles = ny // SUB + (margin > 0)
    own = subs_of((SUB, nz)) >= margin
    parts = [[], []]
    for tile in range(tiles):
        row = start + SUB * tile
        q_rows = slab_q[SUB * tile : SUB * tile + SUB]
        acc = [jnp.zeros((SUB, nz), F32) for _ in range(2)]

        def beside(x):
            return get(x, row - 1) + get(x, row + 1)

        for first, last in spans:
            s_low, s_mid = beside(first - 1), beside(first)
            v_low, v_mid = get(first - 1, row), get(first, row)
            for x in range(first, last):
                v_high, s_high = get(x + 1, row), beside(x + 1)
                across = v_low + v_high
                column = (PACK * x) % (2 * nz)
                half = q_rows[:, column // nz * nz : column // nz * nz + nz]
                rest = s_mid + across
                total = along_z(v_mid + 0.5 * rest, half, column % nz, gz) + rest + 0.5 * (s_low + s_high)
                if stage < 2:
                    after = total * get_inv(x, row)
                    put(x, row, after)
                if 0 <= x < nx:
                    acc[0] = acc[0] + v_mid * total
                    if stage < 2:
                        acc[1] = acc[1] + after * total
                v_low, v_mid, s_low, s_mid = v_mid, v_high, s_mid, s_high
        for k in range(2):
            parts[k].append(acc[k])
    for k in range(2 if stage < 2 else 1):
        part = parts[k]
        total = part[1]
        for other in part[2 : ny // SUB]:
            total = total + other
        total = total + (jnp.where(own, part[0], part[-1]) if margin else part[0])
        sums[2 * stage + k] = total


def inner_kernel(
    w0_ref, inv_ref, slab_ref, halo_ref, a_ref, i_ref, b_ref, c_ref, sum_ref, slabs_ref,
):
    nx, ny, nz = w0_ref.shape
    gz = lax.axis_index("gz")
    for x in range(nx):
        for ref, own, halo in ((a_ref, w0_ref[x], halo_ref[0, x]), (i_ref, inv_ref[x], halo_ref[1, x])):
            ref[x, :SUB] = halo
            ref[x, SUB : SUB + ny] = own
            ref[x, SUB + ny :] = halo
    for k in range(2):
        slabs_ref[3 * k, :SUB] = halo_ref[k, nx]
        slabs_ref[3 * k, SUB : SUB + ny] = slab_ref[k]
        slabs_ref[3 * k, SUB + ny :] = halo_ref[k, nx]
    sums = {}
    for stage in range(3):
        source, target = (a_ref, b_ref, c_ref)[stage], (b_ref, c_ref, None)[stage]
        start, size = SUB - 2 + stage, ny if stage == 2 else ny + SUB
        v = slabs_ref[stage, start : start + size]
        s = slabs_ref[stage, start - 1 : start - 1 + size] + slabs_ref[stage, start + 1 : start + 1 + size]
        q, after = slab_step(v, s, slabs_ref[3, start : start + size] if stage < 2 else None)
        if stage < 2:
            slabs_ref[stage + 1, start : start + size] = after

        def put(x, row, value):
            target[x, row : row + SUB] = value

        sweep(
            stage, [(1 + stage, nx - 1 - stage)], nx, ny, nz, gz,
            lambda x, row: source[x, row : row + SUB], lambda x, row: i_ref[x, row : row + SUB],
            put, q, sums,
        )
    for k in range(5):
        sum_ref[k] = sums[k]


def outer_kernel(
    after_ref, a_ref, i_ref, b_ref, c_ref, slab_ref, halo_ref, sum_ref, first_ref, second_ref, stat_ref,
    ea_ref, eb_ref, ec_ref, slabs_ref, total_ref, ei_ref, si_ref,
):
    nx, ny, nz = a_ref.shape[0], a_ref.shape[1] - 2 * SUB, a_ref.shape[2]
    ring = ny + SUB
    gz = lax.axis_index("gz")
    gx = lax.axis_index("gx")
    odd = lax.rem(gx, 2) == 1
    has_low, has_high = gx > 0, gx < lax.axis_size("gx") - 1

    def low(k):
        return jnp.where(has_low, jnp.where(odd, first_ref[k], second_ref[k]), 0.0)

    def high(k):
        return jnp.where(has_high, jnp.where(odd, second_ref[k], first_ref[k]), 0.0)

    for ref, at, plane in (
        [(ea_ref, k, low(k)) for k in range(3)] + [(ea_ref, 3 + k, high(k)) for k in range(3)]
        + [(ei_ref, k, low(3 + k)) for k in range(2)] + [(ei_ref, 2 + k, high(3 + k)) for k in range(2)]
    ):
        ref[at, :SUB] = plane[ny:]
        ref[at, SUB : SUB + ny] = plane[:ny]
        ref[at, SUB + ny :] = plane[ny:]

    lane = lanes_of((ring, nz))
    lo5, hi5 = low(5), high(5)
    slab_w = jnp.where(lane < 3 * PACK, hi5, 0.0) + jnp.where(lane >= nz - 3 * PACK, lo5, 0.0)
    lo5, hi5 = pltpu.roll(lo5, nz // 2, 1), pltpu.roll(hi5, nz // 2, 1)
    slab_i = jnp.where(lane < 2 * PACK, hi5, 0.0) + jnp.where(lane >= nz - 2 * PACK, lo5, 0.0)
    for ref, k, beyond in ((slabs_ref, 0, slab_w), (si_ref, 1, slab_i)):
        ref[0, SUB : SUB + ny, :nz] = slab_ref[k]
        ref[0, SUB : SUB + ny, nz:] = beyond[:ny]
        for rows in (slice(0, SUB), slice(SUB + ny, SUB + ring)):
            ref[0, rows, :nz] = halo_ref[k, nx]
            ref[0, rows, nz:] = beyond[ny:]

    def reader(inside_ref, edge_ref, first, count):
        def get(x, row):
            if first <= x < nx - first:
                return inside_ref[x, row : row + SUB]
            at = x - (first - count) if x < first else x - (nx - first) + count
            return edge_ref[at, row : row + SUB]

        return get

    sums = {}
    for stage in range(3):
        get = reader((a_ref, b_ref, c_ref)[stage], (ea_ref, eb_ref, ec_ref)[stage], stage, 3)
        start, size = SUB - 2 + stage, ny if stage == 2 else ring
        v = slabs_ref[stage, start : start + size]
        s = slabs_ref[stage, start - 1 : start - 1 + size] + slabs_ref[stage, start + 1 : start + 1 + size]
        q, after = slab_step(v, s, si_ref[0, start : start + size] if stage < 2 else None)
        if stage < 2:
            slabs_ref[stage + 1, start : start + size] = after

        def put(x, row, value):
            edge_ref = (eb_ref, ec_ref)[stage]
            at = x - (stage - 2) if x < nx // 2 else x - (nx - 1 - stage) + 3
            edge_ref[at, row : row + SUB] = value

        sweep(
            stage, [(stage - 2, stage + 1), (nx - 1 - stage, nx + 2 - stage)], nx, ny, nz, gz,
            get, reader(i_ref, ei_ref, 0, 2), put, q, sums,
        )

    total_ref[0:1] = stat_ref[0, 0:1]
    for k in range(5):
        total_ref[k + 1 : k + 2] = jnp.sum(sums[k] + sum_ref[k], axis=0, keepdims=True)
    total_ref[6:8] = jnp.zeros((2, nz), F32)
    here = (lax.axis_index("gx") * lax.axis_size("gy") + lax.axis_index("gy")) * lax.axis_size("gz") + gz
    count = jnp.sum(stat_ref[1], axis=1, keepdims=True)
    total_ref[8:16] = jnp.where(lanes_of((SUB, nz)) == here, count, 0.0)


def shift_left(v, amount, lane):
    rows = v.shape[0]
    if amount < LANES:
        turned = pltpu.roll(v, LANES - amount, 1)
        below = pltpu.roll(turned, rows - 1, 0)
        return jnp.where(lane < LANES - amount, turned, below)
    return jnp.concatenate([v[amount // LANES :], v[: amount // LANES]], axis=0)


def plan_kernel(after_ref, label_ref, plan_ref):
    rows = label_ref.shape[0]
    lane = lanes_of((rows, LANES))
    row = subs_of((rows, LANES))
    heart = label_ref[...] == 1
    ones = heart.astype(jnp.bfloat16)
    upper = (subs_of((LANES, LANES)) < lanes_of((LANES, LANES))).astype(jnp.bfloat16)
    in_row = jnp.dot(ones, upper, preferred_element_type=F32)
    totals = jnp.dot(ones, jnp.ones((LANES, LANES), jnp.bfloat16), preferred_element_type=F32)
    lower = (subs_of((rows, rows)) > lanes_of((rows, rows))).astype(jnp.bfloat16)
    before = jnp.dot(lower, totals.astype(jnp.bfloat16), preferred_element_type=F32)
    rank = (in_row + before).astype(jnp.int32)
    way = jnp.where(heart, row * LANES + lane - rank, 0)
    plan = jnp.zeros((rows, LANES), jnp.int32)
    step = 1
    while step < rows * LANES:
        moving = jnp.where((way & step) != 0, way, 0)
        arriving = shift_left(moving, step, lane)
        plan = plan | (arriving & step)
        way = (way - moving) | arriving
        step *= 2
    plan_ref[...] = plan


def galerkin(t):
    g00, g01, g02, g12, g22 = t[0] - t[1], t[1] - t[2], t[2] - t[3], t[3] - t[4], t[4] - t[5]
    g11 = g02
    l10, l20 = g01 / g00, g02 / g00
    d1 = g11 - l10 * g01
    m21 = g12 - l20 * g01
    ok1 = d1 > 1e-6 * g11
    d1 = jnp.where(ok1, d1, 1.0)
    l21 = jnp.where(ok1, m21 / d1, 0.0)
    d2 = g22 - l20 * g02 - l21 * m21
    ok2 = ok1 & (d2 > 1e-6 * g22)
    d2 = jnp.where(ok2, d2, 1.0)
    y1 = t[1] - l10 * t[0]
    y2 = t[2] - l20 * t[0] - l21 * y1
    c2 = jnp.where(ok2, y2 / d2, 0.0)
    c1 = jnp.where(ok1, y1 / d1 - l21 * c2, 0.0)
    c0 = t[0] / g00 - l10 * c1 - l20 * c2
    return c0, c1, c2


def couple_kernel(stage, slot_rows, after_ref, inside_ref, edge_ref, slabs_ref, plan_ref, list_ref, value_ref):
    nx, nz = inside_ref.shape[0], inside_ref.shape[2]
    ny = inside_ref.shape[1] - 2 * SUB
    rows = nx * ny
    gz = lax.axis_index("gz")

    def get(x, row):
        if stage <= x < nx - stage:
            return inside_ref[x, row : row + SUB]
        return edge_ref[x - (stage - 3) if x < stage else x - (nx - stage) + 3, row : row + SUB]

    for tile in range(ny // SUB):
        row = SUB + SUB * tile
        slab = slabs_ref[stage, row : row + SUB, :nz]
        v_low, v_mid = get(-1, row), get(0, row)
        for x in range(nx):
            v_high = get(x + 1, row)
            beside = get(x, row - 1) + get(x, row + 1)
            at = ny * x + SUB * tile
            value_ref[at : at + SUB] = (
                along_z(v_mid, slab, PACK * x, gz) + beside + (v_low + v_high) - 6.0 * v_mid
            )
            v_low, v_mid = v_mid, v_high
    lane = lanes_of((rows, LANES))
    value = value_ref[...]
    plan = plan_ref[...]
    step = 1
    while step < rows * LANES:
        value = jnp.where((plan & step) != 0, shift_left(value, step, lane), value)
        step *= 2
    list_ref[...] = value[:slot_rows]


def add_kernel(a_ref, b_ref, after_ref, out_ref):
    out_ref[...] = a_ref[...] + b_ref[...]


def place_kernel(n_sums, *refs):
    sum_refs, refs = refs[:n_sums], refs[n_sums:]
    list_refs, refs = refs[:3], refs[3:]
    coef_ref, *out_refs, buf_ref = refs
    total = sum_refs[0][...]
    for ref in sum_refs[1:]:
        total = total + ref[...]
    sums = jnp.sum(total[0:8], axis=1, keepdims=True)
    t = [jnp.broadcast_to(sums[k : k + 1], (1, LANES)) for k in range(6)]
    coefs = galerkin(t)
    for k in range(3):
        coef_ref[k : k + 1] = coefs[k]
    value = coefs[0] * list_refs[0][...] + coefs[1] * list_refs[1][...] + coefs[2] * list_refs[2][...]
    slot_rows = value.shape[0]
    n_y, n_z = lax.axis_size("gy"), lax.axis_size("gz")
    counts = total[8:16]
    dev = lanes_of((SUB, LANES))
    mine = lax.rem(dev, n_y * n_z) == lax.axis_index("gy") * n_z + lax.axis_index("gz")
    gx = lax.axis_index("gx")
    first = subs_of((SUB, LANES)) == 0
    offset = jnp.sum(jnp.where(first & mine & (dev < gx * n_y * n_z), counts, 0.0)).astype(jnp.int32)
    count = jnp.sum(jnp.where(first & mine & (dev // (n_y * n_z) == gx), counts, 0.0)).astype(jnp.int32)
    shape = (slot_rows, LANES)
    slots = jnp.where(subs_of(shape) * LANES + lanes_of(shape) < count, value, 0.0)
    slots = jnp.concatenate([slots, jnp.zeros((SUB, LANES), F32)], axis=0)
    inner = lax.rem(offset, LANES)
    turned = pltpu.roll(slots, inner, 1)
    above = pltpu.roll(turned, 1, 0)
    moved = jnp.where(lanes_of((slot_rows + SUB, LANES)) >= inner, turned, above)
    buf_ref[...] = jnp.zeros_like(buf_ref)
    buf_ref[pl.ds(offset // LANES, slot_rows + SUB), :] = moved
    for k, out_ref in enumerate(out_refs):
        size = out_ref.shape[0]
        out_ref[...] = buf_ref[pl.ds(pl.multiple_of((gx ^ k) * size, SUB), size), :]


def potential_kernel(coef_ref, a_ref, b_ref, c_ref, eb_ref, ec_ref, x_ref):
    nx, ny, nz = x_ref.shape
    own = slice(SUB, SUB + ny)
    c0, c1, c2 = [coef_ref[k : k + 1] for k in range(3)]
    for x in range(nx):
        w1 = b_ref[x, own] if 1 <= x < nx - 1 else eb_ref[2 if x == 0 else 3, own]
        w2 = c_ref[x, own] if 2 <= x < nx - 2 else ec_ref[x + 1 if x < 2 else x - (nx - 2) + 3, own]
        x_ref[x] = c0 * a_ref[x, own] + c1 * w1 + c2 * w2


def membrane_kernel(
    half_ref, slope_ref, tau_ref, cond_ref, rev_ref, after_ref, v_ref, gates_ref, cot_ref,
    base_ref, sum_ref, factor_ref, coef_ref,
):
    n_states, rows = gates_ref.shape[:2]
    v = v_ref[...]

    def state(g, carry):
        total, current = carry
        inv_slope = 1.0 / slope_ref[g]
        tau_base = tau_ref[g]
        scaled = (v - half_ref[g]) * inv_slope
        gate = gates_ref[g]
        cot = cot_ref[g]
        steady = 1.0 / (1.0 + jnp.exp(-scaled))
        bell = jnp.exp(-scaled * scaled)
        rate = TIME_STEP / (tau_base * (0.5 + bell))
        decay = jnp.exp(-rate)
        steady_slope = steady * (1.0 - steady)
        decay_slope = decay * rate * rate * ((tau_base / TIME_STEP) * bell * (-2.0 * scaled))
        change = (steady_slope * (1.0 - decay) + (gate - steady) * decay_slope) * inv_slope
        base_ref[g] = cot * decay
        coef_ref[0, pl.ds(g, 1)] = jnp.full((1, LANES), TIME_STEP * cond_ref[g])
        coef_ref[1, pl.ds(g, 1)] = jnp.full((1, LANES), rev_ref[g])
        return total + cot * change, current + cond_ref[g] * gate

    zero = jnp.zeros((rows, LANES), F32)
    total, current = lax.fori_loop(0, n_states, state, (zero, zero), unroll=2)
    sum_ref[...] = total
    factor_ref[...] = 1.0 - TIME_STEP * current


def finish_kernel(coef_ref, vcot_ref, v_ref, sum_ref, factor_ref, base_ref, *refs):
    *landed_refs, volt_ref, gate_ref = refs
    landed = landed_refs[0][...]
    for ref in landed_refs[1:]:
        landed = landed + ref[...]
    cot = vcot_ref[...] + landed
    v = v_ref[...]
    volt_ref[...] = cot * factor_ref[...] + sum_ref[...]
    for g in range(base_ref.shape[0]):
        gate_ref[g] = base_ref[g] - (coef_ref[0, g : g + 1] * cot) * (v - coef_ref[1, g : g + 1])


def both_ways(up, down, axis):
    count = lax.axis_size(axis)
    low = lax.ppermute(up, axis, [(i, i + 1) for i in range(count - 1)])
    high = lax.ppermute(down, axis, [(i + 1, i) for i in range(count - 1)])
    return low, high


def swap(value, partner):
    n_gz = lax.axis_size("gz")
    pairs = [
        (x * n_gz + z, to * n_gz + z if to != x else x * n_gz + (z ^ 1))
        for x, to in enumerate(partner) for z in range(n_gz)
    ]
    return lax.ppermute(value, ("gx", "gz"), pairs)


def pair_swaps(first, second):
    count = lax.axis_size("gx")
    between = [0] + [i + 1 if i % 2 else i - 1 for i in range(1, count - 1)] + [count - 1]
    return swap(first, [i ^ 1 for i in range(count)]), swap(second, between)


def block_partners(count, k, slots, block):
    def apart(tile, owner):
        return owner * block >= (tile + 1) * slots or (owner + 1) * block <= count * block - (count - tile) * slots

    return [i if apart(i, i ^ k) and apart(i ^ k, i) else i ^ k for i in range(count)]


def reduce_over(value, axis):
    count = lax.axis_size(axis)
    step = 1
    while step < count:
        value = value + lax.ppermute(value, axis, [(i, i ^ step) for i in range(count)])
        step *= 2
    return value


def local(
    potential_cot, damping, tissue_label, heart_index, voltage, gates, voltage_cot, gates_cot,
    half_voltage, gate_slope, tau_base, conductance, reversal,
):
    nx, ny, nz = potential_cot.shape
    rows = nx * ny
    ring = ny + SUB
    n_gx, n_gy = lax.axis_size("gx"), lax.axis_size("gy")
    n_states = gates.shape[0]
    block_rows = voltage.shape[1] // LANES
    slot_rows = heart_index.shape[3] // LANES
    block = shape_of(nx, ny, nz)
    flat = lambda a: a.reshape(rows, LANES)
    cells = lambda a: a.reshape(block_rows, LANES)
    states = lambda a: a.reshape(n_states, block_rows, LANES)

    w0, inv, packed, stat = call(
        start_kernel, (block, block, shape_of(2, ny, nz), shape_of(2, SUB, nz)), 3,
        specs=[HBM] * 3,
        scratch=[
            pltpu.VMEM((nx, ny, nz), F32), pltpu.VMEM((nx, ny, nz), F32), pltpu.VMEM((nx, ny, nz), jnp.int32),
            pltpu.SemaphoreType.DMA((3, 2)),
        ],
    )(in_hbm(potential_cot), in_hbm(damping), in_hbm(tissue_label))

    got = lax.ppermute(packed, "gz", [(0, 1), (1, 0)])
    plan = call(plan_kernel, jax.ShapeDtypeStruct((rows, LANES), jnp.int32), 2, cost=6_000_000)(
        stat, flat(tissue_label)
    )

    face = shape_of(nx + 1, SUB, nz)
    slab_shape = shape_of(2, ny, nz)
    x_shapes = (shape_of(2, nx + 1, SUB, nz), shape_of(6, ring, nz), shape_of(6, ring, nz))
    if n_gy == 2:
        slab, mine = call(y_face_one_kernel, (slab_shape, face), 4)(w0, inv, packed, got)
        halo = (lax.ppermute(mine, "gy", [(0, 1), (1, 0)]),)
    else:
        slab, up, down = call(y_faces_kernel, (slab_shape, face, face), 4)(w0, inv, packed, got)
        halo = both_ways(up, down, "gy")
    edge_rows, first, second = call(
        functools.partial(x_faces_kernel, n_gy == 2), x_shapes, 4 + len(halo)
    )(plan, w0, inv, slab, *halo)
    first, second = pair_swaps(first, second)

    tall = ring + SUB
    planes = shape_of(nx, tall, nz)
    edges = shape_of(6, tall, nz)
    in0, in_inv, in1, in2, in_sums = call(
        inner_kernel,
        (planes,) * 4 + (shape_of(5, SUB, nz),),
        4,
        scratch=[pltpu.VMEM((4, tall, nz), F32)],
        cost=6_000_000,
    )(w0, inv, slab, edge_rows)
    base, total_change, factor, state_coefs = call(
        membrane_kernel,
        (
            shape_of(n_states, block_rows, LANES), shape_of(block_rows, LANES), shape_of(block_rows, LANES),
            shape_of(2, n_states, LANES),
        ),
        9,
        specs=[SMEM] * 5 + [VMEM] * 4,
        cost=6_000_000,
    )(
        half_voltage, gate_slope, tau_base, conductance, reversal,
        in_sums, cells(voltage), states(gates), states(gates_cot),
    )
    ends0, ends1, ends2, slabs, sums = call(
        outer_kernel,
        (edges,) * 3 + (shape_of(3, tall, 2 * nz), shape_of(16, nz)),
        11,
        scratch=[pltpu.VMEM((4, tall, nz), F32), pltpu.VMEM((1, tall, 2 * nz), F32)],
    )(state_coefs, in0, in_inv, in1, in2, slab, edge_rows, in_sums, first, second, stat)

    def couple(stage, after, inside, ends):
        return call(
            functools.partial(couple_kernel, stage, slot_rows),
            shape_of(slot_rows, LANES),
            5,
            scratch=[pltpu.VMEM((rows, LANES), F32)],
            cost=6_000_000,
        )(after, inside, ends, slabs, plan)

    def add(value, axis, step, after):
        got = lax.ppermute(value, axis, [(i, i ^ step) for i in range(lax.axis_size(axis))])
        return call(add_kernel, shape_of(16, nz), 3)(value, got, after)

    list0 = couple(0, sums, in0, ends0)
    sums = add(sums, "gz", 1, list0)
    list1 = couple(1, sums, in1, ends1)
    sums = add(sums, "gy", 1, list1)
    for step in [2**k for k in range(1, n_gy.bit_length() - 1)]:
        sums = add(sums, "gy", step, list1)
    list2 = couple(2, sums, in2, ends2)
    if n_gx <= 4:
        sums = [sums] + [lax.ppermute(sums, "gx", [(i, i ^ k) for i in range(n_gx)]) for k in range(1, n_gx)]
    else:
        sums = [reduce_over(sums, "gx")]

    coefs, *blocks = call(
        functools.partial(place_kernel, len(sums)),
        (shape_of(SUB, LANES),) + (shape_of(block_rows, LANES),) * n_gx,
        len(sums) + 3,
        scratch=[pltpu.VMEM((n_gx * block_rows + slot_rows + SUB, LANES), F32)],
    )(*sums, list0, list1, list2)
    landed = blocks[:1] + [
        swap(blocks[k], block_partners(n_gx, k, slot_rows, block_rows)) for k in range(1, n_gx)
    ]

    solution = call(potential_kernel, block, 6)(coefs, in0, in1, in2, ends1, ends2)
    volt_grad, gate_grad = call(
        finish_kernel,
        (shape_of(block_rows, LANES), shape_of(n_states, block_rows, LANES)),
        6 + n_gx,
    )(state_coefs, cells(voltage_cot), cells(voltage), total_change, factor, base, *landed)
    return solution, volt_grad.reshape(voltage.shape), gate_grad.reshape(gates.shape)


def solution(mesh):
    grid = P(("groups", "gx"), "gy", "gz")
    cells = P(("groups", "gy", "gz"), "gx")
    states = P(None, ("groups", "gy", "gz"), "gx")
    in_specs = (
        grid, grid, grid, P(("groups", "gx"), "gy", "gz", None), cells, states, cells, states,
        P(), P(), P(), P(), P(),
    )
    return jax.shard_map(
        local, mesh=mesh, in_specs=in_specs, out_specs=(grid, cells, states), check_vma=False
    )
```

```python
import functools

import jax
import jax.numpy as jnp
from jax import lax
from jax.experimental import pallas as pl
from jax.experimental.pallas import tpu as pltpu
from jax.sharding import PartitionSpec as P

TIME_STEP = 0.5
LANES = 128
SUB = 8
PACK = 8
F32 = jnp.float32

VMEM = pl.BlockSpec(memory_space=pltpu.VMEM)
SMEM = pl.BlockSpec(memory_space=pltpu.SMEM)
HBM = pl.BlockSpec(memory_space=pltpu.HBM)


def shape_of(*dims):
    return jax.ShapeDtypeStruct(dims, F32)


def call(kernel, out_shape, n_in, specs=None, outs=None, scratch=(), cost=2_000_000, limit=32):
    return pl.pallas_call(
        kernel,
        out_shape=out_shape,
        in_specs=specs if specs is not None else [VMEM] * n_in,
        out_specs=outs if outs is not None else jax.tree.map(lambda _: VMEM, out_shape),
        scratch_shapes=list(scratch),
        compiler_params=pltpu.CompilerParams(vmem_limit_bytes=limit * 1024 * 1024),
        cost_estimate=pl.CostEstimate(flops=cost, bytes_accessed=cost, transcendentals=0),
    )


def in_hbm(array):
    return pltpu.with_memory_space_constraint(array, pltpu.HBM)


def lanes_of(shape):
    return lax.broadcasted_iota(jnp.int32, shape, len(shape) - 1)


def subs_of(shape):
    return lax.broadcasted_iota(jnp.int32, shape, len(shape) - 2)


def start_kernel(
    right_hbm, damping_hbm, label_hbm, w0_ref, inv_ref, pack_ref, stat_ref, right_ref, damping_ref, label_ref, sems
):
    nx, ny, nz = right_ref.shape
    parts = sems.shape[1]
    size = nx // parts
    copies = []
    for part in range(parts):
        here = pl.ds(part * size, size)
        for k, (source, target) in enumerate(
            ((right_hbm, right_ref), (damping_hbm, damping_ref), (label_hbm, label_ref))
        ):
            copies.append(pltpu.make_async_copy(source.at[here], target.at[here], sems.at[k, part]))
            copies[-1].start()
    gz = lax.axis_index("gz")
    lane = lanes_of((ny, nz))
    packed_w = jnp.zeros((ny, nz), F32)
    packed_i = jnp.zeros((ny, nz), F32)
    energy = jnp.zeros((ny, nz), F32)
    cells = jnp.zeros((ny, nz), F32)
    for x in range(nx):
        if x % size == 0:
            for k in range(3):
                copies[3 * (x // size) + k].wait()
        label = label_ref[x].astype(F32)
        right = right_ref[x]
        inv = 1.0 / (12.0 + damping_ref[x] * (1.0 + 3.0 * label))
        w0 = right * inv
        w0_ref[x] = w0
        inv_ref[x] = inv
        energy = energy + right * w0
        cells = cells + label
        turn = (PACK * x + 3) % nz
        begin = PACK * x + 3 * gz
        chosen = (lane >= begin) & (lane < begin + 3)
        packed_w = jnp.where(chosen, pltpu.roll(w0, turn, 1), packed_w)
        packed_i = jnp.where(chosen, pltpu.roll(inv, turn, 1), packed_i)
    pack_ref[0] = packed_w
    pack_ref[1] = packed_i
    stat_ref[0] = jnp.broadcast_to(jnp.sum(energy, axis=0, keepdims=True), (SUB, nz))
    stat_ref[1] = jnp.broadcast_to(jnp.sum(cells, axis=0, keepdims=True), (SUB, nz))


def steps_of(axis):
    return 1 if lax.axis_size(axis) == 2 else 2


def upper_in(axis, step):
    return lax.rem(lax.axis_index(axis), 2) == step


def has_partner(axis, step):
    here = lax.axis_index(axis)
    return jnp.where(upper_in(axis, step), here < lax.axis_size(axis) - 1, here > 0)


def unpack_rows(tile, step):
    sub = subs_of(tile.shape)
    up, there = upper_in("gy", step), has_partner("gy", step)
    depth = jnp.where(there, jnp.where(up, SUB - 1 - sub, sub), -1)
    return jnp.where(depth >= 5, tile, 0.0), jnp.where(depth >= 6, pltpu.roll(tile, 4, 0), 0.0)


def halo_rows(tiles):
    w_tile, i_tile = unpack_rows(tiles[0], 0)
    for step, tile in enumerate(tiles[1:], 1):
        w_more, i_more = unpack_rows(tile, step)
        w_tile, i_tile = w_tile + w_more, i_tile + i_more
    return w_tile, i_tile


def faces_kernel(n_y, w0_ref, inv_ref, own_ref, got_ref, slab_ref, *refs):
    y_refs, x_refs, edge_refs = refs[:n_y], refs[n_y : n_y + 2], refs[n_y + 2 :]
    nx, ny, nz = w0_ref.shape
    sub = subs_of((SUB, nz))
    lane = lanes_of((ny, nz))
    slab_ref[...] = own_ref[...] + got_ref[...]
    for step, face_ref in enumerate(y_refs):
        up = upper_in("gy", step)
        keep_w = jnp.where(up, sub, SUB - 1 - sub) >= 5
        for x in range(nx + 1):
            w_rows, i_rows = (w0_ref.at[x], inv_ref.at[x]) if x < nx else (slab_ref.at[0], slab_ref.at[1])
            w_face = jnp.where(up, w_rows[ny - SUB :], w_rows[:SUB])
            i_face = jnp.where(up, i_rows[ny - SUB :], i_rows[:SUB])
            face_ref[x] = jnp.where(keep_w, w_face, pltpu.roll(i_face, 4, 0))
    slab_w = slab_ref[0]
    half = pltpu.roll(slab_ref[1], nz // 2, 1)
    up_slab = jnp.where(lane >= nz - 3 * PACK, slab_w, half)
    down_slab = jnp.where(lane < 3 * PACK, slab_w, half)
    for step, face_ref in enumerate(x_refs):
        up = upper_in("gx", step)
        first = jnp.where(up, nx - 3, 0)
        for k in range(3):
            face_ref[k] = w0_ref[first + k]
        for k in range(2):
            face_ref[3 + k] = inv_ref[jnp.where(up, nx - 2, 0) + k]
        face_ref[5] = jnp.where(up, up_slab, down_slab)
        for y_step, y_ref in enumerate(y_refs):
            edge_ref = edge_refs[step * n_y + y_step]
            for k in range(3):
                edge_ref[k] = y_ref[first + k]
            edge_ref[3] = y_ref[nx]


def slab_step(v, s, inv):
    width = v.shape[1]
    across = pltpu.roll(v, PACK, 1) + pltpu.roll(v, width - PACK, 1)
    q = v + 0.5 * (s + across)
    if inv is None:
        return q, None
    total = (
        pltpu.roll(q, 1, 1) + pltpu.roll(q, width - 1, 1) + s + across
        + 0.5 * (pltpu.roll(s, PACK, 1) + pltpu.roll(s, width - PACK, 1))
    )
    return q, total * inv


def along_z(q, half, column, gz):
    nz = q.shape[1]
    lane = lanes_of(q.shape)
    entry = (nz - 1) * (1 - gz)
    turn = lax.rem(entry - (column + 3 - gz) + 2 * nz, nz)
    up = jnp.where(lane == nz - 1, 0.0, pltpu.roll(q, nz - 1, 1))
    down = jnp.where(lane == 0, 0.0, pltpu.roll(q, 1, 1))
    return up + down + jnp.where(lane == entry, pltpu.roll(half, turn, 1), 0.0)


def sweep(stage, spans, nx, ny, nz, gz, get, get_inv, put, slab_q, sums):
    margin = 2 - stage
    start = SUB - margin
    tiles = ny // SUB + (margin > 0)
    own = subs_of((SUB, nz)) >= margin
    parts = [[], []]
    for tile in range(tiles):
        row = start + SUB * tile
        q_rows = slab_q[SUB * tile : SUB * tile + SUB]
        acc = [jnp.zeros((SUB, nz), F32) for _ in range(2)]

        def beside(x):
            return get(x, row - 1) + get(x, row + 1)

        for first, last in spans:
            s_low, s_mid = beside(first - 1), beside(first)
            v_low, v_mid = get(first - 1, row), get(first, row)
            for x in range(first, last):
                v_high, s_high = get(x + 1, row), beside(x + 1)
                across = v_low + v_high
                column = (PACK * x) % (2 * nz)
                half = q_rows[:, column // nz * nz : column // nz * nz + nz]
                rest = s_mid + across
                total = along_z(v_mid + 0.5 * rest, half, column % nz, gz) + rest + 0.5 * (s_low + s_high)
                if stage < 2:
                    after = total * get_inv(x, row)
                    put(x, row, after)
                if 0 <= x < nx:
                    acc[0] = acc[0] + v_mid * total
                    if stage < 2:
                        acc[1] = acc[1] + after * total
                v_low, v_mid, s_low, s_mid = v_mid, v_high, s_mid, s_high
        for k in range(2):
            parts[k].append(acc[k])
    for k in range(2 if stage < 2 else 1):
        part = parts[k]
        total = part[1]
        for other in part[2 : ny // SUB]:
            total = total + other
        total = total + (jnp.where(own, part[0], part[-1]) if margin else part[0])
        sums[2 * stage + k] = total


def inner_kernel(n_y, w0_ref, inv_ref, slab_ref, *refs):
    y_refs, (a_ref, i_ref, b_ref, c_ref, sum_ref, own_slab_ref, slabs_ref) = refs[:n_y], refs[n_y:]
    nx, ny, nz = w0_ref.shape
    gz = lax.axis_index("gz")
    for x in range(nx + 1):
        halos = halo_rows([ref[x] for ref in y_refs])
        for k in range(2):
            if x < nx:
                ref, own = (a_ref, i_ref)[k].at[x], (w0_ref, inv_ref)[k][x]
            else:
                ref, own = own_slab_ref.at[k], slab_ref[k]
            ref[:SUB] = halos[k]
            ref[SUB : SUB + ny] = own
            ref[SUB + ny :] = halos[k]
    for k in range(2):
        slabs_ref[3 * k] = own_slab_ref[k]
    sums = {}
    for stage in range(3):
        source, target = (a_ref, b_ref, c_ref)[stage], (b_ref, c_ref, None)[stage]
        start, size = SUB - 2 + stage, ny if stage == 2 else ny + SUB
        v = slabs_ref[stage, start : start + size]
        s = slabs_ref[stage, start - 1 : start - 1 + size] + slabs_ref[stage, start + 1 : start + 1 + size]
        q, after = slab_step(v, s, slabs_ref[3, start : start + size] if stage < 2 else None)
        if stage < 2:
            slabs_ref[stage + 1, start : start + size] = after

        def put(x, row, value):
            target[x, row : row + SUB] = value

        sweep(
            stage, [(1 + stage, nx - 1 - stage)], nx, ny, nz, gz,
            lambda x, row: source[x, row : row + SUB], lambda x, row: i_ref[x, row : row + SUB],
            put, q, sums,
        )
    for k in range(5):
        sum_ref[k] = sums[k]


def outer_kernel(
    n_y, after_ref, a_ref, i_ref, b_ref, c_ref, slab_ref, sum_ref, stat_ref, *refs
):
    x_refs, corner_refs = refs[:2], refs[2 : 2 + 2 * n_y]
    ea_ref, eb_ref, ec_ref, slabs_ref, total_ref, ei_ref, si_ref = refs[2 + 2 * n_y :]
    nx, ny, nz = a_ref.shape[0], a_ref.shape[1] - 2 * SUB, a_ref.shape[2]
    ring = ny + SUB
    gz = lax.axis_index("gz")
    odd = lax.rem(lax.axis_index("gx"), 2) == 1

    def beyond(upper, read):
        there = has_partner("gx", 0) if upper else has_partner("gx", 1)
        swapped = has_partner("gx", 1) if upper else has_partner("gx", 0)
        first, second = read(0), read(1)
        if upper:
            return jnp.where(jnp.where(odd, swapped, there), jnp.where(odd, second, first), 0.0)
        return jnp.where(jnp.where(odd, swapped, there), jnp.where(odd, first, second), 0.0)

    def write(ref, at, own, halo):
        ref[at, :SUB] = halo
        ref[at, SUB : SUB + ny] = own
        ref[at, SUB + ny :] = halo

    lane_tile, lane = lanes_of((SUB, nz)), lanes_of((ny, nz))
    slab_parts = []
    for side, upper in enumerate((False, True)):
        tiles = [
            halo_rows([beyond(upper, lambda step: corner_refs[step * n_y + j][k]) for j in range(n_y)])
            for k in range(4)
        ]
        for k in range(3):
            write(ea_ref, 3 * side + k, beyond(upper, lambda step: x_refs[step][k]), tiles[k][0])
        for k in range(2):
            own = beyond(upper, lambda step: x_refs[step][3 + k])
            write(ei_ref, 2 * side + k, own, tiles[k if upper else k + 1][1])
        own = beyond(upper, lambda step: x_refs[step][5])

        def near(value, lanes, planes):
            return jnp.where(lanes < planes * PACK if upper else lanes >= nz - planes * PACK, value, 0.0)

        slab_parts.append((
            near(own, lane, 3), near(tiles[3][0], lane_tile, 3),
            near(pltpu.roll(own, nz // 2, 1), lane, 2), near(tiles[3][1], lane_tile, 2),
        ))

    low, high = slab_parts
    for ref, k in ((slabs_ref, 0), (si_ref, 1)):
        ref[0, :, :nz] = slab_ref[k]
        ref[0, SUB : SUB + ny, nz:] = low[2 * k] + high[2 * k]
        ref[0, :SUB, nz:] = low[2 * k + 1] + high[2 * k + 1]
        ref[0, SUB + ny :, nz:] = low[2 * k + 1] + high[2 * k + 1]

    def reader(inside_ref, edge_ref, first, count):
        def get(x, row):
            if first <= x < nx - first:
                return inside_ref[x, row : row + SUB]
            at = x - (first - count) if x < first else x - (nx - first) + count
            return edge_ref[at, row : row + SUB]

        return get

    sums = {}
    for stage in range(3):
        get = reader((a_ref, b_ref, c_ref)[stage], (ea_ref, eb_ref, ec_ref)[stage], stage, 3)
        start, size = SUB - 2 + stage, ny if stage == 2 else ring
        v = slabs_ref[stage, start : start + size]
        s = slabs_ref[stage, start - 1 : start - 1 + size] + slabs_ref[stage, start + 1 : start + 1 + size]
        q, after = slab_step(v, s, si_ref[0, start : start + size] if stage < 2 else None)
        if stage < 2:
            slabs_ref[stage + 1, start : start + size] = after

        def put(x, row, value):
            edge_ref = (eb_ref, ec_ref)[stage]
            at = x - (stage - 2) if x < nx // 2 else x - (nx - 1 - stage) + 3
            edge_ref[at, row : row + SUB] = value

        sweep(
            stage, [(stage - 2, stage + 1), (nx - 1 - stage, nx + 2 - stage)], nx, ny, nz, gz,
            get, reader(i_ref, ei_ref, 0, 2), put, q, sums,
        )

    total_ref[0:1] = stat_ref[0, 0:1]
    for k in range(5):
        total_ref[k + 1 : k + 2] = jnp.sum(sums[k] + sum_ref[k], axis=0, keepdims=True)
    total_ref[6:8] = jnp.zeros((2, nz), F32)
    here = (lax.axis_index("gx") * lax.axis_size("gy") + lax.axis_index("gy")) * lax.axis_size("gz") + gz
    count = jnp.sum(stat_ref[1], axis=1, keepdims=True)
    total_ref[8:16] = jnp.where(lanes_of((SUB, nz)) == here, count, 0.0)


def shift_left(v, amount, lane):
    rows = v.shape[0]
    if amount < LANES:
        turned = pltpu.roll(v, LANES - amount, 1)
        below = pltpu.roll(turned, rows - 1, 0)
        return jnp.where(lane < LANES - amount, turned, below)
    return jnp.concatenate([v[amount // LANES :], v[: amount // LANES]], axis=0)


def plan_kernel(after_ref, label_ref, plan_ref):
    rows = label_ref.shape[0]
    lane = lanes_of((rows, LANES))
    row = subs_of((rows, LANES))
    heart = label_ref[...] == 1
    ones = heart.astype(jnp.bfloat16)
    upper = (subs_of((LANES, LANES)) < lanes_of((LANES, LANES))).astype(jnp.bfloat16)
    in_row = jnp.dot(ones, upper, preferred_element_type=F32)
    totals = jnp.dot(ones, jnp.ones((LANES, LANES), jnp.bfloat16), preferred_element_type=F32)
    lower = (subs_of((rows, rows)) > lanes_of((rows, rows))).astype(jnp.bfloat16)
    before = jnp.dot(lower, totals.astype(jnp.bfloat16), preferred_element_type=F32)
    rank = (in_row + before).astype(jnp.int32)
    way = jnp.where(heart, row * LANES + lane - rank, 0)
    plan = jnp.zeros((rows, LANES), jnp.int32)
    step = 1
    while step < rows * LANES:
        moving = jnp.where((way & step) != 0, way, 0)
        arriving = shift_left(moving, step, lane)
        plan = plan | (arriving & step)
        way = (way - moving) | arriving
        step *= 2
    plan_ref[...] = plan


def galerkin(t):
    g00, g01, g02, g12, g22 = t[0] - t[1], t[1] - t[2], t[2] - t[3], t[3] - t[4], t[4] - t[5]
    g11 = g02
    l10, l20 = g01 / g00, g02 / g00
    d1 = g11 - l10 * g01
    m21 = g12 - l20 * g01
    ok1 = d1 > 1e-6 * g11
    d1 = jnp.where(ok1, d1, 1.0)
    l21 = jnp.where(ok1, m21 / d1, 0.0)
    d2 = g22 - l20 * g02 - l21 * m21
    ok2 = ok1 & (d2 > 1e-6 * g22)
    d2 = jnp.where(ok2, d2, 1.0)
    y1 = t[1] - l10 * t[0]
    y2 = t[2] - l20 * t[0] - l21 * y1
    c2 = jnp.where(ok2, y2 / d2, 0.0)
    c1 = jnp.where(ok1, y1 / d1 - l21 * c2, 0.0)
    c0 = t[0] / g00 - l10 * c1 - l20 * c2
    return c0, c1, c2


def couple_kernel(stage, slot_rows, after_ref, inside_ref, edge_ref, slabs_ref, plan_ref, list_ref, value_ref):
    nx, nz = inside_ref.shape[0], inside_ref.shape[2]
    ny = inside_ref.shape[1] - 2 * SUB
    rows = nx * ny
    gz = lax.axis_index("gz")

    def get(x, row):
        if stage <= x < nx - stage:
            return inside_ref[x, row : row + SUB]
        return edge_ref[x - (stage - 3) if x < stage else x - (nx - stage) + 3, row : row + SUB]

    for tile in range(ny // SUB):
        row = SUB + SUB * tile
        slab = slabs_ref[stage, row : row + SUB, :nz]
        v_low, v_mid = get(-1, row), get(0, row)
        for x in range(nx):
            v_high = get(x + 1, row)
            beside = get(x, row - 1) + get(x, row + 1)
            at = ny * x + SUB * tile
            value_ref[at : at + SUB] = (
                along_z(v_mid, slab, PACK * x, gz) + beside + (v_low + v_high) - 6.0 * v_mid
            )
            v_low, v_mid = v_mid, v_high
    lane = lanes_of((rows, LANES))
    value = value_ref[...]
    plan = plan_ref[...]
    step = 1
    while step < rows * LANES:
        value = jnp.where((plan & step) != 0, shift_left(value, step, lane), value)
        step *= 2
    list_ref[...] = value[:slot_rows]


def add_kernel(a_ref, b_ref, after_ref, out_ref):
    out_ref[...] = a_ref[...] + b_ref[...]


def place_kernel(n_sums, *refs):
    sum_refs, refs = refs[:n_sums], refs[n_sums:]
    list_refs, refs = refs[:3], refs[3:]
    coef_ref, *out_refs, buf_ref = refs
    total = sum_refs[0][...]
    for ref in sum_refs[1:]:
        total = total + ref[...]
    sums = jnp.sum(total[0:8], axis=1, keepdims=True)
    t = [jnp.broadcast_to(sums[k : k + 1], (1, LANES)) for k in range(6)]
    coefs = galerkin(t)
    for k in range(3):
        coef_ref[k : k + 1] = coefs[k]
    value = coefs[0] * list_refs[0][...] + coefs[1] * list_refs[1][...] + coefs[2] * list_refs[2][...]
    slot_rows = value.shape[0]
    n_y, n_z = lax.axis_size("gy"), lax.axis_size("gz")
    counts = total[8:16]
    dev = lanes_of((SUB, LANES))
    mine = lax.rem(dev, n_y * n_z) == lax.axis_index("gy") * n_z + lax.axis_index("gz")
    gx = lax.axis_index("gx")
    first = subs_of((SUB, LANES)) == 0
    offset = jnp.sum(jnp.where(first & mine & (dev < gx * n_y * n_z), counts, 0.0)).astype(jnp.int32)
    count = jnp.sum(jnp.where(first & mine & (dev // (n_y * n_z) == gx), counts, 0.0)).astype(jnp.int32)
    shape = (slot_rows, LANES)
    slots = jnp.where(subs_of(shape) * LANES + lanes_of(shape) < count, value, 0.0)
    slots = jnp.concatenate([slots, jnp.zeros((SUB, LANES), F32)], axis=0)
    inner = lax.rem(offset, LANES)
    turned = pltpu.roll(slots, inner, 1)
    above = pltpu.roll(turned, 1, 0)
    moved = jnp.where(lanes_of((slot_rows + SUB, LANES)) >= inner, turned, above)
    buf_ref[...] = jnp.zeros_like(buf_ref)
    buf_ref[pl.ds(offset // LANES, slot_rows + SUB), :] = moved
    for k, out_ref in enumerate(out_refs):
        size = out_ref.shape[0]
        out_ref[...] = buf_ref[pl.ds(pl.multiple_of((gx ^ k) * size, SUB), size), :]


def potential_kernel(coef_ref, a_ref, b_ref, c_ref, eb_ref, ec_ref, x_ref):
    nx, ny, nz = x_ref.shape
    own = slice(SUB, SUB + ny)
    c0, c1, c2 = [coef_ref[k : k + 1] for k in range(3)]
    for x in range(nx):
        w1 = b_ref[x, own] if 1 <= x < nx - 1 else eb_ref[2 if x == 0 else 3, own]
        w2 = c_ref[x, own] if 2 <= x < nx - 2 else ec_ref[x + 1 if x < 2 else x - (nx - 2) + 3, own]
        x_ref[x] = c0 * a_ref[x, own] + c1 * w1 + c2 * w2


def membrane_kernel(
    half_ref, slope_ref, tau_ref, cond_ref, rev_ref, after_ref, v_ref, gates_ref, cot_ref,
    base_ref, sum_ref, factor_ref, coef_ref,
):
    n_states, rows = gates_ref.shape[:2]
    v = v_ref[...]

    def state(g, carry):
        total, current = carry
        inv_slope = 1.0 / slope_ref[g]
        tau_base = tau_ref[g]
        scaled = (v - half_ref[g]) * inv_slope
        gate = gates_ref[g]
        cot = cot_ref[g]
        steady = 1.0 / (1.0 + jnp.exp(-scaled))
        bell = jnp.exp(-scaled * scaled)
        rate = TIME_STEP / (tau_base * (0.5 + bell))
        decay = jnp.exp(-rate)
        steady_slope = steady * (1.0 - steady)
        decay_slope = decay * rate * rate * ((tau_base / TIME_STEP) * bell * (-2.0 * scaled))
        change = (steady_slope * (1.0 - decay) + (gate - steady) * decay_slope) * inv_slope
        base_ref[g] = cot * decay
        coef_ref[0, pl.ds(g, 1)] = jnp.full((1, LANES), TIME_STEP * cond_ref[g])
        coef_ref[1, pl.ds(g, 1)] = jnp.full((1, LANES), rev_ref[g])
        return total + cot * change, current + cond_ref[g] * gate

    zero = jnp.zeros((rows, LANES), F32)
    total, current = lax.fori_loop(0, n_states, state, (zero, zero), unroll=2)
    sum_ref[...] = total
    factor_ref[...] = 1.0 - TIME_STEP * current


def finish_kernel(coef_ref, vcot_ref, v_ref, sum_ref, factor_ref, base_ref, *refs):
    *landed_refs, volt_ref, gate_ref = refs
    landed = landed_refs[0][...]
    for ref in landed_refs[1:]:
        landed = landed + ref[...]
    cot = vcot_ref[...] + landed
    v = v_ref[...]
    volt_ref[...] = cot * factor_ref[...] + sum_ref[...]
    for g in range(base_ref.shape[0]):
        gate_ref[g] = base_ref[g] - (coef_ref[0, g : g + 1] * cot) * (v - coef_ref[1, g : g + 1])


def partners(axis, step):
    count = lax.axis_size(axis)
    if step == 0:
        return [i ^ 1 for i in range(count)]
    return [0] + [i + 1 if i % 2 else i - 1 for i in range(1, count - 1)] + [count - 1]


def swap(value, x_to=None, y_to=None):
    n_x, n_y, n_z = [lax.axis_size(axis) for axis in ("gx", "gy", "gz")]
    pairs = []
    for x in range(n_x):
        for y in range(n_y):
            to_x, to_y = x_to[x] if x_to else x, y_to[y] if y_to else y
            alone = (x_to and to_x == x) or (y_to and to_y == y)
            for z in range(n_z):
                to = (x, y, z ^ 1) if alone else (to_x, to_y, z)
                pairs.append(((x * n_y + y) * n_z + z, (to[0] * n_y + to[1]) * n_z + to[2]))
    return lax.ppermute(value, ("gx", "gy", "gz"), pairs)


def block_partners(count, k, slots, block):
    def apart(tile, owner):
        return owner * block >= (tile + 1) * slots or (owner + 1) * block <= count * block - (count - tile) * slots

    return [i if apart(i, i ^ k) and apart(i ^ k, i) else i ^ k for i in range(count)]


def reduce_over(value, axis):
    count = lax.axis_size(axis)
    step = 1
    while step < count:
        value = value + lax.ppermute(value, axis, [(i, i ^ step) for i in range(count)])
        step *= 2
    return value


def local(
    potential_cot, damping, tissue_label, heart_index, voltage, gates, voltage_cot, gates_cot,
    half_voltage, gate_slope, tau_base, conductance, reversal,
):
    nx, ny, nz = potential_cot.shape
    rows = nx * ny
    ring = ny + SUB
    n_gx, n_gy = lax.axis_size("gx"), lax.axis_size("gy")
    n_states = gates.shape[0]
    block_rows = voltage.shape[1] // LANES
    slot_rows = heart_index.shape[3] // LANES
    block = shape_of(nx, ny, nz)
    flat = lambda a: a.reshape(rows, LANES)
    cells = lambda a: a.reshape(block_rows, LANES)
    states = lambda a: a.reshape(n_states, block_rows, LANES)

    w0, inv, packed, stat = call(
        start_kernel, (block, block, shape_of(2, ny, nz), shape_of(2, SUB, nz)), 3,
        specs=[HBM] * 3,
        scratch=[
            pltpu.VMEM((nx, ny, nz), F32), pltpu.VMEM((nx, ny, nz), F32), pltpu.VMEM((nx, ny, nz), jnp.int32),
            pltpu.SemaphoreType.DMA((3, 2)),
        ],
    )(in_hbm(potential_cot), in_hbm(damping), in_hbm(tissue_label))

    got = lax.ppermute(packed, "gz", [(0, 1), (1, 0)])
    plan = call(plan_kernel, jax.ShapeDtypeStruct((rows, LANES), jnp.int32), 2, cost=6_000_000)(
        stat, flat(tissue_label)
    )

    n_y = steps_of("gy")
    shapes = (
        (shape_of(2, ny, nz),) + (shape_of(nx + 1, SUB, nz),) * n_y + (shape_of(6, ny, nz),) * 2
        + (shape_of(4, SUB, nz),) * (2 * n_y)
    )
    slab, *faces = call(functools.partial(faces_kernel, n_y), shapes, 4)(w0, inv, packed, got)
    along_y, along_x, across = faces[:n_y], faces[n_y : n_y + 2], faces[n_y + 2 :]
    y_to = [partners("gy", step) for step in range(n_y)]
    x_to = [partners("gx", step) for step in range(2)]
    along_y = [swap(face, y_to=y_to[j]) for j, face in enumerate(along_y)]
    along_x = [swap(face, x_to=x_to[i]) for i, face in enumerate(along_x)]
    across = [swap(face, x_to=x_to[k // n_y], y_to=y_to[k % n_y]) for k, face in enumerate(across)]

    tall = ring + SUB
    planes = shape_of(nx, tall, nz)
    edges = shape_of(6, tall, nz)
    in0, in_inv, in1, in2, in_sums, own_slab = call(
        functools.partial(inner_kernel, n_y),
        (planes,) * 4 + (shape_of(5, SUB, nz), shape_of(2, tall, nz)),
        3 + n_y,
        scratch=[pltpu.VMEM((4, tall, nz), F32)],
        cost=6_000_000,
    )(w0, inv, slab, *along_y)
    ends0, ends1, ends2, slabs, sums = call(
        functools.partial(outer_kernel, n_y),
        (edges,) * 3 + (shape_of(3, tall, 2 * nz), shape_of(16, nz)),
        10 + 2 * n_y,
        scratch=[pltpu.VMEM((4, tall, nz), F32), pltpu.VMEM((1, tall, 2 * nz), F32)],
    )(plan, in0, in_inv, in1, in2, own_slab, in_sums, stat, *along_x, *across)

    def couple(stage, after, inside, ends):
        return call(
            functools.partial(couple_kernel, stage, slot_rows),
            shape_of(slot_rows, LANES),
            5,
            scratch=[pltpu.VMEM((rows, LANES), F32)],
            cost=6_000_000,
        )(after, inside, ends, slabs, plan)

    def add(value, axis, step, after):
        got = lax.ppermute(value, axis, [(i, i ^ step) for i in range(lax.axis_size(axis))])
        return call(add_kernel, shape_of(16, nz), 3)(value, got, after)

    list0 = couple(0, sums, in0, ends0)
    sums = add(sums, "gz", 1, list0)
    list1 = couple(1, sums, in1, ends1)
    sums = add(sums, "gy", 1, list1)
    for step in [2**k for k in range(1, n_gy.bit_length() - 1)]:
        sums = add(sums, "gy", step, list1)
    list2 = couple(2, sums, in2, ends2)
    if n_gx <= 4:
        sums = [sums] + [lax.ppermute(sums, "gx", [(i, i ^ k) for i in range(n_gx)]) for k in range(1, n_gx)]
    else:
        sums = [reduce_over(sums, "gx")]

    coefs, *blocks = call(
        functools.partial(place_kernel, len(sums)),
        (shape_of(SUB, LANES),) + (shape_of(block_rows, LANES),) * n_gx,
        len(sums) + 3,
        scratch=[pltpu.VMEM((n_gx * block_rows + slot_rows + SUB, LANES), F32)],
    )(*sums, list0, list1, list2)
    landed = blocks[:1] + [
        swap(blocks[k], x_to=block_partners(n_gx, k, slot_rows, block_rows)) for k in [2, 1] + list(range(3, n_gx))
    ]

    solution = call(potential_kernel, block, 6)(coefs, in0, in1, in2, ends1, ends2)
    base, total_change, factor, state_coefs = call(
        membrane_kernel,
        (
            shape_of(n_states, block_rows, LANES), shape_of(block_rows, LANES), shape_of(block_rows, LANES),
            shape_of(2, n_states, LANES),
        ),
        9,
        specs=[SMEM] * 5 + [VMEM] * 4,
        cost=6_000_000,
    )(
        half_voltage, gate_slope, tau_base, conductance, reversal,
        coefs, cells(voltage), states(gates), states(gates_cot),
    )
    volt_grad, gate_grad = call(
        finish_kernel,
        (shape_of(block_rows, LANES), shape_of(n_states, block_rows, LANES)),
        6 + n_gx,
    )(state_coefs, cells(voltage_cot), cells(voltage), total_change, factor, base, *landed)
    return solution, volt_grad.reshape(voltage.shape), gate_grad.reshape(gates.shape)


def solution(mesh):
    grid = P(("groups", "gx"), "gy", "gz")
    cells = P(("groups", "gy", "gz"), "gx")
    states = P(None, ("groups", "gy", "gz"), "gx")
    in_specs = (
        grid, grid, grid, P(("groups", "gx"), "gy", "gz", None), cells, states, cells, states,
        P(), P(), P(), P(), P(),
    )
    return jax.shard_map(
        local, mesh=mesh, in_specs=in_specs, out_specs=(grid, cells, states), check_vma=False
    )
```

```python
import functools

import jax
import jax.numpy as jnp
from jax import lax
from jax.experimental import pallas as pl
from jax.experimental.pallas import tpu as pltpu
from jax.sharding import PartitionSpec as P

TIME_STEP = 0.5
LANES = 128
SUB = 8
PACK = 8
COUNT_LANE = 4 * PACK
F32 = jnp.float32

VMEM = pl.BlockSpec(memory_space=pltpu.VMEM)
SMEM = pl.BlockSpec(memory_space=pltpu.SMEM)
HBM = pl.BlockSpec(memory_space=pltpu.HBM)


def shape_of(*dims):
    return jax.ShapeDtypeStruct(dims, F32)


def call(kernel, out_shape, n_in, specs=None, outs=None, scratch=(), cost=2_000_000, limit=32):
    return pl.pallas_call(
        kernel,
        out_shape=out_shape,
        in_specs=specs if specs is not None else [VMEM] * n_in,
        out_specs=outs if outs is not None else jax.tree.map(lambda _: VMEM, out_shape),
        scratch_shapes=list(scratch),
        compiler_params=pltpu.CompilerParams(vmem_limit_bytes=limit * 1024 * 1024),
        cost_estimate=pl.CostEstimate(flops=cost, bytes_accessed=cost, transcendentals=0),
    )


def in_hbm(array):
    return pltpu.with_memory_space_constraint(array, pltpu.HBM)


def lanes_of(shape):
    return lax.broadcasted_iota(jnp.int32, shape, len(shape) - 1)


def subs_of(shape):
    return lax.broadcasted_iota(jnp.int32, shape, len(shape) - 2)


def start_kernel(
    right_hbm, damping_hbm, label_hbm, w0_ref, inv_ref, pack_ref, stat_ref, right_ref, damping_ref, label_ref, sems
):
    nx, ny, nz = right_ref.shape
    parts = sems.shape[1]
    size = nx // parts
    copies = []
    for part in range(parts):
        here = pl.ds(part * size, size)
        for k, (source, target) in enumerate(
            ((right_hbm, right_ref), (damping_hbm, damping_ref), (label_hbm, label_ref))
        ):
            copies.append(pltpu.make_async_copy(source.at[here], target.at[here], sems.at[k, part]))
            copies[-1].start()
    gz = lax.axis_index("gz")
    lane = lanes_of((ny, nz))
    packed_w = jnp.zeros((ny, nz), F32)
    packed_i = jnp.zeros((ny, nz), F32)
    energy = jnp.zeros((ny, nz), F32)
    cells = jnp.zeros((ny, nz), F32)
    for x in range(nx):
        if x % size == 0:
            for k in range(3):
                copies[3 * (x // size) + k].wait()
        label = label_ref[x].astype(F32)
        right = right_ref[x]
        inv = 1.0 / (12.0 + damping_ref[x] * (1.0 + 3.0 * label))
        w0 = right * inv
        w0_ref[x] = w0
        inv_ref[x] = inv
        energy = energy + right * w0
        cells = cells + label
        turn = (PACK * x + 3) % nz
        begin = PACK * x + 3 * gz
        chosen = (lane >= begin) & (lane < begin + 3)
        packed_w = jnp.where(chosen, pltpu.roll(w0, turn, 1), packed_w)
        packed_i = jnp.where(chosen, pltpu.roll(inv, turn, 1), packed_i)
    pack_ref[0] = packed_w
    pack_ref[1] = packed_i
    stat_ref[0] = jnp.broadcast_to(jnp.sum(energy, axis=0, keepdims=True), (SUB, nz))
    stat_ref[1] = jnp.broadcast_to(jnp.sum(cells, axis=0, keepdims=True), (SUB, nz))


def steps_of(axis):
    return 1 if lax.axis_size(axis) == 2 else 2


def upper_in(axis, step):
    return lax.rem(lax.axis_index(axis), 2) == step


def has_partner(axis, step):
    here = lax.axis_index(axis)
    return jnp.where(upper_in(axis, step), here < lax.axis_size(axis) - 1, here > 0)


def unpack_rows(tile, step):
    sub = subs_of(tile.shape)
    up, there = upper_in("gy", step), has_partner("gy", step)
    depth = jnp.where(there, jnp.where(up, SUB - 1 - sub, sub), -1)
    return jnp.where(depth >= 5, tile, 0.0), jnp.where(depth >= 6, pltpu.roll(tile, 4, 0), 0.0)


def halo_rows(tiles):
    w_tile, i_tile = unpack_rows(tiles[0], 0)
    for step, tile in enumerate(tiles[1:], 1):
        w_more, i_more = unpack_rows(tile, step)
        w_tile, i_tile = w_tile + w_more, i_tile + i_more
    return w_tile, i_tile


def faces_kernel(n_y, w0_ref, inv_ref, own_ref, got_ref, stat_ref, slab_ref, *refs):
    y_refs, x_refs, edge_refs = refs[:n_y], refs[n_y : n_y + 2], refs[n_y + 2 :]
    nx, ny, nz = w0_ref.shape
    sub = subs_of((SUB, nz))
    lane = lanes_of((ny, nz))
    slab_ref[...] = own_ref[...] + got_ref[...]
    for step, face_ref in enumerate(y_refs):
        up = upper_in("gy", step)
        keep_w = jnp.where(up, sub, SUB - 1 - sub) >= 5
        for x in range(nx + 1):
            w_rows, i_rows = (w0_ref.at[x], inv_ref.at[x]) if x < nx else (slab_ref.at[0], slab_ref.at[1])
            w_face = jnp.where(up, w_rows[ny - SUB :], w_rows[:SUB])
            i_face = jnp.where(up, i_rows[ny - SUB :], i_rows[:SUB])
            face_ref[x] = jnp.where(keep_w, w_face, pltpu.roll(i_face, 4, 0))
    cells = jnp.sum(stat_ref[1, 0:1], axis=1, keepdims=True)
    slab_w = slab_ref[0]
    half = pltpu.roll(slab_ref[1], nz // 2, 1)
    up_slab = jnp.where(lane >= nz - 3 * PACK, slab_w, half)
    down_slab = jnp.where(lane < 3 * PACK, slab_w, half)
    for step, face_ref in enumerate(x_refs):
        up = upper_in("gx", step)
        first = jnp.where(up, nx - 3, 0)
        for k in range(3):
            face_ref[k] = w0_ref[first + k]
        for k in range(2):
            face_ref[3 + k] = inv_ref[jnp.where(up, nx - 2, 0) + k]
        face_ref[5] = jnp.where(lane == COUNT_LANE, cells, jnp.where(up, up_slab, down_slab))
        for y_step, y_ref in enumerate(y_refs):
            edge_ref = edge_refs[step * n_y + y_step]
            for k in range(3):
                edge_ref[k] = y_ref[first + k]
            edge_ref[3] = y_ref[nx]


def slab_step(v, s, inv):
    width = v.shape[1]
    across = pltpu.roll(v, PACK, 1) + pltpu.roll(v, width - PACK, 1)
    q = v + 0.5 * (s + across)
    if inv is None:
        return q, None
    total = (
        pltpu.roll(q, 1, 1) + pltpu.roll(q, width - 1, 1) + s + across
        + 0.5 * (pltpu.roll(s, PACK, 1) + pltpu.roll(s, width - PACK, 1))
    )
    return q, total * inv


def along_z(q, half, column, gz):
    nz = q.shape[1]
    lane = lanes_of(q.shape)
    entry = (nz - 1) * (1 - gz)
    turn = lax.rem(entry - (column + 3 - gz) + 2 * nz, nz)
    up = jnp.where(lane == nz - 1, 0.0, pltpu.roll(q, nz - 1, 1))
    down = jnp.where(lane == 0, 0.0, pltpu.roll(q, 1, 1))
    return up + down + jnp.where(lane == entry, pltpu.roll(half, turn, 1), 0.0)


def sweep(stage, spans, nx, ny, nz, gz, get, get_inv, put, slab_q, sums):
    margin = 2 - stage
    start = SUB - margin
    tiles = ny // SUB + (margin > 0)
    own = subs_of((SUB, nz)) >= margin
    parts = [[], []]
    for tile in range(tiles):
        row = start + SUB * tile
        q_rows = slab_q[SUB * tile : SUB * tile + SUB]
        acc = [jnp.zeros((SUB, nz), F32) for _ in range(2)]

        def beside(x):
            return get(x, row - 1) + get(x, row + 1)

        for first, last in spans:
            s_low, s_mid = beside(first - 1), beside(first)
            v_low, v_mid = get(first - 1, row), get(first, row)
            for x in range(first, last):
                v_high, s_high = get(x + 1, row), beside(x + 1)
                across = v_low + v_high
                column = (PACK * x) % (2 * nz)
                half = q_rows[:, column // nz * nz : column // nz * nz + nz]
                rest = s_mid + across
                total = along_z(v_mid + 0.5 * rest, half, column % nz, gz) + rest + 0.5 * (s_low + s_high)
                if stage < 2:
                    after = total * get_inv(x, row)
                    put(x, row, after)
                if 0 <= x < nx:
                    acc[0] = acc[0] + v_mid * total
                    if stage < 2:
                        acc[1] = acc[1] + after * total
                v_low, v_mid, s_low, s_mid = v_mid, v_high, s_mid, s_high
        for k in range(2):
            parts[k].append(acc[k])
    for k in range(2 if stage < 2 else 1):
        part = parts[k]
        total = part[1]
        for other in part[2 : ny // SUB]:
            total = total + other
        total = total + (jnp.where(own, part[0], part[-1]) if margin else part[0])
        sums[2 * stage + k] = total


def inner_kernel(n_y, w0_ref, inv_ref, slab_ref, *refs):
    y_refs, (a_ref, i_ref, b_ref, c_ref, sum_ref, own_slab_ref, slabs_ref) = refs[:n_y], refs[n_y:]
    nx, ny, nz = w0_ref.shape
    gz = lax.axis_index("gz")
    for x in range(nx + 1):
        halos = halo_rows([ref[x] for ref in y_refs])
        for k in range(2):
            if x < nx:
                ref, own = (a_ref, i_ref)[k].at[x], (w0_ref, inv_ref)[k][x]
            else:
                ref, own = own_slab_ref.at[k], slab_ref[k]
            ref[:SUB] = halos[k]
            ref[SUB : SUB + ny] = own
            ref[SUB + ny :] = halos[k]
    for k in range(2):
        slabs_ref[3 * k] = own_slab_ref[k]
    sums = {}
    for stage in range(3):
        source, target = (a_ref, b_ref, c_ref)[stage], (b_ref, c_ref, None)[stage]
        start, size = SUB - 2 + stage, ny if stage == 2 else ny + SUB
        v = slabs_ref[stage, start : start + size]
        s = slabs_ref[stage, start - 1 : start - 1 + size] + slabs_ref[stage, start + 1 : start + 1 + size]
        q, after = slab_step(v, s, slabs_ref[3, start : start + size] if stage < 2 else None)
        if stage < 2:
            slabs_ref[stage + 1, start : start + size] = after

        def put(x, row, value):
            target[x, row : row + SUB] = value

        sweep(
            stage, [(1 + stage, nx - 1 - stage)], nx, ny, nz, gz,
            lambda x, row: source[x, row : row + SUB], lambda x, row: i_ref[x, row : row + SUB],
            put, q, sums,
        )
    for k in range(5):
        sum_ref[k] = sums[k]


def outer_kernel(
    n_y, column_total, after_ref, a_ref, i_ref, b_ref, c_ref, slab_ref, sum_ref, stat_ref, *refs
):
    x_refs, corner_refs = refs[:2], refs[2 : 2 + 2 * n_y]
    ea_ref, eb_ref, ec_ref, slabs_ref, total_ref, where_ref, ei_ref, si_ref = refs[2 + 2 * n_y :]
    nx, ny, nz = a_ref.shape[0], a_ref.shape[1] - 2 * SUB, a_ref.shape[2]
    ring = ny + SUB
    gz = lax.axis_index("gz")
    odd = lax.rem(lax.axis_index("gx"), 2) == 1

    def beyond(upper, read):
        there = has_partner("gx", 0) if upper else has_partner("gx", 1)
        swapped = has_partner("gx", 1) if upper else has_partner("gx", 0)
        first, second = read(0), read(1)
        if upper:
            return jnp.where(jnp.where(odd, swapped, there), jnp.where(odd, second, first), 0.0)
        return jnp.where(jnp.where(odd, swapped, there), jnp.where(odd, first, second), 0.0)

    def write(ref, at, own, halo):
        ref[at, :SUB] = halo
        ref[at, SUB : SUB + ny] = own
        ref[at, SUB + ny :] = halo

    lane_tile, lane = lanes_of((SUB, nz)), lanes_of((ny, nz))
    slab_parts = []
    for side, upper in enumerate((False, True)):
        tiles = [
            halo_rows([beyond(upper, lambda step: corner_refs[step * n_y + j][k]) for j in range(n_y)])
            for k in range(4)
        ]
        for k in range(3):
            write(ea_ref, 3 * side + k, beyond(upper, lambda step: x_refs[step][k]), tiles[k][0])
        for k in range(2):
            own = beyond(upper, lambda step: x_refs[step][3 + k])
            write(ei_ref, 2 * side + k, own, tiles[k if upper else k + 1][1])
        own = beyond(upper, lambda step: x_refs[step][5])

        def near(value, lanes, planes):
            return jnp.where(lanes < planes * PACK if upper else lanes >= nz - planes * PACK, value, 0.0)

        slab_parts.append((
            near(own, lane, 3), near(tiles[3][0], lane_tile, 3),
            near(pltpu.roll(own, nz // 2, 1), lane, 2), near(tiles[3][1], lane_tile, 2),
            own[0:1, COUNT_LANE : COUNT_LANE + 1],
        ))

    low, high = slab_parts
    for ref, k in ((slabs_ref, 0), (si_ref, 1)):
        ref[0, :, :nz] = slab_ref[k]
        ref[0, SUB : SUB + ny, nz:] = low[2 * k] + high[2 * k]
        ref[0, :SUB, nz:] = low[2 * k + 1] + high[2 * k + 1]
        ref[0, SUB + ny :, nz:] = low[2 * k + 1] + high[2 * k + 1]

    def reader(inside_ref, edge_ref, first, count):
        def get(x, row):
            if first <= x < nx - first:
                return inside_ref[x, row : row + SUB]
            at = x - (first - count) if x < first else x - (nx - first) + count
            return edge_ref[at, row : row + SUB]

        return get

    sums = {}
    for stage in range(3):
        get = reader((a_ref, b_ref, c_ref)[stage], (ea_ref, eb_ref, ec_ref)[stage], stage, 3)
        start, size = SUB - 2 + stage, ny if stage == 2 else ring
        v = slabs_ref[stage, start : start + size]
        s = slabs_ref[stage, start - 1 : start - 1 + size] + slabs_ref[stage, start + 1 : start + 1 + size]
        q, after = slab_step(v, s, si_ref[0, start : start + size] if stage < 2 else None)
        if stage < 2:
            slabs_ref[stage + 1, start : start + size] = after

        def put(x, row, value):
            edge_ref = (eb_ref, ec_ref)[stage]
            at = x - (stage - 2) if x < nx // 2 else x - (nx - 1 - stage) + 3
            edge_ref[at, row : row + SUB] = value

        sweep(
            stage, [(stage - 2, stage + 1), (nx - 1 - stage, nx + 2 - stage)], nx, ny, nz, gz,
            get, reader(i_ref, ei_ref, 0, 2), put, q, sums,
        )

    total_ref[0:1] = stat_ref[0, 0:1]
    for k in range(5):
        total_ref[k + 1 : k + 2] = jnp.sum(sums[k] + sum_ref[k], axis=0, keepdims=True)
    total_ref[6:8] = jnp.zeros((2, nz), F32)
    gx, n_x = lax.axis_index("gx"), lax.axis_size("gx")
    count = jnp.sum(stat_ref[1, 0:1], axis=1, keepdims=True)
    below, above = [part[4] for part in slab_parts]
    begin = jnp.where(
        gx == 0, 0.0,
        jnp.where(gx == 1, below, jnp.where(gx == n_x - 1, column_total - count, column_total - count - above)),
    )
    where_ref[0:1] = jnp.broadcast_to(begin, (1, nz))
    where_ref[1:2] = jnp.broadcast_to(count, (1, nz))
    where_ref[2:8] = jnp.zeros((6, nz), F32)


def shift_left(v, amount, lane):
    rows = v.shape[0]
    if amount < LANES:
        turned = pltpu.roll(v, LANES - amount, 1)
        below = pltpu.roll(turned, rows - 1, 0)
        return jnp.where(lane < LANES - amount, turned, below)
    return jnp.concatenate([v[amount // LANES :], v[: amount // LANES]], axis=0)


def plan_kernel(after_ref, label_ref, plan_ref):
    rows = label_ref.shape[0]
    lane = lanes_of((rows, LANES))
    row = subs_of((rows, LANES))
    heart = label_ref[...] == 1
    ones = heart.astype(jnp.bfloat16)
    upper = (subs_of((LANES, LANES)) < lanes_of((LANES, LANES))).astype(jnp.bfloat16)
    in_row = jnp.dot(ones, upper, preferred_element_type=F32)
    totals = jnp.dot(ones, jnp.ones((LANES, LANES), jnp.bfloat16), preferred_element_type=F32)
    lower = (subs_of((rows, rows)) > lanes_of((rows, rows))).astype(jnp.bfloat16)
    before = jnp.dot(lower, totals.astype(jnp.bfloat16), preferred_element_type=F32)
    rank = (in_row + before).astype(jnp.int32)
    way = jnp.where(heart, row * LANES + lane - rank, 0)
    plan = jnp.zeros((rows, LANES), jnp.int32)
    step = 1
    while step < rows * LANES:
        moving = jnp.where((way & step) != 0, way, 0)
        arriving = shift_left(moving, step, lane)
        plan = plan | (arriving & step)
        way = (way - moving) | arriving
        step *= 2
    plan_ref[...] = plan


def galerkin(t):
    g00, g01, g02, g12, g22 = t[0] - t[1], t[1] - t[2], t[2] - t[3], t[3] - t[4], t[4] - t[5]
    g11 = g02
    l10, l20 = g01 / g00, g02 / g00
    d1 = g11 - l10 * g01
    m21 = g12 - l20 * g01
    ok1 = d1 > 1e-6 * g11
    d1 = jnp.where(ok1, d1, 1.0)
    l21 = jnp.where(ok1, m21 / d1, 0.0)
    d2 = g22 - l20 * g02 - l21 * m21
    ok2 = ok1 & (d2 > 1e-6 * g22)
    d2 = jnp.where(ok2, d2, 1.0)
    y1 = t[1] - l10 * t[0]
    y2 = t[2] - l20 * t[0] - l21 * y1
    c2 = jnp.where(ok2, y2 / d2, 0.0)
    c1 = jnp.where(ok1, y1 / d1 - l21 * c2, 0.0)
    c0 = t[0] / g00 - l10 * c1 - l20 * c2
    return c0, c1, c2


def couple_kernel(stage, slot_rows, after_ref, inside_ref, edge_ref, slabs_ref, plan_ref, list_ref, value_ref):
    nx, nz = inside_ref.shape[0], inside_ref.shape[2]
    ny = inside_ref.shape[1] - 2 * SUB
    rows = nx * ny
    gz = lax.axis_index("gz")

    def get(x, row):
        if stage <= x < nx - stage:
            return inside_ref[x, row : row + SUB]
        return edge_ref[x - (stage - 3) if x < stage else x - (nx - stage) + 3, row : row + SUB]

    for tile in range(ny // SUB):
        row = SUB + SUB * tile
        slab = slabs_ref[stage, row : row + SUB, :nz]
        v_low, v_mid = get(-1, row), get(0, row)
        for x in range(nx):
            v_high = get(x + 1, row)
            beside = get(x, row - 1) + get(x, row + 1)
            at = ny * x + SUB * tile
            value_ref[at : at + SUB] = (
                along_z(v_mid, slab, PACK * x, gz) + beside + (v_low + v_high) - 6.0 * v_mid
            )
            v_low, v_mid = v_mid, v_high
    lane = lanes_of((rows, LANES))
    value = value_ref[...]
    plan = plan_ref[...]
    step = 1
    while step < rows * LANES:
        value = jnp.where((plan & step) != 0, shift_left(value, step, lane), value)
        step *= 2
    list_ref[...] = value[:slot_rows]


def add_kernel(a_ref, b_ref, after_ref, out_ref):
    out_ref[...] = a_ref[...] + b_ref[...]


def place_kernel(where_ref, total_ref, *refs):
    list_refs, out_refs, buf_ref = refs[:3], refs[3:-1], refs[-1]
    slot_rows = list_refs[0].shape[0]
    size = (out_refs[0].shape[0] - SUB) // 3
    gx = lax.axis_index("gx")
    offset = jnp.max(where_ref[0:1]).astype(jnp.int32)
    count = jnp.max(where_ref[1:2]).astype(jnp.int32)
    shape = (slot_rows, LANES)
    listed = subs_of(shape) * LANES + lanes_of(shape) < count
    inner = lax.rem(offset, LANES)
    kept = lanes_of((slot_rows + SUB, LANES)) >= inner
    buf_ref[...] = jnp.zeros_like(buf_ref)
    for k, list_ref in enumerate(list_refs):
        slots = jnp.where(listed, list_ref[...], 0.0)
        slots = jnp.concatenate([slots, jnp.zeros((SUB, LANES), F32)], axis=0)
        turned = pltpu.roll(slots, inner, 1)
        buf_ref[k, pl.ds(offset // LANES, slot_rows + SUB), :] = jnp.where(kept, turned, pltpu.roll(turned, 1, 0))
    for block, out_ref in enumerate(out_refs):
        begin = pl.multiple_of((gx ^ block) * size, SUB)
        for k in range(3):
            out_ref[k * size : k * size + size] = buf_ref[k, pl.ds(begin, size), :]
        out_ref[3 * size :] = total_ref[...]


def membrane_kernel(
    half_ref, slope_ref, tau_ref, cond_ref, rev_ref, after_ref, v_ref, gates_ref, cot_ref,
    base_ref, sum_ref, factor_ref, coef_ref,
):
    n_states, rows = gates_ref.shape[:2]
    v = v_ref[...]

    def state(g, carry):
        total, current = carry
        inv_slope = 1.0 / slope_ref[g]
        tau_base = tau_ref[g]
        scaled = (v - half_ref[g]) * inv_slope
        gate = gates_ref[g]
        cot = cot_ref[g]
        steady = 1.0 / (1.0 + jnp.exp(-scaled))
        bell = jnp.exp(-scaled * scaled)
        rate = TIME_STEP / (tau_base * (0.5 + bell))
        decay = jnp.exp(-rate)
        steady_slope = steady * (1.0 - steady)
        decay_slope = decay * rate * rate * ((tau_base / TIME_STEP) * bell * (-2.0 * scaled))
        change = (steady_slope * (1.0 - decay) + (gate - steady) * decay_slope) * inv_slope
        base_ref[g] = cot * decay
        coef_ref[0, pl.ds(g, 1)] = jnp.full((1, LANES), TIME_STEP * cond_ref[g])
        coef_ref[1, pl.ds(g, 1)] = jnp.full((1, LANES), rev_ref[g])
        return total + cot * change, current + cond_ref[g] * gate

    zero = jnp.zeros((rows, LANES), F32)
    total, current = lax.fori_loop(0, n_states, state, (zero, zero), unroll=2)
    sum_ref[...] = total
    factor_ref[...] = 1.0 - TIME_STEP * current


def finish_kernel(
    n_blocks, coef_ref, vcot_ref, v_ref, sum_ref, factor_ref, base_ref, a_ref, b_ref, c_ref, eb_ref, ec_ref, *refs
):
    block_refs, (x_ref, volt_ref, gate_ref) = refs[:n_blocks], refs[n_blocks:]
    size = (block_refs[0].shape[0] - SUB) // 3
    total = block_refs[0][3 * size :]
    for ref in block_refs[1:]:
        total = total + ref[3 * size :]
    sums = jnp.sum(total, axis=1, keepdims=True)
    c0, c1, c2 = galerkin([jnp.broadcast_to(sums[k : k + 1], (1, LANES)) for k in range(6)])
    landed = jnp.zeros((size, LANES), F32)
    for k, c in enumerate((c0, c1, c2)):
        part = block_refs[0][k * size : k * size + size]
        for ref in block_refs[1:]:
            part = part + ref[k * size : k * size + size]
        landed = landed + c * part
    cot = vcot_ref[...] + landed
    v = v_ref[...]
    volt_ref[...] = cot * factor_ref[...] + sum_ref[...]
    for g in range(base_ref.shape[0]):
        gate_ref[g] = base_ref[g] - (coef_ref[0, g : g + 1] * cot) * (v - coef_ref[1, g : g + 1])
    nx, ny, nz = x_ref.shape
    own = slice(SUB, SUB + ny)
    for x in range(nx):
        w1 = b_ref[x, own] if 1 <= x < nx - 1 else eb_ref[2 if x == 0 else 3, own]
        w2 = c_ref[x, own] if 2 <= x < nx - 2 else ec_ref[x + 1 if x < 2 else x - (nx - 2) + 3, own]
        x_ref[x] = c0 * a_ref[x, own] + c1 * w1 + c2 * w2


def partners(axis, step):
    count = lax.axis_size(axis)
    if step == 0:
        return [i ^ 1 for i in range(count)]
    return [0] + [i + 1 if i % 2 else i - 1 for i in range(1, count - 1)] + [count - 1]


def swap(value, x_to=None, y_to=None):
    n_x, n_y, n_z = [lax.axis_size(axis) for axis in ("gx", "gy", "gz")]
    pairs = []
    for x in range(n_x):
        for y in range(n_y):
            to_x, to_y = x_to[x] if x_to else x, y_to[y] if y_to else y
            alone = (x_to and to_x == x) or (y_to and to_y == y)
            for z in range(n_z):
                to = (x, y, z ^ 1) if alone else (to_x, to_y, z)
                pairs.append(((x * n_y + y) * n_z + z, (to[0] * n_y + to[1]) * n_z + to[2]))
    return lax.ppermute(value, ("gx", "gy", "gz"), pairs)


def local(
    potential_cot, damping, tissue_label, heart_index, voltage, gates, voltage_cot, gates_cot,
    half_voltage, gate_slope, tau_base, conductance, reversal,
):
    nx, ny, nz = potential_cot.shape
    rows = nx * ny
    ring = ny + SUB
    n_gx, n_gy = lax.axis_size("gx"), lax.axis_size("gy")
    n_states = gates.shape[0]
    block_rows = voltage.shape[1] // LANES
    slot_rows = heart_index.shape[3] // LANES
    block = shape_of(nx, ny, nz)
    flat = lambda a: a.reshape(rows, LANES)
    cells = lambda a: a.reshape(block_rows, LANES)
    states = lambda a: a.reshape(n_states, block_rows, LANES)

    w0, inv, packed, stat = call(
        start_kernel, (block, block, shape_of(2, ny, nz), shape_of(2, SUB, nz)), 3,
        specs=[HBM] * 3,
        scratch=[
            pltpu.VMEM((nx, ny, nz), F32), pltpu.VMEM((nx, ny, nz), F32), pltpu.VMEM((nx, ny, nz), jnp.int32),
            pltpu.SemaphoreType.DMA((3, 2)),
        ],
    )(in_hbm(potential_cot), in_hbm(damping), in_hbm(tissue_label))

    got = lax.ppermute(packed, "gz", [(0, 1), (1, 0)])
    plan = call(plan_kernel, jax.ShapeDtypeStruct((rows, LANES), jnp.int32), 2, cost=6_000_000)(
        stat, flat(tissue_label)
    )

    n_y = steps_of("gy")
    shapes = (
        (shape_of(2, ny, nz),) + (shape_of(nx + 1, SUB, nz),) * n_y + (shape_of(6, ny, nz),) * 2
        + (shape_of(4, SUB, nz),) * (2 * n_y)
    )
    slab, *faces = call(functools.partial(faces_kernel, n_y), shapes, 5)(w0, inv, packed, got, stat)
    along_y, along_x, across = faces[:n_y], faces[n_y : n_y + 2], faces[n_y + 2 :]
    y_to = [partners("gy", step) for step in range(n_y)]
    x_to = [partners("gx", step) for step in range(2)]
    along_y = [swap(face, y_to=y_to[j]) for j, face in enumerate(along_y)]
    along_x = [swap(face, x_to=x_to[i]) for i, face in enumerate(along_x)]
    across = [swap(face, x_to=x_to[k // n_y], y_to=y_to[k % n_y]) for k, face in enumerate(across)]

    tall = ring + SUB
    planes = shape_of(nx, tall, nz)
    edges = shape_of(6, tall, nz)
    in0, in_inv, in1, in2, in_sums, own_slab = call(
        functools.partial(inner_kernel, n_y),
        (planes,) * 4 + (shape_of(5, SUB, nz), shape_of(2, tall, nz)),
        3 + n_y,
        scratch=[pltpu.VMEM((4, tall, nz), F32)],
        cost=6_000_000,
    )(w0, inv, slab, *along_y)
    ends0, ends1, ends2, slabs, sums, where = call(
        functools.partial(outer_kernel, n_y, float(n_gx * voltage.shape[1])),
        (edges,) * 3 + (shape_of(3, tall, 2 * nz), shape_of(SUB, nz), shape_of(SUB, nz)),
        10 + 2 * n_y,
        scratch=[pltpu.VMEM((4, tall, nz), F32), pltpu.VMEM((1, tall, 2 * nz), F32)],
    )(plan, in0, in_inv, in1, in2, own_slab, in_sums, stat, *along_x, *across)

    def couple(stage, after, inside, ends):
        return call(
            functools.partial(couple_kernel, stage, slot_rows),
            shape_of(slot_rows, LANES),
            5,
            scratch=[pltpu.VMEM((rows, LANES), F32)],
            cost=6_000_000,
        )(after, inside, ends, slabs, plan)

    def add(value, axis, step, after):
        got = lax.ppermute(value, axis, [(i, i ^ step) for i in range(lax.axis_size(axis))])
        return call(add_kernel, shape_of(SUB, nz), 3)(value, got, after)

    list0 = couple(0, sums, in0, ends0)
    sums = add(sums, "gz", 1, list0)
    list1 = couple(1, sums, in1, ends1)
    list2 = couple(2, list1, in2, ends2)
    for step in [2**k for k in range(n_gy.bit_length() - 1)]:
        sums = add(sums, "gy", step, list2)
    if n_gx > 4:
        counts = lax.all_gather(jnp.sum(stat[1, 0]), "gx")
        begin = jnp.sum(jnp.where(jnp.arange(n_gx) < lax.axis_index("gx"), counts, 0.0))
        where = where.at[0].set(begin)
    blocks = call(
        place_kernel,
        (shape_of(3 * block_rows + SUB, LANES),) * n_gx,
        5,
        scratch=[pltpu.VMEM((3, n_gx * block_rows + slot_rows + SUB, LANES), F32)],
    )(where, sums, list0, list1, list2)
    got = [
        lax.ppermute(blocks[k], "gx", [(i, i ^ k) for i in range(n_gx)]) for k in [2, 1] + list(range(3, n_gx))
    ]

    base, total_change, factor, state_coefs = call(
        membrane_kernel,
        (
            shape_of(n_states, block_rows, LANES), shape_of(block_rows, LANES), shape_of(block_rows, LANES),
            shape_of(2, n_states, LANES),
        ),
        9,
        specs=[SMEM] * 5 + [VMEM] * 4,
        cost=6_000_000,
    )(
        half_voltage, gate_slope, tau_base, conductance, reversal,
        blocks[0], cells(voltage), states(gates), states(gates_cot),
    )
    solution, volt_grad, gate_grad = call(
        functools.partial(finish_kernel, n_gx),
        (block, shape_of(block_rows, LANES), shape_of(n_states, block_rows, LANES)),
        11 + n_gx,
    )(
        state_coefs, cells(voltage_cot), cells(voltage), total_change, factor, base,
        in0, in1, in2, ends1, ends2, blocks[0], *got,
    )
    return solution, volt_grad.reshape(voltage.shape), gate_grad.reshape(gates.shape)


def solution(mesh):
    grid = P(("groups", "gx"), "gy", "gz")
    cells = P(("groups", "gy", "gz"), "gx")
    states = P(None, ("groups", "gy", "gz"), "gx")
    in_specs = (
        grid, grid, grid, P(("groups", "gx"), "gy", "gz", None), cells, states, cells, states,
        P(), P(), P(), P(), P(),
    )
    return jax.shard_map(
        local, mesh=mesh, in_specs=in_specs, out_specs=(grid, cells, states), check_vma=False
    )
```

```python
import functools

import jax
import jax.numpy as jnp
from jax import lax
from jax.experimental import pallas as pl
from jax.experimental.pallas import tpu as pltpu
from jax.sharding import PartitionSpec as P

TIME_STEP = 0.5
LANES = 128
SUB = 8
PACK = 8
COUNT_LANE = 4 * PACK
F32 = jnp.float32

VMEM = pl.BlockSpec(memory_space=pltpu.VMEM)
SMEM = pl.BlockSpec(memory_space=pltpu.SMEM)
HBM = pl.BlockSpec(memory_space=pltpu.HBM)


def shape_of(*dims):
    return jax.ShapeDtypeStruct(dims, F32)


def call(kernel, out_shape, n_in, specs=None, outs=None, scratch=(), cost=2_000_000, limit=32):
    return pl.pallas_call(
        kernel,
        out_shape=out_shape,
        in_specs=specs if specs is not None else [VMEM] * n_in,
        out_specs=outs if outs is not None else jax.tree.map(lambda _: VMEM, out_shape),
        scratch_shapes=list(scratch),
        compiler_params=pltpu.CompilerParams(vmem_limit_bytes=limit * 1024 * 1024),
        cost_estimate=pl.CostEstimate(flops=cost, bytes_accessed=cost, transcendentals=0),
    )


def in_hbm(array):
    return pltpu.with_memory_space_constraint(array, pltpu.HBM)


def lanes_of(shape):
    return lax.broadcasted_iota(jnp.int32, shape, len(shape) - 1)


def subs_of(shape):
    return lax.broadcasted_iota(jnp.int32, shape, len(shape) - 2)


def start_kernel(
    right_hbm, damping_hbm, label_hbm, w0_ref, inv_ref, pack_ref, stat_ref, right_ref, damping_ref, label_ref, sems
):
    nx, ny, nz = right_ref.shape
    parts = sems.shape[1]
    size = nx // parts
    copies = []
    for part in range(parts):
        here = pl.ds(part * size, size)
        for k, (source, target) in enumerate(
            ((right_hbm, right_ref), (damping_hbm, damping_ref), (label_hbm, label_ref))
        ):
            copies.append(pltpu.make_async_copy(source.at[here], target.at[here], sems.at[k, part]))
            copies[-1].start()
    gz = lax.axis_index("gz")
    lane = lanes_of((ny, nz))
    packed_w = jnp.zeros((ny, nz), F32)
    packed_i = jnp.zeros((ny, nz), F32)
    energy = jnp.zeros((ny, nz), F32)
    cells = jnp.zeros((ny, nz), F32)
    for x in range(nx):
        if x % size == 0:
            for k in range(3):
                copies[3 * (x // size) + k].wait()
        label = label_ref[x].astype(F32)
        right = right_ref[x]
        inv = 1.0 / (12.0 + damping_ref[x] * (1.0 + 3.0 * label))
        w0 = right * inv
        w0_ref[x] = w0
        inv_ref[x] = inv
        energy = energy + right * w0
        cells = cells + label
        turn = (PACK * x + 3) % nz
        begin = PACK * x + 3 * gz
        chosen = (lane >= begin) & (lane < begin + 3)
        packed_w = jnp.where(chosen, pltpu.roll(w0, turn, 1), packed_w)
        packed_i = jnp.where(chosen, pltpu.roll(inv, turn, 1), packed_i)
    pack_ref[0] = packed_w
    pack_ref[1] = packed_i
    stat_ref[0] = jnp.broadcast_to(jnp.sum(energy, axis=0, keepdims=True), (SUB, nz))
    stat_ref[1] = jnp.broadcast_to(jnp.sum(cells, axis=0, keepdims=True), (SUB, nz))


def steps_of(axis):
    return 1 if lax.axis_size(axis) == 2 else 2


def upper_in(axis, step):
    return lax.rem(lax.axis_index(axis), 2) == step


def has_partner(axis, step):
    here = lax.axis_index(axis)
    return jnp.where(upper_in(axis, step), here < lax.axis_size(axis) - 1, here > 0)


def unpack_rows(tile, step):
    sub = subs_of(tile.shape)
    up, there = upper_in("gy", step), has_partner("gy", step)
    depth = jnp.where(there, jnp.where(up, SUB - 1 - sub, sub), -1)
    return jnp.where(depth >= 5, tile, 0.0), jnp.where(depth >= 6, pltpu.roll(tile, 4, 0), 0.0)


def halo_rows(tiles):
    w_tile, i_tile = unpack_rows(tiles[0], 0)
    for step, tile in enumerate(tiles[1:], 1):
        w_more, i_more = unpack_rows(tile, step)
        w_tile, i_tile = w_tile + w_more, i_tile + i_more
    return w_tile, i_tile


def faces_kernel(n_y, w0_ref, inv_ref, own_ref, got_ref, stat_ref, slab_ref, *refs):
    y_refs, x_refs, edge_refs = refs[:n_y], refs[n_y : n_y + 2], refs[n_y + 2 :]
    nx, ny, nz = w0_ref.shape
    sub = subs_of((SUB, nz))
    lane = lanes_of((ny, nz))
    slab_ref[...] = own_ref[...] + got_ref[...]
    for step, face_ref in enumerate(y_refs):
        up = upper_in("gy", step)
        keep_w = jnp.where(up, sub, SUB - 1 - sub) >= 5
        for x in range(nx + 1):
            w_rows, i_rows = (w0_ref.at[x], inv_ref.at[x]) if x < nx else (slab_ref.at[0], slab_ref.at[1])
            w_face = jnp.where(up, w_rows[ny - SUB :], w_rows[:SUB])
            i_face = jnp.where(up, i_rows[ny - SUB :], i_rows[:SUB])
            face_ref[x] = jnp.where(keep_w, w_face, pltpu.roll(i_face, 4, 0))
    cells = jnp.sum(stat_ref[1, 0:1], axis=1, keepdims=True)
    slab_w = slab_ref[0]
    half = pltpu.roll(slab_ref[1], nz // 2, 1)
    up_slab = jnp.where(lane >= nz - 3 * PACK, slab_w, half)
    down_slab = jnp.where(lane < 3 * PACK, slab_w, half)
    for step, face_ref in enumerate(x_refs):
        up = upper_in("gx", step)
        first = jnp.where(up, nx - 3, 0)
        for k in range(3):
            face_ref[k] = w0_ref[first + k]
        for k in range(2):
            face_ref[3 + k] = inv_ref[jnp.where(up, nx - 2, 0) + k]
        face_ref[5] = jnp.where(lane == COUNT_LANE, cells, jnp.where(up, up_slab, down_slab))
        for y_step, y_ref in enumerate(y_refs):
            edge_ref = edge_refs[step * n_y + y_step]
            for k in range(3):
                edge_ref[k] = y_ref[first + k]
            edge_ref[3] = y_ref[nx]


def slab_step(v, s, inv):
    width = v.shape[1]
    across = pltpu.roll(v, PACK, 1) + pltpu.roll(v, width - PACK, 1)
    q = v + 0.5 * (s + across)
    if inv is None:
        return q, None
    total = (
        pltpu.roll(q, 1, 1) + pltpu.roll(q, width - 1, 1) + s + across
        + 0.5 * (pltpu.roll(s, PACK, 1) + pltpu.roll(s, width - PACK, 1))
    )
    return q, total * inv


def along_z(q, half, column, gz):
    nz = q.shape[1]
    lane = lanes_of(q.shape)
    entry = (nz - 1) * (1 - gz)
    turn = lax.rem(entry - (column + 3 - gz) + 2 * nz, nz)
    up = jnp.where(lane == nz - 1, 0.0, pltpu.roll(q, nz - 1, 1))
    down = jnp.where(lane == 0, 0.0, pltpu.roll(q, 1, 1))
    return up + down + jnp.where(lane == entry, pltpu.roll(half, turn, 1), 0.0)


def sweep(stage, spans, nx, ny, nz, gz, get, get_inv, put, slab_q, sums):
    margin = 2 - stage
    start = SUB - margin
    tiles = ny // SUB + (margin > 0)
    own = subs_of((SUB, nz)) >= margin
    parts = [[], []]
    for tile in range(tiles):
        row = start + SUB * tile
        q_rows = slab_q[SUB * tile : SUB * tile + SUB]
        acc = [jnp.zeros((SUB, nz), F32) for _ in range(2)]

        def beside(x):
            return get(x, row - 1) + get(x, row + 1)

        for first, last in spans:
            s_low, s_mid = beside(first - 1), beside(first)
            v_low, v_mid = get(first - 1, row), get(first, row)
            for x in range(first, last):
                v_high, s_high = get(x + 1, row), beside(x + 1)
                across = v_low + v_high
                column = (PACK * x) % (2 * nz)
                half = q_rows[:, column // nz * nz : column // nz * nz + nz]
                rest = s_mid + across
                total = along_z(v_mid + 0.5 * rest, half, column % nz, gz) + rest + 0.5 * (s_low + s_high)
                if stage < 2:
                    after = total * get_inv(x, row)
                    put(x, row, after)
                if 0 <= x < nx:
                    acc[0] = acc[0] + v_mid * total
                    if stage < 2:
                        acc[1] = acc[1] + after * total
                v_low, v_mid, s_low, s_mid = v_mid, v_high, s_mid, s_high
        for k in range(2):
            parts[k].append(acc[k])
    for k in range(2 if stage < 2 else 1):
        part = parts[k]
        total = part[1]
        for other in part[2 : ny // SUB]:
            total = total + other
        total = total + (jnp.where(own, part[0], part[-1]) if margin else part[0])
        sums[2 * stage + k] = total


def inner_kernel(n_y, w0_ref, inv_ref, slab_ref, *refs):
    y_refs, (a_ref, i_ref, b_ref, c_ref, sum_ref, own_slab_ref, slabs_ref) = refs[:n_y], refs[n_y:]
    nx, ny, nz = w0_ref.shape
    gz = lax.axis_index("gz")
    for x in range(nx + 1):
        halos = halo_rows([ref[x] for ref in y_refs])
        for k in range(2):
            if x < nx:
                ref, own = (a_ref, i_ref)[k].at[x], (w0_ref, inv_ref)[k][x]
            else:
                ref, own = own_slab_ref.at[k], slab_ref[k]
            ref[:SUB] = halos[k]
            ref[SUB : SUB + ny] = own
            ref[SUB + ny :] = halos[k]
    for k in range(2):
        slabs_ref[3 * k] = own_slab_ref[k]
    sums = {}
    for stage in range(3):
        source, target = (a_ref, b_ref, c_ref)[stage], (b_ref, c_ref, None)[stage]
        start, size = SUB - 2 + stage, ny if stage == 2 else ny + SUB
        v = slabs_ref[stage, start : start + size]
        s = slabs_ref[stage, start - 1 : start - 1 + size] + slabs_ref[stage, start + 1 : start + 1 + size]
        q, after = slab_step(v, s, slabs_ref[3, start : start + size] if stage < 2 else None)
        if stage < 2:
            slabs_ref[stage + 1, start : start + size] = after

        def put(x, row, value):
            target[x, row : row + SUB] = value

        sweep(
            stage, [(1 + stage, nx - 1 - stage)], nx, ny, nz, gz,
            lambda x, row: source[x, row : row + SUB], lambda x, row: i_ref[x, row : row + SUB],
            put, q, sums,
        )
    for k in range(5):
        sum_ref[k] = sums[k]


def outer_kernel(
    n_y, column_total, after_ref, a_ref, i_ref, b_ref, c_ref, slab_ref, sum_ref, stat_ref, *refs
):
    x_refs, corner_refs = refs[:2], refs[2 : 2 + 2 * n_y]
    ea_ref, eb_ref, ec_ref, slabs_ref, total_ref, where_ref, ei_ref, si_ref = refs[2 + 2 * n_y :]
    nx, ny, nz = a_ref.shape[0], a_ref.shape[1] - 2 * SUB, a_ref.shape[2]
    ring = ny + SUB
    gz = lax.axis_index("gz")
    odd = lax.rem(lax.axis_index("gx"), 2) == 1

    def beyond(upper, read):
        there = has_partner("gx", 0) if upper else has_partner("gx", 1)
        swapped = has_partner("gx", 1) if upper else has_partner("gx", 0)
        first, second = read(0), read(1)
        if upper:
            return jnp.where(jnp.where(odd, swapped, there), jnp.where(odd, second, first), 0.0)
        return jnp.where(jnp.where(odd, swapped, there), jnp.where(odd, first, second), 0.0)

    def write(ref, at, own, halo):
        ref[at, :SUB] = halo
        ref[at, SUB : SUB + ny] = own
        ref[at, SUB + ny :] = halo

    lane_tile, lane = lanes_of((SUB, nz)), lanes_of((ny, nz))
    slab_parts = []
    for side, upper in enumerate((False, True)):
        tiles = [
            halo_rows([beyond(upper, lambda step: corner_refs[step * n_y + j][k]) for j in range(n_y)])
            for k in range(4)
        ]
        for k in range(3):
            write(ea_ref, 3 * side + k, beyond(upper, lambda step: x_refs[step][k]), tiles[k][0])
        for k in range(2):
            own = beyond(upper, lambda step: x_refs[step][3 + k])
            write(ei_ref, 2 * side + k, own, tiles[k if upper else k + 1][1])
        own = beyond(upper, lambda step: x_refs[step][5])

        def near(value, lanes, planes):
            return jnp.where(lanes < planes * PACK if upper else lanes >= nz - planes * PACK, value, 0.0)

        slab_parts.append((
            near(own, lane, 3), near(tiles[3][0], lane_tile, 3),
            near(pltpu.roll(own, nz // 2, 1), lane, 2), near(tiles[3][1], lane_tile, 2),
            own[0:1, COUNT_LANE : COUNT_LANE + 1],
        ))

    low, high = slab_parts
    for ref, k in ((slabs_ref, 0), (si_ref, 1)):
        ref[0, :, :nz] = slab_ref[k]
        ref[0, SUB : SUB + ny, nz:] = low[2 * k] + high[2 * k]
        ref[0, :SUB, nz:] = low[2 * k + 1] + high[2 * k + 1]
        ref[0, SUB + ny :, nz:] = low[2 * k + 1] + high[2 * k + 1]

    def reader(inside_ref, edge_ref, first, count):
        def get(x, row):
            if first <= x < nx - first:
                return inside_ref[x, row : row + SUB]
            at = x - (first - count) if x < first else x - (nx - first) + count
            return edge_ref[at, row : row + SUB]

        return get

    sums = {}
    for stage in range(3):
        get = reader((a_ref, b_ref, c_ref)[stage], (ea_ref, eb_ref, ec_ref)[stage], stage, 3)
        start, size = SUB - 2 + stage, ny if stage == 2 else ring
        v = slabs_ref[stage, start : start + size]
        s = slabs_ref[stage, start - 1 : start - 1 + size] + slabs_ref[stage, start + 1 : start + 1 + size]
        q, after = slab_step(v, s, si_ref[0, start : start + size] if stage < 2 else None)
        if stage < 2:
            slabs_ref[stage + 1, start : start + size] = after

        def put(x, row, value):
            edge_ref = (eb_ref, ec_ref)[stage]
            at = x - (stage - 2) if x < nx // 2 else x - (nx - 1 - stage) + 3
            edge_ref[at, row : row + SUB] = value

        sweep(
            stage, [(stage - 2, stage + 1), (nx - 1 - stage, nx + 2 - stage)], nx, ny, nz, gz,
            get, reader(i_ref, ei_ref, 0, 2), put, q, sums,
        )

    total_ref[0:1] = stat_ref[0, 0:1]
    for k in range(5):
        total_ref[k + 1 : k + 2] = jnp.sum(sums[k] + sum_ref[k], axis=0, keepdims=True)
    total_ref[6:8] = jnp.zeros((2, nz), F32)
    gx, n_x = lax.axis_index("gx"), lax.axis_size("gx")
    count = jnp.sum(stat_ref[1, 0:1], axis=1, keepdims=True)
    below, above = [part[4] for part in slab_parts]
    begin = jnp.where(
        gx == 0, 0.0,
        jnp.where(gx == 1, below, jnp.where(gx == n_x - 1, column_total - count, column_total - count - above)),
    )
    where_ref[0:1] = jnp.broadcast_to(begin, (1, nz))
    where_ref[1:2] = jnp.broadcast_to(count, (1, nz))
    where_ref[2:8] = jnp.zeros((6, nz), F32)


def shift_left(v, amount, lane):
    rows = v.shape[0]
    if amount < LANES:
        turned = pltpu.roll(v, LANES - amount, 1)
        below = pltpu.roll(turned, rows - 1, 0)
        return jnp.where(lane < LANES - amount, turned, below)
    return jnp.concatenate([v[amount // LANES :], v[: amount // LANES]], axis=0)


def plan_kernel(after_ref, label_ref, plan_ref):
    rows = label_ref.shape[0]
    lane = lanes_of((rows, LANES))
    row = subs_of((rows, LANES))
    heart = label_ref[...] == 1
    ones = heart.astype(jnp.bfloat16)
    upper = (subs_of((LANES, LANES)) < lanes_of((LANES, LANES))).astype(jnp.bfloat16)
    in_row = jnp.dot(ones, upper, preferred_element_type=F32)
    totals = jnp.dot(ones, jnp.ones((LANES, LANES), jnp.bfloat16), preferred_element_type=F32)
    lower = (subs_of((rows, rows)) > lanes_of((rows, rows))).astype(jnp.bfloat16)
    before = jnp.dot(lower, totals.astype(jnp.bfloat16), preferred_element_type=F32)
    rank = (in_row + before).astype(jnp.int32)
    way = jnp.where(heart, row * LANES + lane - rank, 0)
    plan = jnp.zeros((rows, LANES), jnp.int32)
    step = 1
    while step < rows * LANES:
        moving = jnp.where((way & step) != 0, way, 0)
        arriving = shift_left(moving, step, lane)
        plan = plan | (arriving & step)
        way = (way - moving) | arriving
        step *= 2
    plan_ref[...] = plan


def galerkin(t):
    g00, g01, g02, g12, g22 = t[0] - t[1], t[1] - t[2], t[2] - t[3], t[3] - t[4], t[4] - t[5]
    g11 = g02
    l10, l20 = g01 / g00, g02 / g00
    d1 = g11 - l10 * g01
    m21 = g12 - l20 * g01
    ok1 = d1 > 1e-6 * g11
    d1 = jnp.where(ok1, d1, 1.0)
    l21 = jnp.where(ok1, m21 / d1, 0.0)
    d2 = g22 - l20 * g02 - l21 * m21
    ok2 = ok1 & (d2 > 1e-6 * g22)
    d2 = jnp.where(ok2, d2, 1.0)
    y1 = t[1] - l10 * t[0]
    y2 = t[2] - l20 * t[0] - l21 * y1
    c2 = jnp.where(ok2, y2 / d2, 0.0)
    c1 = jnp.where(ok1, y1 / d1 - l21 * c2, 0.0)
    c0 = t[0] / g00 - l10 * c1 - l20 * c2
    return c0, c1, c2


def couple_kernel(stage, slot_rows, after_ref, inside_ref, edge_ref, slabs_ref, plan_ref, list_ref, value_ref):
    nx, nz = inside_ref.shape[0], inside_ref.shape[2]
    ny = inside_ref.shape[1] - 2 * SUB
    rows = nx * ny
    gz = lax.axis_index("gz")

    def get(x, row):
        if stage <= x < nx - stage:
            return inside_ref[x, row : row + SUB]
        return edge_ref[x - (stage - 3) if x < stage else x - (nx - stage) + 3, row : row + SUB]

    for tile in range(ny // SUB):
        row = SUB + SUB * tile
        slab = slabs_ref[stage, row : row + SUB, :nz]
        v_low, v_mid = get(-1, row), get(0, row)
        for x in range(nx):
            v_high = get(x + 1, row)
            beside = get(x, row - 1) + get(x, row + 1)
            at = ny * x + SUB * tile
            value_ref[at : at + SUB] = (
                along_z(v_mid, slab, PACK * x, gz) + beside + (v_low + v_high) - 6.0 * v_mid
            )
            v_low, v_mid = v_mid, v_high
    lane = lanes_of((rows, LANES))
    value = value_ref[...]
    plan = plan_ref[...]
    step = 1
    while step < rows * LANES:
        value = jnp.where((plan & step) != 0, shift_left(value, step, lane), value)
        step *= 2
    list_ref[...] = value[:slot_rows]


def add_kernel(a_ref, b_ref, after_ref, out_ref):
    out_ref[...] = a_ref[...] + b_ref[...]


def place_kernel(where_ref, total_ref, *refs):
    list_refs, out_refs, buf_ref = refs[:3], refs[3:-1], refs[-1]
    slot_rows = list_refs[0].shape[0]
    size = (out_refs[0].shape[0] - SUB) // 3
    gx = lax.axis_index("gx")
    offset = jnp.max(where_ref[0:1]).astype(jnp.int32)
    count = jnp.max(where_ref[1:2]).astype(jnp.int32)
    shape = (slot_rows, LANES)
    listed = subs_of(shape) * LANES + lanes_of(shape) < count
    inner = lax.rem(offset, LANES)
    kept = lanes_of((slot_rows + SUB, LANES)) >= inner
    buf_ref[...] = jnp.zeros_like(buf_ref)
    for k, list_ref in enumerate(list_refs):
        slots = jnp.where(listed, list_ref[...], 0.0)
        slots = jnp.concatenate([slots, jnp.zeros((SUB, LANES), F32)], axis=0)
        turned = pltpu.roll(slots, inner, 1)
        buf_ref[k, pl.ds(offset // LANES, slot_rows + SUB), :] = jnp.where(kept, turned, pltpu.roll(turned, 1, 0))
    for block, out_ref in enumerate(out_refs):
        begin = pl.multiple_of((gx ^ block) * size, SUB)
        for k in range(3):
            out_ref[k * size : k * size + size] = buf_ref[k, pl.ds(begin, size), :]
        out_ref[3 * size :] = total_ref[...]


def membrane_kernel(
    half_ref, slope_ref, tau_ref, cond_ref, rev_ref, after_ref, v_ref, gates_ref, cot_ref,
    base_ref, sum_ref, factor_ref, coef_ref,
):
    n_states, rows = gates_ref.shape[:2]
    v = v_ref[...]

    def state(g, carry):
        total, current = carry
        inv_slope = 1.0 / slope_ref[g]
        tau_base = tau_ref[g]
        scaled = (v - half_ref[g]) * inv_slope
        gate = gates_ref[g]
        cot = cot_ref[g]
        steady = 1.0 / (1.0 + jnp.exp(-scaled))
        bell = jnp.exp(-scaled * scaled)
        rate = TIME_STEP / (tau_base * (0.5 + bell))
        decay = jnp.exp(-rate)
        steady_slope = steady * (1.0 - steady)
        decay_slope = decay * rate * rate * ((tau_base / TIME_STEP) * bell * (-2.0 * scaled))
        change = (steady_slope * (1.0 - decay) + (gate - steady) * decay_slope) * inv_slope
        base_ref[g] = cot * decay
        coef_ref[0, pl.ds(g, 1)] = jnp.full((1, LANES), TIME_STEP * cond_ref[g])
        coef_ref[1, pl.ds(g, 1)] = jnp.full((1, LANES), rev_ref[g])
        return total + cot * change, current + cond_ref[g] * gate

    zero = jnp.zeros((rows, LANES), F32)
    total, current = lax.fori_loop(0, n_states, state, (zero, zero), unroll=2)
    sum_ref[...] = total
    factor_ref[...] = 1.0 - TIME_STEP * current


def finish_kernel(
    alone, coef_ref, vcot_ref, v_ref, sum_ref, factor_ref, base_ref, a_ref, b_ref, c_ref, eb_ref, ec_ref, *refs
):
    n_small, n_large = len(alone[0]), len(alone[1])
    own_ref, small_refs, large_refs = refs[0], refs[1 : 1 + n_small], refs[1 + n_small : 1 + n_small + n_large]
    x_ref, volt_ref, gate_ref = refs[1 + n_small + n_large :]
    size = (own_ref.shape[0] - SUB) // 3
    gx = lax.axis_index("gx")

    def is_one(flags):
        found = gx < 0
        for place, flag in enumerate(flags):
            if flag:
                found = found | (gx == place)
        return found

    total = own_ref[3 * size :]
    for flags, ref in zip(alone[0], small_refs):
        total = total + jnp.where(is_one(flags), ref[...], 0.0)
    for flags, ref in zip(alone[1], large_refs):
        total = total + jnp.where(is_one(flags), 0.0, ref[3 * size :])
    sums = jnp.sum(total, axis=1, keepdims=True)
    c0, c1, c2 = galerkin([jnp.broadcast_to(sums[k : k + 1], (1, LANES)) for k in range(6)])
    landed = jnp.zeros((size, LANES), F32)
    for k, c in enumerate((c0, c1, c2)):
        part = own_ref[k * size : k * size + size]
        for ref in large_refs:
            part = part + ref[k * size : k * size + size]
        landed = landed + c * part
    cot = vcot_ref[...] + landed
    v = v_ref[...]
    volt_ref[...] = cot * factor_ref[...] + sum_ref[...]
    for g in range(base_ref.shape[0]):
        gate_ref[g] = base_ref[g] - (coef_ref[0, g : g + 1] * cot) * (v - coef_ref[1, g : g + 1])
    nx, ny, nz = x_ref.shape
    own = slice(SUB, SUB + ny)
    for x in range(nx):
        w1 = b_ref[x, own] if 1 <= x < nx - 1 else eb_ref[2 if x == 0 else 3, own]
        w2 = c_ref[x, own] if 2 <= x < nx - 2 else ec_ref[x + 1 if x < 2 else x - (nx - 2) + 3, own]
        x_ref[x] = c0 * a_ref[x, own] + c1 * w1 + c2 * w2


def partners(axis, step):
    count = lax.axis_size(axis)
    if step == 0:
        return [i ^ 1 for i in range(count)]
    return [0] + [i + 1 if i % 2 else i - 1 for i in range(1, count - 1)] + [count - 1]


def swap(value, x_to=None, y_to=None):
    n_x, n_y, n_z = [lax.axis_size(axis) for axis in ("gx", "gy", "gz")]
    pairs = []
    for x in range(n_x):
        for y in range(n_y):
            to_x, to_y = x_to[x] if x_to else x, y_to[y] if y_to else y
            alone = (x_to and to_x == x) or (y_to and to_y == y)
            for z in range(n_z):
                to = (x, y, z ^ 1) if alone else (to_x, to_y, z)
                pairs.append(((x * n_y + y) * n_z + z, (to[0] * n_y + to[1]) * n_z + to[2]))
    return lax.ppermute(value, ("gx", "gy", "gz"), pairs)


def never_meet(count, k, slots, block):
    def apart(tile, owner):
        return owner * block >= (tile + 1) * slots or (owner + 1) * block <= count * block - (count - tile) * slots

    return [apart(i, i ^ k) and apart(i ^ k, i) for i in range(count)]


def local(
    potential_cot, damping, tissue_label, heart_index, voltage, gates, voltage_cot, gates_cot,
    half_voltage, gate_slope, tau_base, conductance, reversal,
):
    nx, ny, nz = potential_cot.shape
    rows = nx * ny
    ring = ny + SUB
    n_gx, n_gy = lax.axis_size("gx"), lax.axis_size("gy")
    n_states = gates.shape[0]
    block_rows = voltage.shape[1] // LANES
    slot_rows = heart_index.shape[3] // LANES
    block = shape_of(nx, ny, nz)
    flat = lambda a: a.reshape(rows, LANES)
    cells = lambda a: a.reshape(block_rows, LANES)
    states = lambda a: a.reshape(n_states, block_rows, LANES)

    w0, inv, packed, stat = call(
        start_kernel, (block, block, shape_of(2, ny, nz), shape_of(2, SUB, nz)), 3,
        specs=[HBM] * 3,
        scratch=[
            pltpu.VMEM((nx, ny, nz), F32), pltpu.VMEM((nx, ny, nz), F32), pltpu.VMEM((nx, ny, nz), jnp.int32),
            pltpu.SemaphoreType.DMA((3, 2)),
        ],
    )(in_hbm(potential_cot), in_hbm(damping), in_hbm(tissue_label))

    got = lax.ppermute(packed, "gz", [(0, 1), (1, 0)])
    plan = call(plan_kernel, jax.ShapeDtypeStruct((rows, LANES), jnp.int32), 2, cost=6_000_000)(
        stat, flat(tissue_label)
    )

    n_y = steps_of("gy")
    shapes = (
        (shape_of(2, ny, nz),) + (shape_of(nx + 1, SUB, nz),) * n_y + (shape_of(6, ny, nz),) * 2
        + (shape_of(4, SUB, nz),) * (2 * n_y)
    )
    slab, *faces = call(functools.partial(faces_kernel, n_y), shapes, 5)(w0, inv, packed, got, stat)
    along_y, along_x, across = faces[:n_y], faces[n_y : n_y + 2], faces[n_y + 2 :]
    y_to = [partners("gy", step) for step in range(n_y)]
    x_to = [partners("gx", step) for step in range(2)]
    along_y = [swap(face, y_to=y_to[j]) for j, face in enumerate(along_y)]
    along_x = [swap(face, x_to=x_to[i]) for i, face in enumerate(along_x)]
    across = [swap(face, x_to=x_to[k // n_y], y_to=y_to[k % n_y]) for k, face in enumerate(across)]

    tall = ring + SUB
    planes = shape_of(nx, tall, nz)
    edges = shape_of(6, tall, nz)
    in0, in_inv, in1, in2, in_sums, own_slab = call(
        functools.partial(inner_kernel, n_y),
        (planes,) * 4 + (shape_of(5, SUB, nz), shape_of(2, tall, nz)),
        3 + n_y,
        scratch=[pltpu.VMEM((4, tall, nz), F32)],
        cost=6_000_000,
    )(w0, inv, slab, *along_y)
    ends0, ends1, ends2, slabs, sums, where = call(
        functools.partial(outer_kernel, n_y, float(n_gx * voltage.shape[1])),
        (edges,) * 3 + (shape_of(3, tall, 2 * nz), shape_of(SUB, nz), shape_of(SUB, nz)),
        10 + 2 * n_y,
        scratch=[pltpu.VMEM((4, tall, nz), F32), pltpu.VMEM((1, tall, 2 * nz), F32)],
    )(plan, in0, in_inv, in1, in2, own_slab, in_sums, stat, *along_x, *across)

    def couple(stage, after, inside, ends):
        return call(
            functools.partial(couple_kernel, stage, slot_rows),
            shape_of(slot_rows, LANES),
            5,
            scratch=[pltpu.VMEM((rows, LANES), F32)],
            cost=6_000_000,
        )(after, inside, ends, slabs, plan)

    def add(value, axis, step, after):
        got = lax.ppermute(value, axis, [(i, i ^ step) for i in range(lax.axis_size(axis))])
        return call(add_kernel, shape_of(SUB, nz), 3)(value, got, after)

    list0 = couple(0, sums, in0, ends0)
    sums = add(sums, "gz", 1, list0)
    list1 = couple(1, sums, in1, ends1)
    list2 = couple(2, list1, in2, ends2)
    for step in [2**k for k in range(n_gy.bit_length() - 1)]:
        sums = add(sums, "gy", step, list2)
    if n_gx > 4:
        counts = lax.all_gather(jnp.sum(stat[1, 0]), "gx")
        begin = jnp.sum(jnp.where(jnp.arange(n_gx) < lax.axis_index("gx"), counts, 0.0))
        where = where.at[0].set(begin)
    blocks = call(
        place_kernel,
        (shape_of(3 * block_rows + SUB, LANES),) * n_gx,
        5,
        scratch=[pltpu.VMEM((3, n_gx * block_rows + slot_rows + SUB, LANES), F32)],
    )(where, sums, list0, list1, list2)
    apart = {k: never_meet(n_gx, k, slot_rows, block_rows) for k in range(1, n_gx)}
    small, meets = [], []
    for k in range(1, n_gx):
        if any(apart[k]):
            small.append(swap(sums, x_to=[i ^ k if apart[k][i] else i for i in range(n_gx)]))
        meets.append(not all(apart[k]))
    order = [k for k in [2, 3, 1] + list(range(4, n_gx)) if k < n_gx and meets[k - 1]]
    large = [swap(blocks[k], x_to=[i if apart[k][i] else i ^ k for i in range(n_gx)]) for k in order]
    alone = [[apart[k] for k in range(1, n_gx) if any(apart[k])], [apart[k] for k in order]]

    base, total_change, factor, state_coefs = call(
        membrane_kernel,
        (
            shape_of(n_states, block_rows, LANES), shape_of(block_rows, LANES), shape_of(block_rows, LANES),
            shape_of(2, n_states, LANES),
        ),
        9,
        specs=[SMEM] * 5 + [VMEM] * 4,
        cost=6_000_000,
    )(
        half_voltage, gate_slope, tau_base, conductance, reversal,
        blocks[0], cells(voltage), states(gates), states(gates_cot),
    )
    solution, volt_grad, gate_grad = call(
        functools.partial(finish_kernel, alone),
        (block, shape_of(block_rows, LANES), shape_of(n_states, block_rows, LANES)),
        12 + len(small) + len(large),
    )(
        state_coefs, cells(voltage_cot), cells(voltage), total_change, factor, base,
        in0, in1, in2, ends1, ends2, blocks[0], *small, *large,
    )
    return solution, volt_grad.reshape(voltage.shape), gate_grad.reshape(gates.shape)


def solution(mesh):
    grid = P(("groups", "gx"), "gy", "gz")
    cells = P(("groups", "gy", "gz"), "gx")
    states = P(None, ("groups", "gy", "gz"), "gx")
    in_specs = (
        grid, grid, grid, P(("groups", "gx"), "gy", "gz", None), cells, states, cells, states,
        P(), P(), P(), P(), P(),
    )
    return jax.shard_map(
        local, mesh=mesh, in_specs=in_specs, out_specs=(grid, cells, states), check_vma=False
    )
```

```python
import functools

import jax
import jax.numpy as jnp
from jax import lax
from jax.experimental import pallas as pl
from jax.experimental.pallas import tpu as pltpu
from jax.sharding import PartitionSpec as P

TIME_STEP = 0.5
LANES = 128
SUB = 8
PACK = 8
COUNT_LANE = 4 * PACK
F32 = jnp.float32

VMEM = pl.BlockSpec(memory_space=pltpu.VMEM)
SMEM = pl.BlockSpec(memory_space=pltpu.SMEM)
HBM = pl.BlockSpec(memory_space=pltpu.HBM)


def shape_of(*dims):
    return jax.ShapeDtypeStruct(dims, F32)


def call(kernel, out_shape, n_in, specs=None, outs=None, scratch=(), cost=2_000_000, limit=32):
    return pl.pallas_call(
        kernel,
        out_shape=out_shape,
        in_specs=specs if specs is not None else [VMEM] * n_in,
        out_specs=outs if outs is not None else jax.tree.map(lambda _: VMEM, out_shape),
        scratch_shapes=list(scratch),
        compiler_params=pltpu.CompilerParams(vmem_limit_bytes=limit * 1024 * 1024),
        cost_estimate=pl.CostEstimate(flops=cost, bytes_accessed=cost, transcendentals=0),
    )


def in_hbm(array):
    return pltpu.with_memory_space_constraint(array, pltpu.HBM)


def lanes_of(shape):
    return lax.broadcasted_iota(jnp.int32, shape, len(shape) - 1)


def subs_of(shape):
    return lax.broadcasted_iota(jnp.int32, shape, len(shape) - 2)


def start_kernel(
    right_hbm, damping_hbm, label_hbm, w0_ref, inv_ref, pack_ref, stat_ref, right_ref, damping_ref, label_ref, sems
):
    nx, ny, nz = right_ref.shape
    parts = sems.shape[1]
    size = nx // parts
    copies = []
    for part in range(parts):
        here = pl.ds(part * size, size)
        for k, (source, target) in enumerate(
            ((right_hbm, right_ref), (damping_hbm, damping_ref), (label_hbm, label_ref))
        ):
            copies.append(pltpu.make_async_copy(source.at[here], target.at[here], sems.at[k, part]))
            copies[-1].start()
    gz = lax.axis_index("gz")
    lane = lanes_of((ny, nz))
    packed_w = jnp.zeros((ny, nz), F32)
    packed_i = jnp.zeros((ny, nz), F32)
    energy = jnp.zeros((ny, nz), F32)
    cells = jnp.zeros((ny, nz), F32)
    for x in range(nx):
        if x % size == 0:
            for k in range(3):
                copies[3 * (x // size) + k].wait()
        label = label_ref[x].astype(F32)
        right = right_ref[x]
        inv = 1.0 / (12.0 + damping_ref[x] * (1.0 + 3.0 * label))
        w0 = right * inv
        w0_ref[x] = w0
        inv_ref[x] = inv
        energy = energy + right * w0
        cells = cells + label
        turn = (PACK * x + 3) % nz
        begin = PACK * x + 3 * gz
        chosen = (lane >= begin) & (lane < begin + 3)
        packed_w = jnp.where(chosen, pltpu.roll(w0, turn, 1), packed_w)
        packed_i = jnp.where(chosen, pltpu.roll(inv, turn, 1), packed_i)
    pack_ref[0] = packed_w
    pack_ref[1] = packed_i
    stat_ref[0] = jnp.broadcast_to(jnp.sum(energy, axis=0, keepdims=True), (SUB, nz))
    stat_ref[1] = jnp.broadcast_to(jnp.sum(cells, axis=0, keepdims=True), (SUB, nz))


def steps_of(axis):
    return 1 if lax.axis_size(axis) == 2 else 2


def upper_in(axis, step):
    return lax.rem(lax.axis_index(axis), 2) == step


def has_partner(axis, step):
    here = lax.axis_index(axis)
    return jnp.where(upper_in(axis, step), here < lax.axis_size(axis) - 1, here > 0)


def unpack_rows(tile, step):
    sub = subs_of(tile.shape)
    up, there = upper_in("gy", step), has_partner("gy", step)
    depth = jnp.where(there, jnp.where(up, SUB - 1 - sub, sub), -1)
    return jnp.where(depth >= 5, tile, 0.0), jnp.where(depth >= 6, pltpu.roll(tile, 4, 0), 0.0)


def halo_rows(tiles):
    w_tile, i_tile = unpack_rows(tiles[0], 0)
    for step, tile in enumerate(tiles[1:], 1):
        w_more, i_more = unpack_rows(tile, step)
        w_tile, i_tile = w_tile + w_more, i_tile + i_more
    return w_tile, i_tile


def faces_kernel(n_y, w0_ref, inv_ref, own_ref, got_ref, stat_ref, slab_ref, *refs):
    y_refs, x_refs, edge_refs = refs[:n_y], refs[n_y : n_y + 2], refs[n_y + 2 :]
    nx, ny, nz = w0_ref.shape
    sub = subs_of((SUB, nz))
    lane = lanes_of((ny, nz))
    slab_ref[...] = own_ref[...] + got_ref[...]
    for step, face_ref in enumerate(y_refs):
        up = upper_in("gy", step)
        keep_w = jnp.where(up, sub, SUB - 1 - sub) >= 5
        for x in range(nx + 1):
            w_rows, i_rows = (w0_ref.at[x], inv_ref.at[x]) if x < nx else (slab_ref.at[0], slab_ref.at[1])
            w_face = jnp.where(up, w_rows[ny - SUB :], w_rows[:SUB])
            i_face = jnp.where(up, i_rows[ny - SUB :], i_rows[:SUB])
            face_ref[x] = jnp.where(keep_w, w_face, pltpu.roll(i_face, 4, 0))
    cells = jnp.sum(stat_ref[1, 0:1], axis=1, keepdims=True)
    slab_w = slab_ref[0]
    half = pltpu.roll(slab_ref[1], nz // 2, 1)
    up_slab = jnp.where(lane >= nz - 3 * PACK, slab_w, half)
    down_slab = jnp.where(lane < 3 * PACK, slab_w, half)
    for step, face_ref in enumerate(x_refs):
        up = upper_in("gx", step)
        first = jnp.where(up, nx - 3, 0)
        for k in range(3):
            face_ref[k] = w0_ref[first + k]
        for k in range(2):
            face_ref[3 + k] = inv_ref[jnp.where(up, nx - 2, 0) + k]
        face_ref[5] = jnp.where(lane == COUNT_LANE, cells, jnp.where(up, up_slab, down_slab))
        for y_step, y_ref in enumerate(y_refs):
            edge_ref = edge_refs[step * n_y + y_step]
            for k in range(3):
                edge_ref[k] = y_ref[first + k]
            edge_ref[3] = y_ref[nx]


def slab_step(v, s, inv):
    width = v.shape[1]
    across = pltpu.roll(v, PACK, 1) + pltpu.roll(v, width - PACK, 1)
    q = v + 0.5 * (s + across)
    if inv is None:
        return q, None
    total = (
        pltpu.roll(q, 1, 1) + pltpu.roll(q, width - 1, 1) + s + across
        + 0.5 * (pltpu.roll(s, PACK, 1) + pltpu.roll(s, width - PACK, 1))
    )
    return q, total * inv


def along_z(q, half, column, gz):
    nz = q.shape[1]
    lane = lanes_of(q.shape)
    entry = (nz - 1) * (1 - gz)
    turn = lax.rem(entry - (column + 3 - gz) + 2 * nz, nz)
    up = jnp.where(lane == nz - 1, 0.0, pltpu.roll(q, nz - 1, 1))
    down = jnp.where(lane == 0, 0.0, pltpu.roll(q, 1, 1))
    return up + down + jnp.where(lane == entry, pltpu.roll(half, turn, 1), 0.0)


def sweep(stage, spans, nx, ny, nz, gz, get, get_inv, put, slab_q, sums):
    margin = 2 - stage
    start = SUB - margin
    tiles = ny // SUB + (margin > 0)
    own = subs_of((SUB, nz)) >= margin
    parts = [[], []]
    for tile in range(tiles):
        row = start + SUB * tile
        q_rows = slab_q[SUB * tile : SUB * tile + SUB]
        acc = [jnp.zeros((SUB, nz), F32) for _ in range(2)]

        def beside(x):
            return get(x, row - 1) + get(x, row + 1)

        for first, last in spans:
            s_low, s_mid = beside(first - 1), beside(first)
            v_low, v_mid = get(first - 1, row), get(first, row)
            for x in range(first, last):
                v_high, s_high = get(x + 1, row), beside(x + 1)
                across = v_low + v_high
                column = (PACK * x) % (2 * nz)
                half = q_rows[:, column // nz * nz : column // nz * nz + nz]
                rest = s_mid + across
                total = along_z(v_mid + 0.5 * rest, half, column % nz, gz) + rest + 0.5 * (s_low + s_high)
                if stage < 2:
                    after = total * get_inv(x, row)
                    put(x, row, after)
                if 0 <= x < nx:
                    acc[0] = acc[0] + v_mid * total
                    if stage < 2:
                        acc[1] = acc[1] + after * total
                v_low, v_mid, s_low, s_mid = v_mid, v_high, s_mid, s_high
        for k in range(2):
            parts[k].append(acc[k])
    for k in range(2 if stage < 2 else 1):
        part = parts[k]
        total = part[1]
        for other in part[2 : ny // SUB]:
            total = total + other
        total = total + (jnp.where(own, part[0], part[-1]) if margin else part[0])
        sums[2 * stage + k] = total


def inner_kernel(n_y, w0_ref, inv_ref, slab_ref, *refs):
    y_refs, (a_ref, i_ref, b_ref, c_ref, sum_ref, own_slab_ref, slabs_ref) = refs[:n_y], refs[n_y:]
    nx, ny, nz = w0_ref.shape
    gz = lax.axis_index("gz")
    for x in range(nx + 1):
        halos = halo_rows([ref[x] for ref in y_refs])
        for k in range(2):
            if x < nx:
                ref, own = (a_ref, i_ref)[k].at[x], (w0_ref, inv_ref)[k][x]
            else:
                ref, own = own_slab_ref.at[k], slab_ref[k]
            ref[:SUB] = halos[k]
            ref[SUB : SUB + ny] = own
            ref[SUB + ny :] = halos[k]
    for k in range(2):
        slabs_ref[3 * k] = own_slab_ref[k]
    sums = {}
    for stage in range(3):
        source, target = (a_ref, b_ref, c_ref)[stage], (b_ref, c_ref, None)[stage]
        start, size = SUB - 2 + stage, ny if stage == 2 else ny + SUB
        v = slabs_ref[stage, start : start + size]
        s = slabs_ref[stage, start - 1 : start - 1 + size] + slabs_ref[stage, start + 1 : start + 1 + size]
        q, after = slab_step(v, s, slabs_ref[3, start : start + size] if stage < 2 else None)
        if stage < 2:
            slabs_ref[stage + 1, start : start + size] = after

        def put(x, row, value):
            target[x, row : row + SUB] = value

        sweep(
            stage, [(1 + stage, nx - 1 - stage)], nx, ny, nz, gz,
            lambda x, row: source[x, row : row + SUB], lambda x, row: i_ref[x, row : row + SUB],
            put, q, sums,
        )
    for k in range(5):
        sum_ref[k] = sums[k]


def outer_kernel(
    n_y, column_total, after_ref, a_ref, i_ref, b_ref, c_ref, slab_ref, sum_ref, stat_ref, *refs
):
    x_refs, corner_refs = refs[:2], refs[2 : 2 + 2 * n_y]
    ea_ref, eb_ref, ec_ref, slabs_ref, total_ref, where_ref, ei_ref, si_ref = refs[2 + 2 * n_y :]
    nx, ny, nz = a_ref.shape[0], a_ref.shape[1] - 2 * SUB, a_ref.shape[2]
    ring = ny + SUB
    gz = lax.axis_index("gz")
    odd = lax.rem(lax.axis_index("gx"), 2) == 1

    def beyond(upper, read):
        there = has_partner("gx", 0) if upper else has_partner("gx", 1)
        swapped = has_partner("gx", 1) if upper else has_partner("gx", 0)
        first, second = read(0), read(1)
        if upper:
            return jnp.where(jnp.where(odd, swapped, there), jnp.where(odd, second, first), 0.0)
        return jnp.where(jnp.where(odd, swapped, there), jnp.where(odd, first, second), 0.0)

    def write(ref, at, own, halo):
        ref[at, :SUB] = halo
        ref[at, SUB : SUB + ny] = own
        ref[at, SUB + ny :] = halo

    lane_tile, lane = lanes_of((SUB, nz)), lanes_of((ny, nz))
    slab_parts = []
    for side, upper in enumerate((False, True)):
        tiles = [
            halo_rows([beyond(upper, lambda step: corner_refs[step * n_y + j][k]) for j in range(n_y)])
            for k in range(4)
        ]
        for k in range(3):
            write(ea_ref, 3 * side + k, beyond(upper, lambda step: x_refs[step][k]), tiles[k][0])
        for k in range(2):
            own = beyond(upper, lambda step: x_refs[step][3 + k])
            write(ei_ref, 2 * side + k, own, tiles[k if upper else k + 1][1])
        own = beyond(upper, lambda step: x_refs[step][5])

        def near(value, lanes, planes):
            return jnp.where(lanes < planes * PACK if upper else lanes >= nz - planes * PACK, value, 0.0)

        slab_parts.append((
            near(own, lane, 3), near(tiles[3][0], lane_tile, 3),
            near(pltpu.roll(own, nz // 2, 1), lane, 2), near(tiles[3][1], lane_tile, 2),
            own[0:1, COUNT_LANE : COUNT_LANE + 1],
        ))

    low, high = slab_parts
    for ref, k in ((slabs_ref, 0), (si_ref, 1)):
        ref[0, :, :nz] = slab_ref[k]
        ref[0, SUB : SUB + ny, nz:] = low[2 * k] + high[2 * k]
        ref[0, :SUB, nz:] = low[2 * k + 1] + high[2 * k + 1]
        ref[0, SUB + ny :, nz:] = low[2 * k + 1] + high[2 * k + 1]

    def reader(inside_ref, edge_ref, first, count):
        def get(x, row):
            if first <= x < nx - first:
                return inside_ref[x, row : row + SUB]
            at = x - (first - count) if x < first else x - (nx - first) + count
            return edge_ref[at, row : row + SUB]

        return get

    sums = {}
    for stage in range(3):
        get = reader((a_ref, b_ref, c_ref)[stage], (ea_ref, eb_ref, ec_ref)[stage], stage, 3)
        start, size = SUB - 2 + stage, ny if stage == 2 else ring
        v = slabs_ref[stage, start : start + size]
        s = slabs_ref[stage, start - 1 : start - 1 + size] + slabs_ref[stage, start + 1 : start + 1 + size]
        q, after = slab_step(v, s, si_ref[0, start : start + size] if stage < 2 else None)
        if stage < 2:
            slabs_ref[stage + 1, start : start + size] = after

        def put(x, row, value):
            edge_ref = (eb_ref, ec_ref)[stage]
            at = x - (stage - 2) if x < nx // 2 else x - (nx - 1 - stage) + 3
            edge_ref[at, row : row + SUB] = value

        sweep(
            stage, [(stage - 2, stage + 1), (nx - 1 - stage, nx + 2 - stage)], nx, ny, nz, gz,
            get, reader(i_ref, ei_ref, 0, 2), put, q, sums,
        )

    total_ref[0:1] = stat_ref[0, 0:1]
    for k in range(5):
        total_ref[k + 1 : k + 2] = jnp.sum(sums[k] + sum_ref[k], axis=0, keepdims=True)
    total_ref[6:8] = jnp.zeros((2, nz), F32)
    gx, n_x = lax.axis_index("gx"), lax.axis_size("gx")
    count = jnp.sum(stat_ref[1, 0:1], axis=1, keepdims=True)
    below, above = [part[4] for part in slab_parts]
    begin = jnp.where(
        gx == 0, 0.0,
        jnp.where(gx == 1, below, jnp.where(gx == n_x - 1, column_total - count, column_total - count - above)),
    )
    where_ref[0:1] = jnp.broadcast_to(begin, (1, nz))
    where_ref[1:2] = jnp.broadcast_to(count, (1, nz))
    where_ref[2:8] = jnp.zeros((6, nz), F32)


def shift_left(v, amount, lane):
    rows = v.shape[0]
    if amount < LANES:
        turned = pltpu.roll(v, LANES - amount, 1)
        below = pltpu.roll(turned, rows - 1, 0)
        return jnp.where(lane < LANES - amount, turned, below)
    return jnp.concatenate([v[amount // LANES :], v[: amount // LANES]], axis=0)


def plan_kernel(after_ref, label_ref, plan_ref):
    rows = label_ref.shape[0]
    lane = lanes_of((rows, LANES))
    row = subs_of((rows, LANES))
    heart = label_ref[...] == 1
    ones = heart.astype(jnp.bfloat16)
    upper = (subs_of((LANES, LANES)) < lanes_of((LANES, LANES))).astype(jnp.bfloat16)
    in_row = jnp.dot(ones, upper, preferred_element_type=F32)
    totals = jnp.dot(ones, jnp.ones((LANES, LANES), jnp.bfloat16), preferred_element_type=F32)
    lower = (subs_of((rows, rows)) > lanes_of((rows, rows))).astype(jnp.bfloat16)
    before = jnp.dot(lower, totals.astype(jnp.bfloat16), preferred_element_type=F32)
    rank = (in_row + before).astype(jnp.int32)
    way = jnp.where(heart, row * LANES + lane - rank, 0)
    plan = jnp.zeros((rows, LANES), jnp.int32)
    step = 1
    while step < rows * LANES:
        moving = jnp.where((way & step) != 0, way, 0)
        arriving = shift_left(moving, step, lane)
        plan = plan | (arriving & step)
        way = (way - moving) | arriving
        step *= 2
    plan_ref[...] = plan


def galerkin(t):
    g00, g01, g02, g12, g22 = t[0] - t[1], t[1] - t[2], t[2] - t[3], t[3] - t[4], t[4] - t[5]
    g11 = g02
    l10, l20 = g01 / g00, g02 / g00
    d1 = g11 - l10 * g01
    m21 = g12 - l20 * g01
    ok1 = d1 > 1e-6 * g11
    d1 = jnp.where(ok1, d1, 1.0)
    l21 = jnp.where(ok1, m21 / d1, 0.0)
    d2 = g22 - l20 * g02 - l21 * m21
    ok2 = ok1 & (d2 > 1e-6 * g22)
    d2 = jnp.where(ok2, d2, 1.0)
    y1 = t[1] - l10 * t[0]
    y2 = t[2] - l20 * t[0] - l21 * y1
    c2 = jnp.where(ok2, y2 / d2, 0.0)
    c1 = jnp.where(ok1, y1 / d1 - l21 * c2, 0.0)
    c0 = t[0] / g00 - l10 * c1 - l20 * c2
    return c0, c1, c2


def couple_kernel(stage, slot_rows, after_ref, inside_ref, edge_ref, slabs_ref, plan_ref, list_ref, value_ref):
    nx, nz = inside_ref.shape[0], inside_ref.shape[2]
    ny = inside_ref.shape[1] - 2 * SUB
    rows = nx * ny
    gz = lax.axis_index("gz")

    def get(x, row):
        if stage <= x < nx - stage:
            return inside_ref[x, row : row + SUB]
        return edge_ref[x - (stage - 3) if x < stage else x - (nx - stage) + 3, row : row + SUB]

    for tile in range(ny // SUB):
        row = SUB + SUB * tile
        slab = slabs_ref[stage, row : row + SUB, :nz]
        v_low, v_mid = get(-1, row), get(0, row)
        for x in range(nx):
            v_high = get(x + 1, row)
            beside = get(x, row - 1) + get(x, row + 1)
            at = ny * x + SUB * tile
            value_ref[at : at + SUB] = (
                along_z(v_mid, slab, PACK * x, gz) + beside + (v_low + v_high) - 6.0 * v_mid
            )
            v_low, v_mid = v_mid, v_high
    lane = lanes_of((rows, LANES))
    value = value_ref[...]
    plan = plan_ref[...]
    step = 1
    while step < rows * LANES:
        value = jnp.where((plan & step) != 0, shift_left(value, step, lane), value)
        step *= 2
    list_ref[...] = value[:slot_rows]


def add_kernel(a_ref, b_ref, after_ref, out_ref):
    out_ref[...] = a_ref[...] + b_ref[...]


def place_kernel(where_ref, total_ref, *refs):
    list_refs, out_refs, buf_ref = refs[:3], refs[3:-1], refs[-1]
    slot_rows = list_refs[0].shape[0]
    size = (out_refs[0].shape[0] - SUB) // 3
    gx = lax.axis_index("gx")
    offset = jnp.max(where_ref[0:1]).astype(jnp.int32)
    count = jnp.max(where_ref[1:2]).astype(jnp.int32)
    shape = (slot_rows, LANES)
    listed = subs_of(shape) * LANES + lanes_of(shape) < count
    inner = lax.rem(offset, LANES)
    kept = lanes_of((slot_rows + SUB, LANES)) >= inner
    buf_ref[...] = jnp.zeros_like(buf_ref)
    for k, list_ref in enumerate(list_refs):
        slots = jnp.where(listed, list_ref[...], 0.0)
        slots = jnp.concatenate([slots, jnp.zeros((SUB, LANES), F32)], axis=0)
        turned = pltpu.roll(slots, inner, 1)
        buf_ref[k, pl.ds(offset // LANES, slot_rows + SUB), :] = jnp.where(kept, turned, pltpu.roll(turned, 1, 0))
    for block, out_ref in enumerate(out_refs):
        begin = pl.multiple_of((gx ^ block) * size, SUB)
        for k in range(3):
            out_ref[k * size : k * size + size] = buf_ref[k, pl.ds(begin, size), :]
        out_ref[3 * size :] = total_ref[...]


def membrane_kernel(
    half_ref, slope_ref, tau_ref, cond_ref, rev_ref, after_ref, v_ref, gates_ref, cot_ref,
    base_ref, sum_ref, factor_ref, coef_ref,
):
    n_states, rows = gates_ref.shape[:2]
    v = v_ref[...]

    def state(g, carry):
        total, current = carry
        inv_slope = 1.0 / slope_ref[g]
        tau_base = tau_ref[g]
        scaled = (v - half_ref[g]) * inv_slope
        gate = gates_ref[g]
        cot = cot_ref[g]
        steady = 1.0 / (1.0 + jnp.exp(-scaled))
        bell = jnp.exp(-scaled * scaled)
        rate = TIME_STEP / (tau_base * (0.5 + bell))
        decay = jnp.exp(-rate)
        steady_slope = steady * (1.0 - steady)
        decay_slope = decay * rate * rate * ((tau_base / TIME_STEP) * bell * (-2.0 * scaled))
        change = (steady_slope * (1.0 - decay) + (gate - steady) * decay_slope) * inv_slope
        base_ref[g] = cot * decay
        coef_ref[0, pl.ds(g, 1)] = jnp.full((1, LANES), TIME_STEP * cond_ref[g])
        coef_ref[1, pl.ds(g, 1)] = jnp.full((1, LANES), rev_ref[g])
        return total + cot * change, current + cond_ref[g] * gate

    zero = jnp.zeros((rows, LANES), F32)
    total, current = lax.fori_loop(0, n_states, state, (zero, zero), unroll=2)
    sum_ref[...] = total
    factor_ref[...] = 1.0 - TIME_STEP * current


def finish_kernel(
    alone, coef_ref, vcot_ref, v_ref, sum_ref, factor_ref, base_ref, a_ref, b_ref, c_ref, eb_ref, ec_ref, *refs
):
    n_small, n_large = len(alone[0]), len(alone[1])
    own_ref, small_refs, large_refs = refs[0], refs[1 : 1 + n_small], refs[1 + n_small : 1 + n_small + n_large]
    x_ref, volt_ref, gate_ref = refs[1 + n_small + n_large :]
    size = (own_ref.shape[0] - SUB) // 3
    gx = lax.axis_index("gx")

    def is_one(flags):
        found = gx < 0
        for place, flag in enumerate(flags):
            if flag:
                found = found | (gx == place)
        return found

    total = own_ref[3 * size :]
    for flags, ref in zip(alone[0], small_refs):
        total = total + jnp.where(is_one(flags), ref[...], 0.0)
    for flags, ref in zip(alone[1], large_refs):
        total = total + jnp.where(is_one(flags), 0.0, ref[3 * size :])
    sums = jnp.sum(total, axis=1, keepdims=True)
    c0, c1, c2 = galerkin([jnp.broadcast_to(sums[k : k + 1], (1, LANES)) for k in range(6)])
    landed = jnp.zeros((size, LANES), F32)
    for k, c in enumerate((c0, c1, c2)):
        part = own_ref[k * size : k * size + size]
        for ref in large_refs:
            part = part + ref[k * size : k * size + size]
        landed = landed + c * part
    cot = vcot_ref[...] + landed
    v = v_ref[...]
    volt_ref[...] = cot * factor_ref[...] + sum_ref[...]
    for g in range(base_ref.shape[0]):
        gate_ref[g] = base_ref[g] - (coef_ref[0, g : g + 1] * cot) * (v - coef_ref[1, g : g + 1])
    nx, ny, nz = x_ref.shape
    own = slice(SUB, SUB + ny)
    for x in range(nx):
        w1 = b_ref[x, own] if 1 <= x < nx - 1 else eb_ref[2 if x == 0 else 3, own]
        w2 = c_ref[x, own] if 2 <= x < nx - 2 else ec_ref[x + 1 if x < 2 else x - (nx - 2) + 3, own]
        x_ref[x] = c0 * a_ref[x, own] + c1 * w1 + c2 * w2


def partners(axis, step):
    count = lax.axis_size(axis)
    if step == 0:
        return [i ^ 1 for i in range(count)]
    return [0] + [i + 1 if i % 2 else i - 1 for i in range(1, count - 1)] + [count - 1]


def swap(value, x_to=None, y_to=None):
    n_x, n_y, n_z = [lax.axis_size(axis) for axis in ("gx", "gy", "gz")]
    pairs = []
    for x in range(n_x):
        for y in range(n_y):
            to_x, to_y = x_to[x] if x_to else x, y_to[y] if y_to else y
            alone = (x_to and to_x == x) or (y_to and to_y == y)
            for z in range(n_z):
                to = (x, y, z ^ 1) if alone else (to_x, to_y, z)
                pairs.append(((x * n_y + y) * n_z + z, (to[0] * n_y + to[1]) * n_z + to[2]))
    return lax.ppermute(value, ("gx", "gy", "gz"), pairs)


def never_meet(count, k, slots, block):
    def apart(tile, owner):
        return owner * block >= (tile + 1) * slots or (owner + 1) * block <= count * block - (count - tile) * slots

    return [apart(i, i ^ k) and apart(i ^ k, i) for i in range(count)]


def local(
    potential_cot, damping, tissue_label, heart_index, voltage, gates, voltage_cot, gates_cot,
    half_voltage, gate_slope, tau_base, conductance, reversal,
):
    nx, ny, nz = potential_cot.shape
    rows = nx * ny
    ring = ny + SUB
    n_gx, n_gy = lax.axis_size("gx"), lax.axis_size("gy")
    n_states = gates.shape[0]
    block_rows = voltage.shape[1] // LANES
    slot_rows = heart_index.shape[3] // LANES
    block = shape_of(nx, ny, nz)
    flat = lambda a: a.reshape(rows, LANES)
    cells = lambda a: a.reshape(block_rows, LANES)
    states = lambda a: a.reshape(n_states, block_rows, LANES)

    w0, inv, packed, stat = call(
        start_kernel, (block, block, shape_of(2, ny, nz), shape_of(2, SUB, nz)), 3,
        specs=[HBM] * 3,
        scratch=[
            pltpu.VMEM((nx, ny, nz), F32), pltpu.VMEM((nx, ny, nz), F32), pltpu.VMEM((nx, ny, nz), jnp.int32),
            pltpu.SemaphoreType.DMA((3, 2)),
        ],
    )(in_hbm(potential_cot), in_hbm(damping), in_hbm(tissue_label))

    got = lax.ppermute(packed, "gz", [(0, 1), (1, 0)])
    plan = call(plan_kernel, jax.ShapeDtypeStruct((rows, LANES), jnp.int32), 2, cost=6_000_000)(
        stat, flat(tissue_label)
    )

    n_y = steps_of("gy")
    shapes = (
        (shape_of(2, ny, nz),) + (shape_of(nx + 1, SUB, nz),) * n_y + (shape_of(6, ny, nz),) * 2
        + (shape_of(4, SUB, nz),) * (2 * n_y)
    )
    slab, *faces = call(functools.partial(faces_kernel, n_y), shapes, 5)(w0, inv, packed, got, stat)
    along_y, along_x, across = faces[:n_y], faces[n_y : n_y + 2], faces[n_y + 2 :]
    y_to = [partners("gy", step) for step in range(n_y)]
    x_to = [partners("gx", step) for step in range(2)]
    along_y = [swap(face, y_to=y_to[j]) for j, face in enumerate(along_y)]
    along_x = [swap(along_x[i], x_to=x_to[i]) for i in (1, 0)][::-1]
    across = [swap(face, x_to=x_to[k // n_y], y_to=y_to[k % n_y]) for k, face in enumerate(across)]

    tall = ring + SUB
    planes = shape_of(nx, tall, nz)
    edges = shape_of(6, tall, nz)
    in0, in_inv, in1, in2, in_sums, own_slab = call(
        functools.partial(inner_kernel, n_y),
        (planes,) * 4 + (shape_of(5, SUB, nz), shape_of(2, tall, nz)),
        3 + n_y,
        scratch=[pltpu.VMEM((4, tall, nz), F32)],
        cost=6_000_000,
    )(w0, inv, slab, *along_y)
    ends0, ends1, ends2, slabs, sums, where = call(
        functools.partial(outer_kernel, n_y, float(n_gx * voltage.shape[1])),
        (edges,) * 3 + (shape_of(3, tall, 2 * nz), shape_of(SUB, nz), shape_of(SUB, nz)),
        10 + 2 * n_y,
        scratch=[pltpu.VMEM((4, tall, nz), F32), pltpu.VMEM((1, tall, 2 * nz), F32)],
    )(plan, in0, in_inv, in1, in2, own_slab, in_sums, stat, *along_x, *across)

    def couple(stage, after, inside, ends):
        return call(
            functools.partial(couple_kernel, stage, slot_rows),
            shape_of(slot_rows, LANES),
            5,
            scratch=[pltpu.VMEM((rows, LANES), F32)],
            cost=6_000_000,
        )(after, inside, ends, slabs, plan)

    def add(value, axis, step, after):
        got = lax.ppermute(value, axis, [(i, i ^ step) for i in range(lax.axis_size(axis))])
        return call(add_kernel, shape_of(SUB, nz), 3)(value, got, after)

    list0 = couple(0, sums, in0, ends0)
    sums = add(sums, "gz", 1, list0)
    list1 = couple(1, sums, in1, ends1)
    list2 = couple(2, list1, in2, ends2)
    for step in [2**k for k in range(n_gy.bit_length() - 1)]:
        sums = add(sums, "gy", step, list2)
    if n_gx > 4:
        counts = lax.all_gather(jnp.sum(stat[1, 0]), "gx")
        begin = jnp.sum(jnp.where(jnp.arange(n_gx) < lax.axis_index("gx"), counts, 0.0))
        where = where.at[0].set(begin)
    blocks = call(
        place_kernel,
        (shape_of(3 * block_rows + SUB, LANES),) * n_gx,
        5,
        scratch=[pltpu.VMEM((3, n_gx * block_rows + slot_rows + SUB, LANES), F32)],
    )(where, sums, list0, list1, list2)
    apart = {k: never_meet(n_gx, k, slot_rows, block_rows) for k in range(1, n_gx)}
    small, meets = [], []
    for k in range(1, n_gx):
        if any(apart[k]):
            small.append(swap(sums, x_to=[i ^ k if apart[k][i] else i for i in range(n_gx)]))
        meets.append(not all(apart[k]))
    order = [k for k in [2, 3, 1] + list(range(4, n_gx)) if k < n_gx and meets[k - 1]]
    large = [swap(blocks[k], x_to=[i if apart[k][i] else i ^ k for i in range(n_gx)]) for k in order]
    alone = [[apart[k] for k in range(1, n_gx) if any(apart[k])], [apart[k] for k in order]]

    base, total_change, factor, state_coefs = call(
        membrane_kernel,
        (
            shape_of(n_states, block_rows, LANES), shape_of(block_rows, LANES), shape_of(block_rows, LANES),
            shape_of(2, n_states, LANES),
        ),
        9,
        specs=[SMEM] * 5 + [VMEM] * 4,
        cost=6_000_000,
    )(
        half_voltage, gate_slope, tau_base, conductance, reversal,
        blocks[0], cells(voltage), states(gates), states(gates_cot),
    )
    solution, volt_grad, gate_grad = call(
        functools.partial(finish_kernel, alone),
        (block, shape_of(block_rows, LANES), shape_of(n_states, block_rows, LANES)),
        12 + len(small) + len(large),
    )(
        state_coefs, cells(voltage_cot), cells(voltage), total_change, factor, base,
        in0, in1, in2, ends1, ends2, blocks[0], *small, *large,
    )
    return solution, volt_grad.reshape(voltage.shape), gate_grad.reshape(gates.shape)


def solution(mesh):
    grid = P(("groups", "gx"), "gy", "gz")
    cells = P(("groups", "gy", "gz"), "gx")
    states = P(None, ("groups", "gy", "gz"), "gx")
    in_specs = (
        grid, grid, grid, P(("groups", "gx"), "gy", "gz", None), cells, states, cells, states,
        P(), P(), P(), P(), P(),
    )
    return jax.shard_map(
        local, mesh=mesh, in_specs=in_specs, out_specs=(grid, cells, states), check_vma=False
    )
```

```python
import functools

import jax
import jax.numpy as jnp
from jax import lax
from jax.experimental import pallas as pl
from jax.experimental.pallas import tpu as pltpu
from jax.sharding import PartitionSpec as P

TIME_STEP = 0.5
LANES = 128
SUB = 8
PACK = 8
COUNT_LANE = 4 * PACK
F32 = jnp.float32

VMEM = pl.BlockSpec(memory_space=pltpu.VMEM)
SMEM = pl.BlockSpec(memory_space=pltpu.SMEM)
HBM = pl.BlockSpec(memory_space=pltpu.HBM)


def shape_of(*dims):
    return jax.ShapeDtypeStruct(dims, F32)


def call(kernel, out_shape, n_in, specs=None, outs=None, scratch=(), cost=2_000_000, limit=32):
    return pl.pallas_call(
        kernel,
        out_shape=out_shape,
        in_specs=specs if specs is not None else [VMEM] * n_in,
        out_specs=outs if outs is not None else jax.tree.map(lambda _: VMEM, out_shape),
        scratch_shapes=list(scratch),
        compiler_params=pltpu.CompilerParams(vmem_limit_bytes=limit * 1024 * 1024),
        cost_estimate=pl.CostEstimate(flops=cost, bytes_accessed=cost, transcendentals=0),
    )


def in_hbm(array):
    return pltpu.with_memory_space_constraint(array, pltpu.HBM)


def lanes_of(shape):
    return lax.broadcasted_iota(jnp.int32, shape, len(shape) - 1)


def subs_of(shape):
    return lax.broadcasted_iota(jnp.int32, shape, len(shape) - 2)


def start_kernel(
    right_hbm, damping_hbm, label_hbm, w0_ref, inv_ref, pack_ref, stat_ref, right_ref, damping_ref, label_ref, sems
):
    nx, ny, nz = right_ref.shape
    parts = sems.shape[1]
    size = nx // parts
    copies = []
    for part in range(parts):
        here = pl.ds(part * size, size)
        for k, (source, target) in enumerate(
            ((right_hbm, right_ref), (damping_hbm, damping_ref), (label_hbm, label_ref))
        ):
            copies.append(pltpu.make_async_copy(source.at[here], target.at[here], sems.at[k, part]))
            copies[-1].start()
    gz = lax.axis_index("gz")
    lane = lanes_of((ny, nz))
    packed_w = jnp.zeros((ny, nz), F32)
    packed_i = jnp.zeros((ny, nz), F32)
    energy = jnp.zeros((ny, nz), F32)
    cells = jnp.zeros((ny, nz), F32)
    for x in range(nx):
        if x % size == 0:
            for k in range(3):
                copies[3 * (x // size) + k].wait()
        label = label_ref[x].astype(F32)
        right = right_ref[x]
        inv = 1.0 / (12.0 + damping_ref[x] * (1.0 + 3.0 * label))
        w0 = right * inv
        w0_ref[x] = w0
        inv_ref[x] = inv
        energy = energy + right * w0
        cells = cells + label
        turn = (PACK * x + 3) % nz
        begin = PACK * x + 3 * gz
        chosen = (lane >= begin) & (lane < begin + 3)
        packed_w = jnp.where(chosen, pltpu.roll(w0, turn, 1), packed_w)
        packed_i = jnp.where(chosen, pltpu.roll(inv, turn, 1), packed_i)
    pack_ref[0] = packed_w
    pack_ref[1] = packed_i
    stat_ref[0] = jnp.broadcast_to(jnp.sum(energy, axis=0, keepdims=True), (SUB, nz))
    stat_ref[1] = jnp.broadcast_to(jnp.sum(cells, axis=0, keepdims=True), (SUB, nz))


def steps_of(axis):
    return 1 if lax.axis_size(axis) == 2 else 2


def upper_in(axis, step):
    return lax.rem(lax.axis_index(axis), 2) == step


def has_partner(axis, step):
    here = lax.axis_index(axis)
    return jnp.where(upper_in(axis, step), here < lax.axis_size(axis) - 1, here > 0)


def unpack_rows(tile, step):
    sub = subs_of(tile.shape)
    up, there = upper_in("gy", step), has_partner("gy", step)
    depth = jnp.where(there, jnp.where(up, SUB - 1 - sub, sub), -1)
    return jnp.where(depth >= 5, tile, 0.0), jnp.where(depth >= 6, pltpu.roll(tile, 4, 0), 0.0)


def halo_rows(tiles):
    w_tile, i_tile = unpack_rows(tiles[0], 0)
    for step, tile in enumerate(tiles[1:], 1):
        w_more, i_more = unpack_rows(tile, step)
        w_tile, i_tile = w_tile + w_more, i_tile + i_more
    return w_tile, i_tile


def faces_kernel(n_y, w0_ref, inv_ref, own_ref, got_ref, stat_ref, slab_ref, *refs):
    y_refs, x_refs, edge_refs = refs[:n_y], refs[n_y : n_y + 2], refs[n_y + 2 :]
    nx, ny, nz = w0_ref.shape
    sub = subs_of((SUB, nz))
    lane = lanes_of((ny, nz))
    slab_ref[...] = own_ref[...] + got_ref[...]
    for step, face_ref in enumerate(y_refs):
        up = upper_in("gy", step)
        keep_w = jnp.where(up, sub, SUB - 1 - sub) >= 5
        for x in range(nx + 1):
            w_rows, i_rows = (w0_ref.at[x], inv_ref.at[x]) if x < nx else (slab_ref.at[0], slab_ref.at[1])
            w_face = jnp.where(up, w_rows[ny - SUB :], w_rows[:SUB])
            i_face = jnp.where(up, i_rows[ny - SUB :], i_rows[:SUB])
            face_ref[x] = jnp.where(keep_w, w_face, pltpu.roll(i_face, 4, 0))
    cells = jnp.sum(stat_ref[1, 0:1], axis=1, keepdims=True)
    slab_w = slab_ref[0]
    half = pltpu.roll(slab_ref[1], nz // 2, 1)
    up_slab = jnp.where(lane >= nz - 3 * PACK, slab_w, half)
    down_slab = jnp.where(lane < 3 * PACK, slab_w, half)
    for step, face_ref in enumerate(x_refs):
        up = upper_in("gx", step)
        first = jnp.where(up, nx - 3, 0)
        for k in range(3):
            face_ref[k] = w0_ref[first + k]
        for k in range(2):
            face_ref[3 + k] = inv_ref[jnp.where(up, nx - 2, 0) + k]
        face_ref[5] = jnp.where(lane == COUNT_LANE, cells, jnp.where(up, up_slab, down_slab))
        for y_step, y_ref in enumerate(y_refs):
            edge_ref = edge_refs[step * n_y + y_step]
            for k in range(3):
                edge_ref[k] = y_ref[first + k]
            edge_ref[3] = y_ref[nx]


def slab_step(v, s, inv):
    width = v.shape[1]
    across = pltpu.roll(v, PACK, 1) + pltpu.roll(v, width - PACK, 1)
    q = v + 0.5 * (s + across)
    if inv is None:
        return q, None
    total = (
        pltpu.roll(q, 1, 1) + pltpu.roll(q, width - 1, 1) + s + across
        + 0.5 * (pltpu.roll(s, PACK, 1) + pltpu.roll(s, width - PACK, 1))
    )
    return q, total * inv


def along_z(q, half, column, gz):
    nz = q.shape[1]
    lane = lanes_of(q.shape)
    entry = (nz - 1) * (1 - gz)
    turn = lax.rem(entry - (column + 3 - gz) + 2 * nz, nz)
    up = jnp.where(lane == nz - 1, 0.0, pltpu.roll(q, nz - 1, 1))
    down = jnp.where(lane == 0, 0.0, pltpu.roll(q, 1, 1))
    return up + down + jnp.where(lane == entry, pltpu.roll(half, turn, 1), 0.0)


def sweep(stage, spans, nx, ny, nz, gz, get, get_inv, put, slab_q, sums):
    margin = 2 - stage
    start = SUB - margin
    tiles = ny // SUB + (margin > 0)
    own = subs_of((SUB, nz)) >= margin
    parts = [[], []]
    for tile in range(tiles):
        row = start + SUB * tile
        q_rows = slab_q[SUB * tile : SUB * tile + SUB]
        acc = [jnp.zeros((SUB, nz), F32) for _ in range(2)]

        def beside(x):
            return get(x, row - 1) + get(x, row + 1)

        for first, last in spans:
            s_low, s_mid = beside(first - 1), beside(first)
            v_low, v_mid = get(first - 1, row), get(first, row)
            for x in range(first, last):
                v_high, s_high = get(x + 1, row), beside(x + 1)
                across = v_low + v_high
                column = (PACK * x) % (2 * nz)
                half = q_rows[:, column // nz * nz : column // nz * nz + nz]
                rest = s_mid + across
                total = along_z(v_mid + 0.5 * rest, half, column % nz, gz) + rest + 0.5 * (s_low + s_high)
                if stage < 2:
                    after = total * get_inv(x, row)
                    put(x, row, after)
                if 0 <= x < nx:
                    acc[0] = acc[0] + v_mid * total
                    if stage < 2:
                        acc[1] = acc[1] + after * total
                v_low, v_mid, s_low, s_mid = v_mid, v_high, s_mid, s_high
        for k in range(2):
            parts[k].append(acc[k])
    for k in range(2 if stage < 2 else 1):
        part = parts[k]
        total = part[1]
        for other in part[2 : ny // SUB]:
            total = total + other
        total = total + (jnp.where(own, part[0], part[-1]) if margin else part[0])
        sums[2 * stage + k] = total


def inner_kernel(n_y, w0_ref, inv_ref, slab_ref, *refs):
    y_refs, (a_ref, i_ref, b_ref, c_ref, sum_ref, own_slab_ref, slabs_ref) = refs[:n_y], refs[n_y:]
    nx, ny, nz = w0_ref.shape
    gz = lax.axis_index("gz")
    for x in range(nx + 1):
        halos = halo_rows([ref[x] for ref in y_refs])
        for k in range(2):
            if x < nx:
                ref, own = (a_ref, i_ref)[k].at[x], (w0_ref, inv_ref)[k][x]
            else:
                ref, own = own_slab_ref.at[k], slab_ref[k]
            ref[:SUB] = halos[k]
            ref[SUB : SUB + ny] = own
            ref[SUB + ny :] = halos[k]
    for k in range(2):
        slabs_ref[3 * k] = own_slab_ref[k]
    sums = {}
    for stage in range(3):
        source, target = (a_ref, b_ref, c_ref)[stage], (b_ref, c_ref, None)[stage]
        start, size = SUB - 2 + stage, ny if stage == 2 else ny + SUB
        v = slabs_ref[stage, start : start + size]
        s = slabs_ref[stage, start - 1 : start - 1 + size] + slabs_ref[stage, start + 1 : start + 1 + size]
        q, after = slab_step(v, s, slabs_ref[3, start : start + size] if stage < 2 else None)
        if stage < 2:
            slabs_ref[stage + 1, start : start + size] = after

        def put(x, row, value):
            target[x, row : row + SUB] = value

        sweep(
            stage, [(1 + stage, nx - 1 - stage)], nx, ny, nz, gz,
            lambda x, row: source[x, row : row + SUB], lambda x, row: i_ref[x, row : row + SUB],
            put, q, sums,
        )
    for k in range(5):
        sum_ref[k] = sums[k]


def outer_kernel(
    n_y, column_total, after_ref, a_ref, i_ref, b_ref, c_ref, slab_ref, sum_ref, stat_ref, *refs
):
    x_refs, corner_refs = refs[1::-1], refs[2 : 2 + 2 * n_y]
    ea_ref, eb_ref, ec_ref, slabs_ref, total_ref, where_ref, ei_ref, si_ref = refs[2 + 2 * n_y :]
    nx, ny, nz = a_ref.shape[0], a_ref.shape[1] - 2 * SUB, a_ref.shape[2]
    ring = ny + SUB
    gz = lax.axis_index("gz")
    odd = lax.rem(lax.axis_index("gx"), 2) == 1

    def beyond(upper, read):
        there = has_partner("gx", 0) if upper else has_partner("gx", 1)
        swapped = has_partner("gx", 1) if upper else has_partner("gx", 0)
        first, second = read(0), read(1)
        if upper:
            return jnp.where(jnp.where(odd, swapped, there), jnp.where(odd, second, first), 0.0)
        return jnp.where(jnp.where(odd, swapped, there), jnp.where(odd, first, second), 0.0)

    def write(ref, at, own, halo):
        ref[at, :SUB] = halo
        ref[at, SUB : SUB + ny] = own
        ref[at, SUB + ny :] = halo

    lane_tile, lane = lanes_of((SUB, nz)), lanes_of((ny, nz))
    slab_parts = []
    for side, upper in enumerate((False, True)):
        tiles = [
            halo_rows([beyond(upper, lambda step: corner_refs[step * n_y + j][k]) for j in range(n_y)])
            for k in range(4)
        ]
        for k in range(3):
            write(ea_ref, 3 * side + k, beyond(upper, lambda step: x_refs[step][k]), tiles[k][0])
        for k in range(2):
            own = beyond(upper, lambda step: x_refs[step][3 + k])
            write(ei_ref, 2 * side + k, own, tiles[k if upper else k + 1][1])
        own = beyond(upper, lambda step: x_refs[step][5])

        def near(value, lanes, planes):
            return jnp.where(lanes < planes * PACK if upper else lanes >= nz - planes * PACK, value, 0.0)

        slab_parts.append((
            near(own, lane, 3), near(tiles[3][0], lane_tile, 3),
            near(pltpu.roll(own, nz // 2, 1), lane, 2), near(tiles[3][1], lane_tile, 2),
            own[0:1, COUNT_LANE : COUNT_LANE + 1],
        ))

    low, high = slab_parts
    for ref, k in ((slabs_ref, 0), (si_ref, 1)):
        ref[0, :, :nz] = slab_ref[k]
        ref[0, SUB : SUB + ny, nz:] = low[2 * k] + high[2 * k]
        ref[0, :SUB, nz:] = low[2 * k + 1] + high[2 * k + 1]
        ref[0, SUB + ny :, nz:] = low[2 * k + 1] + high[2 * k + 1]

    def reader(inside_ref, edge_ref, first, count):
        def get(x, row):
            if first <= x < nx - first:
                return inside_ref[x, row : row + SUB]
            at = x - (first - count) if x < first else x - (nx - first) + count
            return edge_ref[at, row : row + SUB]

        return get

    sums = {}
    for stage in range(3):
        get = reader((a_ref, b_ref, c_ref)[stage], (ea_ref, eb_ref, ec_ref)[stage], stage, 3)
        start, size = SUB - 2 + stage, ny if stage == 2 else ring
        v = slabs_ref[stage, start : start + size]
        s = slabs_ref[stage, start - 1 : start - 1 + size] + slabs_ref[stage, start + 1 : start + 1 + size]
        q, after = slab_step(v, s, si_ref[0, start : start + size] if stage < 2 else None)
        if stage < 2:
            slabs_ref[stage + 1, start : start + size] = after

        def put(x, row, value):
            edge_ref = (eb_ref, ec_ref)[stage]
            at = x - (stage - 2) if x < nx // 2 else x - (nx - 1 - stage) + 3
            edge_ref[at, row : row + SUB] = value

        sweep(
            stage, [(stage - 2, stage + 1), (nx - 1 - stage, nx + 2 - stage)], nx, ny, nz, gz,
            get, reader(i_ref, ei_ref, 0, 2), put, q, sums,
        )

    total_ref[0:1] = stat_ref[0, 0:1]
    for k in range(5):
        total_ref[k + 1 : k + 2] = jnp.sum(sums[k] + sum_ref[k], axis=0, keepdims=True)
    total_ref[6:8] = jnp.zeros((2, nz), F32)
    gx, n_x = lax.axis_index("gx"), lax.axis_size("gx")
    count = jnp.sum(stat_ref[1, 0:1], axis=1, keepdims=True)
    below, above = [part[4] for part in slab_parts]
    begin = jnp.where(
        gx == 0, 0.0,
        jnp.where(gx == 1, below, jnp.where(gx == n_x - 1, column_total - count, column_total - count - above)),
    )
    where_ref[0:1] = jnp.broadcast_to(begin, (1, nz))
    where_ref[1:2] = jnp.broadcast_to(count, (1, nz))
    where_ref[2:8] = jnp.zeros((6, nz), F32)


def shift_left(v, amount, lane):
    rows = v.shape[0]
    if amount < LANES:
        turned = pltpu.roll(v, LANES - amount, 1)
        below = pltpu.roll(turned, rows - 1, 0)
        return jnp.where(lane < LANES - amount, turned, below)
    return jnp.concatenate([v[amount // LANES :], v[: amount // LANES]], axis=0)


def plan_kernel(after_ref, label_ref, plan_ref):
    rows = label_ref.shape[0]
    lane = lanes_of((rows, LANES))
    row = subs_of((rows, LANES))
    heart = label_ref[...] == 1
    ones = heart.astype(jnp.bfloat16)
    upper = (subs_of((LANES, LANES)) < lanes_of((LANES, LANES))).astype(jnp.bfloat16)
    in_row = jnp.dot(ones, upper, preferred_element_type=F32)
    totals = jnp.dot(ones, jnp.ones((LANES, LANES), jnp.bfloat16), preferred_element_type=F32)
    lower = (subs_of((rows, rows)) > lanes_of((rows, rows))).astype(jnp.bfloat16)
    before = jnp.dot(lower, totals.astype(jnp.bfloat16), preferred_element_type=F32)
    rank = (in_row + before).astype(jnp.int32)
    way = jnp.where(heart, row * LANES + lane - rank, 0)
    plan = jnp.zeros((rows, LANES), jnp.int32)
    step = 1
    while step < rows * LANES:
        moving = jnp.where((way & step) != 0, way, 0)
        arriving = shift_left(moving, step, lane)
        plan = plan | (arriving & step)
        way = (way - moving) | arriving
        step *= 2
    plan_ref[...] = plan


def galerkin(t):
    g00, g01, g02, g12, g22 = t[0] - t[1], t[1] - t[2], t[2] - t[3], t[3] - t[4], t[4] - t[5]
    g11 = g02
    l10, l20 = g01 / g00, g02 / g00
    d1 = g11 - l10 * g01
    m21 = g12 - l20 * g01
    ok1 = d1 > 1e-6 * g11
    d1 = jnp.where(ok1, d1, 1.0)
    l21 = jnp.where(ok1, m21 / d1, 0.0)
    d2 = g22 - l20 * g02 - l21 * m21
    ok2 = ok1 & (d2 > 1e-6 * g22)
    d2 = jnp.where(ok2, d2, 1.0)
    y1 = t[1] - l10 * t[0]
    y2 = t[2] - l20 * t[0] - l21 * y1
    c2 = jnp.where(ok2, y2 / d2, 0.0)
    c1 = jnp.where(ok1, y1 / d1 - l21 * c2, 0.0)
    c0 = t[0] / g00 - l10 * c1 - l20 * c2
    return c0, c1, c2


def couple_kernel(stage, slot_rows, after_ref, inside_ref, edge_ref, slabs_ref, plan_ref, list_ref, value_ref):
    nx, nz = inside_ref.shape[0], inside_ref.shape[2]
    ny = inside_ref.shape[1] - 2 * SUB
    rows = nx * ny
    gz = lax.axis_index("gz")

    def get(x, row):
        if stage <= x < nx - stage:
            return inside_ref[x, row : row + SUB]
        return edge_ref[x - (stage - 3) if x < stage else x - (nx - stage) + 3, row : row + SUB]

    for tile in range(ny // SUB):
        row = SUB + SUB * tile
        slab = slabs_ref[stage, row : row + SUB, :nz]
        v_low, v_mid = get(-1, row), get(0, row)
        for x in range(nx):
            v_high = get(x + 1, row)
            beside = get(x, row - 1) + get(x, row + 1)
            at = ny * x + SUB * tile
            value_ref[at : at + SUB] = (
                along_z(v_mid, slab, PACK * x, gz) + beside + (v_low + v_high) - 6.0 * v_mid
            )
            v_low, v_mid = v_mid, v_high
    lane = lanes_of((rows, LANES))
    value = value_ref[...]
    plan = plan_ref[...]
    step = 1
    while step < rows * LANES:
        value = jnp.where((plan & step) != 0, shift_left(value, step, lane), value)
        step *= 2
    list_ref[...] = value[:slot_rows]


def add_kernel(a_ref, b_ref, after_ref, out_ref):
    out_ref[...] = a_ref[...] + b_ref[...]


def place_kernel(where_ref, total_ref, *refs):
    list_refs, out_refs, buf_ref = refs[:3], refs[3:-1], refs[-1]
    slot_rows = list_refs[0].shape[0]
    size = (out_refs[0].shape[0] - SUB) // 3
    gx = lax.axis_index("gx")
    offset = jnp.max(where_ref[0:1]).astype(jnp.int32)
    count = jnp.max(where_ref[1:2]).astype(jnp.int32)
    shape = (slot_rows, LANES)
    listed = subs_of(shape) * LANES + lanes_of(shape) < count
    inner = lax.rem(offset, LANES)
    kept = lanes_of((slot_rows + SUB, LANES)) >= inner
    buf_ref[...] = jnp.zeros_like(buf_ref)
    for k, list_ref in enumerate(list_refs):
        slots = jnp.where(listed, list_ref[...], 0.0)
        slots = jnp.concatenate([slots, jnp.zeros((SUB, LANES), F32)], axis=0)
        turned = pltpu.roll(slots, inner, 1)
        buf_ref[k, pl.ds(offset // LANES, slot_rows + SUB), :] = jnp.where(kept, turned, pltpu.roll(turned, 1, 0))
    for block, out_ref in enumerate(out_refs):
        begin = pl.multiple_of((gx ^ block) * size, SUB)
        for k in range(3):
            out_ref[k * size : k * size + size] = buf_ref[k, pl.ds(begin, size), :]
        out_ref[3 * size :] = total_ref[...]


def membrane_kernel(
    half_ref, slope_ref, tau_ref, cond_ref, rev_ref, after_ref, v_ref, gates_ref, cot_ref,
    base_ref, sum_ref, factor_ref, coef_ref,
):
    n_states, rows = gates_ref.shape[:2]
    v = v_ref[...]

    def state(g, carry):
        total, current = carry
        inv_slope = 1.0 / slope_ref[g]
        tau_base = tau_ref[g]
        scaled = (v - half_ref[g]) * inv_slope
        gate = gates_ref[g]
        cot = cot_ref[g]
        steady = 1.0 / (1.0 + jnp.exp(-scaled))
        bell = jnp.exp(-scaled * scaled)
        rate = TIME_STEP / (tau_base * (0.5 + bell))
        decay = jnp.exp(-rate)
        steady_slope = steady * (1.0 - steady)
        decay_slope = decay * rate * rate * ((tau_base / TIME_STEP) * bell * (-2.0 * scaled))
        change = (steady_slope * (1.0 - decay) + (gate - steady) * decay_slope) * inv_slope
        base_ref[g] = cot * decay
        coef_ref[0, pl.ds(g, 1)] = jnp.full((1, LANES), TIME_STEP * cond_ref[g])
        coef_ref[1, pl.ds(g, 1)] = jnp.full((1, LANES), rev_ref[g])
        return total + cot * change, current + cond_ref[g] * gate

    zero = jnp.zeros((rows, LANES), F32)
    total, current = lax.fori_loop(0, n_states, state, (zero, zero), unroll=2)
    sum_ref[...] = total
    factor_ref[...] = 1.0 - TIME_STEP * current


def finish_kernel(
    alone, coef_ref, vcot_ref, v_ref, sum_ref, factor_ref, base_ref, a_ref, b_ref, c_ref, eb_ref, ec_ref, *refs
):
    n_small, n_large = len(alone[0]), len(alone[1])
    own_ref, small_refs, large_refs = refs[0], refs[1 : 1 + n_small], refs[1 + n_small : 1 + n_small + n_large]
    x_ref, volt_ref, gate_ref = refs[1 + n_small + n_large :]
    size = (own_ref.shape[0] - SUB) // 3
    gx = lax.axis_index("gx")

    def is_one(flags):
        found = gx < 0
        for place, flag in enumerate(flags):
            if flag:
                found = found | (gx == place)
        return found

    total = own_ref[3 * size :]
    for flags, ref in zip(alone[0], small_refs):
        total = total + jnp.where(is_one(flags), ref[...], 0.0)
    for flags, ref in zip(alone[1], large_refs):
        total = total + jnp.where(is_one(flags), 0.0, ref[3 * size :])
    sums = jnp.sum(total, axis=1, keepdims=True)
    c0, c1, c2 = galerkin([jnp.broadcast_to(sums[k : k + 1], (1, LANES)) for k in range(6)])
    landed = jnp.zeros((size, LANES), F32)
    for k, c in enumerate((c0, c1, c2)):
        part = own_ref[k * size : k * size + size]
        for ref in large_refs:
            part = part + ref[k * size : k * size + size]
        landed = landed + c * part
    cot = vcot_ref[...] + landed
    v = v_ref[...]
    volt_ref[...] = cot * factor_ref[...] + sum_ref[...]
    for g in range(base_ref.shape[0]):
        gate_ref[g] = base_ref[g] - (coef_ref[0, g : g + 1] * cot) * (v - coef_ref[1, g : g + 1])
    nx, ny, nz = x_ref.shape
    own = slice(SUB, SUB + ny)
    for x in range(nx):
        w1 = b_ref[x, own] if 1 <= x < nx - 1 else eb_ref[2 if x == 0 else 3, own]
        w2 = c_ref[x, own] if 2 <= x < nx - 2 else ec_ref[x + 1 if x < 2 else x - (nx - 2) + 3, own]
        x_ref[x] = c0 * a_ref[x, own] + c1 * w1 + c2 * w2


def partners(axis, step):
    count = lax.axis_size(axis)
    if step == 0:
        return [i ^ 1 for i in range(count)]
    return [0] + [i + 1 if i % 2 else i - 1 for i in range(1, count - 1)] + [count - 1]


def swap(value, x_to=None, y_to=None):
    n_x, n_y, n_z = [lax.axis_size(axis) for axis in ("gx", "gy", "gz")]
    pairs = []
    for x in range(n_x):
        for y in range(n_y):
            to_x, to_y = x_to[x] if x_to else x, y_to[y] if y_to else y
            alone = (x_to and to_x == x) or (y_to and to_y == y)
            for z in range(n_z):
                to = (x, y, z ^ 1) if alone else (to_x, to_y, z)
                pairs.append(((x * n_y + y) * n_z + z, (to[0] * n_y + to[1]) * n_z + to[2]))
    return lax.ppermute(value, ("gx", "gy", "gz"), pairs)


def never_meet(count, k, slots, block):
    def apart(tile, owner):
        return owner * block >= (tile + 1) * slots or (owner + 1) * block <= count * block - (count - tile) * slots

    return [apart(i, i ^ k) and apart(i ^ k, i) for i in range(count)]


def local(
    potential_cot, damping, tissue_label, heart_index, voltage, gates, voltage_cot, gates_cot,
    half_voltage, gate_slope, tau_base, conductance, reversal,
):
    nx, ny, nz = potential_cot.shape
    rows = nx * ny
    ring = ny + SUB
    n_gx, n_gy = lax.axis_size("gx"), lax.axis_size("gy")
    n_states = gates.shape[0]
    block_rows = voltage.shape[1] // LANES
    slot_rows = heart_index.shape[3] // LANES
    block = shape_of(nx, ny, nz)
    flat = lambda a: a.reshape(rows, LANES)
    cells = lambda a: a.reshape(block_rows, LANES)
    states = lambda a: a.reshape(n_states, block_rows, LANES)

    w0, inv, packed, stat = call(
        start_kernel, (block, block, shape_of(2, ny, nz), shape_of(2, SUB, nz)), 3,
        specs=[HBM] * 3,
        scratch=[
            pltpu.VMEM((nx, ny, nz), F32), pltpu.VMEM((nx, ny, nz), F32), pltpu.VMEM((nx, ny, nz), jnp.int32),
            pltpu.SemaphoreType.DMA((3, 2)),
        ],
    )(in_hbm(potential_cot), in_hbm(damping), in_hbm(tissue_label))

    got = lax.ppermute(packed, "gz", [(0, 1), (1, 0)])
    plan = call(plan_kernel, jax.ShapeDtypeStruct((rows, LANES), jnp.int32), 2, cost=6_000_000)(
        stat, flat(tissue_label)
    )

    n_y = steps_of("gy")
    shapes = (
        (shape_of(2, ny, nz),) + (shape_of(nx + 1, SUB, nz),) * n_y + (shape_of(6, ny, nz),) * 2
        + (shape_of(4, SUB, nz),) * (2 * n_y)
    )
    slab, *faces = call(functools.partial(faces_kernel, n_y), shapes, 5)(w0, inv, packed, got, stat)
    along_y, along_x, across = faces[:n_y], faces[n_y : n_y + 2], faces[n_y + 2 :]
    y_to = [partners("gy", step) for step in range(n_y)]
    x_to = [partners("gx", step) for step in range(2)]
    along_y = [swap(face, y_to=y_to[j]) for j, face in enumerate(along_y)]
    along_x = [swap(face, x_to=x_to[i]) for i, face in enumerate(along_x)]
    across = [swap(face, x_to=x_to[k // n_y], y_to=y_to[k % n_y]) for k, face in enumerate(across)]

    tall = ring + SUB
    planes = shape_of(nx, tall, nz)
    edges = shape_of(6, tall, nz)
    in0, in_inv, in1, in2, in_sums, own_slab = call(
        functools.partial(inner_kernel, n_y),
        (planes,) * 4 + (shape_of(5, SUB, nz), shape_of(2, tall, nz)),
        3 + n_y,
        scratch=[pltpu.VMEM((4, tall, nz), F32)],
        cost=6_000_000,
    )(w0, inv, slab, *along_y)
    ends0, ends1, ends2, slabs, sums, where = call(
        functools.partial(outer_kernel, n_y, float(n_gx * voltage.shape[1])),
        (edges,) * 3 + (shape_of(3, tall, 2 * nz), shape_of(SUB, nz), shape_of(SUB, nz)),
        10 + 2 * n_y,
        scratch=[pltpu.VMEM((4, tall, nz), F32), pltpu.VMEM((1, tall, 2 * nz), F32)],
    )(plan, in0, in_inv, in1, in2, own_slab, in_sums, stat, *along_x[::-1], *across)

    def couple(stage, after, inside, ends):
        return call(
            functools.partial(couple_kernel, stage, slot_rows),
            shape_of(slot_rows, LANES),
            5,
            scratch=[pltpu.VMEM((rows, LANES), F32)],
            cost=6_000_000,
        )(after, inside, ends, slabs, plan)

    def add(value, axis, step, after):
        got = lax.ppermute(value, axis, [(i, i ^ step) for i in range(lax.axis_size(axis))])
        return call(add_kernel, shape_of(SUB, nz), 3)(value, got, after)

    list0 = couple(0, sums, in0, ends0)
    sums = add(sums, "gz", 1, list0)
    list1 = couple(1, sums, in1, ends1)
    list2 = couple(2, list1, in2, ends2)
    for step in [2**k for k in range(n_gy.bit_length() - 1)]:
        sums = add(sums, "gy", step, list2)
    if n_gx > 4:
        counts = lax.all_gather(jnp.sum(stat[1, 0]), "gx")
        begin = jnp.sum(jnp.where(jnp.arange(n_gx) < lax.axis_index("gx"), counts, 0.0))
        where = where.at[0].set(begin)
    blocks = call(
        place_kernel,
        (shape_of(3 * block_rows + SUB, LANES),) * n_gx,
        5,
        scratch=[pltpu.VMEM((3, n_gx * block_rows + slot_rows + SUB, LANES), F32)],
    )(where, sums, list0, list1, list2)
    apart = {k: never_meet(n_gx, k, slot_rows, block_rows) for k in range(1, n_gx)}
    small, meets = [], []
    for k in range(1, n_gx):
        if any(apart[k]):
            small.append(swap(sums, x_to=[i ^ k if apart[k][i] else i for i in range(n_gx)]))
        meets.append(not all(apart[k]))
    order = [k for k in [2, 3, 1] + list(range(4, n_gx)) if k < n_gx and meets[k - 1]]
    large = [swap(blocks[k], x_to=[i if apart[k][i] else i ^ k for i in range(n_gx)]) for k in order]
    alone = [[apart[k] for k in range(1, n_gx) if any(apart[k])], [apart[k] for k in order]]

    base, total_change, factor, state_coefs = call(
        membrane_kernel,
        (
            shape_of(n_states, block_rows, LANES), shape_of(block_rows, LANES), shape_of(block_rows, LANES),
            shape_of(2, n_states, LANES),
        ),
        9,
        specs=[SMEM] * 5 + [VMEM] * 4,
        cost=6_000_000,
    )(
        half_voltage, gate_slope, tau_base, conductance, reversal,
        blocks[0], cells(voltage), states(gates), states(gates_cot),
    )
    solution, volt_grad, gate_grad = call(
        functools.partial(finish_kernel, alone),
        (block, shape_of(block_rows, LANES), shape_of(n_states, block_rows, LANES)),
        12 + len(small) + len(large),
    )(
        state_coefs, cells(voltage_cot), cells(voltage), total_change, factor, base,
        in0, in1, in2, ends1, ends2, blocks[0], *small, *large,
    )
    return solution, volt_grad.reshape(voltage.shape), gate_grad.reshape(gates.shape)


def solution(mesh):
    grid = P(("groups", "gx"), "gy", "gz")
    cells = P(("groups", "gy", "gz"), "gx")
    states = P(None, ("groups", "gy", "gz"), "gx")
    in_specs = (
        grid, grid, grid, P(("groups", "gx"), "gy", "gz", None), cells, states, cells, states,
        P(), P(), P(), P(), P(),
    )
    return jax.shard_map(
        local, mesh=mesh, in_specs=in_specs, out_specs=(grid, cells, states), check_vma=False
    )
```

```python
import functools

import jax
import jax.numpy as jnp
from jax import lax
from jax.experimental import pallas as pl
from jax.experimental.pallas import tpu as pltpu
from jax.sharding import PartitionSpec as P

TIME_STEP = 0.5
LANES = 128
SUB = 8
PACK = 8
COUNT_LANE = 4 * PACK
F32 = jnp.float32

VMEM = pl.BlockSpec(memory_space=pltpu.VMEM)
SMEM = pl.BlockSpec(memory_space=pltpu.SMEM)
HBM = pl.BlockSpec(memory_space=pltpu.HBM)


def shape_of(*dims):
    return jax.ShapeDtypeStruct(dims, F32)


def call(kernel, out_shape, n_in, specs=None, outs=None, scratch=(), cost=2_000_000, limit=32):
    return pl.pallas_call(
        kernel,
        out_shape=out_shape,
        in_specs=specs if specs is not None else [VMEM] * n_in,
        out_specs=outs if outs is not None else jax.tree.map(lambda _: VMEM, out_shape),
        scratch_shapes=list(scratch),
        compiler_params=pltpu.CompilerParams(vmem_limit_bytes=limit * 1024 * 1024),
        cost_estimate=pl.CostEstimate(flops=cost, bytes_accessed=cost, transcendentals=0),
    )


def in_hbm(array):
    return pltpu.with_memory_space_constraint(array, pltpu.HBM)


def lanes_of(shape):
    return lax.broadcasted_iota(jnp.int32, shape, len(shape) - 1)


def subs_of(shape):
    return lax.broadcasted_iota(jnp.int32, shape, len(shape) - 2)


def start_kernel(
    right_hbm, damping_hbm, label_hbm, w0_ref, inv_ref, pack_ref, stat_ref, right_ref, damping_ref, label_ref, sems
):
    nx, ny, nz = right_ref.shape
    parts = sems.shape[1]
    size = nx // parts
    copies = []
    for part in range(parts):
        here = pl.ds(part * size, size)
        for k, (source, target) in enumerate(
            ((right_hbm, right_ref), (damping_hbm, damping_ref), (label_hbm, label_ref))
        ):
            copies.append(pltpu.make_async_copy(source.at[here], target.at[here], sems.at[k, part]))
            copies[-1].start()
    gz = lax.axis_index("gz")
    lane = lanes_of((ny, nz))
    packed_w = jnp.zeros((ny, nz), F32)
    packed_i = jnp.zeros((ny, nz), F32)
    energy = jnp.zeros((ny, nz), F32)
    cells = jnp.zeros((ny, nz), F32)
    for x in range(nx):
        if x % size == 0:
            for k in range(3):
                copies[3 * (x // size) + k].wait()
        label = label_ref[x].astype(F32)
        right = right_ref[x]
        inv = 1.0 / (12.0 + damping_ref[x] * (1.0 + 3.0 * label))
        w0 = right * inv
        w0_ref[x] = w0
        inv_ref[x] = inv
        energy = energy + right * w0
        cells = cells + label
        turn = (PACK * x + 3) % nz
        begin = PACK * x + 3 * gz
        chosen = (lane >= begin) & (lane < begin + 3)
        packed_w = jnp.where(chosen, pltpu.roll(w0, turn, 1), packed_w)
        packed_i = jnp.where(chosen, pltpu.roll(inv, turn, 1), packed_i)
    pack_ref[0] = packed_w
    pack_ref[1] = packed_i
    stat_ref[0] = jnp.broadcast_to(jnp.sum(energy, axis=0, keepdims=True), (SUB, nz))
    stat_ref[1] = jnp.broadcast_to(jnp.sum(cells, axis=0, keepdims=True), (SUB, nz))


def steps_of(axis):
    return 1 if lax.axis_size(axis) == 2 else 2


def upper_in(axis, step):
    return lax.rem(lax.axis_index(axis), 2) == step


def has_partner(axis, step):
    here = lax.axis_index(axis)
    return jnp.where(upper_in(axis, step), here < lax.axis_size(axis) - 1, here > 0)


def unpack_rows(tile, step):
    sub = subs_of(tile.shape)
    up, there = upper_in("gy", step), has_partner("gy", step)
    depth = jnp.where(there, jnp.where(up, SUB - 1 - sub, sub), -1)
    return jnp.where(depth >= 5, tile, 0.0), jnp.where(depth >= 6, pltpu.roll(tile, 4, 0), 0.0)


def halo_rows(tiles):
    w_tile, i_tile = unpack_rows(tiles[0], 0)
    for step, tile in enumerate(tiles[1:], 1):
        w_more, i_more = unpack_rows(tile, step)
        w_tile, i_tile = w_tile + w_more, i_tile + i_more
    return w_tile, i_tile


def faces_kernel(n_y, w0_ref, inv_ref, own_ref, got_ref, stat_ref, slab_ref, *refs):
    y_refs, x_refs, edge_refs = refs[:n_y], refs[n_y : n_y + 2], refs[n_y + 2 :]
    nx, ny, nz = w0_ref.shape
    sub = subs_of((SUB, nz))
    lane = lanes_of((ny, nz))
    slab_ref[...] = own_ref[...] + got_ref[...]
    for step, face_ref in enumerate(y_refs):
        up = upper_in("gy", step)
        keep_w = jnp.where(up, sub, SUB - 1 - sub) >= 5
        for x in range(nx + 1):
            w_rows, i_rows = (w0_ref.at[x], inv_ref.at[x]) if x < nx else (slab_ref.at[0], slab_ref.at[1])
            w_face = jnp.where(up, w_rows[ny - SUB :], w_rows[:SUB])
            i_face = jnp.where(up, i_rows[ny - SUB :], i_rows[:SUB])
            face_ref[x] = jnp.where(keep_w, w_face, pltpu.roll(i_face, 4, 0))
    cells = jnp.sum(stat_ref[1, 0:1], axis=1, keepdims=True)
    slab_w = slab_ref[0]
    half = pltpu.roll(slab_ref[1], nz // 2, 1)
    up_slab = jnp.where(lane >= nz - 3 * PACK, slab_w, half)
    down_slab = jnp.where(lane < 3 * PACK, slab_w, half)
    for step, face_ref in enumerate(x_refs):
        up = upper_in("gx", step)
        first = jnp.where(up, nx - 3, 0)
        for k in range(3):
            face_ref[k] = w0_ref[first + k]
        for k in range(2):
            face_ref[3 + k] = inv_ref[jnp.where(up, nx - 2, 0) + k]
        face_ref[5] = jnp.where(lane == COUNT_LANE, cells, jnp.where(up, up_slab, down_slab))
        for y_step, y_ref in enumerate(y_refs):
            edge_ref = edge_refs[step * n_y + y_step]
            for k in range(3):
                edge_ref[k] = y_ref[first + k]
            edge_ref[3] = y_ref[nx]


def slab_step(v, s, inv):
    width = v.shape[1]
    across = pltpu.roll(v, PACK, 1) + pltpu.roll(v, width - PACK, 1)
    q = v + 0.5 * (s + across)
    if inv is None:
        return q, None
    total = (
        pltpu.roll(q, 1, 1) + pltpu.roll(q, width - 1, 1) + s + across
        + 0.5 * (pltpu.roll(s, PACK, 1) + pltpu.roll(s, width - PACK, 1))
    )
    return q, total * inv


def along_z(q, half, column, gz):
    nz = q.shape[1]
    lane = lanes_of(q.shape)
    entry = (nz - 1) * (1 - gz)
    turn = lax.rem(entry - (column + 3 - gz) + 2 * nz, nz)
    up = jnp.where(lane == nz - 1, 0.0, pltpu.roll(q, nz - 1, 1))
    down = jnp.where(lane == 0, 0.0, pltpu.roll(q, 1, 1))
    return up + down + jnp.where(lane == entry, pltpu.roll(half, turn, 1), 0.0)


def sweep(stage, spans, nx, ny, nz, gz, get, get_inv, put, slab_q, sums):
    margin = 2 - stage
    start = SUB - margin
    tiles = ny // SUB + (margin > 0)
    own = subs_of((SUB, nz)) >= margin
    parts = [[], []]
    for tile in range(tiles):
        row = start + SUB * tile
        q_rows = slab_q[SUB * tile : SUB * tile + SUB]
        acc = [jnp.zeros((SUB, nz), F32) for _ in range(2)]

        def beside(x):
            return get(x, row - 1) + get(x, row + 1)

        for first, last in spans:
            s_low, s_mid = beside(first - 1), beside(first)
            v_low, v_mid = get(first - 1, row), get(first, row)
            for x in range(first, last):
                v_high, s_high = get(x + 1, row), beside(x + 1)
                across = v_low + v_high
                column = (PACK * x) % (2 * nz)
                half = q_rows[:, column // nz * nz : column // nz * nz + nz]
                rest = s_mid + across
                total = along_z(v_mid + 0.5 * rest, half, column % nz, gz) + rest + 0.5 * (s_low + s_high)
                if stage < 2:
                    after = total * get_inv(x, row)
                    put(x, row, after)
                if 0 <= x < nx:
                    acc[0] = acc[0] + v_mid * total
                    if stage < 2:
                        acc[1] = acc[1] + after * total
                v_low, v_mid, s_low, s_mid = v_mid, v_high, s_mid, s_high
        for k in range(2):
            parts[k].append(acc[k])
    for k in range(2 if stage < 2 else 1):
        part = parts[k]
        total = part[1]
        for other in part[2 : ny // SUB]:
            total = total + other
        total = total + (jnp.where(own, part[0], part[-1]) if margin else part[0])
        sums[2 * stage + k] = total


def inner_kernel(n_y, w0_ref, inv_ref, slab_ref, *refs):
    y_refs, (a_ref, i_ref, b_ref, c_ref, sum_ref, own_slab_ref, slabs_ref) = refs[:n_y], refs[n_y:]
    nx, ny, nz = w0_ref.shape
    gz = lax.axis_index("gz")
    for x in range(nx + 1):
        halos = halo_rows([ref[x] for ref in y_refs])
        for k in range(2):
            if x < nx:
                ref, own = (a_ref, i_ref)[k].at[x], (w0_ref, inv_ref)[k][x]
            else:
                ref, own = own_slab_ref.at[k], slab_ref[k]
            ref[:SUB] = halos[k]
            ref[SUB : SUB + ny] = own
            ref[SUB + ny :] = halos[k]
    for k in range(2):
        slabs_ref[3 * k] = own_slab_ref[k]
    sums = {}
    for stage in range(3):
        source, target = (a_ref, b_ref, c_ref)[stage], (b_ref, c_ref, None)[stage]
        start, size = SUB - 2 + stage, ny if stage == 2 else ny + SUB
        v = slabs_ref[stage, start : start + size]
        s = slabs_ref[stage, start - 1 : start - 1 + size] + slabs_ref[stage, start + 1 : start + 1 + size]
        q, after = slab_step(v, s, slabs_ref[3, start : start + size] if stage < 2 else None)
        if stage < 2:
            slabs_ref[stage + 1, start : start + size] = after

        def put(x, row, value):
            target[x, row : row + SUB] = value

        sweep(
            stage, [(1 + stage, nx - 1 - stage)], nx, ny, nz, gz,
            lambda x, row: source[x, row : row + SUB], lambda x, row: i_ref[x, row : row + SUB],
            put, q, sums,
        )
    for k in range(5):
        sum_ref[k] = sums[k]


def outer_kernel(
    n_y, column_total, after_ref, a_ref, i_ref, b_ref, c_ref, slab_ref, sum_ref, stat_ref, *refs
):
    x_refs, corner_refs = refs[:2], refs[2 : 2 + 2 * n_y]
    ea_ref, eb_ref, ec_ref, slabs_ref, total_ref, where_ref, ei_ref, si_ref = refs[2 + 2 * n_y :]
    nx, ny, nz = a_ref.shape[0], a_ref.shape[1] - 2 * SUB, a_ref.shape[2]
    ring = ny + SUB
    gz = lax.axis_index("gz")
    odd = lax.rem(lax.axis_index("gx"), 2) == 1

    def beyond(upper, read):
        there = has_partner("gx", 0) if upper else has_partner("gx", 1)
        swapped = has_partner("gx", 1) if upper else has_partner("gx", 0)
        first, second = read(0), read(1)
        if upper:
            return jnp.where(jnp.where(odd, swapped, there), jnp.where(odd, second, first), 0.0)
        return jnp.where(jnp.where(odd, swapped, there), jnp.where(odd, first, second), 0.0)

    def write(ref, at, own, halo):
        ref[at, :SUB] = halo
        ref[at, SUB : SUB + ny] = own
        ref[at, SUB + ny :] = halo

    lane_tile, lane = lanes_of((SUB, nz)), lanes_of((ny, nz))
    slab_parts = []
    for side, upper in enumerate((False, True)):
        tiles = [
            halo_rows([beyond(upper, lambda step: corner_refs[step * n_y + j][k]) for j in range(n_y)])
            for k in range(4)
        ]
        for k in range(3):
            write(ea_ref, 3 * side + k, beyond(upper, lambda step: x_refs[step][k]), tiles[k][0])
        for k in range(2):
            own = beyond(upper, lambda step: x_refs[step][3 + k])
            write(ei_ref, 2 * side + k, own, tiles[k if upper else k + 1][1])
        own = beyond(upper, lambda step: x_refs[step][5])

        def near(value, lanes, planes):
            return jnp.where(lanes < planes * PACK if upper else lanes >= nz - planes * PACK, value, 0.0)

        slab_parts.append((
            near(own, lane, 3), near(tiles[3][0], lane_tile, 3),
            near(pltpu.roll(own, nz // 2, 1), lane, 2), near(tiles[3][1], lane_tile, 2),
            own[0:1, COUNT_LANE : COUNT_LANE + 1],
        ))

    low, high = slab_parts
    for ref, k in ((slabs_ref, 0), (si_ref, 1)):
        ref[0, :, :nz] = slab_ref[k]
        ref[0, SUB : SUB + ny, nz:] = low[2 * k] + high[2 * k]
        ref[0, :SUB, nz:] = low[2 * k + 1] + high[2 * k + 1]
        ref[0, SUB + ny :, nz:] = low[2 * k + 1] + high[2 * k + 1]

    def reader(inside_ref, edge_ref, first, count):
        def get(x, row):
            if first <= x < nx - first:
                return inside_ref[x, row : row + SUB]
            at = x - (first - count) if x < first else x - (nx - first) + count
            return edge_ref[at, row : row + SUB]

        return get

    sums = {}
    for stage in range(3):
        get = reader((a_ref, b_ref, c_ref)[stage], (ea_ref, eb_ref, ec_ref)[stage], stage, 3)
        start, size = SUB - 2 + stage, ny if stage == 2 else ring
        v = slabs_ref[stage, start : start + size]
        s = slabs_ref[stage, start - 1 : start - 1 + size] + slabs_ref[stage, start + 1 : start + 1 + size]
        q, after = slab_step(v, s, si_ref[0, start : start + size] if stage < 2 else None)
        if stage < 2:
            slabs_ref[stage + 1, start : start + size] = after

        def put(x, row, value):
            edge_ref = (eb_ref, ec_ref)[stage]
            at = x - (stage - 2) if x < nx // 2 else x - (nx - 1 - stage) + 3
            edge_ref[at, row : row + SUB] = value

        sweep(
            stage, [(stage - 2, stage + 1), (nx - 1 - stage, nx + 2 - stage)], nx, ny, nz, gz,
            get, reader(i_ref, ei_ref, 0, 2), put, q, sums,
        )

    total_ref[0:1] = stat_ref[0, 0:1]
    for k in range(5):
        total_ref[k + 1 : k + 2] = jnp.sum(sums[k] + sum_ref[k], axis=0, keepdims=True)
    total_ref[6:8] = jnp.zeros((2, nz), F32)
    gx, n_x = lax.axis_index("gx"), lax.axis_size("gx")
    count = jnp.sum(stat_ref[1, 0:1], axis=1, keepdims=True)
    below, above = [part[4] for part in slab_parts]
    begin = jnp.where(
        gx == 0, 0.0,
        jnp.where(gx == 1, below, jnp.where(gx == n_x - 1, column_total - count, column_total - count - above)),
    )
    where_ref[0:1] = jnp.broadcast_to(begin, (1, nz))
    where_ref[1:2] = jnp.broadcast_to(count, (1, nz))
    where_ref[2:8] = jnp.zeros((6, nz), F32)


def shift_up(v, amount):
    if amount < SUB:
        return pltpu.roll(v, v.shape[0] - amount, 0)
    return jnp.concatenate([v[amount:], v[:amount]], axis=0)


def plan_kernel(after_ref, label_ref, index_ref, plan_ref, lane_ref):
    rows, slot_rows = label_ref.shape[0], index_ref.shape[0]
    wide = -(-(slot_rows + 1) // LANES) * LANES
    shape = (rows, LANES)
    lane, row = lanes_of(shape), subs_of(shape)
    ones = (label_ref[...] == 1).astype(jnp.bfloat16)
    totals = jnp.dot(ones, jnp.ones((LANES, LANES), jnp.bfloat16), preferred_element_type=F32)
    lower = (subs_of((rows, rows)) > lanes_of((rows, rows))).astype(jnp.bfloat16)
    before = jnp.dot(lower, totals.astype(jnp.bfloat16), preferred_element_type=F32).astype(jnp.int32)
    target, first = lax.div(before, LANES), lax.rem(before, LANES)
    listed = jnp.concatenate(
        [lax.rem(index_ref[...], LANES).astype(F32), jnp.zeros((wide - slot_rows, LANES), F32)], axis=0
    ).astype(jnp.bfloat16)
    spread = jnp.concatenate([target] * (wide // LANES), axis=1)
    place = lanes_of((rows, wide))
    here = jnp.dot((spread == place).astype(jnp.bfloat16), listed, preferred_element_type=F32)
    after = jnp.dot((spread + 1 == place).astype(jnp.bfloat16), listed, preferred_element_type=F32)
    lane_ref[...] = jnp.where(lane >= first, here, after).astype(jnp.int32)
    wrapped = (lane < first).astype(jnp.int32)
    filled = lane - first + LANES * wrapped < totals.astype(jnp.int32)
    way = jnp.where(filled, row - target - wrapped, 0)
    plan = jnp.zeros(shape, jnp.int32)
    step = 1
    while step < rows:
        moving = jnp.where((way & step) != 0, way, 0)
        arriving = shift_up(moving, step)
        plan = plan | (arriving & step)
        way = (way - moving) | arriving
        step *= 2
    plan_ref[...] = plan


def galerkin(t):
    g00, g01, g02, g12, g22 = t[0] - t[1], t[1] - t[2], t[2] - t[3], t[3] - t[4], t[4] - t[5]
    g11 = g02
    l10, l20 = g01 / g00, g02 / g00
    d1 = g11 - l10 * g01
    m21 = g12 - l20 * g01
    ok1 = d1 > 1e-6 * g11
    d1 = jnp.where(ok1, d1, 1.0)
    l21 = jnp.where(ok1, m21 / d1, 0.0)
    d2 = g22 - l20 * g02 - l21 * m21
    ok2 = ok1 & (d2 > 1e-6 * g22)
    d2 = jnp.where(ok2, d2, 1.0)
    y1 = t[1] - l10 * t[0]
    y2 = t[2] - l20 * t[0] - l21 * y1
    c2 = jnp.where(ok2, y2 / d2, 0.0)
    c1 = jnp.where(ok1, y1 / d1 - l21 * c2, 0.0)
    c0 = t[0] / g00 - l10 * c1 - l20 * c2
    return c0, c1, c2


def couple_kernel(
    stage, slot_rows, after_ref, inside_ref, edge_ref, slabs_ref, plan_ref, lane_ref, list_ref, value_ref
):
    nx, nz = inside_ref.shape[0], inside_ref.shape[2]
    ny = inside_ref.shape[1] - 2 * SUB
    rows = nx * ny
    gz = lax.axis_index("gz")

    def get(x, row):
        if stage <= x < nx - stage:
            return inside_ref[x, row : row + SUB]
        return edge_ref[x - (stage - 3) if x < stage else x - (nx - stage) + 3, row : row + SUB]

    for tile in range(ny // SUB):
        row = SUB + SUB * tile
        slab = slabs_ref[stage, row : row + SUB, :nz]
        v_low, v_mid = get(-1, row), get(0, row)
        for x in range(nx):
            v_high = get(x + 1, row)
            beside = get(x, row - 1) + get(x, row + 1)
            at = ny * x + SUB * tile
            value_ref[at : at + SUB] = (
                along_z(v_mid, slab, PACK * x, gz) + beside + (v_low + v_high) - 6.0 * v_mid
            )
            v_low, v_mid = v_mid, v_high
    value = jnp.take_along_axis(value_ref[...], lane_ref[...], axis=1)
    plan = plan_ref[...]
    step = 1
    while step < rows:
        value = jnp.where((plan & step) != 0, shift_up(value, step), value)
        step *= 2
    list_ref[...] = value[:slot_rows]


def add_kernel(a_ref, b_ref, after_ref, out_ref):
    out_ref[...] = a_ref[...] + b_ref[...]


def place_kernel(where_ref, total_ref, *refs):
    list_refs, out_refs, buf_ref = refs[:3], refs[3:-1], refs[-1]
    slot_rows = list_refs[0].shape[0]
    size = (out_refs[0].shape[0] - SUB) // 3
    gx = lax.axis_index("gx")
    offset = jnp.max(where_ref[0:1]).astype(jnp.int32)
    count = jnp.max(where_ref[1:2]).astype(jnp.int32)
    shape = (slot_rows, LANES)
    listed = subs_of(shape) * LANES + lanes_of(shape) < count
    inner = lax.rem(offset, LANES)
    kept = lanes_of((slot_rows + SUB, LANES)) >= inner
    buf_ref[...] = jnp.zeros_like(buf_ref)
    for k, list_ref in enumerate(list_refs):
        slots = jnp.where(listed, list_ref[...], 0.0)
        slots = jnp.concatenate([slots, jnp.zeros((SUB, LANES), F32)], axis=0)
        turned = pltpu.roll(slots, inner, 1)
        buf_ref[k, pl.ds(offset // LANES, slot_rows + SUB), :] = jnp.where(kept, turned, pltpu.roll(turned, 1, 0))
    for block, out_ref in enumerate(out_refs):
        begin = pl.multiple_of((gx ^ block) * size, SUB)
        for k in range(3):
            out_ref[k * size : k * size + size] = buf_ref[k, pl.ds(begin, size), :]
        out_ref[3 * size :] = total_ref[...]


def membrane_kernel(
    half_ref, slope_ref, tau_ref, cond_ref, rev_ref, after_ref, v_ref, gates_ref, cot_ref,
    base_ref, sum_ref, factor_ref, coef_ref,
):
    n_states, rows = gates_ref.shape[:2]
    v = v_ref[...]

    def state(g, carry):
        total, current = carry
        inv_slope = 1.0 / slope_ref[g]
        tau_base = tau_ref[g]
        scaled = (v - half_ref[g]) * inv_slope
        gate = gates_ref[g]
        cot = cot_ref[g]
        steady = 1.0 / (1.0 + jnp.exp(-scaled))
        bell = jnp.exp(-scaled * scaled)
        rate = TIME_STEP / (tau_base * (0.5 + bell))
        decay = jnp.exp(-rate)
        steady_slope = steady * (1.0 - steady)
        decay_slope = decay * rate * rate * ((tau_base / TIME_STEP) * bell * (-2.0 * scaled))
        change = (steady_slope * (1.0 - decay) + (gate - steady) * decay_slope) * inv_slope
        base_ref[g] = cot * decay
        coef_ref[0, pl.ds(g, 1)] = jnp.full((1, LANES), TIME_STEP * cond_ref[g])
        coef_ref[1, pl.ds(g, 1)] = jnp.full((1, LANES), rev_ref[g])
        return total + cot * change, current + cond_ref[g] * gate

    zero = jnp.zeros((rows, LANES), F32)
    total, current = lax.fori_loop(0, n_states, state, (zero, zero), unroll=2)
    sum_ref[...] = total
    factor_ref[...] = 1.0 - TIME_STEP * current


def finish_kernel(
    alone, coef_ref, vcot_ref, v_ref, sum_ref, factor_ref, base_ref, a_ref, b_ref, c_ref, eb_ref, ec_ref, *refs
):
    n_small, n_large = len(alone[0]), len(alone[1])
    own_ref, small_refs, large_refs = refs[0], refs[1 : 1 + n_small], refs[1 + n_small : 1 + n_small + n_large]
    x_ref, volt_ref, gate_ref = refs[1 + n_small + n_large :]
    size = (own_ref.shape[0] - SUB) // 3
    gx = lax.axis_index("gx")

    def is_one(flags):
        found = gx < 0
        for place, flag in enumerate(flags):
            if flag:
                found = found | (gx == place)
        return found

    total = own_ref[3 * size :]
    for flags, ref in zip(alone[0], small_refs):
        total = total + jnp.where(is_one(flags), ref[...], 0.0)
    for flags, ref in zip(alone[1], large_refs):
        total = total + jnp.where(is_one(flags), 0.0, ref[3 * size :])
    sums = jnp.sum(total, axis=1, keepdims=True)
    c0, c1, c2 = galerkin([jnp.broadcast_to(sums[k : k + 1], (1, LANES)) for k in range(6)])
    landed = jnp.zeros((size, LANES), F32)
    for k, c in enumerate((c0, c1, c2)):
        part = own_ref[k * size : k * size + size]
        for ref in large_refs:
            part = part + ref[k * size : k * size + size]
        landed = landed + c * part
    cot = vcot_ref[...] + landed
    v = v_ref[...]
    volt_ref[...] = cot * factor_ref[...] + sum_ref[...]
    for g in range(base_ref.shape[0]):
        gate_ref[g] = base_ref[g] - (coef_ref[0, g : g + 1] * cot) * (v - coef_ref[1, g : g + 1])
    nx, ny, nz = x_ref.shape
    own = slice(SUB, SUB + ny)
    for x in range(nx):
        w1 = b_ref[x, own] if 1 <= x < nx - 1 else eb_ref[2 if x == 0 else 3, own]
        w2 = c_ref[x, own] if 2 <= x < nx - 2 else ec_ref[x + 1 if x < 2 else x - (nx - 2) + 3, own]
        x_ref[x] = c0 * a_ref[x, own] + c1 * w1 + c2 * w2


def partners(axis, step):
    count = lax.axis_size(axis)
    if step == 0:
        return [i ^ 1 for i in range(count)]
    return [0] + [i + 1 if i % 2 else i - 1 for i in range(1, count - 1)] + [count - 1]


def swap(value, x_to=None, y_to=None):
    n_x, n_y, n_z = [lax.axis_size(axis) for axis in ("gx", "gy", "gz")]
    pairs = []
    for x in range(n_x):
        for y in range(n_y):
            to_x, to_y = x_to[x] if x_to else x, y_to[y] if y_to else y
            alone = (x_to and to_x == x) or (y_to and to_y == y)
            for z in range(n_z):
                to = (x, y, z ^ 1) if alone else (to_x, to_y, z)
                pairs.append(((x * n_y + y) * n_z + z, (to[0] * n_y + to[1]) * n_z + to[2]))
    return lax.ppermute(value, ("gx", "gy", "gz"), pairs)


def never_meet(count, k, slots, block):
    def apart(tile, owner):
        return owner * block >= (tile + 1) * slots or (owner + 1) * block <= count * block - (count - tile) * slots

    return [apart(i, i ^ k) and apart(i ^ k, i) for i in range(count)]


def local(
    potential_cot, damping, tissue_label, heart_index, voltage, gates, voltage_cot, gates_cot,
    half_voltage, gate_slope, tau_base, conductance, reversal,
):
    nx, ny, nz = potential_cot.shape
    rows = nx * ny
    ring = ny + SUB
    n_gx, n_gy = lax.axis_size("gx"), lax.axis_size("gy")
    n_states = gates.shape[0]
    block_rows = voltage.shape[1] // LANES
    slot_rows = heart_index.shape[3] // LANES
    block = shape_of(nx, ny, nz)
    flat = lambda a: a.reshape(rows, LANES)
    cells = lambda a: a.reshape(block_rows, LANES)
    states = lambda a: a.reshape(n_states, block_rows, LANES)

    w0, inv, packed, stat = call(
        start_kernel, (block, block, shape_of(2, ny, nz), shape_of(2, SUB, nz)), 3,
        specs=[HBM] * 3,
        scratch=[
            pltpu.VMEM((nx, ny, nz), F32), pltpu.VMEM((nx, ny, nz), F32), pltpu.VMEM((nx, ny, nz), jnp.int32),
            pltpu.SemaphoreType.DMA((3, 2)),
        ],
    )(in_hbm(potential_cot), in_hbm(damping), in_hbm(tissue_label))

    got = lax.ppermute(packed, "gz", [(0, 1), (1, 0)])
    cells_shape = jax.ShapeDtypeStruct((rows, LANES), jnp.int32)
    plan, lanes = call(plan_kernel, (cells_shape, cells_shape), 3, cost=6_000_000)(
        stat, flat(tissue_label), heart_index.reshape(slot_rows, LANES)
    )

    n_y = steps_of("gy")
    shapes = (
        (shape_of(2, ny, nz),) + (shape_of(nx + 1, SUB, nz),) * n_y + (shape_of(6, ny, nz),) * 2
        + (shape_of(4, SUB, nz),) * (2 * n_y)
    )
    slab, *faces = call(functools.partial(faces_kernel, n_y), shapes, 5)(w0, inv, packed, got, stat)
    along_y, along_x, across = faces[:n_y], faces[n_y : n_y + 2], faces[n_y + 2 :]
    y_to = [partners("gy", step) for step in range(n_y)]
    x_to = [partners("gx", step) for step in range(2)]
    along_y = [swap(face, y_to=y_to[j]) for j, face in enumerate(along_y)]
    along_x = [swap(face, x_to=x_to[i]) for i, face in enumerate(along_x)]
    across = [swap(face, x_to=x_to[k // n_y], y_to=y_to[k % n_y]) for k, face in enumerate(across)]

    tall = ring + SUB
    planes = shape_of(nx, tall, nz)
    edges = shape_of(6, tall, nz)
    in0, in_inv, in1, in2, in_sums, own_slab = call(
        functools.partial(inner_kernel, n_y),
        (planes,) * 4 + (shape_of(5, SUB, nz), shape_of(2, tall, nz)),
        3 + n_y,
        scratch=[pltpu.VMEM((4, tall, nz), F32)],
        cost=6_000_000,
    )(w0, inv, slab, *along_y)
    ends0, ends1, ends2, slabs, sums, where = call(
        functools.partial(outer_kernel, n_y, float(n_gx * voltage.shape[1])),
        (edges,) * 3 + (shape_of(3, tall, 2 * nz), shape_of(SUB, nz), shape_of(SUB, nz)),
        10 + 2 * n_y,
        scratch=[pltpu.VMEM((4, tall, nz), F32), pltpu.VMEM((1, tall, 2 * nz), F32)],
    )(plan, in0, in_inv, in1, in2, own_slab, in_sums, stat, *along_x, *across)

    def couple(stage, after, inside, ends):
        return call(
            functools.partial(couple_kernel, stage, slot_rows),
            shape_of(slot_rows, LANES),
            6,
            scratch=[pltpu.VMEM((rows, LANES), F32)],
            cost=6_000_000,
        )(after, inside, ends, slabs, plan, lanes)

    def add(value, axis, step, after):
        got = lax.ppermute(value, axis, [(i, i ^ step) for i in range(lax.axis_size(axis))])
        return call(add_kernel, shape_of(SUB, nz), 3)(value, got, after)

    list0 = couple(0, sums, in0, ends0)
    sums = add(sums, "gz", 1, list0)
    list1 = couple(1, sums, in1, ends1)
    list2 = couple(2, list1, in2, ends2)
    for step in [2**k for k in range(n_gy.bit_length() - 1)]:
        sums = add(sums, "gy", step, list2)
    if n_gx > 4:
        counts = lax.all_gather(jnp.sum(stat[1, 0]), "gx")
        begin = jnp.sum(jnp.where(jnp.arange(n_gx) < lax.axis_index("gx"), counts, 0.0))
        where = where.at[0].set(begin)
    blocks = call(
        place_kernel,
        (shape_of(3 * block_rows + SUB, LANES),) * n_gx,
        5,
        scratch=[pltpu.VMEM((3, n_gx * block_rows + slot_rows + SUB, LANES), F32)],
    )(where, sums, list0, list1, list2)
    apart = {k: never_meet(n_gx, k, slot_rows, block_rows) for k in range(1, n_gx)}
    small, meets = [], []
    for k in range(1, n_gx):
        if any(apart[k]):
            small.append(swap(sums, x_to=[i ^ k if apart[k][i] else i for i in range(n_gx)]))
        meets.append(not all(apart[k]))
    order = [k for k in [2, 3, 1] + list(range(4, n_gx)) if k < n_gx and meets[k - 1]]
    large = [swap(blocks[k], x_to=[i if apart[k][i] else i ^ k for i in range(n_gx)]) for k in order]
    alone = [[apart[k] for k in range(1, n_gx) if any(apart[k])], [apart[k] for k in order]]

    base, total_change, factor, state_coefs = call(
        membrane_kernel,
        (
            shape_of(n_states, block_rows, LANES), shape_of(block_rows, LANES), shape_of(block_rows, LANES),
            shape_of(2, n_states, LANES),
        ),
        9,
        specs=[SMEM] * 5 + [VMEM] * 4,
        cost=6_000_000,
    )(
        half_voltage, gate_slope, tau_base, conductance, reversal,
        blocks[0], cells(voltage), states(gates), states(gates_cot),
    )
    solution, volt_grad, gate_grad = call(
        functools.partial(finish_kernel, alone),
        (block, shape_of(block_rows, LANES), shape_of(n_states, block_rows, LANES)),
        12 + len(small) + len(large),
    )(
        state_coefs, cells(voltage_cot), cells(voltage), total_change, factor, base,
        in0, in1, in2, ends1, ends2, blocks[0], *small, *large,
    )
    return solution, volt_grad.reshape(voltage.shape), gate_grad.reshape(gates.shape)


def solution(mesh):
    grid = P(("groups", "gx"), "gy", "gz")
    cells = P(("groups", "gy", "gz"), "gx")
    states = P(None, ("groups", "gy", "gz"), "gx")
    in_specs = (
        grid, grid, grid, P(("groups", "gx"), "gy", "gz", None), cells, states, cells, states,
        P(), P(), P(), P(), P(),
    )
    return jax.shard_map(
        local, mesh=mesh, in_specs=in_specs, out_specs=(grid, cells, states), check_vma=False
    )
```

```python
import functools

import jax
import jax.numpy as jnp
from jax import lax
from jax.experimental import pallas as pl
from jax.experimental.pallas import tpu as pltpu
from jax.sharding import PartitionSpec as P

TIME_STEP = 0.5
LANES = 128
SUB = 8
PACK = 8
COUNT_LANE = 4 * PACK
F32 = jnp.float32

VMEM = pl.BlockSpec(memory_space=pltpu.VMEM)
SMEM = pl.BlockSpec(memory_space=pltpu.SMEM)
HBM = pl.BlockSpec(memory_space=pltpu.HBM)


def shape_of(*dims):
    return jax.ShapeDtypeStruct(dims, F32)


def call(kernel, out_shape, n_in, specs=None, outs=None, scratch=(), cost=2_000_000, limit=32):
    return pl.pallas_call(
        kernel,
        out_shape=out_shape,
        in_specs=specs if specs is not None else [VMEM] * n_in,
        out_specs=outs if outs is not None else jax.tree.map(lambda _: VMEM, out_shape),
        scratch_shapes=list(scratch),
        compiler_params=pltpu.CompilerParams(vmem_limit_bytes=limit * 1024 * 1024),
        cost_estimate=pl.CostEstimate(flops=cost, bytes_accessed=cost, transcendentals=0),
    )


def in_hbm(array):
    return pltpu.with_memory_space_constraint(array, pltpu.HBM)


def lanes_of(shape):
    return lax.broadcasted_iota(jnp.int32, shape, len(shape) - 1)


def subs_of(shape):
    return lax.broadcasted_iota(jnp.int32, shape, len(shape) - 2)


def start_kernel(
    right_hbm, damping_hbm, label_hbm, w0_ref, inv_ref, pack_ref, stat_ref, right_ref, damping_ref, label_ref, sems
):
    nx, ny, nz = right_ref.shape
    parts = sems.shape[1]
    size = nx // parts
    copies = []
    for part in range(parts):
        here = pl.ds(part * size, size)
        for k, (source, target) in enumerate(
            ((right_hbm, right_ref), (damping_hbm, damping_ref), (label_hbm, label_ref))
        ):
            copies.append(pltpu.make_async_copy(source.at[here], target.at[here], sems.at[k, part]))
            copies[-1].start()
    gz = lax.axis_index("gz")
    lane = lanes_of((ny, nz))
    packed_w = jnp.zeros((ny, nz), F32)
    packed_i = jnp.zeros((ny, nz), F32)
    energy = jnp.zeros((ny, nz), F32)
    cells = jnp.zeros((ny, nz), F32)
    for x in range(nx):
        if x % size == 0:
            for k in range(3):
                copies[3 * (x // size) + k].wait()
        label = label_ref[x].astype(F32)
        right = right_ref[x]
        inv = 1.0 / (12.0 + damping_ref[x] * (1.0 + 3.0 * label))
        w0 = right * inv
        w0_ref[x] = w0
        inv_ref[x] = inv
        energy = energy + right * w0
        cells = cells + label
        turn = (PACK * x + 3) % nz
        begin = PACK * x + 3 * gz
        chosen = (lane >= begin) & (lane < begin + 3)
        packed_w = jnp.where(chosen, pltpu.roll(w0, turn, 1), packed_w)
        packed_i = jnp.where(chosen, pltpu.roll(inv, turn, 1), packed_i)
    pack_ref[0] = packed_w
    pack_ref[1] = packed_i
    stat_ref[0] = jnp.broadcast_to(jnp.sum(energy, axis=0, keepdims=True), (SUB, nz))
    stat_ref[1] = jnp.broadcast_to(jnp.sum(cells, axis=0, keepdims=True), (SUB, nz))


def steps_of(axis):
    return 1 if lax.axis_size(axis) == 2 else 2


def upper_in(axis, step):
    return lax.rem(lax.axis_index(axis), 2) == step


def has_partner(axis, step):
    here = lax.axis_index(axis)
    return jnp.where(upper_in(axis, step), here < lax.axis_size(axis) - 1, here > 0)


def unpack_rows(tile, step):
    sub = subs_of(tile.shape)
    up, there = upper_in("gy", step), has_partner("gy", step)
    depth = jnp.where(there, jnp.where(up, SUB - 1 - sub, sub), -1)
    return jnp.where(depth >= 5, tile, 0.0), jnp.where(depth >= 6, pltpu.roll(tile, 4, 0), 0.0)


def halo_rows(tiles):
    w_tile, i_tile = unpack_rows(tiles[0], 0)
    for step, tile in enumerate(tiles[1:], 1):
        w_more, i_more = unpack_rows(tile, step)
        w_tile, i_tile = w_tile + w_more, i_tile + i_more
    return w_tile, i_tile


def faces_kernel(n_y, w0_ref, inv_ref, own_ref, got_ref, stat_ref, slab_ref, *refs):
    y_refs, x_refs, edge_refs = refs[:n_y], refs[n_y : n_y + 2], refs[n_y + 2 :]
    nx, ny, nz = w0_ref.shape
    sub = subs_of((SUB, nz))
    lane = lanes_of((ny, nz))
    slab_ref[...] = own_ref[...] + got_ref[...]
    for step, face_ref in enumerate(y_refs):
        up = upper_in("gy", step)
        keep_w = jnp.where(up, sub, SUB - 1 - sub) >= 5
        for x in range(nx + 1):
            w_rows, i_rows = (w0_ref.at[x], inv_ref.at[x]) if x < nx else (slab_ref.at[0], slab_ref.at[1])
            w_face = jnp.where(up, w_rows[ny - SUB :], w_rows[:SUB])
            i_face = jnp.where(up, i_rows[ny - SUB :], i_rows[:SUB])
            face_ref[x] = jnp.where(keep_w, w_face, pltpu.roll(i_face, 4, 0))
    cells = jnp.sum(stat_ref[1, 0:1], axis=1, keepdims=True)
    slab_w = slab_ref[0]
    half = pltpu.roll(slab_ref[1], nz // 2, 1)
    up_slab = jnp.where(lane >= nz - 3 * PACK, slab_w, half)
    down_slab = jnp.where(lane < 3 * PACK, slab_w, half)
    for step, face_ref in enumerate(x_refs):
        up = upper_in("gx", step)
        first = jnp.where(up, nx - 3, 0)
        for k in range(3):
            face_ref[k] = w0_ref[first + k]
        for k in range(2):
            face_ref[3 + k] = inv_ref[jnp.where(up, nx - 2, 0) + k]
        face_ref[5] = jnp.where(lane == COUNT_LANE, cells, jnp.where(up, up_slab, down_slab))
        for y_step, y_ref in enumerate(y_refs):
            edge_ref = edge_refs[step * n_y + y_step]
            for k in range(3):
                edge_ref[k] = y_ref[first + k]
            edge_ref[3] = y_ref[nx]


def slab_step(v, s, inv):
    width = v.shape[1]
    across = pltpu.roll(v, PACK, 1) + pltpu.roll(v, width - PACK, 1)
    q = v + 0.5 * (s + across)
    if inv is None:
        return q, None
    total = (
        pltpu.roll(q, 1, 1) + pltpu.roll(q, width - 1, 1) + s + across
        + 0.5 * (pltpu.roll(s, PACK, 1) + pltpu.roll(s, width - PACK, 1))
    )
    return q, total * inv


def along_z(q, half, column, gz):
    nz = q.shape[1]
    lane = lanes_of(q.shape)
    entry = (nz - 1) * (1 - gz)
    turn = lax.rem(entry - (column + 3 - gz) + 2 * nz, nz)
    up = jnp.where(lane == nz - 1, 0.0, pltpu.roll(q, nz - 1, 1))
    down = jnp.where(lane == 0, 0.0, pltpu.roll(q, 1, 1))
    return up + down + jnp.where(lane == entry, pltpu.roll(half, turn, 1), 0.0)


def sweep(stage, spans, nx, ny, nz, gz, get, get_inv, put, slab_q, sums):
    margin = 2 - stage
    start = SUB - margin
    tiles = ny // SUB + (margin > 0)
    own = subs_of((SUB, nz)) >= margin
    parts = [[], []]
    for tile in range(tiles):
        row = start + SUB * tile
        q_rows = slab_q[SUB * tile : SUB * tile + SUB]
        acc = [jnp.zeros((SUB, nz), F32) for _ in range(2)]

        def beside(x):
            return get(x, row - 1) + get(x, row + 1)

        for first, last in spans:
            s_low, s_mid = beside(first - 1), beside(first)
            v_low, v_mid = get(first - 1, row), get(first, row)
            for x in range(first, last):
                v_high, s_high = get(x + 1, row), beside(x + 1)
                across = v_low + v_high
                column = (PACK * x) % (2 * nz)
                half = q_rows[:, column // nz * nz : column // nz * nz + nz]
                rest = s_mid + across
                total = along_z(v_mid + 0.5 * rest, half, column % nz, gz) + rest + 0.5 * (s_low + s_high)
                if stage < 2:
                    after = total * get_inv(x, row)
                    put(x, row, after)
                if 0 <= x < nx:
                    acc[0] = acc[0] + v_mid * total
                    if stage < 2:
                        acc[1] = acc[1] + after * total
                v_low, v_mid, s_low, s_mid = v_mid, v_high, s_mid, s_high
        for k in range(2):
            parts[k].append(acc[k])
    for k in range(2 if stage < 2 else 1):
        part = parts[k]
        total = part[1]
        for other in part[2 : ny // SUB]:
            total = total + other
        total = total + (jnp.where(own, part[0], part[-1]) if margin else part[0])
        sums[2 * stage + k] = total


def inner_kernel(n_y, w0_ref, inv_ref, slab_ref, *refs):
    y_refs, (a_ref, i_ref, b_ref, c_ref, sum_ref, own_slab_ref, slabs_ref) = refs[:n_y], refs[n_y:]
    nx, ny, nz = w0_ref.shape
    gz = lax.axis_index("gz")
    for x in range(nx + 1):
        halos = halo_rows([ref[x] for ref in y_refs])
        for k in range(2):
            if x < nx:
                ref, own = (a_ref, i_ref)[k].at[x], (w0_ref, inv_ref)[k][x]
            else:
                ref, own = own_slab_ref.at[k], slab_ref[k]
            ref[:SUB] = halos[k]
            ref[SUB : SUB + ny] = own
            ref[SUB + ny :] = halos[k]
    for k in range(2):
        slabs_ref[3 * k] = own_slab_ref[k]
    sums = {}
    for stage in range(3):
        source, target = (a_ref, b_ref, c_ref)[stage], (b_ref, c_ref, None)[stage]
        start, size = SUB - 2 + stage, ny if stage == 2 else ny + SUB
        v = slabs_ref[stage, start : start + size]
        s = slabs_ref[stage, start - 1 : start - 1 + size] + slabs_ref[stage, start + 1 : start + 1 + size]
        q, after = slab_step(v, s, slabs_ref[3, start : start + size] if stage < 2 else None)
        if stage < 2:
            slabs_ref[stage + 1, start : start + size] = after

        def put(x, row, value):
            target[x, row : row + SUB] = value

        sweep(
            stage, [(1 + stage, nx - 1 - stage)], nx, ny, nz, gz,
            lambda x, row: source[x, row : row + SUB], lambda x, row: i_ref[x, row : row + SUB],
            put, q, sums,
        )
    for k in range(5):
        sum_ref[k] = sums[k]


def outer_kernel(
    n_y, column_total, after_ref, a_ref, i_ref, b_ref, c_ref, slab_ref, sum_ref, stat_ref, *refs
):
    x_refs, corner_refs = refs[:2], refs[2 : 2 + 2 * n_y]
    ea_ref, eb_ref, ec_ref, slabs_ref, total_ref, where_ref, ei_ref, si_ref = refs[2 + 2 * n_y :]
    nx, ny, nz = a_ref.shape[0], a_ref.shape[1] - 2 * SUB, a_ref.shape[2]
    ring = ny + SUB
    gz = lax.axis_index("gz")
    odd = lax.rem(lax.axis_index("gx"), 2) == 1

    def beyond(upper, read):
        there = has_partner("gx", 0) if upper else has_partner("gx", 1)
        swapped = has_partner("gx", 1) if upper else has_partner("gx", 0)
        first, second = read(0), read(1)
        if upper:
            return jnp.where(jnp.where(odd, swapped, there), jnp.where(odd, second, first), 0.0)
        return jnp.where(jnp.where(odd, swapped, there), jnp.where(odd, first, second), 0.0)

    def write(ref, at, own, halo):
        ref[at, :SUB] = halo
        ref[at, SUB : SUB + ny] = own
        ref[at, SUB + ny :] = halo

    lane_tile, lane = lanes_of((SUB, nz)), lanes_of((ny, nz))
    slab_parts = []
    for side, upper in enumerate((False, True)):
        tiles = [
            halo_rows([beyond(upper, lambda step: corner_refs[step * n_y + j][k]) for j in range(n_y)])
            for k in range(4)
        ]
        for k in range(3):
            write(ea_ref, 3 * side + k, beyond(upper, lambda step: x_refs[step][k]), tiles[k][0])
        for k in range(2):
            own = beyond(upper, lambda step: x_refs[step][3 + k])
            write(ei_ref, 2 * side + k, own, tiles[k if upper else k + 1][1])
        own = beyond(upper, lambda step: x_refs[step][5])

        def near(value, lanes, planes):
            return jnp.where(lanes < planes * PACK if upper else lanes >= nz - planes * PACK, value, 0.0)

        slab_parts.append((
            near(own, lane, 3), near(tiles[3][0], lane_tile, 3),
            near(pltpu.roll(own, nz // 2, 1), lane, 2), near(tiles[3][1], lane_tile, 2),
            own[0:1, COUNT_LANE : COUNT_LANE + 1],
        ))

    low, high = slab_parts
    for ref, k in ((slabs_ref, 0), (si_ref, 1)):
        ref[0, :, :nz] = slab_ref[k]
        ref[0, SUB : SUB + ny, nz:] = low[2 * k] + high[2 * k]
        ref[0, :SUB, nz:] = low[2 * k + 1] + high[2 * k + 1]
        ref[0, SUB + ny :, nz:] = low[2 * k + 1] + high[2 * k + 1]

    def reader(inside_ref, edge_ref, first, count):
        def get(x, row):
            if first <= x < nx - first:
                return inside_ref[x, row : row + SUB]
            at = x - (first - count) if x < first else x - (nx - first) + count
            return edge_ref[at, row : row + SUB]

        return get

    sums = {}
    for stage in range(3):
        get = reader((a_ref, b_ref, c_ref)[stage], (ea_ref, eb_ref, ec_ref)[stage], stage, 3)
        start, size = SUB - 2 + stage, ny if stage == 2 else ring
        v = slabs_ref[stage, start : start + size]
        s = slabs_ref[stage, start - 1 : start - 1 + size] + slabs_ref[stage, start + 1 : start + 1 + size]
        q, after = slab_step(v, s, si_ref[0, start : start + size] if stage < 2 else None)
        if stage < 2:
            slabs_ref[stage + 1, start : start + size] = after

        def put(x, row, value):
            edge_ref = (eb_ref, ec_ref)[stage]
            at = x - (stage - 2) if x < nx // 2 else x - (nx - 1 - stage) + 3
            edge_ref[at, row : row + SUB] = value

        sweep(
            stage, [(stage - 2, stage + 1), (nx - 1 - stage, nx + 2 - stage)], nx, ny, nz, gz,
            get, reader(i_ref, ei_ref, 0, 2), put, q, sums,
        )

    total_ref[0:1] = stat_ref[0, 0:1]
    for k in range(5):
        total_ref[k + 1 : k + 2] = jnp.sum(sums[k] + sum_ref[k], axis=0, keepdims=True)
    total_ref[6:8] = jnp.zeros((2, nz), F32)
    gx, n_x = lax.axis_index("gx"), lax.axis_size("gx")
    count = jnp.sum(stat_ref[1, 0:1], axis=1, keepdims=True)
    below, above = [part[4] for part in slab_parts]
    begin = jnp.where(
        gx == 0, 0.0,
        jnp.where(gx == 1, below, jnp.where(gx == n_x - 1, column_total - count, column_total - count - above)),
    )
    where_ref[0:1] = jnp.broadcast_to(begin, (1, nz))
    where_ref[1:2] = jnp.broadcast_to(count, (1, nz))
    where_ref[2:8] = jnp.zeros((6, nz), F32)


def shift_up(v, amount):
    if amount < SUB:
        return pltpu.roll(v, v.shape[0] - amount, 0)
    return jnp.concatenate([v[amount:], v[:amount]], axis=0)


def plan_kernel(after_ref, label_ref, index_ref, plan_ref, lane_ref):
    rows, slot_rows = label_ref.shape[0], index_ref.shape[0]
    wide = -(-(slot_rows + 1) // LANES) * LANES
    shape = (rows, LANES)
    lane, row = lanes_of(shape), subs_of(shape)
    ones = (label_ref[...] == 1).astype(jnp.bfloat16)
    totals = jnp.dot(ones, jnp.ones((LANES, LANES), jnp.bfloat16), preferred_element_type=F32)
    lower = (subs_of((rows, rows)) > lanes_of((rows, rows))).astype(jnp.bfloat16)
    before = jnp.dot(lower, totals.astype(jnp.bfloat16), preferred_element_type=F32).astype(jnp.int32)
    target, first = lax.div(before, LANES), lax.rem(before, LANES)
    listed = jnp.concatenate(
        [lax.rem(index_ref[...], LANES).astype(F32), jnp.zeros((wide - slot_rows, LANES), F32)], axis=0
    ).astype(jnp.bfloat16)
    spread = jnp.concatenate([target] * (wide // LANES), axis=1)
    place = lanes_of((rows, wide))
    here = jnp.dot((spread == place).astype(jnp.bfloat16), listed, preferred_element_type=F32)
    after = jnp.dot((spread + 1 == place).astype(jnp.bfloat16), listed, preferred_element_type=F32)
    lane_ref[...] = jnp.where(lane >= first, here, after).astype(jnp.int32)
    wrapped = (lane < first).astype(jnp.int32)
    filled = lane - first + LANES * wrapped < totals.astype(jnp.int32)
    way = jnp.where(filled, row - target - wrapped, 0)
    plan = jnp.zeros(shape, jnp.int32)
    step = 1
    while step < rows:
        moving = jnp.where((way & step) != 0, way, 0)
        arriving = shift_up(moving, step)
        plan = plan | (arriving & step)
        way = (way - moving) | arriving
        step *= 2
    plan_ref[...] = plan


def galerkin(t):
    g00, g01, g02, g12, g22 = t[0] - t[1], t[1] - t[2], t[2] - t[3], t[3] - t[4], t[4] - t[5]
    g11 = g02
    l10, l20 = g01 / g00, g02 / g00
    d1 = g11 - l10 * g01
    m21 = g12 - l20 * g01
    ok1 = d1 > 1e-6 * g11
    d1 = jnp.where(ok1, d1, 1.0)
    l21 = jnp.where(ok1, m21 / d1, 0.0)
    d2 = g22 - l20 * g02 - l21 * m21
    ok2 = ok1 & (d2 > 1e-6 * g22)
    d2 = jnp.where(ok2, d2, 1.0)
    y1 = t[1] - l10 * t[0]
    y2 = t[2] - l20 * t[0] - l21 * y1
    c2 = jnp.where(ok2, y2 / d2, 0.0)
    c1 = jnp.where(ok1, y1 / d1 - l21 * c2, 0.0)
    c0 = t[0] / g00 - l10 * c1 - l20 * c2
    return c0, c1, c2


def couple_kernel(
    stage, slot_rows, after_ref, where_ref, inside_ref, edge_ref, slabs_ref, plan_ref, lane_ref, blocks_ref,
    value_ref, buf_ref,
):
    nx, nz = inside_ref.shape[0], inside_ref.shape[2]
    ny = inside_ref.shape[1] - 2 * SUB
    rows = nx * ny
    gz = lax.axis_index("gz")

    def get(x, row):
        if stage <= x < nx - stage:
            return inside_ref[x, row : row + SUB]
        return edge_ref[x - (stage - 3) if x < stage else x - (nx - stage) + 3, row : row + SUB]

    for tile in range(ny // SUB):
        row = SUB + SUB * tile
        slab = slabs_ref[stage, row : row + SUB, :nz]
        v_low, v_mid = get(-1, row), get(0, row)
        for x in range(nx):
            v_high = get(x + 1, row)
            beside = get(x, row - 1) + get(x, row + 1)
            at = ny * x + SUB * tile
            value_ref[at : at + SUB] = (
                along_z(v_mid, slab, PACK * x, gz) + beside + (v_low + v_high) - 6.0 * v_mid
            )
            v_low, v_mid = v_mid, v_high
    value = jnp.take_along_axis(value_ref[...], lane_ref[...], axis=1)
    plan = plan_ref[...]
    step = 1
    while step < rows:
        value = jnp.where((plan & step) != 0, shift_up(value, step), value)
        step *= 2
    offset = jnp.max(where_ref[0:1]).astype(jnp.int32)
    count = jnp.max(where_ref[1:2]).astype(jnp.int32)
    shape = (slot_rows, LANES)
    slots = jnp.where(subs_of(shape) * LANES + lanes_of(shape) < count, value[:slot_rows], 0.0)
    slots = jnp.concatenate([slots, jnp.zeros((SUB, LANES), F32)], axis=0)
    inner = lax.rem(offset, LANES)
    turned = pltpu.roll(slots, inner, 1)
    moved = jnp.where(lanes_of((slot_rows + SUB, LANES)) >= inner, turned, pltpu.roll(turned, 1, 0))
    buf_ref[...] = jnp.zeros_like(buf_ref)
    buf_ref[pl.ds(offset // LANES, slot_rows + SUB), :] = moved
    gx = lax.axis_index("gx")
    n_gx = lax.axis_size("gx")
    size = blocks_ref.shape[0] // n_gx
    for block in range(n_gx):
        begin = pl.multiple_of((gx ^ block) * size, SUB)
        blocks_ref[block * size : block * size + size] = buf_ref[pl.ds(begin, size), :]


def add_kernel(a_ref, b_ref, after_ref, out_ref):
    out_ref[...] = a_ref[...] + b_ref[...]


def pack_kernel(total_ref, *refs):
    list_refs, out_refs = refs[:3], refs[3:]
    size = (out_refs[0].shape[0] - SUB) // 3
    for block, out_ref in enumerate(out_refs):
        for k, list_ref in enumerate(list_refs):
            out_ref[k * size : k * size + size] = list_ref[block * size : block * size + size]
        out_ref[3 * size :] = total_ref[...]


def membrane_kernel(
    half_ref, slope_ref, tau_ref, cond_ref, rev_ref, after_ref, v_ref, gates_ref, cot_ref,
    base_ref, sum_ref, factor_ref, coef_ref,
):
    n_states, rows = gates_ref.shape[:2]
    v = v_ref[...]

    def state(g, carry):
        total, current = carry
        inv_slope = 1.0 / slope_ref[g]
        tau_base = tau_ref[g]
        scaled = (v - half_ref[g]) * inv_slope
        gate = gates_ref[g]
        cot = cot_ref[g]
        steady = 1.0 / (1.0 + jnp.exp(-scaled))
        bell = jnp.exp(-scaled * scaled)
        rate = TIME_STEP / (tau_base * (0.5 + bell))
        decay = jnp.exp(-rate)
        steady_slope = steady * (1.0 - steady)
        decay_slope = decay * rate * rate * ((tau_base / TIME_STEP) * bell * (-2.0 * scaled))
        change = (steady_slope * (1.0 - decay) + (gate - steady) * decay_slope) * inv_slope
        base_ref[g] = cot * decay
        coef_ref[0, pl.ds(g, 1)] = jnp.full((1, LANES), TIME_STEP * cond_ref[g])
        coef_ref[1, pl.ds(g, 1)] = jnp.full((1, LANES), rev_ref[g])
        return total + cot * change, current + cond_ref[g] * gate

    zero = jnp.zeros((rows, LANES), F32)
    total, current = lax.fori_loop(0, n_states, state, (zero, zero), unroll=2)
    sum_ref[...] = total
    factor_ref[...] = 1.0 - TIME_STEP * current


def finish_kernel(
    alone, coef_ref, vcot_ref, v_ref, sum_ref, factor_ref, base_ref, a_ref, b_ref, c_ref, eb_ref, ec_ref, *refs
):
    n_small, n_large = len(alone[0]), len(alone[1])
    own_ref, small_refs, large_refs = refs[0], refs[1 : 1 + n_small], refs[1 + n_small : 1 + n_small + n_large]
    x_hbm, volt_ref, gate_hbm, x_ref, gate_ref, sems = refs[1 + n_small + n_large :]
    size = (own_ref.shape[0] - SUB) // 3
    gx = lax.axis_index("gx")

    def is_one(flags):
        found = gx < 0
        for place, flag in enumerate(flags):
            if flag:
                found = found | (gx == place)
        return found

    total = own_ref[3 * size :]
    for flags, ref in zip(alone[0], small_refs):
        total = total + jnp.where(is_one(flags), ref[...], 0.0)
    for flags, ref in zip(alone[1], large_refs):
        total = total + jnp.where(is_one(flags), 0.0, ref[3 * size :])
    sums = jnp.sum(total, axis=1, keepdims=True)
    c0, c1, c2 = galerkin([jnp.broadcast_to(sums[k : k + 1], (1, LANES)) for k in range(6)])
    nx, ny, nz = x_ref.shape
    own = slice(SUB, SUB + ny)
    for x in range(nx):
        w1 = b_ref[x, own] if 1 <= x < nx - 1 else eb_ref[2 if x == 0 else 3, own]
        w2 = c_ref[x, own] if 2 <= x < nx - 2 else ec_ref[x + 1 if x < 2 else x - (nx - 2) + 3, own]
        x_ref[x] = c0 * a_ref[x, own] + c1 * w1 + c2 * w2
    copies = [pltpu.make_async_copy(x_ref, x_hbm, sems.at[0])]
    copies[0].start()
    landed = jnp.zeros((size, LANES), F32)
    for k, c in enumerate((c0, c1, c2)):
        part = own_ref[k * size : k * size + size]
        for ref in large_refs:
            part = part + ref[k * size : k * size + size]
        landed = landed + c * part
    cot = vcot_ref[...] + landed
    v = v_ref[...]
    volt_ref[...] = cot * factor_ref[...] + sum_ref[...]
    n_states = base_ref.shape[0]
    half = n_states // 2
    for part, (begin, end) in enumerate(((0, half), (half, n_states))):
        for g in range(begin, end):
            gate_ref[g] = base_ref[g] - (coef_ref[0, g : g + 1] * cot) * (v - coef_ref[1, g : g + 1])
        here = pl.ds(begin, end - begin)
        copies.append(pltpu.make_async_copy(gate_ref.at[here], gate_hbm.at[here], sems.at[1 + part]))
        copies[-1].start()
    for copy in copies:
        copy.wait()


def partners(axis, step):
    count = lax.axis_size(axis)
    if step == 0:
        return [i ^ 1 for i in range(count)]
    return [0] + [i + 1 if i % 2 else i - 1 for i in range(1, count - 1)] + [count - 1]


def swap(value, x_to=None, y_to=None):
    n_x, n_y, n_z = [lax.axis_size(axis) for axis in ("gx", "gy", "gz")]
    pairs = []
    for x in range(n_x):
        for y in range(n_y):
            to_x, to_y = x_to[x] if x_to else x, y_to[y] if y_to else y
            alone = (x_to and to_x == x) or (y_to and to_y == y)
            for z in range(n_z):
                to = (x, y, z ^ 1) if alone else (to_x, to_y, z)
                pairs.append(((x * n_y + y) * n_z + z, (to[0] * n_y + to[1]) * n_z + to[2]))
    return lax.ppermute(value, ("gx", "gy", "gz"), pairs)


def never_meet(count, k, slots, block):
    def apart(tile, owner):
        return owner * block >= (tile + 1) * slots or (owner + 1) * block <= count * block - (count - tile) * slots

    return [apart(i, i ^ k) and apart(i ^ k, i) for i in range(count)]


def local(
    potential_cot, damping, tissue_label, heart_index, voltage, gates, voltage_cot, gates_cot,
    half_voltage, gate_slope, tau_base, conductance, reversal,
):
    nx, ny, nz = potential_cot.shape
    rows = nx * ny
    ring = ny + SUB
    n_gx, n_gy = lax.axis_size("gx"), lax.axis_size("gy")
    n_states = gates.shape[0]
    block_rows = voltage.shape[1] // LANES
    slot_rows = heart_index.shape[3] // LANES
    block = shape_of(nx, ny, nz)
    flat = lambda a: a.reshape(rows, LANES)
    cells = lambda a: a.reshape(block_rows, LANES)
    states = lambda a: a.reshape(n_states, block_rows, LANES)

    w0, inv, packed, stat = call(
        start_kernel, (block, block, shape_of(2, ny, nz), shape_of(2, SUB, nz)), 3,
        specs=[HBM] * 3,
        scratch=[
            pltpu.VMEM((nx, ny, nz), F32), pltpu.VMEM((nx, ny, nz), F32), pltpu.VMEM((nx, ny, nz), jnp.int32),
            pltpu.SemaphoreType.DMA((3, 2)),
        ],
    )(in_hbm(potential_cot), in_hbm(damping), in_hbm(tissue_label))

    got = lax.ppermute(packed, "gz", [(0, 1), (1, 0)])
    cells_shape = jax.ShapeDtypeStruct((rows, LANES), jnp.int32)
    plan, lanes = call(plan_kernel, (cells_shape, cells_shape), 3, cost=6_000_000)(
        stat, flat(tissue_label), heart_index.reshape(slot_rows, LANES)
    )

    n_y = steps_of("gy")
    shapes = (
        (shape_of(2, ny, nz),) + (shape_of(nx + 1, SUB, nz),) * n_y + (shape_of(6, ny, nz),) * 2
        + (shape_of(4, SUB, nz),) * (2 * n_y)
    )
    slab, *faces = call(functools.partial(faces_kernel, n_y), shapes, 5)(w0, inv, packed, got, stat)
    along_y, along_x, across = faces[:n_y], faces[n_y : n_y + 2], faces[n_y + 2 :]
    y_to = [partners("gy", step) for step in range(n_y)]
    x_to = [partners("gx", step) for step in range(2)]
    along_y = [swap(face, y_to=y_to[j]) for j, face in enumerate(along_y)]
    along_x = [swap(face, x_to=x_to[i]) for i, face in enumerate(along_x)]
    across = [swap(face, x_to=x_to[k // n_y], y_to=y_to[k % n_y]) for k, face in enumerate(across)]

    tall = ring + SUB
    planes = shape_of(nx, tall, nz)
    edges = shape_of(6, tall, nz)
    in0, in_inv, in1, in2, in_sums, own_slab = call(
        functools.partial(inner_kernel, n_y),
        (planes,) * 4 + (shape_of(5, SUB, nz), shape_of(2, tall, nz)),
        3 + n_y,
        scratch=[pltpu.VMEM((4, tall, nz), F32)],
        cost=6_000_000,
    )(w0, inv, slab, *along_y)
    ends0, ends1, ends2, slabs, sums, where = call(
        functools.partial(outer_kernel, n_y, float(n_gx * voltage.shape[1])),
        (edges,) * 3 + (shape_of(3, tall, 2 * nz), shape_of(SUB, nz), shape_of(SUB, nz)),
        10 + 2 * n_y,
        scratch=[pltpu.VMEM((4, tall, nz), F32), pltpu.VMEM((1, tall, 2 * nz), F32)],
    )(plan, in0, in_inv, in1, in2, own_slab, in_sums, stat, *along_x, *across)

    if n_gx > 4:
        counts = lax.all_gather(jnp.sum(stat[1, 0]), "gx")
        begin = jnp.sum(jnp.where(jnp.arange(n_gx) < lax.axis_index("gx"), counts, 0.0))
        where = where.at[0].set(begin)

    def couple(stage, after, inside, ends):
        return call(
            functools.partial(couple_kernel, stage, slot_rows),
            shape_of(n_gx * block_rows, LANES),
            7,
            scratch=[
                pltpu.VMEM((rows, LANES), F32), pltpu.VMEM((n_gx * block_rows + slot_rows + SUB, LANES), F32),
            ],
            cost=6_000_000,
        )(after, where, inside, ends, slabs, plan, lanes)

    def add(value, axis, step, after):
        got = lax.ppermute(value, axis, [(i, i ^ step) for i in range(lax.axis_size(axis))])
        return call(add_kernel, shape_of(SUB, nz), 3)(value, got, after)

    list0 = couple(0, sums, in0, ends0)
    sums = add(sums, "gz", 1, list0)
    list1 = couple(1, sums, in1, ends1)
    list2 = couple(2, list1, in2, ends2)
    for step in [2**k for k in range(n_gy.bit_length() - 1)]:
        sums = add(sums, "gy", step, list2)
    blocks = call(pack_kernel, (shape_of(3 * block_rows + SUB, LANES),) * n_gx, 4)(sums, list0, list1, list2)
    apart = {k: never_meet(n_gx, k, slot_rows, block_rows) for k in range(1, n_gx)}
    small, meets = [], []
    for k in range(1, n_gx):
        if any(apart[k]):
            small.append(swap(sums, x_to=[i ^ k if apart[k][i] else i for i in range(n_gx)]))
        meets.append(not all(apart[k]))
    order = [k for k in [2, 3, 1] + list(range(4, n_gx)) if k < n_gx and meets[k - 1]]
    large = [swap(blocks[k], x_to=[i if apart[k][i] else i ^ k for i in range(n_gx)]) for k in order]
    alone = [[apart[k] for k in range(1, n_gx) if any(apart[k])], [apart[k] for k in order]]

    base, total_change, factor, state_coefs = call(
        membrane_kernel,
        (
            shape_of(n_states, block_rows, LANES), shape_of(block_rows, LANES), shape_of(block_rows, LANES),
            shape_of(2, n_states, LANES),
        ),
        9,
        specs=[SMEM] * 5 + [VMEM] * 4,
        cost=6_000_000,
    )(
        half_voltage, gate_slope, tau_base, conductance, reversal,
        blocks[0], cells(voltage), states(gates), states(gates_cot),
    )
    solution, volt_grad, gate_grad = call(
        functools.partial(finish_kernel, alone),
        (block, shape_of(block_rows, LANES), shape_of(n_states, block_rows, LANES)),
        12 + len(small) + len(large),
        outs=(HBM, VMEM, HBM),
        scratch=[
            pltpu.VMEM((nx, ny, nz), F32), pltpu.VMEM((n_states, block_rows, LANES), F32),
            pltpu.SemaphoreType.DMA((3,)),
        ],
    )(
        state_coefs, cells(voltage_cot), cells(voltage), total_change, factor, base,
        in0, in1, in2, ends1, ends2, blocks[0], *small, *large,
    )
    return solution, volt_grad.reshape(voltage.shape), gate_grad.reshape(gates.shape)


def solution(mesh):
    grid = P(("groups", "gx"), "gy", "gz")
    cells = P(("groups", "gy", "gz"), "gx")
    states = P(None, ("groups", "gy", "gz"), "gx")
    in_specs = (
        grid, grid, grid, P(("groups", "gx"), "gy", "gz", None), cells, states, cells, states,
        P(), P(), P(), P(), P(),
    )
    return jax.shard_map(
        local, mesh=mesh, in_specs=in_specs, out_specs=(grid, cells, states), check_vma=False
    )
```

```python
import functools

import jax
import jax.numpy as jnp
from jax import lax
from jax.experimental import pallas as pl
from jax.experimental.pallas import tpu as pltpu
from jax.sharding import PartitionSpec as P

TIME_STEP = 0.5
LANES = 128
SUB = 8
PACK = 8
COUNT_LANE = 4 * PACK
F32 = jnp.float32

VMEM = pl.BlockSpec(memory_space=pltpu.VMEM)
SMEM = pl.BlockSpec(memory_space=pltpu.SMEM)
HBM = pl.BlockSpec(memory_space=pltpu.HBM)


def shape_of(*dims):
    return jax.ShapeDtypeStruct(dims, F32)


def call(kernel, out_shape, n_in, specs=None, outs=None, scratch=(), cost=2_000_000, limit=32):
    return pl.pallas_call(
        kernel,
        out_shape=out_shape,
        in_specs=specs if specs is not None else [VMEM] * n_in,
        out_specs=outs if outs is not None else jax.tree.map(lambda _: VMEM, out_shape),
        scratch_shapes=list(scratch),
        compiler_params=pltpu.CompilerParams(vmem_limit_bytes=limit * 1024 * 1024),
        cost_estimate=pl.CostEstimate(flops=cost, bytes_accessed=cost, transcendentals=0),
    )


def in_hbm(array):
    return pltpu.with_memory_space_constraint(array, pltpu.HBM)


def lanes_of(shape):
    return lax.broadcasted_iota(jnp.int32, shape, len(shape) - 1)


def subs_of(shape):
    return lax.broadcasted_iota(jnp.int32, shape, len(shape) - 2)


def start_kernel(right_ref, damping_ref, label_ref, w0_ref, inv_ref, pack_ref, stat_ref):
    nx, ny, nz = right_ref.shape
    gz = lax.axis_index("gz")
    lane = lanes_of((ny, nz))
    packed_w = jnp.zeros((ny, nz), F32)
    packed_i = jnp.zeros((ny, nz), F32)
    energy = jnp.zeros((ny, nz), F32)
    cells = jnp.zeros((ny, nz), F32)
    for x in range(nx):
        label = label_ref[x].astype(F32)
        right = right_ref[x]
        inv = 1.0 / (12.0 + damping_ref[x] * (1.0 + 3.0 * label))
        w0 = right * inv
        w0_ref[x] = w0
        inv_ref[x] = inv
        energy = energy + right * w0
        cells = cells + label
        turn = (PACK * x + 3) % nz
        begin = PACK * x + 3 * gz
        chosen = (lane >= begin) & (lane < begin + 3)
        packed_w = jnp.where(chosen, pltpu.roll(w0, turn, 1), packed_w)
        packed_i = jnp.where(chosen, pltpu.roll(inv, turn, 1), packed_i)
    pack_ref[0] = packed_w
    pack_ref[1] = packed_i
    stat_ref[0] = jnp.broadcast_to(jnp.sum(energy, axis=0, keepdims=True), (SUB, nz))
    stat_ref[1] = jnp.broadcast_to(jnp.sum(cells, axis=0, keepdims=True), (SUB, nz))


def steps_of(axis):
    return 1 if lax.axis_size(axis) == 2 else 2


def upper_in(axis, step):
    return lax.rem(lax.axis_index(axis), 2) == step


def has_partner(axis, step):
    here = lax.axis_index(axis)
    return jnp.where(upper_in(axis, step), here < lax.axis_size(axis) - 1, here > 0)


def unpack_rows(tile, step):
    sub = subs_of(tile.shape)
    up, there = upper_in("gy", step), has_partner("gy", step)
    depth = jnp.where(there, jnp.where(up, SUB - 1 - sub, sub), -1)
    return jnp.where(depth >= 5, tile, 0.0), jnp.where(depth >= 6, pltpu.roll(tile, 4, 0), 0.0)


def halo_rows(tiles):
    w_tile, i_tile = unpack_rows(tiles[0], 0)
    for step, tile in enumerate(tiles[1:], 1):
        w_more, i_more = unpack_rows(tile, step)
        w_tile, i_tile = w_tile + w_more, i_tile + i_more
    return w_tile, i_tile


def faces_kernel(n_y, w0_ref, inv_ref, own_ref, got_ref, stat_ref, slab_ref, *refs):
    y_refs, x_refs, edge_refs = refs[:n_y], refs[n_y : n_y + 2], refs[n_y + 2 :]
    nx, ny, nz = w0_ref.shape
    sub = subs_of((SUB, nz))
    lane = lanes_of((ny, nz))
    slab_ref[...] = own_ref[...] + got_ref[...]
    for step, face_ref in enumerate(y_refs):
        up = upper_in("gy", step)
        keep_w = jnp.where(up, sub, SUB - 1 - sub) >= 5
        for x in range(nx + 1):
            w_rows, i_rows = (w0_ref.at[x], inv_ref.at[x]) if x < nx else (slab_ref.at[0], slab_ref.at[1])
            w_face = jnp.where(up, w_rows[ny - SUB :], w_rows[:SUB])
            i_face = jnp.where(up, i_rows[ny - SUB :], i_rows[:SUB])
            face_ref[x] = jnp.where(keep_w, w_face, pltpu.roll(i_face, 4, 0))
    cells = jnp.sum(stat_ref[1, 0:1], axis=1, keepdims=True)
    slab_w = slab_ref[0]
    half = pltpu.roll(slab_ref[1], nz // 2, 1)
    up_slab = jnp.where(lane >= nz - 3 * PACK, slab_w, half)
    down_slab = jnp.where(lane < 3 * PACK, slab_w, half)
    for step, face_ref in enumerate(x_refs):
        up = upper_in("gx", step)
        first = jnp.where(up, nx - 3, 0)
        for k in range(3):
            face_ref[k] = w0_ref[first + k]
        for k in range(2):
            face_ref[3 + k] = inv_ref[jnp.where(up, nx - 2, 0) + k]
        face_ref[5] = jnp.where(lane == COUNT_LANE, cells, jnp.where(up, up_slab, down_slab))
        for y_step, y_ref in enumerate(y_refs):
            edge_ref = edge_refs[step * n_y + y_step]
            for k in range(3):
                edge_ref[k] = y_ref[first + k]
            edge_ref[3] = y_ref[nx]


def slab_step(v, s, inv):
    width = v.shape[1]
    across = pltpu.roll(v, PACK, 1) + pltpu.roll(v, width - PACK, 1)
    q = v + 0.5 * (s + across)
    if inv is None:
        return q, None
    total = (
        pltpu.roll(q, 1, 1) + pltpu.roll(q, width - 1, 1) + s + across
        + 0.5 * (pltpu.roll(s, PACK, 1) + pltpu.roll(s, width - PACK, 1))
    )
    return q, total * inv


def along_z(q, half, column, gz):
    nz = q.shape[1]
    lane = lanes_of(q.shape)
    entry = (nz - 1) * (1 - gz)
    turn = lax.rem(entry - (column + 3 - gz) + 2 * nz, nz)
    up = jnp.where(lane == nz - 1, 0.0, pltpu.roll(q, nz - 1, 1))
    down = jnp.where(lane == 0, 0.0, pltpu.roll(q, 1, 1))
    return up + down + jnp.where(lane == entry, pltpu.roll(half, turn, 1), 0.0)


def sweep(stage, spans, nx, ny, nz, gz, get, get_inv, put, slab_q, sums):
    margin = 2 - stage
    start = SUB - margin
    tiles = ny // SUB + (margin > 0)
    own = subs_of((SUB, nz)) >= margin
    parts = [[], []]
    for tile in range(tiles):
        row = start + SUB * tile
        q_rows = slab_q[SUB * tile : SUB * tile + SUB]
        acc = [jnp.zeros((SUB, nz), F32) for _ in range(2)]

        def beside(x):
            return get(x, row - 1) + get(x, row + 1)

        for first, last in spans:
            s_low, s_mid = beside(first - 1), beside(first)
            v_low, v_mid = get(first - 1, row), get(first, row)
            for x in range(first, last):
                v_high, s_high = get(x + 1, row), beside(x + 1)
                across = v_low + v_high
                column = (PACK * x) % (2 * nz)
                half = q_rows[:, column // nz * nz : column // nz * nz + nz]
                rest = s_mid + across
                total = along_z(v_mid + 0.5 * rest, half, column % nz, gz) + rest + 0.5 * (s_low + s_high)
                if stage < 2:
                    after = total * get_inv(x, row)
                    put(x, row, after)
                if 0 <= x < nx:
                    acc[0] = acc[0] + v_mid * total
                    if stage < 2:
                        acc[1] = acc[1] + after * total
                v_low, v_mid, s_low, s_mid = v_mid, v_high, s_mid, s_high
        for k in range(2):
            parts[k].append(acc[k])
    for k in range(2 if stage < 2 else 1):
        part = parts[k]
        total = part[1]
        for other in part[2 : ny // SUB]:
            total = total + other
        total = total + (jnp.where(own, part[0], part[-1]) if margin else part[0])
        sums[2 * stage + k] = total


def inner_kernel(n_y, w0_ref, inv_ref, slab_ref, *refs):
    y_refs, (a_ref, i_ref, b_ref, c_ref, sum_ref, own_slab_ref, slabs_ref) = refs[:n_y], refs[n_y:]
    nx, ny, nz = w0_ref.shape
    gz = lax.axis_index("gz")
    for x in range(nx + 1):
        halos = halo_rows([ref[x] for ref in y_refs])
        for k in range(2):
            if x < nx:
                ref, own = (a_ref, i_ref)[k].at[x], (w0_ref, inv_ref)[k][x]
            else:
                ref, own = own_slab_ref.at[k], slab_ref[k]
            ref[:SUB] = halos[k]
            ref[SUB : SUB + ny] = own
            ref[SUB + ny :] = halos[k]
    for k in range(2):
        slabs_ref[3 * k] = own_slab_ref[k]
    sums = {}
    for stage in range(3):
        source, target = (a_ref, b_ref, c_ref)[stage], (b_ref, c_ref, None)[stage]
        start, size = SUB - 2 + stage, ny if stage == 2 else ny + SUB
        v = slabs_ref[stage, start : start + size]
        s = slabs_ref[stage, start - 1 : start - 1 + size] + slabs_ref[stage, start + 1 : start + 1 + size]
        q, after = slab_step(v, s, slabs_ref[3, start : start + size] if stage < 2 else None)
        if stage < 2:
            slabs_ref[stage + 1, start : start + size] = after

        def put(x, row, value):
            target[x, row : row + SUB] = value

        sweep(
            stage, [(1 + stage, nx - 1 - stage)], nx, ny, nz, gz,
            lambda x, row: source[x, row : row + SUB], lambda x, row: i_ref[x, row : row + SUB],
            put, q, sums,
        )
    for k in range(5):
        sum_ref[k] = sums[k]


def outer_kernel(
    n_y, column_total, after_ref, a_ref, i_ref, b_ref, c_ref, slab_ref, sum_ref, stat_ref, *refs
):
    x_refs, corner_refs = refs[:2], refs[2 : 2 + 2 * n_y]
    ea_ref, eb_ref, ec_ref, slabs_ref, total_ref, where_ref, ei_ref, si_ref = refs[2 + 2 * n_y :]
    nx, ny, nz = a_ref.shape[0], a_ref.shape[1] - 2 * SUB, a_ref.shape[2]
    ring = ny + SUB
    gz = lax.axis_index("gz")
    odd = lax.rem(lax.axis_index("gx"), 2) == 1

    def beyond(upper, read):
        there = has_partner("gx", 0) if upper else has_partner("gx", 1)
        swapped = has_partner("gx", 1) if upper else has_partner("gx", 0)
        first, second = read(0), read(1)
        if upper:
            return jnp.where(jnp.where(odd, swapped, there), jnp.where(odd, second, first), 0.0)
        return jnp.where(jnp.where(odd, swapped, there), jnp.where(odd, first, second), 0.0)

    def write(ref, at, own, halo):
        ref[at, :SUB] = halo
        ref[at, SUB : SUB + ny] = own
        ref[at, SUB + ny :] = halo

    lane_tile, lane = lanes_of((SUB, nz)), lanes_of((ny, nz))
    slab_parts = []
    for side, upper in enumerate((False, True)):
        tiles = [
            halo_rows([beyond(upper, lambda step: corner_refs[step * n_y + j][k]) for j in range(n_y)])
            for k in range(4)
        ]
        for k in range(3):
            write(ea_ref, 3 * side + k, beyond(upper, lambda step: x_refs[step][k]), tiles[k][0])
        for k in range(2):
            own = beyond(upper, lambda step: x_refs[step][3 + k])
            write(ei_ref, 2 * side + k, own, tiles[k if upper else k + 1][1])
        own = beyond(upper, lambda step: x_refs[step][5])

        def near(value, lanes, planes):
            return jnp.where(lanes < planes * PACK if upper else lanes >= nz - planes * PACK, value, 0.0)

        slab_parts.append((
            near(own, lane, 3), near(tiles[3][0], lane_tile, 3),
            near(pltpu.roll(own, nz // 2, 1), lane, 2), near(tiles[3][1], lane_tile, 2),
            own[0:1, COUNT_LANE : COUNT_LANE + 1],
        ))

    low, high = slab_parts
    for ref, k in ((slabs_ref, 0), (si_ref, 1)):
        ref[0, :, :nz] = slab_ref[k]
        ref[0, SUB : SUB + ny, nz:] = low[2 * k] + high[2 * k]
        ref[0, :SUB, nz:] = low[2 * k + 1] + high[2 * k + 1]
        ref[0, SUB + ny :, nz:] = low[2 * k + 1] + high[2 * k + 1]

    def reader(inside_ref, edge_ref, first, count):
        def get(x, row):
            if first <= x < nx - first:
                return inside_ref[x, row : row + SUB]
            at = x - (first - count) if x < first else x - (nx - first) + count
            return edge_ref[at, row : row + SUB]

        return get

    sums = {}
    for stage in range(3):
        get = reader((a_ref, b_ref, c_ref)[stage], (ea_ref, eb_ref, ec_ref)[stage], stage, 3)
        start, size = SUB - 2 + stage, ny if stage == 2 else ring
        v = slabs_ref[stage, start : start + size]
        s = slabs_ref[stage, start - 1 : start - 1 + size] + slabs_ref[stage, start + 1 : start + 1 + size]
        q, after = slab_step(v, s, si_ref[0, start : start + size] if stage < 2 else None)
        if stage < 2:
            slabs_ref[stage + 1, start : start + size] = after

        def put(x, row, value):
            edge_ref = (eb_ref, ec_ref)[stage]
            at = x - (stage - 2) if x < nx // 2 else x - (nx - 1 - stage) + 3
            edge_ref[at, row : row + SUB] = value

        sweep(
            stage, [(stage - 2, stage + 1), (nx - 1 - stage, nx + 2 - stage)], nx, ny, nz, gz,
            get, reader(i_ref, ei_ref, 0, 2), put, q, sums,
        )

    total_ref[0:1] = stat_ref[0, 0:1]
    for k in range(5):
        total_ref[k + 1 : k + 2] = jnp.sum(sums[k] + sum_ref[k], axis=0, keepdims=True)
    total_ref[6:8] = jnp.zeros((2, nz), F32)
    gx, n_x = lax.axis_index("gx"), lax.axis_size("gx")
    count = jnp.sum(stat_ref[1, 0:1], axis=1, keepdims=True)
    below, above = [part[4] for part in slab_parts]
    begin = jnp.where(
        gx == 0, 0.0,
        jnp.where(gx == 1, below, jnp.where(gx == n_x - 1, column_total - count, column_total - count - above)),
    )
    where_ref[0:1] = jnp.broadcast_to(begin, (1, nz))
    where_ref[1:2] = jnp.broadcast_to(count, (1, nz))
    where_ref[2:8] = jnp.zeros((6, nz), F32)


def shift_up(v, amount):
    if amount < SUB:
        return pltpu.roll(v, v.shape[0] - amount, 0)
    return jnp.concatenate([v[amount:], v[:amount]], axis=0)


def plan_kernel(after_ref, label_ref, index_ref, plan_ref, lane_ref):
    rows, slot_rows = label_ref.shape[0], index_ref.shape[0]
    wide = -(-(slot_rows + 1) // LANES) * LANES
    shape = (rows, LANES)
    lane, row = lanes_of(shape), subs_of(shape)
    ones = (label_ref[...] == 1).astype(jnp.bfloat16)
    totals = jnp.dot(ones, jnp.ones((LANES, LANES), jnp.bfloat16), preferred_element_type=F32)
    lower = (subs_of((rows, rows)) > lanes_of((rows, rows))).astype(jnp.bfloat16)
    before = jnp.dot(lower, totals.astype(jnp.bfloat16), preferred_element_type=F32).astype(jnp.int32)
    target, first = lax.div(before, LANES), lax.rem(before, LANES)
    listed = jnp.concatenate(
        [lax.rem(index_ref[...], LANES).astype(F32), jnp.zeros((wide - slot_rows, LANES), F32)], axis=0
    ).astype(jnp.bfloat16)
    spread = jnp.concatenate([target] * (wide // LANES), axis=1)
    place = lanes_of((rows, wide))
    here = jnp.dot((spread == place).astype(jnp.bfloat16), listed, preferred_element_type=F32)
    after = jnp.dot((spread + 1 == place).astype(jnp.bfloat16), listed, preferred_element_type=F32)
    lane_ref[...] = jnp.where(lane >= first, here, after).astype(jnp.int32)
    wrapped = (lane < first).astype(jnp.int32)
    filled = lane - first + LANES * wrapped < totals.astype(jnp.int32)
    way = jnp.where(filled, row - target - wrapped, 0)
    plan = jnp.zeros(shape, jnp.int32)
    step = 1
    while step < rows:
        moving = jnp.where((way & step) != 0, way, 0)
        arriving = shift_up(moving, step)
        plan = plan | (arriving & step)
        way = (way - moving) | arriving
        step *= 2
    plan_ref[...] = plan


def galerkin(t):
    g00, g01, g02, g12, g22 = t[0] - t[1], t[1] - t[2], t[2] - t[3], t[3] - t[4], t[4] - t[5]
    g11 = g02
    l10, l20 = g01 / g00, g02 / g00
    d1 = g11 - l10 * g01
    m21 = g12 - l20 * g01
    ok1 = d1 > 1e-6 * g11
    d1 = jnp.where(ok1, d1, 1.0)
    l21 = jnp.where(ok1, m21 / d1, 0.0)
    d2 = g22 - l20 * g02 - l21 * m21
    ok2 = ok1 & (d2 > 1e-6 * g22)
    d2 = jnp.where(ok2, d2, 1.0)
    y1 = t[1] - l10 * t[0]
    y2 = t[2] - l20 * t[0] - l21 * y1
    c2 = jnp.where(ok2, y2 / d2, 0.0)
    c1 = jnp.where(ok1, y1 / d1 - l21 * c2, 0.0)
    c0 = t[0] / g00 - l10 * c1 - l20 * c2
    return c0, c1, c2


def couple_kernel(
    stage, slot_rows, after_ref, where_ref, inside_ref, edge_ref, slabs_ref, plan_ref, lane_ref, blocks_ref,
    value_ref, buf_ref,
):
    nx, nz = inside_ref.shape[0], inside_ref.shape[2]
    ny = inside_ref.shape[1] - 2 * SUB
    rows = nx * ny
    gz = lax.axis_index("gz")

    def get(x, row):
        if stage <= x < nx - stage:
            return inside_ref[x, row : row + SUB]
        return edge_ref[x - (stage - 3) if x < stage else x - (nx - stage) + 3, row : row + SUB]

    for tile in range(ny // SUB):
        row = SUB + SUB * tile
        slab = slabs_ref[stage, row : row + SUB, :nz]
        v_low, v_mid = get(-1, row), get(0, row)
        for x in range(nx):
            v_high = get(x + 1, row)
            beside = get(x, row - 1) + get(x, row + 1)
            at = ny * x + SUB * tile
            value_ref[at : at + SUB] = (
                along_z(v_mid, slab, PACK * x, gz) + beside + (v_low + v_high) - 6.0 * v_mid
            )
            v_low, v_mid = v_mid, v_high
    value = jnp.take_along_axis(value_ref[...], lane_ref[...], axis=1)
    plan = plan_ref[...]
    step = 1
    while step < rows:
        value = jnp.where((plan & step) != 0, shift_up(value, step), value)
        step *= 2
    offset = jnp.max(where_ref[0:1]).astype(jnp.int32)
    count = jnp.max(where_ref[1:2]).astype(jnp.int32)
    shape = (slot_rows, LANES)
    slots = jnp.where(subs_of(shape) * LANES + lanes_of(shape) < count, value[:slot_rows], 0.0)
    slots = jnp.concatenate([slots, jnp.zeros((SUB, LANES), F32)], axis=0)
    inner = lax.rem(offset, LANES)
    turned = pltpu.roll(slots, inner, 1)
    moved = jnp.where(lanes_of((slot_rows + SUB, LANES)) >= inner, turned, pltpu.roll(turned, 1, 0))
    buf_ref[...] = jnp.zeros_like(buf_ref)
    buf_ref[pl.ds(offset // LANES, slot_rows + SUB), :] = moved
    gx = lax.axis_index("gx")
    n_gx = lax.axis_size("gx")
    size = blocks_ref.shape[0] // n_gx
    for block in range(n_gx):
        begin = pl.multiple_of((gx ^ block) * size, SUB)
        blocks_ref[block * size : block * size + size] = buf_ref[pl.ds(begin, size), :]


def add_kernel(a_ref, b_ref, after_ref, out_ref):
    out_ref[...] = a_ref[...] + b_ref[...]


def pack_kernel(total_ref, *refs):
    list_refs, out_refs = refs[:3], refs[3:]
    size = (out_refs[0].shape[0] - SUB) // 3
    for block, out_ref in enumerate(out_refs):
        for k, list_ref in enumerate(list_refs):
            out_ref[k * size : k * size + size] = list_ref[block * size : block * size + size]
        out_ref[3 * size :] = total_ref[...]


def membrane_kernel(
    half_ref, slope_ref, tau_ref, cond_ref, rev_ref, after_ref, v_ref, gates_ref, cot_ref,
    base_ref, sum_ref, factor_ref, coef_ref,
):
    n_states, rows = gates_ref.shape[:2]
    v = v_ref[...]

    def state(g, carry):
        total, current = carry
        inv_slope = 1.0 / slope_ref[g]
        tau_base = tau_ref[g]
        scaled = (v - half_ref[g]) * inv_slope
        gate = gates_ref[g]
        cot = cot_ref[g]
        steady = 1.0 / (1.0 + jnp.exp(-scaled))
        bell = jnp.exp(-scaled * scaled)
        rate = TIME_STEP / (tau_base * (0.5 + bell))
        decay = jnp.exp(-rate)
        steady_slope = steady * (1.0 - steady)
        decay_slope = decay * rate * rate * ((tau_base / TIME_STEP) * bell * (-2.0 * scaled))
        change = (steady_slope * (1.0 - decay) + (gate - steady) * decay_slope) * inv_slope
        base_ref[g] = cot * decay
        coef_ref[0, pl.ds(g, 1)] = jnp.full((1, LANES), TIME_STEP * cond_ref[g])
        coef_ref[1, pl.ds(g, 1)] = jnp.full((1, LANES), rev_ref[g])
        return total + cot * change, current + cond_ref[g] * gate

    zero = jnp.zeros((rows, LANES), F32)
    total, current = lax.fori_loop(0, n_states, state, (zero, zero), unroll=2)
    sum_ref[...] = total
    factor_ref[...] = 1.0 - TIME_STEP * current


def finish_kernel(
    alone, coef_ref, vcot_ref, v_ref, sum_ref, factor_ref, base_ref, a_ref, b_ref, c_ref, eb_ref, ec_ref, *refs
):
    n_small, n_large = len(alone[0]), len(alone[1])
    own_ref, small_refs, large_refs = refs[0], refs[1 : 1 + n_small], refs[1 + n_small : 1 + n_small + n_large]
    x_ref, volt_ref, gate_ref = refs[1 + n_small + n_large :]
    size = (own_ref.shape[0] - SUB) // 3
    gx = lax.axis_index("gx")

    def is_one(flags):
        found = gx < 0
        for place, flag in enumerate(flags):
            if flag:
                found = found | (gx == place)
        return found

    total = own_ref[3 * size :]
    for flags, ref in zip(alone[0], small_refs):
        total = total + jnp.where(is_one(flags), ref[...], 0.0)
    for flags, ref in zip(alone[1], large_refs):
        total = total + jnp.where(is_one(flags), 0.0, ref[3 * size :])
    sums = jnp.sum(total, axis=1, keepdims=True)
    c0, c1, c2 = galerkin([jnp.broadcast_to(sums[k : k + 1], (1, LANES)) for k in range(6)])
    landed = jnp.zeros((size, LANES), F32)
    for k, c in enumerate((c0, c1, c2)):
        part = own_ref[k * size : k * size + size]
        for ref in large_refs:
            part = part + ref[k * size : k * size + size]
        landed = landed + c * part
    cot = vcot_ref[...] + landed
    v = v_ref[...]
    volt_ref[...] = cot * factor_ref[...] + sum_ref[...]
    for g in range(base_ref.shape[0]):
        gate_ref[g] = base_ref[g] - (coef_ref[0, g : g + 1] * cot) * (v - coef_ref[1, g : g + 1])
    nx, ny, nz = x_ref.shape
    own = slice(SUB, SUB + ny)
    for x in range(nx):
        w1 = b_ref[x, own] if 1 <= x < nx - 1 else eb_ref[2 if x == 0 else 3, own]
        w2 = c_ref[x, own] if 2 <= x < nx - 2 else ec_ref[x + 1 if x < 2 else x - (nx - 2) + 3, own]
        x_ref[x] = c0 * a_ref[x, own] + c1 * w1 + c2 * w2


def partners(axis, step):
    count = lax.axis_size(axis)
    if step == 0:
        return [i ^ 1 for i in range(count)]
    return [0] + [i + 1 if i % 2 else i - 1 for i in range(1, count - 1)] + [count - 1]


def swap(value, x_to=None, y_to=None):
    n_x, n_y, n_z = [lax.axis_size(axis) for axis in ("gx", "gy", "gz")]
    pairs = []
    for x in range(n_x):
        for y in range(n_y):
            to_x, to_y = x_to[x] if x_to else x, y_to[y] if y_to else y
            alone = (x_to and to_x == x) or (y_to and to_y == y)
            for z in range(n_z):
                to = (x, y, z ^ 1) if alone else (to_x, to_y, z)
                pairs.append(((x * n_y + y) * n_z + z, (to[0] * n_y + to[1]) * n_z + to[2]))
    return lax.ppermute(value, ("gx", "gy", "gz"), pairs)


def never_meet(count, k, slots, block):
    def apart(tile, owner):
        return owner * block >= (tile + 1) * slots or (owner + 1) * block <= count * block - (count - tile) * slots

    return [apart(i, i ^ k) and apart(i ^ k, i) for i in range(count)]


def local(
    potential_cot, damping, tissue_label, heart_index, voltage, gates, voltage_cot, gates_cot,
    half_voltage, gate_slope, tau_base, conductance, reversal,
):
    nx, ny, nz = potential_cot.shape
    rows = nx * ny
    ring = ny + SUB
    n_gx, n_gy = lax.axis_size("gx"), lax.axis_size("gy")
    n_states = gates.shape[0]
    block_rows = voltage.shape[1] // LANES
    slot_rows = heart_index.shape[3] // LANES
    block = shape_of(nx, ny, nz)
    flat = lambda a: a.reshape(rows, LANES)
    cells = lambda a: a.reshape(block_rows, LANES)
    states = lambda a: a.reshape(n_states, block_rows, LANES)

    w0, inv, packed, stat = call(
        start_kernel, (block, block, shape_of(2, ny, nz), shape_of(2, SUB, nz)), 3,
    )(in_hbm(potential_cot), in_hbm(damping), in_hbm(tissue_label))

    got = lax.ppermute(packed, "gz", [(0, 1), (1, 0)])
    cells_shape = jax.ShapeDtypeStruct((rows, LANES), jnp.int32)
    plan, lanes = call(plan_kernel, (cells_shape, cells_shape), 3, cost=6_000_000)(
        stat, flat(tissue_label), heart_index.reshape(slot_rows, LANES)
    )

    n_y = steps_of("gy")
    shapes = (
        (shape_of(2, ny, nz),) + (shape_of(nx + 1, SUB, nz),) * n_y + (shape_of(6, ny, nz),) * 2
        + (shape_of(4, SUB, nz),) * (2 * n_y)
    )
    slab, *faces = call(functools.partial(faces_kernel, n_y), shapes, 5)(w0, inv, packed, got, stat)
    along_y, along_x, across = faces[:n_y], faces[n_y : n_y + 2], faces[n_y + 2 :]
    y_to = [partners("gy", step) for step in range(n_y)]
    x_to = [partners("gx", step) for step in range(2)]
    along_y = [swap(face, y_to=y_to[j]) for j, face in enumerate(along_y)]
    along_x = [swap(face, x_to=x_to[i]) for i, face in enumerate(along_x)]
    across = [swap(face, x_to=x_to[k // n_y], y_to=y_to[k % n_y]) for k, face in enumerate(across)]

    tall = ring + SUB
    planes = shape_of(nx, tall, nz)
    edges = shape_of(6, tall, nz)
    in0, in_inv, in1, in2, in_sums, own_slab = call(
        functools.partial(inner_kernel, n_y),
        (planes,) * 4 + (shape_of(5, SUB, nz), shape_of(2, tall, nz)),
        3 + n_y,
        scratch=[pltpu.VMEM((4, tall, nz), F32)],
        cost=6_000_000,
    )(w0, inv, slab, *along_y)
    ends0, ends1, ends2, slabs, sums, where = call(
        functools.partial(outer_kernel, n_y, float(n_gx * voltage.shape[1])),
        (edges,) * 3 + (shape_of(3, tall, 2 * nz), shape_of(SUB, nz), shape_of(SUB, nz)),
        10 + 2 * n_y,
        scratch=[pltpu.VMEM((4, tall, nz), F32), pltpu.VMEM((1, tall, 2 * nz), F32)],
    )(plan, in0, in_inv, in1, in2, own_slab, in_sums, stat, *along_x, *across)

    if n_gx > 4:
        counts = lax.all_gather(jnp.sum(stat[1, 0]), "gx")
        begin = jnp.sum(jnp.where(jnp.arange(n_gx) < lax.axis_index("gx"), counts, 0.0))
        where = where.at[0].set(begin)

    def couple(stage, after, inside, ends):
        return call(
            functools.partial(couple_kernel, stage, slot_rows),
            shape_of(n_gx * block_rows, LANES),
            7,
            scratch=[
                pltpu.VMEM((rows, LANES), F32), pltpu.VMEM((n_gx * block_rows + slot_rows + SUB, LANES), F32),
            ],
            cost=6_000_000,
        )(after, where, inside, ends, slabs, plan, lanes)

    def add(value, axis, step, after):
        got = lax.ppermute(value, axis, [(i, i ^ step) for i in range(lax.axis_size(axis))])
        return call(add_kernel, shape_of(SUB, nz), 3)(value, got, after)

    list0 = couple(0, sums, in0, ends0)
    sums = add(sums, "gz", 1, list0)
    list1 = couple(1, sums, in1, ends1)
    list2 = couple(2, list1, in2, ends2)
    for step in [2**k for k in range(n_gy.bit_length() - 1)]:
        sums = add(sums, "gy", step, list2)
    blocks = call(pack_kernel, (shape_of(3 * block_rows + SUB, LANES),) * n_gx, 4)(sums, list0, list1, list2)
    apart = {k: never_meet(n_gx, k, slot_rows, block_rows) for k in range(1, n_gx)}
    small, meets = [], []
    for k in range(1, n_gx):
        if any(apart[k]):
            small.append(swap(sums, x_to=[i ^ k if apart[k][i] else i for i in range(n_gx)]))
        meets.append(not all(apart[k]))
    order = [k for k in [2, 3, 1] + list(range(4, n_gx)) if k < n_gx and meets[k - 1]]
    large = [swap(blocks[k], x_to=[i if apart[k][i] else i ^ k for i in range(n_gx)]) for k in order]
    alone = [[apart[k] for k in range(1, n_gx) if any(apart[k])], [apart[k] for k in order]]

    base, total_change, factor, state_coefs = call(
        membrane_kernel,
        (
            shape_of(n_states, block_rows, LANES), shape_of(block_rows, LANES), shape_of(block_rows, LANES),
            shape_of(2, n_states, LANES),
        ),
        9,
        specs=[SMEM] * 5 + [VMEM] * 4,
        cost=6_000_000,
    )(
        half_voltage, gate_slope, tau_base, conductance, reversal,
        blocks[0], cells(voltage), states(gates), states(gates_cot),
    )
    solution, volt_grad, gate_grad = call(
        functools.partial(finish_kernel, alone),
        (block, shape_of(block_rows, LANES), shape_of(n_states, block_rows, LANES)),
        12 + len(small) + len(large),
    )(
        state_coefs, cells(voltage_cot), cells(voltage), total_change, factor, base,
        in0, in1, in2, ends1, ends2, blocks[0], *small, *large,
    )
    return solution, volt_grad.reshape(voltage.shape), gate_grad.reshape(gates.shape)


def solution(mesh):
    grid = P(("groups", "gx"), "gy", "gz")
    cells = P(("groups", "gy", "gz"), "gx")
    states = P(None, ("groups", "gy", "gz"), "gx")
    in_specs = (
        grid, grid, grid, P(("groups", "gx"), "gy", "gz", None), cells, states, cells, states,
        P(), P(), P(), P(), P(),
    )
    return jax.shard_map(
        local, mesh=mesh, in_specs=in_specs, out_specs=(grid, cells, states), check_vma=False
    )
```

```python
import functools

import jax
import jax.numpy as jnp
from jax import lax
from jax.experimental import pallas as pl
from jax.experimental.pallas import tpu as pltpu
from jax.sharding import PartitionSpec as P

TIME_STEP = 0.5
LANES = 128
SUB = 8
PACK = 8
COUNT_LANE = 4 * PACK
F32 = jnp.float32

VMEM = pl.BlockSpec(memory_space=pltpu.VMEM)
SMEM = pl.BlockSpec(memory_space=pltpu.SMEM)
HBM = pl.BlockSpec(memory_space=pltpu.HBM)


def shape_of(*dims):
    return jax.ShapeDtypeStruct(dims, F32)


def call(kernel, out_shape, n_in, specs=None, outs=None, scratch=(), cost=2_000_000, limit=32):
    return pl.pallas_call(
        kernel,
        out_shape=out_shape,
        in_specs=specs if specs is not None else [VMEM] * n_in,
        out_specs=outs if outs is not None else jax.tree.map(lambda _: VMEM, out_shape),
        scratch_shapes=list(scratch),
        compiler_params=pltpu.CompilerParams(vmem_limit_bytes=limit * 1024 * 1024),
        cost_estimate=pl.CostEstimate(flops=cost, bytes_accessed=cost, transcendentals=0),
    )


def in_hbm(array):
    return pltpu.with_memory_space_constraint(array, pltpu.HBM)


def lanes_of(shape):
    return lax.broadcasted_iota(jnp.int32, shape, len(shape) - 1)


def subs_of(shape):
    return lax.broadcasted_iota(jnp.int32, shape, len(shape) - 2)


def start_kernel(right_ref, damping_ref, label_ref, w0_ref, inv_ref, pack_ref, stat_ref):
    nx, ny, nz = right_ref.shape
    gz = lax.axis_index("gz")
    lane = lanes_of((ny, nz))
    packed_w = jnp.zeros((ny, nz), F32)
    packed_i = jnp.zeros((ny, nz), F32)
    energy = jnp.zeros((ny, nz), F32)
    cells = jnp.zeros((ny, nz), F32)
    for x in range(nx):
        label = label_ref[x].astype(F32)
        right = right_ref[x]
        inv = 1.0 / (12.0 + damping_ref[x] * (1.0 + 3.0 * label))
        w0 = right * inv
        w0_ref[x] = w0
        inv_ref[x] = inv
        energy = energy + right * w0
        cells = cells + label
        turn = (PACK * x + 3) % nz
        begin = PACK * x + 3 * gz
        chosen = (lane >= begin) & (lane < begin + 3)
        packed_w = jnp.where(chosen, pltpu.roll(w0, turn, 1), packed_w)
        packed_i = jnp.where(chosen, pltpu.roll(inv, turn, 1), packed_i)
    pack_ref[0] = packed_w
    pack_ref[1] = packed_i
    stat_ref[0] = jnp.broadcast_to(jnp.sum(energy, axis=0, keepdims=True), (SUB, nz))
    stat_ref[1] = jnp.broadcast_to(jnp.sum(cells, axis=0, keepdims=True), (SUB, nz))


def steps_of(axis):
    return 1 if lax.axis_size(axis) == 2 else 2


def upper_in(axis, step):
    return lax.rem(lax.axis_index(axis), 2) == step


def has_partner(axis, step):
    here = lax.axis_index(axis)
    return jnp.where(upper_in(axis, step), here < lax.axis_size(axis) - 1, here > 0)


def unpack_rows(tile, step):
    sub = subs_of(tile.shape)
    up, there = upper_in("gy", step), has_partner("gy", step)
    depth = jnp.where(there, jnp.where(up, SUB - 1 - sub, sub), -1)
    return jnp.where(depth >= 5, tile, 0.0), jnp.where(depth >= 6, pltpu.roll(tile, 4, 0), 0.0)


def halo_rows(tiles):
    w_tile, i_tile = unpack_rows(tiles[0], 0)
    for step, tile in enumerate(tiles[1:], 1):
        w_more, i_more = unpack_rows(tile, step)
        w_tile, i_tile = w_tile + w_more, i_tile + i_more
    return w_tile, i_tile


def faces_kernel(n_y, w0_ref, inv_ref, own_ref, got_ref, stat_ref, slab_ref, *refs):
    y_refs, x_refs, edge_refs = refs[:n_y], refs[n_y : n_y + 2], refs[n_y + 2 :]
    nx, ny, nz = w0_ref.shape
    sub = subs_of((SUB, nz))
    lane = lanes_of((ny, nz))
    slab_ref[...] = own_ref[...] + got_ref[...]
    for step, face_ref in enumerate(y_refs):
        up = upper_in("gy", step)
        keep_w = jnp.where(up, sub, SUB - 1 - sub) >= 5
        for x in range(nx + 1):
            w_rows, i_rows = (w0_ref.at[x], inv_ref.at[x]) if x < nx else (slab_ref.at[0], slab_ref.at[1])
            w_face = jnp.where(up, w_rows[ny - SUB :], w_rows[:SUB])
            i_face = jnp.where(up, i_rows[ny - SUB :], i_rows[:SUB])
            face_ref[x] = jnp.where(keep_w, w_face, pltpu.roll(i_face, 4, 0))
    cells = jnp.sum(stat_ref[1, 0:1], axis=1, keepdims=True)
    slab_w = slab_ref[0]
    half = pltpu.roll(slab_ref[1], nz // 2, 1)
    up_slab = jnp.where(lane >= nz - 3 * PACK, slab_w, half)
    down_slab = jnp.where(lane < 3 * PACK, slab_w, half)
    for step, face_ref in enumerate(x_refs):
        up = upper_in("gx", step)
        first = jnp.where(up, nx - 3, 0)
        for k in range(3):
            face_ref[k] = w0_ref[first + k]
        for k in range(2):
            face_ref[3 + k] = inv_ref[jnp.where(up, nx - 2, 0) + k]
        face_ref[5] = jnp.where(lane == COUNT_LANE, cells, jnp.where(up, up_slab, down_slab))
        for y_step, y_ref in enumerate(y_refs):
            edge_ref = edge_refs[step * n_y + y_step]
            for k in range(3):
                edge_ref[k] = y_ref[first + k]
            edge_ref[3] = y_ref[nx]


SUMS = (("w0 k0", "w1 k0"), ("w1 n1", "w1 k1", "w2 k1", "w0 n1"), ("w2 k2",))
ORDER = ("w0 r", "w0 k0", "w1 k0", "w1 n1", "w1 k1", "w2 k1", "w2 k2", "w0 n1")


def slab_step(stage, v, s, inv):
    width = v.shape[1]
    across = pltpu.roll(v, PACK, 1) + pltpu.roll(v, width - PACK, 1)
    q = v + 0.5 * (s + across)
    if stage == 2:
        return q, None
    total = (
        pltpu.roll(q, 1, 1) + pltpu.roll(q, width - 1, 1) + s + across
        + 0.5 * (pltpu.roll(s, PACK, 1) + pltpu.roll(s, width - PACK, 1))
    )
    return q, next_vector(stage, v, total, inv)


def next_vector(stage, v, total, inv):
    return v - total * inv if stage == 0 else total * inv


def along_z(q, half, column, gz):
    nz = q.shape[1]
    lane = lanes_of(q.shape)
    entry = (nz - 1) * (1 - gz)
    turn = lax.rem(entry - (column + 3 - gz) + 2 * nz, nz)
    up = jnp.where(lane == nz - 1, 0.0, pltpu.roll(q, nz - 1, 1))
    down = jnp.where(lane == 0, 0.0, pltpu.roll(q, 1, 1))
    return up + down + jnp.where(lane == entry, pltpu.roll(half, turn, 1), 0.0)


def sweep(stage, spans, nx, ny, nz, gz, get, get_inv, put, slab_q, sums, get_right, get_w0, held):
    margin = 2 - stage
    start = SUB - margin
    tiles = ny // SUB + (margin > 0)
    own = subs_of((SUB, nz)) >= margin
    names = SUMS[stage]
    parts = {name: [] for name in names}
    for tile in range(tiles):
        row = start + SUB * tile
        q_rows = slab_q[SUB * tile : SUB * tile + SUB]
        acc = {name: jnp.zeros((SUB, nz), F32) for name in names}

        def beside(x):
            return get(x, row - 1) + get(x, row + 1)

        def rows(name, x):
            ref, at = held[name, x]
            return ref.at[at, row : row + SUB]

        for first, last in spans:
            s_low, s_mid = beside(first - 1), beside(first)
            v_low, v_mid = get(first - 1, row), get(first, row)
            for x in range(first, last):
                v_high, s_high = get(x + 1, row), beside(x + 1)
                across = v_low + v_high
                column = (PACK * x) % (2 * nz)
                half = q_rows[:, column // nz * nz : column // nz * nz + nz]
                rest = s_mid + across
                total = along_z(v_mid + 0.5 * rest, half, column % nz, gz) + rest + 0.5 * (s_low + s_high)
                if stage < 2:
                    after = next_vector(stage, v_mid, total, get_inv(x, row))
                    put(x, row, after)
                if 0 <= x < nx:
                    if stage == 0:
                        k0 = get_right(x, row) - total
                        rows("k0", x)[...] = k0
                        terms = (v_mid * k0, after * k0)
                    elif stage == 1:
                        rows("n1", x)[...] = total
                        k1 = rows("k0", x)[...] - total
                        terms = (v_mid * total, v_mid * k1, after * k1, get_w0(x, row) * total)
                    else:
                        terms = (v_mid * (rows("n1", x)[...] - total),)
                    for name, term in zip(names, terms):
                        acc[name] = acc[name] + term
                v_low, v_mid, s_low, s_mid = v_mid, v_high, s_mid, s_high
        for name in names:
            parts[name].append(acc[name])
    for name in names:
        part = parts[name]
        total = part[1]
        for other in part[2 : ny // SUB]:
            total = total + other
        sums[name] = total + (jnp.where(own, part[0], part[-1]) if margin else part[0])


def inner_kernel(n_y, right_ref, w0_ref, inv_ref, slab_ref, *refs):
    y_refs, refs = refs[:n_y], refs[n_y:]
    a_ref, i_ref, b_ref, c_ref, sum_ref, own_slab_ref, pass_ref, slabs_ref, r_ref, k_ref, n_ref = refs
    nx, ny, nz = w0_ref.shape
    gz = lax.axis_index("gz")
    for x in range(nx + 1):
        halos = halo_rows([ref[x] for ref in y_refs])
        for k in range(2):
            if x < nx:
                ref, own = (a_ref, i_ref)[k].at[x], (w0_ref, inv_ref)[k][x]
            else:
                ref, own = own_slab_ref.at[k], slab_ref[k]
            ref[:SUB] = halos[k]
            ref[SUB : SUB + ny] = own
            ref[SUB + ny :] = halos[k]
    for k in range(2):
        slabs_ref[3 * k] = own_slab_ref[k]
    for x in range(nx):
        r_ref[x, SUB : SUB + ny] = right_ref[x]
    held = {("k0", x): (k_ref, x) for x in range(nx)} | {("n1", x): (n_ref, x) for x in range(nx)}
    held |= {("k0", 1): (pass_ref, 0), ("k0", nx - 2): (pass_ref, 1)}
    held |= {("n1", 2): (pass_ref, 2), ("n1", nx - 3): (pass_ref, 3)}
    sums = {}
    for stage in range(3):
        source, target = (a_ref, b_ref, c_ref)[stage], (b_ref, c_ref, None)[stage]
        start, size = SUB - 2 + stage, ny if stage == 2 else ny + SUB
        v = slabs_ref[stage, start : start + size]
        s = slabs_ref[stage, start - 1 : start - 1 + size] + slabs_ref[stage, start + 1 : start + 1 + size]
        q, after = slab_step(stage, v, s, slabs_ref[3, start : start + size])
        if stage < 2:
            slabs_ref[stage + 1, start : start + size] = after

        def put(x, row, value):
            target[x, row : row + SUB] = value

        sweep(
            stage, [(1 + stage, nx - 1 - stage)], nx, ny, nz, gz,
            lambda x, row: source[x, row : row + SUB], lambda x, row: i_ref[x, row : row + SUB],
            put, q, sums,
            lambda x, row: r_ref[x, row : row + SUB], lambda x, row: a_ref[x, row : row + SUB], held,
        )
    for k, name in enumerate(ORDER[1:]):
        sum_ref[k] = sums[name]


def outer_kernel(
    n_y, column_total, after_ref, right_ref, a_ref, i_ref, b_ref, c_ref, slab_ref, sum_ref, pass_ref, stat_ref, *refs
):
    x_refs, corner_refs = refs[:2], refs[2 : 2 + 2 * n_y]
    ea_ref, eb_ref, ec_ref, slabs_ref, total_ref, where_ref, ei_ref, si_ref, r_ref, k_ref, n_ref = refs[2 + 2 * n_y :]
    nx, ny, nz = a_ref.shape[0], a_ref.shape[1] - 2 * SUB, a_ref.shape[2]
    ring = ny + SUB
    gz = lax.axis_index("gz")
    odd = lax.rem(lax.axis_index("gx"), 2) == 1

    def beyond(upper, read):
        there = has_partner("gx", 0) if upper else has_partner("gx", 1)
        swapped = has_partner("gx", 1) if upper else has_partner("gx", 0)
        first, second = read(0), read(1)
        if upper:
            return jnp.where(jnp.where(odd, swapped, there), jnp.where(odd, second, first), 0.0)
        return jnp.where(jnp.where(odd, swapped, there), jnp.where(odd, first, second), 0.0)

    def write(ref, at, own, halo):
        ref[at, :SUB] = halo
        ref[at, SUB : SUB + ny] = own
        ref[at, SUB + ny :] = halo

    lane_tile, lane = lanes_of((SUB, nz)), lanes_of((ny, nz))
    slab_parts = []
    for side, upper in enumerate((False, True)):
        tiles = [
            halo_rows([beyond(upper, lambda step: corner_refs[step * n_y + j][k]) for j in range(n_y)])
            for k in range(4)
        ]
        for k in range(3):
            write(ea_ref, 3 * side + k, beyond(upper, lambda step: x_refs[step][k]), tiles[k][0])
        for k in range(2):
            own = beyond(upper, lambda step: x_refs[step][3 + k])
            write(ei_ref, 2 * side + k, own, tiles[k if upper else k + 1][1])
        own = beyond(upper, lambda step: x_refs[step][5])

        def near(value, lanes, planes):
            return jnp.where(lanes < planes * PACK if upper else lanes >= nz - planes * PACK, value, 0.0)

        slab_parts.append((
            near(own, lane, 3), near(tiles[3][0], lane_tile, 3),
            near(pltpu.roll(own, nz // 2, 1), lane, 2), near(tiles[3][1], lane_tile, 2),
            own[0:1, COUNT_LANE : COUNT_LANE + 1],
        ))

    low, high = slab_parts
    for ref, k in ((slabs_ref, 0), (si_ref, 1)):
        ref[0, :, :nz] = slab_ref[k]
        ref[0, SUB : SUB + ny, nz:] = low[2 * k] + high[2 * k]
        ref[0, :SUB, nz:] = low[2 * k + 1] + high[2 * k + 1]
        ref[0, SUB + ny :, nz:] = low[2 * k + 1] + high[2 * k + 1]

    def reader(inside_ref, edge_ref, first, count):
        def get(x, row):
            if first <= x < nx - first:
                return inside_ref[x, row : row + SUB]
            at = x - (first - count) if x < first else x - (nx - first) + count
            return edge_ref[at, row : row + SUB]

        return get

    r_ref[0, SUB : SUB + ny] = right_ref[0]
    r_ref[1, SUB : SUB + ny] = right_ref[nx - 1]
    held = {("k0", 0): (k_ref, 0), ("k0", nx - 1): (k_ref, 1), ("k0", 1): (pass_ref, 0), ("k0", nx - 2): (pass_ref, 1)}
    for at, x in enumerate((0, 1, nx - 2, nx - 1)):
        held["n1", x] = (n_ref, at)
    held |= {("n1", 2): (pass_ref, 2), ("n1", nx - 3): (pass_ref, 3)}
    sums = {}
    for stage in range(3):
        get = reader((a_ref, b_ref, c_ref)[stage], (ea_ref, eb_ref, ec_ref)[stage], stage, 3)
        start, size = SUB - 2 + stage, ny if stage == 2 else ring
        v = slabs_ref[stage, start : start + size]
        s = slabs_ref[stage, start - 1 : start - 1 + size] + slabs_ref[stage, start + 1 : start + 1 + size]
        q, after = slab_step(stage, v, s, si_ref[0, start : start + size])
        if stage < 2:
            slabs_ref[stage + 1, start : start + size] = after

        def put(x, row, value):
            edge_ref = (eb_ref, ec_ref)[stage]
            at = x - (stage - 2) if x < nx // 2 else x - (nx - 1 - stage) + 3
            edge_ref[at, row : row + SUB] = value

        sweep(
            stage, [(stage - 2, stage + 1), (nx - 1 - stage, nx + 2 - stage)], nx, ny, nz, gz,
            get, reader(i_ref, ei_ref, 0, 2), put, q, sums,
            lambda x, row: r_ref[0 if x == 0 else 1, row : row + SUB],
            lambda x, row: a_ref[x, row : row + SUB], held,
        )

    total_ref[0:1] = stat_ref[0, 0:1]
    for k, name in enumerate(ORDER[1:]):
        total_ref[k + 1 : k + 2] = jnp.sum(sums[name] + sum_ref[k], axis=0, keepdims=True)
    gx, n_x = lax.axis_index("gx"), lax.axis_size("gx")
    count = jnp.sum(stat_ref[1, 0:1], axis=1, keepdims=True)
    below, above = [part[4] for part in slab_parts]
    begin = jnp.where(
        gx == 0, 0.0,
        jnp.where(gx == 1, below, jnp.where(gx == n_x - 1, column_total - count, column_total - count - above)),
    )
    where_ref[0:1] = jnp.broadcast_to(begin, (1, nz))
    where_ref[1:2] = jnp.broadcast_to(count, (1, nz))
    where_ref[2:8] = jnp.zeros((6, nz), F32)


def shift_up(v, amount):
    if amount < SUB:
        return pltpu.roll(v, v.shape[0] - amount, 0)
    return jnp.concatenate([v[amount:], v[:amount]], axis=0)


def plan_kernel(after_ref, label_ref, index_ref, plan_ref, lane_ref):
    rows, slot_rows = label_ref.shape[0], index_ref.shape[0]
    wide = -(-(slot_rows + 1) // LANES) * LANES
    shape = (rows, LANES)
    lane, row = lanes_of(shape), subs_of(shape)
    ones = (label_ref[...] == 1).astype(jnp.bfloat16)
    totals = jnp.dot(ones, jnp.ones((LANES, LANES), jnp.bfloat16), preferred_element_type=F32)
    lower = (subs_of((rows, rows)) > lanes_of((rows, rows))).astype(jnp.bfloat16)
    before = jnp.dot(lower, totals.astype(jnp.bfloat16), preferred_element_type=F32).astype(jnp.int32)
    target, first = lax.div(before, LANES), lax.rem(before, LANES)
    listed = jnp.concatenate(
        [lax.rem(index_ref[...], LANES).astype(F32), jnp.zeros((wide - slot_rows, LANES), F32)], axis=0
    ).astype(jnp.bfloat16)
    spread = jnp.concatenate([target] * (wide // LANES), axis=1)
    place = lanes_of((rows, wide))
    here = jnp.dot((spread == place).astype(jnp.bfloat16), listed, preferred_element_type=F32)
    after = jnp.dot((spread + 1 == place).astype(jnp.bfloat16), listed, preferred_element_type=F32)
    lane_ref[...] = jnp.where(lane >= first, here, after).astype(jnp.int32)
    wrapped = (lane < first).astype(jnp.int32)
    filled = lane - first + LANES * wrapped < totals.astype(jnp.int32)
    way = jnp.where(filled, row - target - wrapped, 0)
    plan = jnp.zeros(shape, jnp.int32)
    step = 1
    while step < rows:
        moving = jnp.where((way & step) != 0, way, 0)
        arriving = shift_up(moving, step)
        plan = plan | (arriving & step)
        way = (way - moving) | arriving
        step *= 2
    plan_ref[...] = plan


def galerkin(total):
    def add_up(*rows):
        return [jnp.broadcast_to(jnp.sum(row, axis=1, keepdims=True), row.shape) for row in rows]

    row = {name: total[k : k + 1] for k, name in enumerate(ORDER)}
    b0, b2 = row["w0 r"], row["w0 n1"]
    g00, g01, g02 = row["w0 k0"], row["w1 k0"], row["w1 n1"]
    g11, g12, g22 = row["w1 k1"], row["w2 k1"], row["w2 k2"]
    s00, s01, s02, s0, s11, s22 = add_up(g00, g01, g02, b0, g11, g22)
    l10, l20 = s01 / s00, s02 / s00
    h11 = g11 - l10 * (2.0 * g01 - l10 * g00)
    h12 = g12 - l10 * g02 - l20 * (g01 - l10 * g00)
    h22 = g22 - l20 * (2.0 * g02 - l20 * g00)
    y1, y2 = g00 - l10 * b0, b2 - l20 * b0
    d1, s12, s1 = add_up(h11, h12, y1)
    ok1 = d1 > 1e-7 * s11
    d1 = jnp.where(ok1, d1, 1.0)
    l21 = jnp.where(ok1, s12 / d1, 0.0)
    d2, s2 = add_up(h22 - l21 * (2.0 * h12 - l21 * h11), y2 - l21 * y1)
    ok2 = ok1 & (d2 > 1e-7 * s22)
    c2 = jnp.where(ok2, s2 / jnp.where(ok2, d2, 1.0), 0.0)
    c1 = jnp.where(ok1, s1 / d1 - l21 * c2, 0.0)
    c0 = s0 / s00 - l10 * c1 - l20 * c2
    return c0, c1, c2


def couple_kernel(
    stage, slot_rows, after_ref, where_ref, inside_ref, edge_ref, slabs_ref, plan_ref, lane_ref, blocks_ref,
    value_ref, buf_ref,
):
    nx, nz = inside_ref.shape[0], inside_ref.shape[2]
    ny = inside_ref.shape[1] - 2 * SUB
    rows = nx * ny
    gz = lax.axis_index("gz")

    def get(x, row):
        if stage <= x < nx - stage:
            return inside_ref[x, row : row + SUB]
        return edge_ref[x - (stage - 3) if x < stage else x - (nx - stage) + 3, row : row + SUB]

    for tile in range(ny // SUB):
        row = SUB + SUB * tile
        slab = slabs_ref[stage, row : row + SUB, :nz]
        v_low, v_mid = get(-1, row), get(0, row)
        for x in range(nx):
            v_high = get(x + 1, row)
            beside = get(x, row - 1) + get(x, row + 1)
            at = ny * x + SUB * tile
            value_ref[at : at + SUB] = (
                along_z(v_mid, slab, PACK * x, gz) + beside + (v_low + v_high) - 6.0 * v_mid
            )
            v_low, v_mid = v_mid, v_high
    value = jnp.take_along_axis(value_ref[...], lane_ref[...], axis=1)
    plan = plan_ref[...]
    step = 1
    while step < rows:
        value = jnp.where((plan & step) != 0, shift_up(value, step), value)
        step *= 2
    offset = jnp.max(where_ref[0:1]).astype(jnp.int32)
    count = jnp.max(where_ref[1:2]).astype(jnp.int32)
    shape = (slot_rows, LANES)
    slots = jnp.where(subs_of(shape) * LANES + lanes_of(shape) < count, value[:slot_rows], 0.0)
    slots = jnp.concatenate([slots, jnp.zeros((SUB, LANES), F32)], axis=0)
    inner = lax.rem(offset, LANES)
    turned = pltpu.roll(slots, inner, 1)
    moved = jnp.where(lanes_of((slot_rows + SUB, LANES)) >= inner, turned, pltpu.roll(turned, 1, 0))
    buf_ref[...] = jnp.zeros_like(buf_ref)
    buf_ref[pl.ds(offset // LANES, slot_rows + SUB), :] = moved
    gx = lax.axis_index("gx")
    n_gx = lax.axis_size("gx")
    size = blocks_ref.shape[0] // n_gx
    for block in range(n_gx):
        begin = pl.multiple_of((gx ^ block) * size, SUB)
        blocks_ref[block * size : block * size + size] = buf_ref[pl.ds(begin, size), :]


def add_kernel(a_ref, b_ref, after_ref, out_ref):
    out_ref[...] = a_ref[...] + b_ref[...]


def pack_kernel(total_ref, *refs):
    list_refs, out_refs = refs[:3], refs[3:]
    size = (out_refs[0].shape[0] - SUB) // 3
    for block, out_ref in enumerate(out_refs):
        for k, list_ref in enumerate(list_refs):
            out_ref[k * size : k * size + size] = list_ref[block * size : block * size + size]
        out_ref[3 * size :] = total_ref[...]


def membrane_kernel(
    half_ref, slope_ref, tau_ref, cond_ref, rev_ref, after_ref, v_ref, gates_ref, cot_ref,
    base_ref, sum_ref, factor_ref, coef_ref,
):
    n_states, rows = gates_ref.shape[:2]
    v = v_ref[...]

    def state(g, carry):
        total, current = carry
        inv_slope = 1.0 / slope_ref[g]
        tau_base = tau_ref[g]
        scaled = (v - half_ref[g]) * inv_slope
        gate = gates_ref[g]
        cot = cot_ref[g]
        steady = 1.0 / (1.0 + jnp.exp(-scaled))
        bell = jnp.exp(-scaled * scaled)
        rate = TIME_STEP / (tau_base * (0.5 + bell))
        decay = jnp.exp(-rate)
        steady_slope = steady * (1.0 - steady)
        decay_slope = decay * rate * rate * ((tau_base / TIME_STEP) * bell * (-2.0 * scaled))
        change = (steady_slope * (1.0 - decay) + (gate - steady) * decay_slope) * inv_slope
        base_ref[g] = cot * decay
        coef_ref[0, pl.ds(g, 1)] = jnp.full((1, LANES), TIME_STEP * cond_ref[g])
        coef_ref[1, pl.ds(g, 1)] = jnp.full((1, LANES), rev_ref[g])
        return total + cot * change, current + cond_ref[g] * gate

    zero = jnp.zeros((rows, LANES), F32)
    total, current = lax.fori_loop(0, n_states, state, (zero, zero), unroll=2)
    sum_ref[...] = total
    factor_ref[...] = 1.0 - TIME_STEP * current


def finish_kernel(
    alone, coef_ref, vcot_ref, v_ref, sum_ref, factor_ref, base_ref, a_ref, b_ref, c_ref, eb_ref, ec_ref, *refs
):
    n_small, n_large = len(alone[0]), len(alone[1])
    own_ref, small_refs, large_refs = refs[0], refs[1 : 1 + n_small], refs[1 + n_small : 1 + n_small + n_large]
    x_ref, volt_ref, gate_ref = refs[1 + n_small + n_large :]
    size = (own_ref.shape[0] - SUB) // 3
    gx = lax.axis_index("gx")

    def is_one(flags):
        found = gx < 0
        for place, flag in enumerate(flags):
            if flag:
                found = found | (gx == place)
        return found

    total = own_ref[3 * size :]
    for flags, ref in zip(alone[0], small_refs):
        total = total + jnp.where(is_one(flags), ref[...], 0.0)
    for flags, ref in zip(alone[1], large_refs):
        total = total + jnp.where(is_one(flags), 0.0, ref[3 * size :])
    c0, c1, c2 = galerkin(total)
    landed = jnp.zeros((size, LANES), F32)
    for k, c in enumerate((c0, c1, c2)):
        part = own_ref[k * size : k * size + size]
        for ref in large_refs:
            part = part + ref[k * size : k * size + size]
        landed = landed + c * part
    cot = vcot_ref[...] + landed
    v = v_ref[...]
    volt_ref[...] = cot * factor_ref[...] + sum_ref[...]
    for g in range(base_ref.shape[0]):
        gate_ref[g] = base_ref[g] - (coef_ref[0, g : g + 1] * cot) * (v - coef_ref[1, g : g + 1])
    nx, ny, nz = x_ref.shape
    own = slice(SUB, SUB + ny)
    for x in range(nx):
        w1 = b_ref[x, own] if 1 <= x < nx - 1 else eb_ref[2 if x == 0 else 3, own]
        w2 = c_ref[x, own] if 2 <= x < nx - 2 else ec_ref[x + 1 if x < 2 else x - (nx - 2) + 3, own]
        x_ref[x] = c0 * a_ref[x, own] + c1 * w1 + c2 * w2


def partners(axis, step):
    count = lax.axis_size(axis)
    if step == 0:
        return [i ^ 1 for i in range(count)]
    return [0] + [i + 1 if i % 2 else i - 1 for i in range(1, count - 1)] + [count - 1]


def swap(value, x_to=None, y_to=None):
    n_x, n_y, n_z = [lax.axis_size(axis) for axis in ("gx", "gy", "gz")]
    pairs = []
    for x in range(n_x):
        for y in range(n_y):
            to_x, to_y = x_to[x] if x_to else x, y_to[y] if y_to else y
            alone = (x_to and to_x == x) or (y_to and to_y == y)
            for z in range(n_z):
                to = (x, y, z ^ 1) if alone else (to_x, to_y, z)
                pairs.append(((x * n_y + y) * n_z + z, (to[0] * n_y + to[1]) * n_z + to[2]))
    return lax.ppermute(value, ("gx", "gy", "gz"), pairs)


def never_meet(count, k, slots, block):
    def apart(tile, owner):
        return owner * block >= (tile + 1) * slots or (owner + 1) * block <= count * block - (count - tile) * slots

    return [apart(i, i ^ k) and apart(i ^ k, i) for i in range(count)]


def local(
    potential_cot, damping, tissue_label, heart_index, voltage, gates, voltage_cot, gates_cot,
    half_voltage, gate_slope, tau_base, conductance, reversal,
):
    nx, ny, nz = potential_cot.shape
    rows = nx * ny
    ring = ny + SUB
    n_gx, n_gy = lax.axis_size("gx"), lax.axis_size("gy")
    n_states = gates.shape[0]
    block_rows = voltage.shape[1] // LANES
    slot_rows = heart_index.shape[3] // LANES
    block = shape_of(nx, ny, nz)
    flat = lambda a: a.reshape(rows, LANES)
    cells = lambda a: a.reshape(block_rows, LANES)
    states = lambda a: a.reshape(n_states, block_rows, LANES)

    w0, inv, packed, stat = call(
        start_kernel, (block, block, shape_of(2, ny, nz), shape_of(2, SUB, nz)), 3,
    )(in_hbm(potential_cot), in_hbm(damping), in_hbm(tissue_label))

    got = lax.ppermute(packed, "gz", [(0, 1), (1, 0)])
    cells_shape = jax.ShapeDtypeStruct((rows, LANES), jnp.int32)
    plan, lanes = call(plan_kernel, (cells_shape, cells_shape), 3, cost=6_000_000)(
        stat, flat(tissue_label), heart_index.reshape(slot_rows, LANES)
    )

    n_y = steps_of("gy")
    shapes = (
        (shape_of(2, ny, nz),) + (shape_of(nx + 1, SUB, nz),) * n_y + (shape_of(6, ny, nz),) * 2
        + (shape_of(4, SUB, nz),) * (2 * n_y)
    )
    slab, *faces = call(functools.partial(faces_kernel, n_y), shapes, 5)(w0, inv, packed, got, stat)
    along_y, along_x, across = faces[:n_y], faces[n_y : n_y + 2], faces[n_y + 2 :]
    y_to = [partners("gy", step) for step in range(n_y)]
    x_to = [partners("gx", step) for step in range(2)]
    along_y = [swap(face, y_to=y_to[j]) for j, face in enumerate(along_y)]
    along_x = [swap(face, x_to=x_to[i]) for i, face in enumerate(along_x)]
    across = [swap(face, x_to=x_to[k // n_y], y_to=y_to[k % n_y]) for k, face in enumerate(across)]

    tall = ring + SUB
    planes = shape_of(nx, tall, nz)
    edges = shape_of(6, tall, nz)
    in0, in_inv, in1, in2, in_sums, own_slab, passed = call(
        functools.partial(inner_kernel, n_y),
        (planes,) * 4 + (shape_of(len(ORDER) - 1, SUB, nz), shape_of(2, tall, nz), shape_of(4, tall, nz)),
        4 + n_y,
        scratch=[pltpu.VMEM((4, tall, nz), F32)] + [pltpu.VMEM((nx, tall, nz), F32)] * 3,
        cost=6_000_000,
    )(potential_cot, w0, inv, slab, *along_y)
    ends0, ends1, ends2, slabs, sums, where = call(
        functools.partial(outer_kernel, n_y, float(n_gx * voltage.shape[1])),
        (edges,) * 3 + (shape_of(3, tall, 2 * nz), shape_of(SUB, nz), shape_of(SUB, nz)),
        12 + 2 * n_y,
        scratch=[
            pltpu.VMEM((4, tall, nz), F32), pltpu.VMEM((1, tall, 2 * nz), F32),
            pltpu.VMEM((2, tall, nz), F32), pltpu.VMEM((2, tall, nz), F32), pltpu.VMEM((4, tall, nz), F32),
        ],
    )(plan, potential_cot, in0, in_inv, in1, in2, own_slab, in_sums, passed, stat, *along_x, *across)

    if n_gx > 4:
        counts = lax.all_gather(jnp.sum(stat[1, 0]), "gx")
        begin = jnp.sum(jnp.where(jnp.arange(n_gx) < lax.axis_index("gx"), counts, 0.0))
        where = where.at[0].set(begin)

    def couple(stage, after, inside, ends):
        return call(
            functools.partial(couple_kernel, stage, slot_rows),
            shape_of(n_gx * block_rows, LANES),
            7,
            scratch=[
                pltpu.VMEM((rows, LANES), F32), pltpu.VMEM((n_gx * block_rows + slot_rows + SUB, LANES), F32),
            ],
            cost=6_000_000,
        )(after, where, inside, ends, slabs, plan, lanes)

    def add(value, axis, step, after):
        got = lax.ppermute(value, axis, [(i, i ^ step) for i in range(lax.axis_size(axis))])
        return call(add_kernel, shape_of(SUB, nz), 3)(value, got, after)

    list0 = couple(0, sums, in0, ends0)
    sums = add(sums, "gz", 1, list0)
    list1 = couple(1, sums, in1, ends1)
    list2 = couple(2, list1, in2, ends2)
    for step in [2**k for k in range(n_gy.bit_length() - 1)]:
        sums = add(sums, "gy", step, list2)
    blocks = call(pack_kernel, (shape_of(3 * block_rows + SUB, LANES),) * n_gx, 4)(sums, list0, list1, list2)
    apart = {k: never_meet(n_gx, k, slot_rows, block_rows) for k in range(1, n_gx)}
    small, meets = [], []
    for k in range(1, n_gx):
        if any(apart[k]):
            small.append(swap(sums, x_to=[i ^ k if apart[k][i] else i for i in range(n_gx)]))
        meets.append(not all(apart[k]))
    order = [k for k in [2, 3, 1] + list(range(4, n_gx)) if k < n_gx and meets[k - 1]]
    large = [swap(blocks[k], x_to=[i if apart[k][i] else i ^ k for i in range(n_gx)]) for k in order]
    alone = [[apart[k] for k in range(1, n_gx) if any(apart[k])], [apart[k] for k in order]]

    base, total_change, factor, state_coefs = call(
        membrane_kernel,
        (
            shape_of(n_states, block_rows, LANES), shape_of(block_rows, LANES), shape_of(block_rows, LANES),
            shape_of(2, n_states, LANES),
        ),
        9,
        specs=[SMEM] * 5 + [VMEM] * 4,
        cost=6_000_000,
    )(
        half_voltage, gate_slope, tau_base, conductance, reversal,
        blocks[0], cells(voltage), states(gates), states(gates_cot),
    )
    solution, volt_grad, gate_grad = call(
        functools.partial(finish_kernel, alone),
        (block, shape_of(block_rows, LANES), shape_of(n_states, block_rows, LANES)),
        12 + len(small) + len(large),
    )(
        state_coefs, cells(voltage_cot), cells(voltage), total_change, factor, base,
        in0, in1, in2, ends1, ends2, blocks[0], *small, *large,
    )
    return solution, volt_grad.reshape(voltage.shape), gate_grad.reshape(gates.shape)


def solution(mesh):
    grid = P(("groups", "gx"), "gy", "gz")
    cells = P(("groups", "gy", "gz"), "gx")
    states = P(None, ("groups", "gy", "gz"), "gx")
    in_specs = (
        grid, grid, grid, P(("groups", "gx"), "gy", "gz", None), cells, states, cells, states,
        P(), P(), P(), P(), P(),
    )
    return jax.shard_map(
        local, mesh=mesh, in_specs=in_specs, out_specs=(grid, cells, states), check_vma=False
    )
```

```python
import functools

import jax
import jax.numpy as jnp
from jax import lax
from jax.experimental import pallas as pl
from jax.experimental.pallas import tpu as pltpu
from jax.sharding import PartitionSpec as P

TIME_STEP = 0.5
LANES = 128
SUB = 8
PACK = 8
COUNT_LANE = 4 * PACK
F32 = jnp.float32

VMEM = pl.BlockSpec(memory_space=pltpu.VMEM)
SMEM = pl.BlockSpec(memory_space=pltpu.SMEM)


def shape_of(*dims):
    return jax.ShapeDtypeStruct(dims, F32)


def call(kernel, out_shape, n_in, specs=None, outs=None, scratch=(), cost=2_000_000, limit=32):
    return pl.pallas_call(
        kernel,
        out_shape=out_shape,
        in_specs=specs if specs is not None else [VMEM] * n_in,
        out_specs=outs if outs is not None else jax.tree.map(lambda _: VMEM, out_shape),
        scratch_shapes=list(scratch),
        compiler_params=pltpu.CompilerParams(vmem_limit_bytes=limit * 1024 * 1024),
        cost_estimate=pl.CostEstimate(flops=cost, bytes_accessed=cost, transcendentals=0),
    )


def in_hbm(array):
    return pltpu.with_memory_space_constraint(array, pltpu.HBM)


def lanes_of(shape):
    return lax.broadcasted_iota(jnp.int32, shape, len(shape) - 1)


def subs_of(shape):
    return lax.broadcasted_iota(jnp.int32, shape, len(shape) - 2)


def start_kernel(right_ref, damping_ref, label_ref, w0_ref, inv_ref, pack_ref, stat_ref):
    nx, ny, nz = right_ref.shape
    gz = lax.axis_index("gz")
    lane = lanes_of((ny, nz))
    packed_w = jnp.zeros((ny, nz), F32)
    packed_i = jnp.zeros((ny, nz), F32)
    energy = jnp.zeros((ny, nz), F32)
    cells = jnp.zeros((ny, nz), F32)
    for x in range(nx):
        label = label_ref[x].astype(F32)
        right = right_ref[x]
        inv = 1.0 / (12.0 + damping_ref[x] * (1.0 + 3.0 * label))
        w0 = right * inv
        w0_ref[x] = w0
        inv_ref[x] = inv
        energy = energy + right * w0
        cells = cells + label
        turn = (PACK * x + 3) % nz
        begin = PACK * x + 3 * gz
        chosen = (lane >= begin) & (lane < begin + 3)
        packed_w = jnp.where(chosen, pltpu.roll(w0, turn, 1), packed_w)
        packed_i = jnp.where(chosen, pltpu.roll(inv, turn, 1), packed_i)
    pack_ref[0] = packed_w
    pack_ref[1] = packed_i
    stat_ref[0] = jnp.broadcast_to(jnp.sum(energy, axis=0, keepdims=True), (SUB, nz))
    stat_ref[1] = jnp.broadcast_to(jnp.sum(cells, axis=0, keepdims=True), (SUB, nz))


def steps_of(axis):
    return 1 if lax.axis_size(axis) == 2 else 2


def upper_in(axis, step):
    return lax.rem(lax.axis_index(axis), 2) == step


def has_partner(axis, step):
    here = lax.axis_index(axis)
    return jnp.where(upper_in(axis, step), here < lax.axis_size(axis) - 1, here > 0)


def unpack_rows(tile, step):
    sub = subs_of(tile.shape)
    up, there = upper_in("gy", step), has_partner("gy", step)
    depth = jnp.where(there, jnp.where(up, SUB - 1 - sub, sub), -1)
    return jnp.where(depth >= 5, tile, 0.0), jnp.where(depth >= 6, pltpu.roll(tile, 4, 0), 0.0)


def halo_rows(tiles):
    w_tile, i_tile = unpack_rows(tiles[0], 0)
    for step, tile in enumerate(tiles[1:], 1):
        w_more, i_more = unpack_rows(tile, step)
        w_tile, i_tile = w_tile + w_more, i_tile + i_more
    return w_tile, i_tile


def faces_kernel(n_y, w0_ref, inv_ref, own_ref, got_ref, stat_ref, slab_ref, *refs):
    y_refs, x_refs, edge_refs = refs[:n_y], refs[n_y : n_y + 2], refs[n_y + 2 :]
    nx, ny, nz = w0_ref.shape
    sub = subs_of((SUB, nz))
    lane = lanes_of((ny, nz))
    slab_ref[...] = own_ref[...] + got_ref[...]
    for step, face_ref in enumerate(y_refs):
        up = upper_in("gy", step)
        keep_w = jnp.where(up, sub, SUB - 1 - sub) >= 5
        for x in range(nx + 1):
            w_rows, i_rows = (w0_ref.at[x], inv_ref.at[x]) if x < nx else (slab_ref.at[0], slab_ref.at[1])
            w_face = jnp.where(up, w_rows[ny - SUB :], w_rows[:SUB])
            i_face = jnp.where(up, i_rows[ny - SUB :], i_rows[:SUB])
            face_ref[x] = jnp.where(keep_w, w_face, pltpu.roll(i_face, 4, 0))
    cells = jnp.sum(stat_ref[1, 0:1], axis=1, keepdims=True)
    slab_w = slab_ref[0]
    half = pltpu.roll(slab_ref[1], nz // 2, 1)
    up_slab = jnp.where(lane >= nz - 3 * PACK, slab_w, half)
    down_slab = jnp.where(lane < 3 * PACK, slab_w, half)
    for step, face_ref in enumerate(x_refs):
        up = upper_in("gx", step)
        first = jnp.where(up, nx - 3, 0)
        for k in range(3):
            face_ref[k] = w0_ref[first + k]
        for k in range(2):
            face_ref[3 + k] = inv_ref[jnp.where(up, nx - 2, 0) + k]
        face_ref[5] = jnp.where(lane == COUNT_LANE, cells, jnp.where(up, up_slab, down_slab))
        for y_step, y_ref in enumerate(y_refs):
            edge_ref = edge_refs[step * n_y + y_step]
            for k in range(3):
                edge_ref[k] = y_ref[first + k]
            edge_ref[3] = y_ref[nx]


SUMS = (("w0 k0", "w1 k0"), ("w1 n1", "w1 k1", "w2 k1", "w0 n1"), ("w2 k2",))
ORDER = ("w0 r", "w0 k0", "w1 k0", "w1 n1", "w1 k1", "w2 k1", "w2 k2", "w0 n1")


def slab_step(stage, v, s, inv):
    width = v.shape[1]
    across = pltpu.roll(v, PACK, 1) + pltpu.roll(v, width - PACK, 1)
    q = v + 0.5 * (s + across)
    if stage == 2:
        return q, None
    total = (
        pltpu.roll(q, 1, 1) + pltpu.roll(q, width - 1, 1) + s + across
        + 0.5 * (pltpu.roll(s, PACK, 1) + pltpu.roll(s, width - PACK, 1))
    )
    return q, next_vector(stage, v, total, inv)


def next_vector(stage, v, total, inv):
    return v - total * inv if stage == 0 else total * inv


def along_z(q, half, column, gz):
    nz = q.shape[1]
    lane = lanes_of(q.shape)
    entry = (nz - 1) * (1 - gz)
    turn = lax.rem(entry - (column + 3 - gz) + 2 * nz, nz)
    up = jnp.where(lane == nz - 1, 0.0, pltpu.roll(q, nz - 1, 1))
    down = jnp.where(lane == 0, 0.0, pltpu.roll(q, 1, 1))
    return up + down + jnp.where(lane == entry, pltpu.roll(half, turn, 1), 0.0)


def sweep(stage, spans, nx, ny, nz, gz, get, get_inv, put, slab_q, sums, get_right, get_w0, held):
    margin = 2 - stage
    start = SUB - margin
    tiles = ny // SUB + (margin > 0)
    own = subs_of((SUB, nz)) >= margin
    names = SUMS[stage]
    parts = {name: [] for name in names}
    for tile in range(tiles):
        row = start + SUB * tile
        q_rows = slab_q[SUB * tile : SUB * tile + SUB]
        acc = {name: jnp.zeros((SUB, nz), F32) for name in names}

        def beside(x):
            return get(x, row - 1) + get(x, row + 1)

        def rows(name, x):
            ref, at = held[name, x]
            return ref.at[at, row : row + SUB]

        for first, last in spans:
            s_low, s_mid = beside(first - 1), beside(first)
            v_low, v_mid = get(first - 1, row), get(first, row)
            for x in range(first, last):
                v_high, s_high = get(x + 1, row), beside(x + 1)
                across = v_low + v_high
                column = (PACK * x) % (2 * nz)
                half = q_rows[:, column // nz * nz : column // nz * nz + nz]
                rest = s_mid + across
                total = along_z(v_mid + 0.5 * rest, half, column % nz, gz) + rest + 0.5 * (s_low + s_high)
                if stage < 2:
                    after = next_vector(stage, v_mid, total, get_inv(x, row))
                    put(x, row, after)
                if 0 <= x < nx:
                    if stage == 0:
                        k0 = get_right(x, row) - total
                        rows("k0", x)[...] = k0
                        terms = (v_mid * k0, after * k0)
                    elif stage == 1:
                        rows("n1", x)[...] = total
                        k1 = rows("k0", x)[...] - total
                        terms = (v_mid * total, v_mid * k1, after * k1, get_w0(x, row) * total)
                    else:
                        terms = (v_mid * (rows("n1", x)[...] - total),)
                    for name, term in zip(names, terms):
                        acc[name] = acc[name] + term
                v_low, v_mid, s_low, s_mid = v_mid, v_high, s_mid, s_high
        for name in names:
            parts[name].append(acc[name])
    for name in names:
        part = parts[name]
        total = part[1]
        for other in part[2 : ny // SUB]:
            total = total + other
        sums[name] = total + (jnp.where(own, part[0], part[-1]) if margin else part[0])


def inner_kernel(n_y, right_ref, w0_ref, inv_ref, slab_ref, *refs):
    y_refs, refs = refs[:n_y], refs[n_y:]
    a_ref, i_ref, b_ref, c_ref, sum_ref, own_slab_ref, pass_ref, slabs_ref, r_ref, k_ref, n_ref = refs
    nx, ny, nz = w0_ref.shape
    gz = lax.axis_index("gz")
    for x in range(nx + 1):
        halos = halo_rows([ref[x] for ref in y_refs])
        for k in range(2):
            if x < nx:
                ref, own = (a_ref, i_ref)[k].at[x], (w0_ref, inv_ref)[k][x]
            else:
                ref, own = own_slab_ref.at[k], slab_ref[k]
            ref[:SUB] = halos[k]
            ref[SUB : SUB + ny] = own
            ref[SUB + ny :] = halos[k]
    for k in range(2):
        slabs_ref[3 * k] = own_slab_ref[k]
    for x in range(nx):
        r_ref[x, SUB : SUB + ny] = right_ref[x]
    held = {("k0", x): (k_ref, x) for x in range(nx)} | {("n1", x): (n_ref, x) for x in range(nx)}
    held |= {("k0", 1): (pass_ref, 0), ("k0", nx - 2): (pass_ref, 1)}
    held |= {("n1", 2): (pass_ref, 2), ("n1", nx - 3): (pass_ref, 3)}
    sums = {}
    for stage in range(3):
        source, target = (a_ref, b_ref, c_ref)[stage], (b_ref, c_ref, None)[stage]
        start, size = SUB - 2 + stage, ny if stage == 2 else ny + SUB
        v = slabs_ref[stage, start : start + size]
        s = slabs_ref[stage, start - 1 : start - 1 + size] + slabs_ref[stage, start + 1 : start + 1 + size]
        q, after = slab_step(stage, v, s, slabs_ref[3, start : start + size])
        if stage < 2:
            slabs_ref[stage + 1, start : start + size] = after

        def put(x, row, value):
            target[x, row : row + SUB] = value

        sweep(
            stage, [(1 + stage, nx - 1 - stage)], nx, ny, nz, gz,
            lambda x, row: source[x, row : row + SUB], lambda x, row: i_ref[x, row : row + SUB],
            put, q, sums,
            lambda x, row: r_ref[x, row : row + SUB], lambda x, row: a_ref[x, row : row + SUB], held,
        )
    for k, name in enumerate(ORDER[1:]):
        sum_ref[k] = sums[name]


def outer_kernel(
    n_y, column_total, after_ref, right_ref, a_ref, i_ref, b_ref, c_ref, slab_ref, sum_ref, pass_ref, stat_ref, *refs
):
    x_refs, corner_refs = refs[:2], refs[2 : 2 + 2 * n_y]
    ea_ref, eb_ref, ec_ref, slabs_ref, total_ref, where_ref, ei_ref, si_ref, r_ref, k_ref, n_ref = refs[2 + 2 * n_y :]
    nx, ny, nz = a_ref.shape[0], a_ref.shape[1] - 2 * SUB, a_ref.shape[2]
    ring = ny + SUB
    gz = lax.axis_index("gz")
    odd = lax.rem(lax.axis_index("gx"), 2) == 1

    def beyond(upper, read):
        there = has_partner("gx", 0) if upper else has_partner("gx", 1)
        swapped = has_partner("gx", 1) if upper else has_partner("gx", 0)
        first, second = read(0), read(1)
        if upper:
            return jnp.where(jnp.where(odd, swapped, there), jnp.where(odd, second, first), 0.0)
        return jnp.where(jnp.where(odd, swapped, there), jnp.where(odd, first, second), 0.0)

    def write(ref, at, own, halo):
        ref[at, :SUB] = halo
        ref[at, SUB : SUB + ny] = own
        ref[at, SUB + ny :] = halo

    lane_tile, lane = lanes_of((SUB, nz)), lanes_of((ny, nz))
    slab_parts = []
    for side, upper in enumerate((False, True)):
        tiles = [
            halo_rows([beyond(upper, lambda step: corner_refs[step * n_y + j][k]) for j in range(n_y)])
            for k in range(4)
        ]
        for k in range(3):
            write(ea_ref, 3 * side + k, beyond(upper, lambda step: x_refs[step][k]), tiles[k][0])
        for k in range(2):
            own = beyond(upper, lambda step: x_refs[step][3 + k])
            write(ei_ref, 2 * side + k, own, tiles[k if upper else k + 1][1])
        own = beyond(upper, lambda step: x_refs[step][5])

        def near(value, lanes, planes):
            return jnp.where(lanes < planes * PACK if upper else lanes >= nz - planes * PACK, value, 0.0)

        slab_parts.append((
            near(own, lane, 3), near(tiles[3][0], lane_tile, 3),
            near(pltpu.roll(own, nz // 2, 1), lane, 2), near(tiles[3][1], lane_tile, 2),
            own[0:1, COUNT_LANE : COUNT_LANE + 1],
        ))

    low, high = slab_parts
    for ref, k in ((slabs_ref, 0), (si_ref, 1)):
        ref[0, :, :nz] = slab_ref[k]
        ref[0, SUB : SUB + ny, nz:] = low[2 * k] + high[2 * k]
        ref[0, :SUB, nz:] = low[2 * k + 1] + high[2 * k + 1]
        ref[0, SUB + ny :, nz:] = low[2 * k + 1] + high[2 * k + 1]

    def reader(inside_ref, edge_ref, first, count):
        def get(x, row):
            if first <= x < nx - first:
                return inside_ref[x, row : row + SUB]
            at = x - (first - count) if x < first else x - (nx - first) + count
            return edge_ref[at, row : row + SUB]

        return get

    r_ref[0, SUB : SUB + ny] = right_ref[0]
    r_ref[1, SUB : SUB + ny] = right_ref[nx - 1]
    held = {("k0", 0): (k_ref, 0), ("k0", nx - 1): (k_ref, 1), ("k0", 1): (pass_ref, 0), ("k0", nx - 2): (pass_ref, 1)}
    for at, x in enumerate((0, 1, nx - 2, nx - 1)):
        held["n1", x] = (n_ref, at)
    held |= {("n1", 2): (pass_ref, 2), ("n1", nx - 3): (pass_ref, 3)}
    sums = {}
    for stage in range(3):
        get = reader((a_ref, b_ref, c_ref)[stage], (ea_ref, eb_ref, ec_ref)[stage], stage, 3)
        start, size = SUB - 2 + stage, ny if stage == 2 else ring
        v = slabs_ref[stage, start : start + size]
        s = slabs_ref[stage, start - 1 : start - 1 + size] + slabs_ref[stage, start + 1 : start + 1 + size]
        q, after = slab_step(stage, v, s, si_ref[0, start : start + size])
        if stage < 2:
            slabs_ref[stage + 1, start : start + size] = after

        def put(x, row, value):
            edge_ref = (eb_ref, ec_ref)[stage]
            at = x - (stage - 2) if x < nx // 2 else x - (nx - 1 - stage) + 3
            edge_ref[at, row : row + SUB] = value

        sweep(
            stage, [(stage - 2, stage + 1), (nx - 1 - stage, nx + 2 - stage)], nx, ny, nz, gz,
            get, reader(i_ref, ei_ref, 0, 2), put, q, sums,
            lambda x, row: r_ref[0 if x == 0 else 1, row : row + SUB],
            lambda x, row: a_ref[x, row : row + SUB], held,
        )

    total_ref[0:1] = stat_ref[0, 0:1]
    for k, name in enumerate(ORDER[1:]):
        total_ref[k + 1 : k + 2] = jnp.sum(sums[name] + sum_ref[k], axis=0, keepdims=True)
    gx, n_x = lax.axis_index("gx"), lax.axis_size("gx")
    count = jnp.sum(stat_ref[1, 0:1], axis=1, keepdims=True)
    below, above = [part[4] for part in slab_parts]
    begin = jnp.where(
        gx == 0, 0.0,
        jnp.where(gx == 1, below, jnp.where(gx == n_x - 1, column_total - count, column_total - count - above)),
    )
    where_ref[0:1] = jnp.broadcast_to(begin, (1, nz))
    where_ref[1:2] = jnp.broadcast_to(count, (1, nz))
    where_ref[2:8] = jnp.zeros((6, nz), F32)


def shift_up(v, amount):
    if amount < SUB:
        return pltpu.roll(v, v.shape[0] - amount, 0)
    return jnp.concatenate([v[amount:], v[:amount]], axis=0)


def plan_kernel(after_ref, label_ref, index_ref, plan_ref, lane_ref):
    rows, slot_rows = label_ref.shape[0], index_ref.shape[0]
    wide = -(-(slot_rows + 1) // LANES) * LANES
    shape = (rows, LANES)
    lane, row = lanes_of(shape), subs_of(shape)
    ones = (label_ref[...] == 1).astype(jnp.bfloat16)
    totals = jnp.dot(ones, jnp.ones((LANES, LANES), jnp.bfloat16), preferred_element_type=F32)
    lower = (subs_of((rows, rows)) > lanes_of((rows, rows))).astype(jnp.bfloat16)
    before = jnp.dot(lower, totals.astype(jnp.bfloat16), preferred_element_type=F32).astype(jnp.int32)
    target, first = lax.div(before, LANES), lax.rem(before, LANES)
    listed = jnp.concatenate(
        [lax.rem(index_ref[...], LANES).astype(F32), jnp.zeros((wide - slot_rows, LANES), F32)], axis=0
    ).astype(jnp.bfloat16)
    spread = jnp.concatenate([target] * (wide // LANES), axis=1)
    place = lanes_of((rows, wide))
    here = jnp.dot((spread == place).astype(jnp.bfloat16), listed, preferred_element_type=F32)
    after = jnp.dot((spread + 1 == place).astype(jnp.bfloat16), listed, preferred_element_type=F32)
    lane_ref[...] = jnp.where(lane >= first, here, after).astype(jnp.int32)
    wrapped = (lane < first).astype(jnp.int32)
    filled = lane - first + LANES * wrapped < totals.astype(jnp.int32)
    way = jnp.where(filled, row - target - wrapped, 0)
    plan = jnp.zeros(shape, jnp.int32)
    step = 1
    while step < rows:
        moving = jnp.where((way & step) != 0, way, 0)
        arriving = shift_up(moving, step)
        plan = plan | (arriving & step)
        way = (way - moving) | arriving
        step *= 2
    plan_ref[...] = plan


def galerkin(total):
    def add_up(*rows):
        return [jnp.broadcast_to(jnp.sum(row, axis=1, keepdims=True), row.shape) for row in rows]

    row = {name: total[k : k + 1] for k, name in enumerate(ORDER)}
    b0, b2 = row["w0 r"], row["w0 n1"]
    g00, g01, g02 = row["w0 k0"], row["w1 k0"], row["w1 n1"]
    g11, g12, g22 = row["w1 k1"], row["w2 k1"], row["w2 k2"]
    s00, s01, s02, s0, s11, s22 = add_up(g00, g01, g02, b0, g11, g22)
    l10, l20 = s01 / s00, s02 / s00
    h11 = g11 - l10 * (2.0 * g01 - l10 * g00)
    h12 = g12 - l10 * g02 - l20 * (g01 - l10 * g00)
    h22 = g22 - l20 * (2.0 * g02 - l20 * g00)
    y1, y2 = g00 - l10 * b0, b2 - l20 * b0
    d1, s12, s1 = add_up(h11, h12, y1)
    ok1 = d1 > 1e-7 * s11
    d1 = jnp.where(ok1, d1, 1.0)
    l21 = jnp.where(ok1, s12 / d1, 0.0)
    d2, s2 = add_up(h22 - l21 * (2.0 * h12 - l21 * h11), y2 - l21 * y1)
    ok2 = ok1 & (d2 > 1e-7 * s22)
    c2 = jnp.where(ok2, s2 / jnp.where(ok2, d2, 1.0), 0.0)
    c1 = jnp.where(ok1, s1 / d1 - l21 * c2, 0.0)
    c0 = s0 / s00 - l10 * c1 - l20 * c2
    return c0, c1, c2


def couple_kernel(
    stage, slot_rows, after_ref, where_ref, inside_ref, edge_ref, slabs_ref, plan_ref, lane_ref, blocks_ref,
    value_ref, buf_ref,
):
    nx, nz = inside_ref.shape[0], inside_ref.shape[2]
    ny = inside_ref.shape[1] - 2 * SUB
    rows = nx * ny
    gz = lax.axis_index("gz")

    def get(x, row):
        if stage <= x < nx - stage:
            return inside_ref[x, row : row + SUB]
        return edge_ref[x - (stage - 3) if x < stage else x - (nx - stage) + 3, row : row + SUB]

    for tile in range(ny // SUB):
        row = SUB + SUB * tile
        slab = slabs_ref[stage, row : row + SUB, :nz]
        v_low, v_mid = get(-1, row), get(0, row)
        for x in range(nx):
            v_high = get(x + 1, row)
            beside = get(x, row - 1) + get(x, row + 1)
            at = ny * x + SUB * tile
            value_ref[at : at + SUB] = (
                along_z(v_mid, slab, PACK * x, gz) + beside + (v_low + v_high) - 6.0 * v_mid
            )
            v_low, v_mid = v_mid, v_high
    value = jnp.take_along_axis(value_ref[...], lane_ref[...], axis=1)
    plan = plan_ref[...]
    step = 1
    while step < rows:
        value = jnp.where((plan & step) != 0, shift_up(value, step), value)
        step *= 2
    offset = jnp.max(where_ref[0:1]).astype(jnp.int32)
    count = jnp.max(where_ref[1:2]).astype(jnp.int32)
    shape = (slot_rows, LANES)
    slots = jnp.where(subs_of(shape) * LANES + lanes_of(shape) < count, value[:slot_rows], 0.0)
    slots = jnp.concatenate([slots, jnp.zeros((SUB, LANES), F32)], axis=0)
    inner = lax.rem(offset, LANES)
    turned = pltpu.roll(slots, inner, 1)
    moved = jnp.where(lanes_of((slot_rows + SUB, LANES)) >= inner, turned, pltpu.roll(turned, 1, 0))
    buf_ref[...] = jnp.zeros_like(buf_ref)
    buf_ref[pl.ds(offset // LANES, slot_rows + SUB), :] = moved
    gx = lax.axis_index("gx")
    n_gx = lax.axis_size("gx")
    size = blocks_ref.shape[0] // n_gx
    for block in range(n_gx):
        begin = pl.multiple_of((gx ^ block) * size, SUB)
        blocks_ref[block * size : block * size + size] = buf_ref[pl.ds(begin, size), :]


def add_kernel(a_ref, b_ref, after_ref, out_ref):
    out_ref[...] = a_ref[...] + b_ref[...]


def pack_kernel(total_ref, *refs):
    list_refs, out_refs = refs[:3], refs[3:]
    size = (out_refs[0].shape[0] - SUB) // 3
    for block, out_ref in enumerate(out_refs):
        for k, list_ref in enumerate(list_refs):
            out_ref[k * size : k * size + size] = list_ref[block * size : block * size + size]
        out_ref[3 * size :] = total_ref[...]


ROUND = (1, 3, 0, 2)
BACK = (2, 0, 3, 1)


def pack_round_kernel(total_ref, *refs):
    list_refs, (own_ref, round_ref, middle_ref, back_ref, rest_ref) = refs[:3], refs[3:]
    size = (own_ref.shape[0] - SUB) // 3
    half = size // 2
    gx = lax.axis_index("gx")
    inside = (gx == 1) | (gx == 2)
    ahead, behind = jnp.where(inside, 2, 1), jnp.where(inside, 1, 2)
    upper = jnp.where(gx >= 2, half, 0)
    for k, list_ref in enumerate(list_refs):
        for out_ref, begin, rows in (
            (own_ref, 0, size), (round_ref, ahead * size, size), (middle_ref, 3 * size, size),
            (back_ref, behind * size + upper, half), (rest_ref, behind * size + (half - upper), half),
        ):
            if not isinstance(begin, int):
                begin = pl.multiple_of(begin, SUB)
            out_ref[k * rows : k * rows + rows] = list_ref[pl.ds(begin, rows), :]
    for out_ref in (own_ref, round_ref, middle_ref, back_ref):
        out_ref[out_ref.shape[0] - SUB :] = total_ref[...]


def land_round(own_ref, round_ref, middle_ref, back_ref, rest_ref, edge_ref):
    size = (own_ref.shape[0] - SUB) // 3
    half = size // 2
    gx = lax.axis_index("gx")
    inside = (gx == 1) | (gx == 2)
    last = lambda ref: ref[ref.shape[0] - SUB :]
    total = last(own_ref) + last(round_ref) + last(back_ref) + jnp.where(inside, last(middle_ref), edge_ref[...])
    parts = []
    for k in range(3):
        whole = slice(k * size, k * size + size)
        back, rest = [ref[k * half : k * half + half] for ref in (back_ref, rest_ref)]
        odd = lax.rem(gx, 2) == 1
        low = jnp.where(odd, jnp.where(gx == 3, rest, 0.0), back)
        high = jnp.where(odd, back, jnp.where(gx == 0, rest, 0.0))
        part = own_ref[whole] + round_ref[whole] + jnp.where(inside, middle_ref[whole], 0.0)
        parts.append(part + jnp.concatenate([low, high], axis=0))
    return total, parts


def land_pairs(alone, own_ref, *refs):
    small_refs, large_refs = refs[: len(alone[0])], refs[len(alone[0]) :]
    size = (own_ref.shape[0] - SUB) // 3
    gx = lax.axis_index("gx")

    def is_one(flags):
        found = gx < 0
        for place, flag in enumerate(flags):
            if flag:
                found = found | (gx == place)
        return found

    total = own_ref[3 * size :]
    for flags, ref in zip(alone[0], small_refs):
        total = total + jnp.where(is_one(flags), ref[...], 0.0)
    for flags, ref in zip(alone[1], large_refs):
        total = total + jnp.where(is_one(flags), 0.0, ref[3 * size :])
    parts = []
    for k in range(3):
        part = own_ref[k * size : k * size + size]
        for ref in large_refs:
            part = part + ref[k * size : k * size + size]
        parts.append(part)
    return total, parts


def membrane_kernel(
    half_ref, slope_ref, tau_ref, cond_ref, rev_ref, after_ref, v_ref, gates_ref, cot_ref,
    base_ref, sum_ref, factor_ref, coef_ref,
):
    n_states, rows = gates_ref.shape[:2]
    v = v_ref[...]

    def state(g, carry):
        total, current = carry
        inv_slope = 1.0 / slope_ref[g]
        tau_base = tau_ref[g]
        scaled = (v - half_ref[g]) * inv_slope
        gate = gates_ref[g]
        cot = cot_ref[g]
        steady = 1.0 / (1.0 + jnp.exp(-scaled))
        bell = jnp.exp(-scaled * scaled)
        rate = TIME_STEP / (tau_base * (0.5 + bell))
        decay = jnp.exp(-rate)
        steady_slope = steady * (1.0 - steady)
        decay_slope = decay * rate * rate * ((tau_base / TIME_STEP) * bell * (-2.0 * scaled))
        change = (steady_slope * (1.0 - decay) + (gate - steady) * decay_slope) * inv_slope
        base_ref[g] = cot * decay
        coef_ref[0, pl.ds(g, 1)] = jnp.full((1, LANES), TIME_STEP * cond_ref[g])
        coef_ref[1, pl.ds(g, 1)] = jnp.full((1, LANES), rev_ref[g])
        return total + cot * change, current + cond_ref[g] * gate

    zero = jnp.zeros((rows, LANES), F32)
    total, current = lax.fori_loop(0, n_states, state, (zero, zero), unroll=2)
    sum_ref[...] = total
    factor_ref[...] = 1.0 - TIME_STEP * current


def finish_kernel(
    land, coef_ref, vcot_ref, v_ref, sum_ref, factor_ref, base_ref, a_ref, b_ref, c_ref, eb_ref, ec_ref, *refs
):
    x_ref, volt_ref, gate_ref = refs[-3:]
    total, parts = land(*refs[:-3])
    c0, c1, c2 = galerkin(total)
    landed = c0 * parts[0] + c1 * parts[1] + c2 * parts[2]
    cot = vcot_ref[...] + landed
    v = v_ref[...]
    volt_ref[...] = cot * factor_ref[...] + sum_ref[...]
    for g in range(base_ref.shape[0]):
        gate_ref[g] = base_ref[g] - (coef_ref[0, g : g + 1] * cot) * (v - coef_ref[1, g : g + 1])
    nx, ny, nz = x_ref.shape
    own = slice(SUB, SUB + ny)
    for x in range(nx):
        w1 = b_ref[x, own] if 1 <= x < nx - 1 else eb_ref[2 if x == 0 else 3, own]
        w2 = c_ref[x, own] if 2 <= x < nx - 2 else ec_ref[x + 1 if x < 2 else x - (nx - 2) + 3, own]
        x_ref[x] = c0 * a_ref[x, own] + c1 * w1 + c2 * w2


def partners(axis, step):
    count = lax.axis_size(axis)
    if step == 0:
        return [i ^ 1 for i in range(count)]
    return [0] + [i + 1 if i % 2 else i - 1 for i in range(1, count - 1)] + [count - 1]


def swap(value, x_to=None, y_to=None):
    n_x, n_y, n_z = [lax.axis_size(axis) for axis in ("gx", "gy", "gz")]
    pairs = []
    for x in range(n_x):
        for y in range(n_y):
            to_x, to_y = x_to[x] if x_to else x, y_to[y] if y_to else y
            alone = (x_to and to_x == x) or (y_to and to_y == y)
            for z in range(n_z):
                to = (x, y, z ^ 1) if alone else (to_x, to_y, z)
                pairs.append(((x * n_y + y) * n_z + z, (to[0] * n_y + to[1]) * n_z + to[2]))
    return lax.ppermute(value, ("gx", "gy", "gz"), pairs)


def never_meet(count, k, slots, block):
    def apart(tile, owner):
        return owner * block >= (tile + 1) * slots or (owner + 1) * block <= count * block - (count - tile) * slots

    return [apart(i, i ^ k) and apart(i ^ k, i) for i in range(count)]


def local(
    potential_cot, damping, tissue_label, heart_index, voltage, gates, voltage_cot, gates_cot,
    half_voltage, gate_slope, tau_base, conductance, reversal,
):
    nx, ny, nz = potential_cot.shape
    rows = nx * ny
    ring = ny + SUB
    n_gx, n_gy = lax.axis_size("gx"), lax.axis_size("gy")
    n_states = gates.shape[0]
    block_rows = voltage.shape[1] // LANES
    slot_rows = heart_index.shape[3] // LANES
    block = shape_of(nx, ny, nz)
    flat = lambda a: a.reshape(rows, LANES)
    cells = lambda a: a.reshape(block_rows, LANES)
    states = lambda a: a.reshape(n_states, block_rows, LANES)

    w0, inv, packed, stat = call(
        start_kernel, (block, block, shape_of(2, ny, nz), shape_of(2, SUB, nz)), 3,
    )(in_hbm(potential_cot), in_hbm(damping), in_hbm(tissue_label))

    got = lax.ppermute(packed, "gz", [(0, 1), (1, 0)])
    cells_shape = jax.ShapeDtypeStruct((rows, LANES), jnp.int32)
    plan, lanes = call(plan_kernel, (cells_shape, cells_shape), 3, cost=6_000_000)(
        stat, flat(tissue_label), heart_index.reshape(slot_rows, LANES)
    )

    n_y = steps_of("gy")
    shapes = (
        (shape_of(2, ny, nz),) + (shape_of(nx + 1, SUB, nz),) * n_y + (shape_of(6, ny, nz),) * 2
        + (shape_of(4, SUB, nz),) * (2 * n_y)
    )
    slab, *faces = call(functools.partial(faces_kernel, n_y), shapes, 5)(w0, inv, packed, got, stat)
    along_y, along_x, across = faces[:n_y], faces[n_y : n_y + 2], faces[n_y + 2 :]
    y_to = [partners("gy", step) for step in range(n_y)]
    x_to = [partners("gx", step) for step in range(2)]
    along_y = [swap(face, y_to=y_to[j]) for j, face in enumerate(along_y)]
    along_x = [swap(face, x_to=x_to[i]) for i, face in enumerate(along_x)]
    across = [swap(face, x_to=x_to[k // n_y], y_to=y_to[k % n_y]) for k, face in enumerate(across)]

    tall = ring + SUB
    planes = shape_of(nx, tall, nz)
    edges = shape_of(6, tall, nz)
    in0, in_inv, in1, in2, in_sums, own_slab, passed = call(
        functools.partial(inner_kernel, n_y),
        (planes,) * 4 + (shape_of(len(ORDER) - 1, SUB, nz), shape_of(2, tall, nz), shape_of(4, tall, nz)),
        4 + n_y,
        scratch=[pltpu.VMEM((4, tall, nz), F32)] + [pltpu.VMEM((nx, tall, nz), F32)] * 3,
        cost=6_000_000,
    )(potential_cot, w0, inv, slab, *along_y)
    ends0, ends1, ends2, slabs, sums, where = call(
        functools.partial(outer_kernel, n_y, float(n_gx * voltage.shape[1])),
        (edges,) * 3 + (shape_of(3, tall, 2 * nz), shape_of(SUB, nz), shape_of(SUB, nz)),
        12 + 2 * n_y,
        scratch=[
            pltpu.VMEM((4, tall, nz), F32), pltpu.VMEM((1, tall, 2 * nz), F32),
            pltpu.VMEM((2, tall, nz), F32), pltpu.VMEM((2, tall, nz), F32), pltpu.VMEM((4, tall, nz), F32),
        ],
    )(plan, potential_cot, in0, in_inv, in1, in2, own_slab, in_sums, passed, stat, *along_x, *across)

    if n_gx > 4:
        counts = lax.all_gather(jnp.sum(stat[1, 0]), "gx")
        begin = jnp.sum(jnp.where(jnp.arange(n_gx) < lax.axis_index("gx"), counts, 0.0))
        where = where.at[0].set(begin)

    def couple(stage, after, inside, ends):
        return call(
            functools.partial(couple_kernel, stage, slot_rows),
            shape_of(n_gx * block_rows, LANES),
            7,
            scratch=[
                pltpu.VMEM((rows, LANES), F32), pltpu.VMEM((n_gx * block_rows + slot_rows + SUB, LANES), F32),
            ],
            cost=6_000_000,
        )(after, where, inside, ends, slabs, plan, lanes)

    def add(value, axis, step, after):
        got = lax.ppermute(value, axis, [(i, i ^ step) for i in range(lax.axis_size(axis))])
        return call(add_kernel, shape_of(SUB, nz), 3)(value, got, after)

    list0 = couple(0, sums, in0, ends0)
    sums = add(sums, "gz", 1, list0)
    list1 = couple(1, sums, in1, ends1)
    list2 = couple(2, list1, in2, ends2)
    for step in [2**k for k in range(n_gy.bit_length() - 1)]:
        sums = add(sums, "gy", step, list2)
    if n_gx == 4 and 2 * slot_rows == 5 * block_rows:
        own, ahead, middle, back, rest = call(
            pack_round_kernel,
            (shape_of(3 * block_rows + SUB, LANES),) * 3
            + (shape_of(3 * block_rows // 2 + SUB, LANES), shape_of(3 * block_rows // 2, LANES)),
            4,
        )(sums, list0, list1, list2)
        arrived = [
            own,
            swap(ahead, x_to=ROUND),
            swap(middle, x_to=partners("gx", 1)),
            swap(back, x_to=BACK),
            swap(rest, x_to=partners("gx", 0)),
            swap(sums, x_to=[3, 1, 2, 0]),
        ]
        land = land_round
    else:
        blocks = call(pack_kernel, (shape_of(3 * block_rows + SUB, LANES),) * n_gx, 4)(sums, list0, list1, list2)
        apart = {k: never_meet(n_gx, k, slot_rows, block_rows) for k in range(1, n_gx)}
        few = [k for k in apart if any(apart[k])]
        many = [k for k in [2, 3, 1] + list(range(4, n_gx)) if k < n_gx and not all(apart[k])]
        arrived = [blocks[0]]
        arrived += [swap(sums, x_to=[i ^ k if apart[k][i] else i for i in range(n_gx)]) for k in few]
        arrived += [swap(blocks[k], x_to=[i if apart[k][i] else i ^ k for i in range(n_gx)]) for k in many]
        land = functools.partial(land_pairs, [[apart[k] for k in few], [apart[k] for k in many]])

    base, total_change, factor, state_coefs = call(
        membrane_kernel,
        (
            shape_of(n_states, block_rows, LANES), shape_of(block_rows, LANES), shape_of(block_rows, LANES),
            shape_of(2, n_states, LANES),
        ),
        9,
        specs=[SMEM] * 5 + [VMEM] * 4,
        cost=6_000_000,
    )(
        half_voltage, gate_slope, tau_base, conductance, reversal,
        arrived[0], cells(voltage), states(gates), states(gates_cot),
    )
    solution, volt_grad, gate_grad = call(
        functools.partial(finish_kernel, land),
        (block, shape_of(block_rows, LANES), shape_of(n_states, block_rows, LANES)),
        11 + len(arrived),
    )(
        state_coefs, cells(voltage_cot), cells(voltage), total_change, factor, base,
        in0, in1, in2, ends1, ends2, *arrived,
    )
    return solution, volt_grad.reshape(voltage.shape), gate_grad.reshape(gates.shape)


def solution(mesh):
    grid = P(("groups", "gx"), "gy", "gz")
    cells = P(("groups", "gy", "gz"), "gx")
    states = P(None, ("groups", "gy", "gz"), "gx")
    in_specs = (
        grid, grid, grid, P(("groups", "gx"), "gy", "gz", None), cells, states, cells, states,
        P(), P(), P(), P(), P(),
    )
    return jax.shard_map(
        local, mesh=mesh, in_specs=in_specs, out_specs=(grid, cells, states), check_vma=False
    )
```

```python
import functools

import jax
import jax.numpy as jnp
from jax import lax
from jax.experimental import pallas as pl
from jax.experimental.pallas import tpu as pltpu
from jax.sharding import PartitionSpec as P

TIME_STEP = 0.5
LANES = 128
SUB = 8
PACK = 8
COUNT_LANE = 4 * PACK
F32 = jnp.float32

VMEM = pl.BlockSpec(memory_space=pltpu.VMEM)
SMEM = pl.BlockSpec(memory_space=pltpu.SMEM)


def shape_of(*dims):
    return jax.ShapeDtypeStruct(dims, F32)


def call(kernel, out_shape, n_in, specs=None, outs=None, scratch=(), cost=2_000_000, limit=32):
    return pl.pallas_call(
        kernel,
        out_shape=out_shape,
        in_specs=specs if specs is not None else [VMEM] * n_in,
        out_specs=outs if outs is not None else jax.tree.map(lambda _: VMEM, out_shape),
        scratch_shapes=list(scratch),
        compiler_params=pltpu.CompilerParams(vmem_limit_bytes=limit * 1024 * 1024),
        cost_estimate=pl.CostEstimate(flops=cost, bytes_accessed=cost, transcendentals=0),
    )


def in_hbm(array):
    return pltpu.with_memory_space_constraint(array, pltpu.HBM)


def lanes_of(shape):
    return lax.broadcasted_iota(jnp.int32, shape, len(shape) - 1)


def subs_of(shape):
    return lax.broadcasted_iota(jnp.int32, shape, len(shape) - 2)


def start_kernel(right_ref, damping_ref, label_ref, w0_ref, inv_ref, pack_ref, stat_ref):
    nx, ny, nz = right_ref.shape
    gz = lax.axis_index("gz")
    lane = lanes_of((ny, nz))
    packed_w = jnp.zeros((ny, nz), F32)
    packed_i = jnp.zeros((ny, nz), F32)
    energy = jnp.zeros((ny, nz), F32)
    cells = jnp.zeros((ny, nz), F32)
    for x in range(nx):
        label = label_ref[x].astype(F32)
        right = right_ref[x]
        inv = 1.0 / (12.0 + damping_ref[x] * (1.0 + 3.0 * label))
        w0 = right * inv
        w0_ref[x] = w0
        inv_ref[x] = inv
        energy = energy + right * w0
        cells = cells + label
        turn = (PACK * x + 3) % nz
        begin = PACK * x + 3 * gz
        chosen = (lane >= begin) & (lane < begin + 3)
        packed_w = jnp.where(chosen, pltpu.roll(w0, turn, 1), packed_w)
        packed_i = jnp.where(chosen, pltpu.roll(inv, turn, 1), packed_i)
    pack_ref[0] = packed_w
    pack_ref[1] = packed_i
    stat_ref[0] = jnp.broadcast_to(jnp.sum(energy, axis=0, keepdims=True), (SUB, nz))
    stat_ref[1] = jnp.broadcast_to(jnp.sum(cells, axis=0, keepdims=True), (SUB, nz))


def steps_of(axis):
    return 1 if lax.axis_size(axis) == 2 else 2


def upper_in(axis, step):
    return lax.rem(lax.axis_index(axis), 2) == step


def has_partner(axis, step):
    here = lax.axis_index(axis)
    return jnp.where(upper_in(axis, step), here < lax.axis_size(axis) - 1, here > 0)


def unpack_rows(tile, step):
    sub = subs_of(tile.shape)
    up, there = upper_in("gy", step), has_partner("gy", step)
    depth = jnp.where(there, jnp.where(up, SUB - 1 - sub, sub), -1)
    return jnp.where(depth >= 5, tile, 0.0), jnp.where(depth >= 6, pltpu.roll(tile, 4, 0), 0.0)


def halo_rows(tiles):
    w_tile, i_tile = unpack_rows(tiles[0], 0)
    for step, tile in enumerate(tiles[1:], 1):
        w_more, i_more = unpack_rows(tile, step)
        w_tile, i_tile = w_tile + w_more, i_tile + i_more
    return w_tile, i_tile


def faces_kernel(n_y, w0_ref, inv_ref, own_ref, got_ref, stat_ref, slab_ref, *refs):
    y_refs, x_refs, edge_refs = refs[:n_y], refs[n_y : n_y + 2], refs[n_y + 2 :]
    nx, ny, nz = w0_ref.shape
    sub = subs_of((SUB, nz))
    lane = lanes_of((ny, nz))
    slab_ref[...] = own_ref[...] + got_ref[...]
    for step, face_ref in enumerate(y_refs):
        up = upper_in("gy", step)
        keep_w = jnp.where(up, sub, SUB - 1 - sub) >= 5
        for x in range(nx + 1):
            w_rows, i_rows = (w0_ref.at[x], inv_ref.at[x]) if x < nx else (slab_ref.at[0], slab_ref.at[1])
            w_face = jnp.where(up, w_rows[ny - SUB :], w_rows[:SUB])
            i_face = jnp.where(up, i_rows[ny - SUB :], i_rows[:SUB])
            face_ref[x] = jnp.where(keep_w, w_face, pltpu.roll(i_face, 4, 0))
    cells = jnp.sum(stat_ref[1, 0:1], axis=1, keepdims=True)
    slab_w = slab_ref[0]
    half = pltpu.roll(slab_ref[1], nz // 2, 1)
    up_slab = jnp.where(lane >= nz - 3 * PACK, slab_w, half)
    down_slab = jnp.where(lane < 3 * PACK, slab_w, half)
    for step, face_ref in enumerate(x_refs):
        up = upper_in("gx", step)
        first = jnp.where(up, nx - 3, 0)
        for k in range(3):
            face_ref[k] = w0_ref[first + k]
        for k in range(2):
            face_ref[3 + k] = inv_ref[jnp.where(up, nx - 2, 0) + k]
        face_ref[5] = jnp.where(lane == COUNT_LANE, cells, jnp.where(up, up_slab, down_slab))
        for y_step, y_ref in enumerate(y_refs):
            edge_ref = edge_refs[step * n_y + y_step]
            for k in range(3):
                edge_ref[k] = y_ref[first + k]
            edge_ref[3] = y_ref[nx]


SUMS = (("w0 k0", "w1 k0"), ("w1 n1", "w1 k1", "w2 k1", "w0 n1"), ("w2 k2",))
ORDER = ("w0 r", "w0 k0", "w1 k0", "w1 n1", "w1 k1", "w2 k1", "w2 k2", "w0 n1")


def slab_step(stage, v, s, inv):
    width = v.shape[1]
    across = pltpu.roll(v, PACK, 1) + pltpu.roll(v, width - PACK, 1)
    q = v + 0.5 * (s + across)
    if stage == 2:
        return q, None
    total = (
        pltpu.roll(q, 1, 1) + pltpu.roll(q, width - 1, 1) + s + across
        + 0.5 * (pltpu.roll(s, PACK, 1) + pltpu.roll(s, width - PACK, 1))
    )
    return q, next_vector(stage, v, total, inv)


def next_vector(stage, v, total, inv):
    return v - total * inv if stage == 0 else total * inv


def along_z(q, half, column, gz):
    nz = q.shape[1]
    lane = lanes_of(q.shape)
    entry = (nz - 1) * (1 - gz)
    turn = lax.rem(entry - (column + 3 - gz) + 2 * nz, nz)
    up = jnp.where(lane == nz - 1, 0.0, pltpu.roll(q, nz - 1, 1))
    down = jnp.where(lane == 0, 0.0, pltpu.roll(q, 1, 1))
    return up + down + jnp.where(lane == entry, pltpu.roll(half, turn, 1), 0.0)


def sweep(stage, spans, nx, ny, nz, gz, get, get_inv, put, slab_q, sums, get_right, get_w0, held):
    margin = 2 - stage
    start = SUB - margin
    tiles = ny // SUB + (margin > 0)
    own = subs_of((SUB, nz)) >= margin
    names = SUMS[stage]
    parts = {name: [] for name in names}
    for tile in range(tiles):
        row = start + SUB * tile
        q_rows = slab_q[SUB * tile : SUB * tile + SUB]
        acc = {name: jnp.zeros((SUB, nz), F32) for name in names}

        def beside(x):
            return get(x, row - 1) + get(x, row + 1)

        def rows(name, x):
            ref, at = held[name, x]
            return ref.at[at, row : row + SUB]

        for first, last in spans:
            s_low, s_mid = beside(first - 1), beside(first)
            v_low, v_mid = get(first - 1, row), get(first, row)
            for x in range(first, last):
                v_high, s_high = get(x + 1, row), beside(x + 1)
                across = v_low + v_high
                column = (PACK * x) % (2 * nz)
                half = q_rows[:, column // nz * nz : column // nz * nz + nz]
                rest = s_mid + across
                total = along_z(v_mid + 0.5 * rest, half, column % nz, gz) + rest + 0.5 * (s_low + s_high)
                if stage < 2:
                    after = next_vector(stage, v_mid, total, get_inv(x, row))
                    put(x, row, after)
                if 0 <= x < nx:
                    if stage == 0:
                        k0 = get_right(x, row) - total
                        rows("k0", x)[...] = k0
                        terms = (v_mid * k0, after * k0)
                    elif stage == 1:
                        rows("n1", x)[...] = total
                        k1 = rows("k0", x)[...] - total
                        terms = (v_mid * total, v_mid * k1, after * k1, get_w0(x, row) * total)
                    else:
                        terms = (v_mid * (rows("n1", x)[...] - total),)
                    for name, term in zip(names, terms):
                        acc[name] = acc[name] + term
                v_low, v_mid, s_low, s_mid = v_mid, v_high, s_mid, s_high
        for name in names:
            parts[name].append(acc[name])
    for name in names:
        part = parts[name]
        total = part[1]
        for other in part[2 : ny // SUB]:
            total = total + other
        sums[name] = total + (jnp.where(own, part[0], part[-1]) if margin else part[0])


def inner_kernel(n_y, right_ref, w0_ref, inv_ref, slab_ref, *refs):
    y_refs, refs = refs[:n_y], refs[n_y:]
    a_ref, i_ref, b_ref, c_ref, sum_ref, own_slab_ref, pass_ref, slabs_ref, r_ref, k_ref, n_ref = refs
    nx, ny, nz = w0_ref.shape
    gz = lax.axis_index("gz")
    for x in range(nx + 1):
        halos = halo_rows([ref[x] for ref in y_refs])
        for k in range(2):
            if x < nx:
                ref, own = (a_ref, i_ref)[k].at[x], (w0_ref, inv_ref)[k][x]
            else:
                ref, own = own_slab_ref.at[k], slab_ref[k]
            ref[:SUB] = halos[k]
            ref[SUB : SUB + ny] = own
            ref[SUB + ny :] = halos[k]
    for k in range(2):
        slabs_ref[3 * k] = own_slab_ref[k]
    for x in range(nx):
        r_ref[x, SUB : SUB + ny] = right_ref[x]
    held = {("k0", x): (k_ref, x) for x in range(nx)} | {("n1", x): (n_ref, x) for x in range(nx)}
    held |= {("k0", 1): (pass_ref, 0), ("k0", nx - 2): (pass_ref, 1)}
    held |= {("n1", 2): (pass_ref, 2), ("n1", nx - 3): (pass_ref, 3)}
    sums = {}
    for stage in range(3):
        source, target = (a_ref, b_ref, c_ref)[stage], (b_ref, c_ref, None)[stage]
        start, size = SUB - 2 + stage, ny if stage == 2 else ny + SUB
        v = slabs_ref[stage, start : start + size]
        s = slabs_ref[stage, start - 1 : start - 1 + size] + slabs_ref[stage, start + 1 : start + 1 + size]
        q, after = slab_step(stage, v, s, slabs_ref[3, start : start + size])
        if stage < 2:
            slabs_ref[stage + 1, start : start + size] = after

        def put(x, row, value):
            target[x, row : row + SUB] = value

        sweep(
            stage, [(1 + stage, nx - 1 - stage)], nx, ny, nz, gz,
            lambda x, row: source[x, row : row + SUB], lambda x, row: i_ref[x, row : row + SUB],
            put, q, sums,
            lambda x, row: r_ref[x, row : row + SUB], lambda x, row: a_ref[x, row : row + SUB], held,
        )
    for k, name in enumerate(ORDER[1:]):
        sum_ref[k] = sums[name]


def outer_kernel(
    n_y, column_total, after_ref, right_ref, a_ref, i_ref, b_ref, c_ref, slab_ref, sum_ref, pass_ref, stat_ref, *refs
):
    x_refs, corner_refs = refs[:2], refs[2 : 2 + 2 * n_y]
    ea_ref, eb_ref, ec_ref, slabs_ref, total_ref, where_ref, ei_ref, si_ref, r_ref, k_ref, n_ref = refs[2 + 2 * n_y :]
    nx, ny, nz = a_ref.shape[0], a_ref.shape[1] - 2 * SUB, a_ref.shape[2]
    ring = ny + SUB
    gz = lax.axis_index("gz")
    odd = lax.rem(lax.axis_index("gx"), 2) == 1

    def beyond(upper, read):
        there = has_partner("gx", 0) if upper else has_partner("gx", 1)
        swapped = has_partner("gx", 1) if upper else has_partner("gx", 0)
        first, second = read(0), read(1)
        if upper:
            return jnp.where(jnp.where(odd, swapped, there), jnp.where(odd, second, first), 0.0)
        return jnp.where(jnp.where(odd, swapped, there), jnp.where(odd, first, second), 0.0)

    def write(ref, at, own, halo):
        ref[at, :SUB] = halo
        ref[at, SUB : SUB + ny] = own
        ref[at, SUB + ny :] = halo

    lane_tile, lane = lanes_of((SUB, nz)), lanes_of((ny, nz))
    slab_parts = []
    for side, upper in enumerate((False, True)):
        tiles = [
            halo_rows([beyond(upper, lambda step: corner_refs[step * n_y + j][k]) for j in range(n_y)])
            for k in range(4)
        ]
        for k in range(3):
            write(ea_ref, 3 * side + k, beyond(upper, lambda step: x_refs[step][k]), tiles[k][0])
        for k in range(2):
            own = beyond(upper, lambda step: x_refs[step][3 + k])
            write(ei_ref, 2 * side + k, own, tiles[k if upper else k + 1][1])
        own = beyond(upper, lambda step: x_refs[step][5])

        def near(value, lanes, planes):
            return jnp.where(lanes < planes * PACK if upper else lanes >= nz - planes * PACK, value, 0.0)

        slab_parts.append((
            near(own, lane, 3), near(tiles[3][0], lane_tile, 3),
            near(pltpu.roll(own, nz // 2, 1), lane, 2), near(tiles[3][1], lane_tile, 2),
            own[0:1, COUNT_LANE : COUNT_LANE + 1],
        ))

    low, high = slab_parts
    for ref, k in ((slabs_ref, 0), (si_ref, 1)):
        ref[0, :, :nz] = slab_ref[k]
        ref[0, SUB : SUB + ny, nz:] = low[2 * k] + high[2 * k]
        ref[0, :SUB, nz:] = low[2 * k + 1] + high[2 * k + 1]
        ref[0, SUB + ny :, nz:] = low[2 * k + 1] + high[2 * k + 1]

    def reader(inside_ref, edge_ref, first, count):
        def get(x, row):
            if first <= x < nx - first:
                return inside_ref[x, row : row + SUB]
            at = x - (first - count) if x < first else x - (nx - first) + count
            return edge_ref[at, row : row + SUB]

        return get

    r_ref[0, SUB : SUB + ny] = right_ref[0]
    r_ref[1, SUB : SUB + ny] = right_ref[nx - 1]
    held = {("k0", 0): (k_ref, 0), ("k0", nx - 1): (k_ref, 1), ("k0", 1): (pass_ref, 0), ("k0", nx - 2): (pass_ref, 1)}
    for at, x in enumerate((0, 1, nx - 2, nx - 1)):
        held["n1", x] = (n_ref, at)
    held |= {("n1", 2): (pass_ref, 2), ("n1", nx - 3): (pass_ref, 3)}
    sums = {}
    for stage in range(3):
        get = reader((a_ref, b_ref, c_ref)[stage], (ea_ref, eb_ref, ec_ref)[stage], stage, 3)
        start, size = SUB - 2 + stage, ny if stage == 2 else ring
        v = slabs_ref[stage, start : start + size]
        s = slabs_ref[stage, start - 1 : start - 1 + size] + slabs_ref[stage, start + 1 : start + 1 + size]
        q, after = slab_step(stage, v, s, si_ref[0, start : start + size])
        if stage < 2:
            slabs_ref[stage + 1, start : start + size] = after

        def put(x, row, value):
            edge_ref = (eb_ref, ec_ref)[stage]
            at = x - (stage - 2) if x < nx // 2 else x - (nx - 1 - stage) + 3
            edge_ref[at, row : row + SUB] = value

        sweep(
            stage, [(stage - 2, stage + 1), (nx - 1 - stage, nx + 2 - stage)], nx, ny, nz, gz,
            get, reader(i_ref, ei_ref, 0, 2), put, q, sums,
            lambda x, row: r_ref[0 if x == 0 else 1, row : row + SUB],
            lambda x, row: a_ref[x, row : row + SUB], held,
        )

    total_ref[0:1] = stat_ref[0, 0:1]
    for k, name in enumerate(ORDER[1:]):
        total_ref[k + 1 : k + 2] = jnp.sum(sums[name] + sum_ref[k], axis=0, keepdims=True)
    gx, n_x = lax.axis_index("gx"), lax.axis_size("gx")
    count = jnp.sum(stat_ref[1, 0:1], axis=1, keepdims=True)
    below, above = [part[4] for part in slab_parts]
    begin = jnp.where(
        gx == 0, 0.0,
        jnp.where(gx == 1, below, jnp.where(gx == n_x - 1, column_total - count, column_total - count - above)),
    )
    where_ref[0:1] = jnp.broadcast_to(begin, (1, nz))
    where_ref[1:2] = jnp.broadcast_to(count, (1, nz))
    where_ref[2:8] = jnp.zeros((6, nz), F32)


def shift_up(v, amount):
    if amount < SUB:
        return pltpu.roll(v, v.shape[0] - amount, 0)
    return jnp.concatenate([v[amount:], v[:amount]], axis=0)


def plan_kernel(after_ref, label_ref, index_ref, plan_ref, lane_ref):
    rows, slot_rows = label_ref.shape[0], index_ref.shape[0]
    wide = -(-(slot_rows + 1) // LANES) * LANES
    shape = (rows, LANES)
    lane, row = lanes_of(shape), subs_of(shape)
    ones = (label_ref[...] == 1).astype(jnp.bfloat16)
    totals = jnp.dot(ones, jnp.ones((LANES, LANES), jnp.bfloat16), preferred_element_type=F32)
    lower = (subs_of((rows, rows)) > lanes_of((rows, rows))).astype(jnp.bfloat16)
    before = jnp.dot(lower, totals.astype(jnp.bfloat16), preferred_element_type=F32).astype(jnp.int32)
    target, first = lax.div(before, LANES), lax.rem(before, LANES)
    listed = jnp.concatenate(
        [lax.rem(index_ref[...], LANES).astype(F32), jnp.zeros((wide - slot_rows, LANES), F32)], axis=0
    ).astype(jnp.bfloat16)
    spread = jnp.concatenate([target] * (wide // LANES), axis=1)
    place = lanes_of((rows, wide))
    here = jnp.dot((spread == place).astype(jnp.bfloat16), listed, preferred_element_type=F32)
    after = jnp.dot((spread + 1 == place).astype(jnp.bfloat16), listed, preferred_element_type=F32)
    lane_ref[...] = jnp.where(lane >= first, here, after).astype(jnp.int32)
    wrapped = (lane < first).astype(jnp.int32)
    filled = lane - first + LANES * wrapped < totals.astype(jnp.int32)
    way = jnp.where(filled, row - target - wrapped, 0)
    plan = jnp.zeros(shape, jnp.int32)
    step = 1
    while step < rows:
        moving = jnp.where((way & step) != 0, way, 0)
        arriving = shift_up(moving, step)
        plan = plan | (arriving & step)
        way = (way - moving) | arriving
        step *= 2
    plan_ref[...] = plan


def galerkin(total):
    def add_up(*rows):
        return [jnp.broadcast_to(jnp.sum(row, axis=1, keepdims=True), row.shape) for row in rows]

    row = {name: total[k : k + 1] for k, name in enumerate(ORDER)}
    b0, b2 = row["w0 r"], row["w0 n1"]
    g00, g01, g02 = row["w0 k0"], row["w1 k0"], row["w1 n1"]
    g11, g12, g22 = row["w1 k1"], row["w2 k1"], row["w2 k2"]
    s00, s01, s02, s0, s11, s22 = add_up(g00, g01, g02, b0, g11, g22)
    l10, l20 = s01 / s00, s02 / s00
    h11 = g11 - l10 * (2.0 * g01 - l10 * g00)
    h12 = g12 - l10 * g02 - l20 * (g01 - l10 * g00)
    h22 = g22 - l20 * (2.0 * g02 - l20 * g00)
    y1, y2 = g00 - l10 * b0, b2 - l20 * b0
    d1, s12, s1 = add_up(h11, h12, y1)
    ok1 = d1 > 1e-7 * s11
    d1 = jnp.where(ok1, d1, 1.0)
    l21 = jnp.where(ok1, s12 / d1, 0.0)
    d2, s2 = add_up(h22 - l21 * (2.0 * h12 - l21 * h11), y2 - l21 * y1)
    ok2 = ok1 & (d2 > 1e-7 * s22)
    c2 = jnp.where(ok2, s2 / jnp.where(ok2, d2, 1.0), 0.0)
    c1 = jnp.where(ok1, s1 / d1 - l21 * c2, 0.0)
    c0 = s0 / s00 - l10 * c1 - l20 * c2
    return c0, c1, c2


def couple_kernel(
    stage, slot_rows, after_ref, where_ref, inside_ref, edge_ref, slabs_ref, plan_ref, lane_ref, blocks_ref,
    value_ref, buf_ref,
):
    nx, nz = inside_ref.shape[0], inside_ref.shape[2]
    ny = inside_ref.shape[1] - 2 * SUB
    rows = nx * ny
    gz = lax.axis_index("gz")

    def get(x, row):
        if stage <= x < nx - stage:
            return inside_ref[x, row : row + SUB]
        return edge_ref[x - (stage - 3) if x < stage else x - (nx - stage) + 3, row : row + SUB]

    for tile in range(ny // SUB):
        row = SUB + SUB * tile
        slab = slabs_ref[stage, row : row + SUB, :nz]
        v_low, v_mid = get(-1, row), get(0, row)
        for x in range(nx):
            v_high = get(x + 1, row)
            beside = get(x, row - 1) + get(x, row + 1)
            at = ny * x + SUB * tile
            value_ref[at : at + SUB] = (
                along_z(v_mid, slab, PACK * x, gz) + beside + (v_low + v_high) - 6.0 * v_mid
            )
            v_low, v_mid = v_mid, v_high
    value = jnp.take_along_axis(value_ref[...], lane_ref[...], axis=1)
    plan = plan_ref[...]
    step = 1
    while step < rows:
        value = jnp.where((plan & step) != 0, shift_up(value, step), value)
        step *= 2
    offset = jnp.max(where_ref[0:1]).astype(jnp.int32)
    count = jnp.max(where_ref[1:2]).astype(jnp.int32)
    shape = (slot_rows, LANES)
    slots = jnp.where(subs_of(shape) * LANES + lanes_of(shape) < count, value[:slot_rows], 0.0)
    slots = jnp.concatenate([slots, jnp.zeros((SUB, LANES), F32)], axis=0)
    inner = lax.rem(offset, LANES)
    turned = pltpu.roll(slots, inner, 1)
    moved = jnp.where(lanes_of((slot_rows + SUB, LANES)) >= inner, turned, pltpu.roll(turned, 1, 0))
    buf_ref[...] = jnp.zeros_like(buf_ref)
    buf_ref[pl.ds(offset // LANES, slot_rows + SUB), :] = moved
    gx = lax.axis_index("gx")
    n_gx = lax.axis_size("gx")
    size = blocks_ref.shape[0] // n_gx
    for block in range(n_gx):
        begin = pl.multiple_of((gx ^ block) * size, SUB)
        blocks_ref[block * size : block * size + size] = buf_ref[pl.ds(begin, size), :]


def add_kernel(a_ref, b_ref, after_ref, out_ref):
    out_ref[...] = a_ref[...] + b_ref[...]


def pack_kernel(total_ref, *refs):
    list_refs, out_refs = refs[:3], refs[3:]
    size = (out_refs[0].shape[0] - SUB) // 3
    for block, out_ref in enumerate(out_refs):
        for k, list_ref in enumerate(list_refs):
            out_ref[k * size : k * size + size] = list_ref[block * size : block * size + size]
        out_ref[3 * size :] = total_ref[...]


ROUND = (1, 3, 0, 2)
BACK = (2, 0, 3, 1)


def pack_round_kernel(total_ref, *refs):
    list_refs, (own_ref, round_ref, middle_ref, back_ref, rest_ref) = refs[:3], refs[3:]
    size = (own_ref.shape[0] - SUB) // 3
    half = size // 2
    gx = lax.axis_index("gx")
    inside = (gx == 1) | (gx == 2)
    ahead, behind = jnp.where(inside, 2, 1), jnp.where(inside, 1, 2)
    upper = jnp.where(gx >= 2, half, 0)
    for k, list_ref in enumerate(list_refs):
        for out_ref, begin, rows in (
            (own_ref, 0, size), (round_ref, ahead * size, size), (middle_ref, 3 * size, size),
            (back_ref, behind * size + upper, half), (rest_ref, behind * size + (half - upper), half),
        ):
            if not isinstance(begin, int):
                begin = pl.multiple_of(begin, SUB)
            out_ref[k * rows : k * rows + rows] = list_ref[pl.ds(begin, rows), :]
    for out_ref in (own_ref, round_ref, middle_ref, back_ref):
        out_ref[out_ref.shape[0] - SUB :] = total_ref[...]


def land_round(own_ref, middle_ref, round_ref, back_ref, rest_ref):
    size = (own_ref.shape[0] - SUB) // 3
    half = size // 2
    gx = lax.axis_index("gx")
    inside = (gx == 1) | (gx == 2)
    last = lambda ref: ref[ref.shape[0] - SUB :]
    total = last(own_ref) + last(round_ref) + last(back_ref) + last(middle_ref)
    parts = []
    for k in range(3):
        whole = slice(k * size, k * size + size)
        back, rest = [ref[k * half : k * half + half] for ref in (back_ref, rest_ref)]
        odd = lax.rem(gx, 2) == 1
        low = jnp.where(odd, jnp.where(gx == 3, rest, 0.0), back)
        high = jnp.where(odd, back, jnp.where(gx == 0, rest, 0.0))
        part = own_ref[whole] + round_ref[whole] + jnp.where(inside, middle_ref[whole], 0.0)
        parts.append(part + jnp.concatenate([low, high], axis=0))
    return total, parts


def land_pairs(alone, own_ref, *refs):
    small_refs, large_refs = refs[: len(alone[0])], refs[len(alone[0]) :]
    size = (own_ref.shape[0] - SUB) // 3
    gx = lax.axis_index("gx")

    def is_one(flags):
        found = gx < 0
        for place, flag in enumerate(flags):
            if flag:
                found = found | (gx == place)
        return found

    total = own_ref[3 * size :]
    for flags, ref in zip(alone[0], small_refs):
        total = total + jnp.where(is_one(flags), ref[...], 0.0)
    for flags, ref in zip(alone[1], large_refs):
        total = total + jnp.where(is_one(flags), 0.0, ref[3 * size :])
    parts = []
    for k in range(3):
        part = own_ref[k * size : k * size + size]
        for ref in large_refs:
            part = part + ref[k * size : k * size + size]
        parts.append(part)
    return total, parts


def membrane_kernel(
    half_ref, slope_ref, tau_ref, cond_ref, rev_ref, after_ref, v_ref, gates_ref, cot_ref,
    base_ref, sum_ref, factor_ref, coef_ref,
):
    n_states, rows = gates_ref.shape[:2]
    v = v_ref[...]

    def state(g, carry):
        total, current = carry
        inv_slope = 1.0 / slope_ref[g]
        tau_base = tau_ref[g]
        scaled = (v - half_ref[g]) * inv_slope
        gate = gates_ref[g]
        cot = cot_ref[g]
        steady = 1.0 / (1.0 + jnp.exp(-scaled))
        bell = jnp.exp(-scaled * scaled)
        rate = TIME_STEP / (tau_base * (0.5 + bell))
        decay = jnp.exp(-rate)
        steady_slope = steady * (1.0 - steady)
        decay_slope = decay * rate * rate * ((tau_base / TIME_STEP) * bell * (-2.0 * scaled))
        change = (steady_slope * (1.0 - decay) + (gate - steady) * decay_slope) * inv_slope
        base_ref[g] = cot * decay
        coef_ref[0, pl.ds(g, 1)] = jnp.full((1, LANES), TIME_STEP * cond_ref[g])
        coef_ref[1, pl.ds(g, 1)] = jnp.full((1, LANES), rev_ref[g])
        return total + cot * change, current + cond_ref[g] * gate

    zero = jnp.zeros((rows, LANES), F32)
    total, current = lax.fori_loop(0, n_states, state, (zero, zero), unroll=2)
    sum_ref[...] = total
    factor_ref[...] = 1.0 - TIME_STEP * current


def finish_kernel(
    land, coef_ref, vcot_ref, v_ref, sum_ref, factor_ref, base_ref, a_ref, b_ref, c_ref, eb_ref, ec_ref, *refs
):
    x_ref, volt_ref, gate_ref = refs[-3:]
    total, parts = land(*refs[:-3])
    c0, c1, c2 = galerkin(total)
    landed = c0 * parts[0] + c1 * parts[1] + c2 * parts[2]
    cot = vcot_ref[...] + landed
    v = v_ref[...]
    volt_ref[...] = cot * factor_ref[...] + sum_ref[...]
    for g in range(base_ref.shape[0]):
        gate_ref[g] = base_ref[g] - (coef_ref[0, g : g + 1] * cot) * (v - coef_ref[1, g : g + 1])
    nx, ny, nz = x_ref.shape
    own = slice(SUB, SUB + ny)
    for x in range(nx):
        w1 = b_ref[x, own] if 1 <= x < nx - 1 else eb_ref[2 if x == 0 else 3, own]
        w2 = c_ref[x, own] if 2 <= x < nx - 2 else ec_ref[x + 1 if x < 2 else x - (nx - 2) + 3, own]
        x_ref[x] = c0 * a_ref[x, own] + c1 * w1 + c2 * w2


def partners(axis, step):
    count = lax.axis_size(axis)
    if step == 0:
        return [i ^ 1 for i in range(count)]
    return [0] + [i + 1 if i % 2 else i - 1 for i in range(1, count - 1)] + [count - 1]


def swap(value, x_to=None, y_to=None):
    n_x, n_y, n_z = [lax.axis_size(axis) for axis in ("gx", "gy", "gz")]
    pairs = []
    for x in range(n_x):
        for y in range(n_y):
            to_x, to_y = x_to[x] if x_to else x, y_to[y] if y_to else y
            alone = (x_to and to_x == x) or (y_to and to_y == y)
            for z in range(n_z):
                to = (x, y, z ^ 1) if alone else (to_x, to_y, z)
                pairs.append(((x * n_y + y) * n_z + z, (to[0] * n_y + to[1]) * n_z + to[2]))
    return lax.ppermute(value, ("gx", "gy", "gz"), pairs)


def swap_by(value, to):
    n_x, n_y, n_z = [lax.axis_size(axis) for axis in ("gx", "gy", "gz")]
    pairs = []
    for x in range(n_x):
        for y in range(n_y):
            to_x, to_y = to(x, y)
            pairs += [((x * n_y + y) * n_z + z, (to_x * n_y + to_y) * n_z + z) for z in range(n_z)]
    return lax.ppermute(value, ("gx", "gy", "gz"), pairs)


def never_meet(count, k, slots, block):
    def apart(tile, owner):
        return owner * block >= (tile + 1) * slots or (owner + 1) * block <= count * block - (count - tile) * slots

    return [apart(i, i ^ k) and apart(i ^ k, i) for i in range(count)]


def local(
    potential_cot, damping, tissue_label, heart_index, voltage, gates, voltage_cot, gates_cot,
    half_voltage, gate_slope, tau_base, conductance, reversal,
):
    nx, ny, nz = potential_cot.shape
    rows = nx * ny
    ring = ny + SUB
    n_gx, n_gy = lax.axis_size("gx"), lax.axis_size("gy")
    n_states = gates.shape[0]
    block_rows = voltage.shape[1] // LANES
    slot_rows = heart_index.shape[3] // LANES
    block = shape_of(nx, ny, nz)
    flat = lambda a: a.reshape(rows, LANES)
    cells = lambda a: a.reshape(block_rows, LANES)
    states = lambda a: a.reshape(n_states, block_rows, LANES)

    w0, inv, packed, stat = call(
        start_kernel, (block, block, shape_of(2, ny, nz), shape_of(2, SUB, nz)), 3,
    )(in_hbm(potential_cot), in_hbm(damping), in_hbm(tissue_label))

    got = lax.ppermute(packed, "gz", [(0, 1), (1, 0)])
    cells_shape = jax.ShapeDtypeStruct((rows, LANES), jnp.int32)
    plan, lanes = call(plan_kernel, (cells_shape, cells_shape), 3, cost=6_000_000)(
        stat, flat(tissue_label), heart_index.reshape(slot_rows, LANES)
    )

    n_y = steps_of("gy")
    shapes = (
        (shape_of(2, ny, nz),) + (shape_of(nx + 1, SUB, nz),) * n_y + (shape_of(6, ny, nz),) * 2
        + (shape_of(4, SUB, nz),) * (2 * n_y)
    )
    slab, *faces = call(functools.partial(faces_kernel, n_y), shapes, 5)(w0, inv, packed, got, stat)
    along_y, along_x, across = faces[:n_y], faces[n_y : n_y + 2], faces[n_y + 2 :]
    y_to = [partners("gy", step) for step in range(n_y)]
    x_to = [partners("gx", step) for step in range(2)]
    along_y = [swap(face, y_to=y_to[j]) for j, face in enumerate(along_y)]
    along_x = [swap(face, x_to=x_to[i]) for i, face in enumerate(along_x)]
    across = [swap(face, x_to=x_to[k // n_y], y_to=y_to[k % n_y]) for k, face in enumerate(across)]

    tall = ring + SUB
    planes = shape_of(nx, tall, nz)
    edges = shape_of(6, tall, nz)
    in0, in_inv, in1, in2, in_sums, own_slab, passed = call(
        functools.partial(inner_kernel, n_y),
        (planes,) * 4 + (shape_of(len(ORDER) - 1, SUB, nz), shape_of(2, tall, nz), shape_of(4, tall, nz)),
        4 + n_y,
        scratch=[pltpu.VMEM((4, tall, nz), F32)] + [pltpu.VMEM((nx, tall, nz), F32)] * 3,
        cost=6_000_000,
    )(potential_cot, w0, inv, slab, *along_y)
    ends0, ends1, ends2, slabs, sums, where = call(
        functools.partial(outer_kernel, n_y, float(n_gx * voltage.shape[1])),
        (edges,) * 3 + (shape_of(3, tall, 2 * nz), shape_of(SUB, nz), shape_of(SUB, nz)),
        12 + 2 * n_y,
        scratch=[
            pltpu.VMEM((4, tall, nz), F32), pltpu.VMEM((1, tall, 2 * nz), F32),
            pltpu.VMEM((2, tall, nz), F32), pltpu.VMEM((2, tall, nz), F32), pltpu.VMEM((4, tall, nz), F32),
        ],
    )(plan, potential_cot, in0, in_inv, in1, in2, own_slab, in_sums, passed, stat, *along_x, *across)

    if n_gx > 4:
        counts = lax.all_gather(jnp.sum(stat[1, 0]), "gx")
        begin = jnp.sum(jnp.where(jnp.arange(n_gx) < lax.axis_index("gx"), counts, 0.0))
        where = where.at[0].set(begin)

    def couple(stage, after, inside, ends):
        return call(
            functools.partial(couple_kernel, stage, slot_rows),
            shape_of(n_gx * block_rows, LANES),
            7,
            scratch=[
                pltpu.VMEM((rows, LANES), F32), pltpu.VMEM((n_gx * block_rows + slot_rows + SUB, LANES), F32),
            ],
            cost=6_000_000,
        )(after, where, inside, ends, slabs, plan, lanes)

    def add(value, axis, step, after):
        got = lax.ppermute(value, axis, [(i, i ^ step) for i in range(lax.axis_size(axis))])
        return call(add_kernel, shape_of(SUB, nz), 3)(value, got, after)

    list0 = couple(0, sums, in0, ends0)
    sums = add(sums, "gz", 1, list0)
    list1 = couple(1, sums, in1, ends1)
    list2 = couple(2, list1, in2, ends2)
    rounds = n_gx == 4 and n_gy == 2 and 2 * slot_rows == 5 * block_rows
    if rounds:
        other = swap_by(sums, lambda x, y: (x if x in (1, 2) else 3 - x, 1 - y))
        sums = call(add_kernel, shape_of(SUB, nz), 3)(sums, other, list2)
    else:
        for step in [2**k for k in range(n_gy.bit_length() - 1)]:
            sums = add(sums, "gy", step, list2)
    if rounds:
        own, ahead, middle, back, rest = call(
            pack_round_kernel,
            (shape_of(3 * block_rows + SUB, LANES),) * 3
            + (shape_of(3 * block_rows // 2 + SUB, LANES), shape_of(3 * block_rows // 2, LANES)),
            4,
        )(sums, list0, list1, list2)
        arrived = [
            own,
            swap_by(middle, lambda x, y: (3 - x, y) if x in (1, 2) else (x, 1 - y)),
            swap(ahead, x_to=ROUND),
            swap(back, x_to=BACK),
            swap(rest, x_to=partners("gx", 0)),
        ]
        land = land_round
    else:
        blocks = call(pack_kernel, (shape_of(3 * block_rows + SUB, LANES),) * n_gx, 4)(sums, list0, list1, list2)
        apart = {k: never_meet(n_gx, k, slot_rows, block_rows) for k in range(1, n_gx)}
        few = [k for k in apart if any(apart[k])]
        many = [k for k in [2, 3, 1] + list(range(4, n_gx)) if k < n_gx and not all(apart[k])]
        arrived = [blocks[0]]
        arrived += [swap(sums, x_to=[i ^ k if apart[k][i] else i for i in range(n_gx)]) for k in few]
        arrived += [swap(blocks[k], x_to=[i if apart[k][i] else i ^ k for i in range(n_gx)]) for k in many]
        land = functools.partial(land_pairs, [[apart[k] for k in few], [apart[k] for k in many]])

    base, total_change, factor, state_coefs = call(
        membrane_kernel,
        (
            shape_of(n_states, block_rows, LANES), shape_of(block_rows, LANES), shape_of(block_rows, LANES),
            shape_of(2, n_states, LANES),
        ),
        9,
        specs=[SMEM] * 5 + [VMEM] * 4,
        cost=6_000_000,
    )(
        half_voltage, gate_slope, tau_base, conductance, reversal,
        arrived[0], cells(voltage), states(gates), states(gates_cot),
    )
    solution, volt_grad, gate_grad = call(
        functools.partial(finish_kernel, land),
        (block, shape_of(block_rows, LANES), shape_of(n_states, block_rows, LANES)),
        11 + len(arrived),
    )(
        state_coefs, cells(voltage_cot), cells(voltage), total_change, factor, base,
        in0, in1, in2, ends1, ends2, *arrived,
    )
    return solution, volt_grad.reshape(voltage.shape), gate_grad.reshape(gates.shape)


def solution(mesh):
    grid = P(("groups", "gx"), "gy", "gz")
    cells = P(("groups", "gy", "gz"), "gx")
    states = P(None, ("groups", "gy", "gz"), "gx")
    in_specs = (
        grid, grid, grid, P(("groups", "gx"), "gy", "gz", None), cells, states, cells, states,
        P(), P(), P(), P(), P(),
    )
    return jax.shard_map(
        local, mesh=mesh, in_specs=in_specs, out_specs=(grid, cells, states), check_vma=False
    )
```

```python
import functools

import jax
import jax.numpy as jnp
from jax import lax
from jax.experimental import pallas as pl
from jax.experimental.pallas import tpu as pltpu
from jax.sharding import PartitionSpec as P

TIME_STEP = 0.5
LANES = 128
SUB = 8
PACK = 8
EDGE_COST = 1_000_000_000
COUNT_LANE = 4 * PACK
F32 = jnp.float32

VMEM = pl.BlockSpec(memory_space=pltpu.VMEM)
SMEM = pl.BlockSpec(memory_space=pltpu.SMEM)


def shape_of(*dims):
    return jax.ShapeDtypeStruct(dims, F32)


def call(kernel, out_shape, n_in, specs=None, outs=None, scratch=(), cost=2_000_000, limit=32):
    return pl.pallas_call(
        kernel,
        out_shape=out_shape,
        in_specs=specs if specs is not None else [VMEM] * n_in,
        out_specs=outs if outs is not None else jax.tree.map(lambda _: VMEM, out_shape),
        scratch_shapes=list(scratch),
        compiler_params=pltpu.CompilerParams(vmem_limit_bytes=limit * 1024 * 1024),
        cost_estimate=pl.CostEstimate(flops=cost, bytes_accessed=cost, transcendentals=0),
    )


def in_hbm(array):
    return pltpu.with_memory_space_constraint(array, pltpu.HBM)


def lanes_of(shape):
    return lax.broadcasted_iota(jnp.int32, shape, len(shape) - 1)


def subs_of(shape):
    return lax.broadcasted_iota(jnp.int32, shape, len(shape) - 2)


def start_kernel(right_ref, damping_ref, label_ref, w0_ref, inv_ref, pack_ref, stat_ref):
    nx, ny, nz = right_ref.shape
    gz = lax.axis_index("gz")
    lane = lanes_of((ny, nz))
    packed_w = jnp.zeros((ny, nz), F32)
    packed_i = jnp.zeros((ny, nz), F32)
    energy = jnp.zeros((ny, nz), F32)
    cells = jnp.zeros((ny, nz), F32)
    for x in range(nx):
        label = label_ref[x].astype(F32)
        right = right_ref[x]
        inv = 1.0 / (12.0 + damping_ref[x] * (1.0 + 3.0 * label))
        w0 = right * inv
        w0_ref[x] = w0
        inv_ref[x] = inv
        energy = energy + right * w0
        cells = cells + label
        turn = (PACK * x + 3) % nz
        begin = PACK * x + 3 * gz
        chosen = (lane >= begin) & (lane < begin + 3)
        packed_w = jnp.where(chosen, pltpu.roll(w0, turn, 1), packed_w)
        packed_i = jnp.where(chosen, pltpu.roll(inv, turn, 1), packed_i)
    pack_ref[0] = packed_w
    pack_ref[1] = packed_i
    stat_ref[0] = jnp.broadcast_to(jnp.sum(energy, axis=0, keepdims=True), (SUB, nz))
    stat_ref[1] = jnp.broadcast_to(jnp.sum(cells, axis=0, keepdims=True), (SUB, nz))


def steps_of(axis):
    return 1 if lax.axis_size(axis) == 2 else 2


def upper_in(axis, step):
    return lax.rem(lax.axis_index(axis), 2) == step


def has_partner(axis, step):
    here = lax.axis_index(axis)
    return jnp.where(upper_in(axis, step), here < lax.axis_size(axis) - 1, here > 0)


def unpack_rows(tile, step):
    sub = subs_of(tile.shape)
    up, there = upper_in("gy", step), has_partner("gy", step)
    depth = jnp.where(there, jnp.where(up, SUB - 1 - sub, sub), -1)
    return jnp.where(depth >= 5, tile, 0.0), jnp.where(depth >= 6, pltpu.roll(tile, 4, 0), 0.0)


def halo_rows(tiles):
    w_tile, i_tile = unpack_rows(tiles[0], 0)
    for step, tile in enumerate(tiles[1:], 1):
        w_more, i_more = unpack_rows(tile, step)
        w_tile, i_tile = w_tile + w_more, i_tile + i_more
    return w_tile, i_tile


def faces_kernel(n_y, w0_ref, inv_ref, own_ref, got_ref, stat_ref, slab_ref, *refs):
    y_refs, x_refs, edge_refs = refs[:n_y], refs[n_y : n_y + 2], refs[n_y + 2 :]
    nx, ny, nz = w0_ref.shape
    sub = subs_of((SUB, nz))
    lane = lanes_of((ny, nz))
    slab_ref[...] = own_ref[...] + got_ref[...]
    for step, face_ref in enumerate(y_refs):
        up = upper_in("gy", step)
        keep_w = jnp.where(up, sub, SUB - 1 - sub) >= 5
        for x in range(nx + 1):
            w_rows, i_rows = (w0_ref.at[x], inv_ref.at[x]) if x < nx else (slab_ref.at[0], slab_ref.at[1])
            w_face = jnp.where(up, w_rows[ny - SUB :], w_rows[:SUB])
            i_face = jnp.where(up, i_rows[ny - SUB :], i_rows[:SUB])
            face_ref[x] = jnp.where(keep_w, w_face, pltpu.roll(i_face, 4, 0))
    cells = jnp.sum(stat_ref[1, 0:1], axis=1, keepdims=True)
    slab_w = slab_ref[0]
    half = pltpu.roll(slab_ref[1], nz // 2, 1)
    up_slab = jnp.where(lane >= nz - 3 * PACK, slab_w, half)
    down_slab = jnp.where(lane < 3 * PACK, slab_w, half)
    for step, face_ref in enumerate(x_refs):
        up = upper_in("gx", step)
        first = jnp.where(up, nx - 3, 0)
        for k in range(3):
            face_ref[k] = w0_ref[first + k]
        for k in range(2):
            face_ref[3 + k] = inv_ref[jnp.where(up, nx - 2, 0) + k]
        face_ref[5] = jnp.where(lane == COUNT_LANE, cells, jnp.where(up, up_slab, down_slab))
        for y_step, y_ref in enumerate(y_refs):
            edge_ref = edge_refs[step * n_y + y_step]
            for k in range(3):
                edge_ref[k] = y_ref[first + k]
            edge_ref[3] = y_ref[nx]


SUMS = (("w0 k0", "w1 k0"), ("w1 n1", "w1 k1", "w2 k1", "w0 n1"), ("w2 k2",))
ORDER = ("w0 r", "w0 k0", "w1 k0", "w1 n1", "w1 k1", "w2 k1", "w2 k2", "w0 n1")


def slab_step(stage, v, s, inv):
    width = v.shape[1]
    across = pltpu.roll(v, PACK, 1) + pltpu.roll(v, width - PACK, 1)
    q = v + 0.5 * (s + across)
    if stage == 2:
        return q, None
    total = (
        pltpu.roll(q, 1, 1) + pltpu.roll(q, width - 1, 1) + s + across
        + 0.5 * (pltpu.roll(s, PACK, 1) + pltpu.roll(s, width - PACK, 1))
    )
    return q, next_vector(stage, v, total, inv)


def next_vector(stage, v, total, inv):
    return v - total * inv if stage == 0 else total * inv


def along_z(q, half, column, gz):
    nz = q.shape[1]
    lane = lanes_of(q.shape)
    entry = (nz - 1) * (1 - gz)
    turn = lax.rem(entry - (column + 3 - gz) + 2 * nz, nz)
    up = jnp.where(lane == nz - 1, 0.0, pltpu.roll(q, nz - 1, 1))
    down = jnp.where(lane == 0, 0.0, pltpu.roll(q, 1, 1))
    return up + down + jnp.where(lane == entry, pltpu.roll(half, turn, 1), 0.0)


def sweep(stage, spans, nx, ny, nz, gz, get, get_inv, put, slab_q, sums, get_right, get_w0, held):
    margin = 2 - stage
    start = SUB - margin
    tiles = ny // SUB + (margin > 0)
    own = subs_of((SUB, nz)) >= margin
    names = SUMS[stage]
    parts = {name: [] for name in names}
    for tile in range(tiles):
        row = start + SUB * tile
        q_rows = slab_q[SUB * tile : SUB * tile + SUB]
        acc = {name: jnp.zeros((SUB, nz), F32) for name in names}

        def beside(x):
            return get(x, row - 1) + get(x, row + 1)

        def rows(name, x):
            ref, at = held[name, x]
            return ref.at[at, row : row + SUB]

        for first, last in spans:
            s_low, s_mid = beside(first - 1), beside(first)
            v_low, v_mid = get(first - 1, row), get(first, row)
            for x in range(first, last):
                v_high, s_high = get(x + 1, row), beside(x + 1)
                across = v_low + v_high
                column = (PACK * x) % (2 * nz)
                half = q_rows[:, column // nz * nz : column // nz * nz + nz]
                rest = s_mid + across
                total = along_z(v_mid + 0.5 * rest, half, column % nz, gz) + rest + 0.5 * (s_low + s_high)
                if stage < 2:
                    after = next_vector(stage, v_mid, total, get_inv(x, row))
                    put(x, row, after)
                if 0 <= x < nx:
                    if stage == 0:
                        k0 = get_right(x, row) - total
                        rows("k0", x)[...] = k0
                        terms = (v_mid * k0, after * k0)
                    elif stage == 1:
                        rows("n1", x)[...] = total
                        k1 = rows("k0", x)[...] - total
                        terms = (v_mid * total, v_mid * k1, after * k1, get_w0(x, row) * total)
                    else:
                        terms = (v_mid * (rows("n1", x)[...] - total),)
                    for name, term in zip(names, terms):
                        acc[name] = acc[name] + term
                v_low, v_mid, s_low, s_mid = v_mid, v_high, s_mid, s_high
        for name in names:
            parts[name].append(acc[name])
    for name in names:
        part = parts[name]
        total = part[1]
        for other in part[2 : ny // SUB]:
            total = total + other
        sums[name] = total + (jnp.where(own, part[0], part[-1]) if margin else part[0])


def inner_kernel(n_y, right_ref, w0_ref, inv_ref, slab_ref, *refs):
    y_refs, refs = refs[:n_y], refs[n_y:]
    a_ref, i_ref, b_ref, c_ref, sum_ref, own_slab_ref, pass_ref, slabs_ref, r_ref, k_ref, n_ref = refs
    nx, ny, nz = w0_ref.shape
    gz = lax.axis_index("gz")
    for x in range(nx + 1):
        halos = halo_rows([ref[x] for ref in y_refs])
        for k in range(2):
            if x < nx:
                ref, own = (a_ref, i_ref)[k].at[x], (w0_ref, inv_ref)[k][x]
            else:
                ref, own = own_slab_ref.at[k], slab_ref[k]
            ref[:SUB] = halos[k]
            ref[SUB : SUB + ny] = own
            ref[SUB + ny :] = halos[k]
    for k in range(2):
        slabs_ref[3 * k] = own_slab_ref[k]
    for x in range(nx):
        r_ref[x, SUB : SUB + ny] = right_ref[x]
    held = {("k0", x): (k_ref, x) for x in range(nx)} | {("n1", x): (n_ref, x) for x in range(nx)}
    held |= {("k0", 1): (pass_ref, 0), ("k0", nx - 2): (pass_ref, 1)}
    held |= {("n1", 2): (pass_ref, 2), ("n1", nx - 3): (pass_ref, 3)}
    sums = {}
    for stage in range(3):
        source, target = (a_ref, b_ref, c_ref)[stage], (b_ref, c_ref, None)[stage]
        start, size = SUB - 2 + stage, ny if stage == 2 else ny + SUB
        v = slabs_ref[stage, start : start + size]
        s = slabs_ref[stage, start - 1 : start - 1 + size] + slabs_ref[stage, start + 1 : start + 1 + size]
        q, after = slab_step(stage, v, s, slabs_ref[3, start : start + size])
        if stage < 2:
            slabs_ref[stage + 1, start : start + size] = after

        def put(x, row, value):
            target[x, row : row + SUB] = value

        sweep(
            stage, [(1 + stage, nx - 1 - stage)], nx, ny, nz, gz,
            lambda x, row: source[x, row : row + SUB], lambda x, row: i_ref[x, row : row + SUB],
            put, q, sums,
            lambda x, row: r_ref[x, row : row + SUB], lambda x, row: a_ref[x, row : row + SUB], held,
        )
    for k, name in enumerate(ORDER[1:]):
        sum_ref[k] = sums[name]


def outer_kernel(
    n_y, column_total, after_ref, right_ref, a_ref, i_ref, b_ref, c_ref, slab_ref, sum_ref, pass_ref, stat_ref, *refs
):
    x_refs, corner_refs = refs[:2], refs[2 : 2 + 2 * n_y]
    ea_ref, eb_ref, ec_ref, slabs_ref, total_ref, where_ref, ei_ref, si_ref, r_ref, k_ref, n_ref = refs[2 + 2 * n_y :]
    nx, ny, nz = a_ref.shape[0], a_ref.shape[1] - 2 * SUB, a_ref.shape[2]
    ring = ny + SUB
    gz = lax.axis_index("gz")
    odd = lax.rem(lax.axis_index("gx"), 2) == 1

    def beyond(upper, read):
        there = has_partner("gx", 0) if upper else has_partner("gx", 1)
        swapped = has_partner("gx", 1) if upper else has_partner("gx", 0)
        first, second = read(0), read(1)
        if upper:
            return jnp.where(jnp.where(odd, swapped, there), jnp.where(odd, second, first), 0.0)
        return jnp.where(jnp.where(odd, swapped, there), jnp.where(odd, first, second), 0.0)

    def write(ref, at, own, halo):
        ref[at, :SUB] = halo
        ref[at, SUB : SUB + ny] = own
        ref[at, SUB + ny :] = halo

    lane_tile, lane = lanes_of((SUB, nz)), lanes_of((ny, nz))
    slab_parts = []
    for side, upper in enumerate((False, True)):
        tiles = [
            halo_rows([beyond(upper, lambda step: corner_refs[step * n_y + j][k]) for j in range(n_y)])
            for k in range(4)
        ]
        for k in range(3):
            write(ea_ref, 3 * side + k, beyond(upper, lambda step: x_refs[step][k]), tiles[k][0])
        for k in range(2):
            own = beyond(upper, lambda step: x_refs[step][3 + k])
            write(ei_ref, 2 * side + k, own, tiles[k if upper else k + 1][1])
        own = beyond(upper, lambda step: x_refs[step][5])

        def near(value, lanes, planes):
            return jnp.where(lanes < planes * PACK if upper else lanes >= nz - planes * PACK, value, 0.0)

        slab_parts.append((
            near(own, lane, 3), near(tiles[3][0], lane_tile, 3),
            near(pltpu.roll(own, nz // 2, 1), lane, 2), near(tiles[3][1], lane_tile, 2),
            own[0:1, COUNT_LANE : COUNT_LANE + 1],
        ))

    low, high = slab_parts
    for ref, k in ((slabs_ref, 0), (si_ref, 1)):
        ref[0, :, :nz] = slab_ref[k]
        ref[0, SUB : SUB + ny, nz:] = low[2 * k] + high[2 * k]
        ref[0, :SUB, nz:] = low[2 * k + 1] + high[2 * k + 1]
        ref[0, SUB + ny :, nz:] = low[2 * k + 1] + high[2 * k + 1]

    def reader(inside_ref, edge_ref, first, count):
        def get(x, row):
            if first <= x < nx - first:
                return inside_ref[x, row : row + SUB]
            at = x - (first - count) if x < first else x - (nx - first) + count
            return edge_ref[at, row : row + SUB]

        return get

    r_ref[0, SUB : SUB + ny] = right_ref[0]
    r_ref[1, SUB : SUB + ny] = right_ref[nx - 1]
    held = {("k0", 0): (k_ref, 0), ("k0", nx - 1): (k_ref, 1), ("k0", 1): (pass_ref, 0), ("k0", nx - 2): (pass_ref, 1)}
    for at, x in enumerate((0, 1, nx - 2, nx - 1)):
        held["n1", x] = (n_ref, at)
    held |= {("n1", 2): (pass_ref, 2), ("n1", nx - 3): (pass_ref, 3)}
    sums = {}
    for stage in range(3):
        get = reader((a_ref, b_ref, c_ref)[stage], (ea_ref, eb_ref, ec_ref)[stage], stage, 3)
        start, size = SUB - 2 + stage, ny if stage == 2 else ring
        v = slabs_ref[stage, start : start + size]
        s = slabs_ref[stage, start - 1 : start - 1 + size] + slabs_ref[stage, start + 1 : start + 1 + size]
        q, after = slab_step(stage, v, s, si_ref[0, start : start + size])
        if stage < 2:
            slabs_ref[stage + 1, start : start + size] = after

        def put(x, row, value):
            edge_ref = (eb_ref, ec_ref)[stage]
            at = x - (stage - 2) if x < nx // 2 else x - (nx - 1 - stage) + 3
            edge_ref[at, row : row + SUB] = value

        sweep(
            stage, [(stage - 2, stage + 1), (nx - 1 - stage, nx + 2 - stage)], nx, ny, nz, gz,
            get, reader(i_ref, ei_ref, 0, 2), put, q, sums,
            lambda x, row: r_ref[0 if x == 0 else 1, row : row + SUB],
            lambda x, row: a_ref[x, row : row + SUB], held,
        )

    total_ref[0:1] = stat_ref[0, 0:1]
    for k, name in enumerate(ORDER[1:]):
        total_ref[k + 1 : k + 2] = jnp.sum(sums[name] + sum_ref[k], axis=0, keepdims=True)
    gx, n_x = lax.axis_index("gx"), lax.axis_size("gx")
    count = jnp.sum(stat_ref[1, 0:1], axis=1, keepdims=True)
    below, above = [part[4] for part in slab_parts]
    begin = jnp.where(
        gx == 0, 0.0,
        jnp.where(gx == 1, below, jnp.where(gx == n_x - 1, column_total - count, column_total - count - above)),
    )
    where_ref[0:1] = jnp.broadcast_to(begin, (1, nz))
    where_ref[1:2] = jnp.broadcast_to(count, (1, nz))
    where_ref[2:8] = jnp.zeros((6, nz), F32)


def shift_up(v, amount):
    if amount < SUB:
        return pltpu.roll(v, v.shape[0] - amount, 0)
    return jnp.concatenate([v[amount:], v[:amount]], axis=0)


def plan_kernel(after_ref, label_ref, index_ref, plan_ref, lane_ref):
    rows, slot_rows = label_ref.shape[0], index_ref.shape[0]
    wide = -(-(slot_rows + 1) // LANES) * LANES
    shape = (rows, LANES)
    lane, row = lanes_of(shape), subs_of(shape)
    ones = (label_ref[...] == 1).astype(jnp.bfloat16)
    totals = jnp.dot(ones, jnp.ones((LANES, LANES), jnp.bfloat16), preferred_element_type=F32)
    lower = (subs_of((rows, rows)) > lanes_of((rows, rows))).astype(jnp.bfloat16)
    before = jnp.dot(lower, totals.astype(jnp.bfloat16), preferred_element_type=F32).astype(jnp.int32)
    target, first = lax.div(before, LANES), lax.rem(before, LANES)
    listed = jnp.concatenate(
        [lax.rem(index_ref[...], LANES).astype(F32), jnp.zeros((wide - slot_rows, LANES), F32)], axis=0
    ).astype(jnp.bfloat16)
    spread = jnp.concatenate([target] * (wide // LANES), axis=1)
    place = lanes_of((rows, wide))
    here = jnp.dot((spread == place).astype(jnp.bfloat16), listed, preferred_element_type=F32)
    after = jnp.dot((spread + 1 == place).astype(jnp.bfloat16), listed, preferred_element_type=F32)
    lane_ref[...] = jnp.where(lane >= first, here, after).astype(jnp.int32)
    wrapped = (lane < first).astype(jnp.int32)
    filled = lane - first + LANES * wrapped < totals.astype(jnp.int32)
    way = jnp.where(filled, row - target - wrapped, 0)
    plan = jnp.zeros(shape, jnp.int32)
    step = 1
    while step < rows:
        moving = jnp.where((way & step) != 0, way, 0)
        arriving = shift_up(moving, step)
        plan = plan | (arriving & step)
        way = (way - moving) | arriving
        step *= 2
    plan_ref[...] = plan


def galerkin(total):
    def add_up(*rows):
        return [jnp.broadcast_to(jnp.sum(row, axis=1, keepdims=True), row.shape) for row in rows]

    row = {name: total[k : k + 1] for k, name in enumerate(ORDER)}
    b0, b2 = row["w0 r"], row["w0 n1"]
    g00, g01, g02 = row["w0 k0"], row["w1 k0"], row["w1 n1"]
    g11, g12, g22 = row["w1 k1"], row["w2 k1"], row["w2 k2"]
    s00, s01, s02, s0, s11, s22 = add_up(g00, g01, g02, b0, g11, g22)
    l10, l20 = s01 / s00, s02 / s00
    h11 = g11 - l10 * (2.0 * g01 - l10 * g00)
    h12 = g12 - l10 * g02 - l20 * (g01 - l10 * g00)
    h22 = g22 - l20 * (2.0 * g02 - l20 * g00)
    y1, y2 = g00 - l10 * b0, b2 - l20 * b0
    d1, s12, s1 = add_up(h11, h12, y1)
    ok1 = d1 > 1e-7 * s11
    d1 = jnp.where(ok1, d1, 1.0)
    l21 = jnp.where(ok1, s12 / d1, 0.0)
    d2, s2 = add_up(h22 - l21 * (2.0 * h12 - l21 * h11), y2 - l21 * y1)
    ok2 = ok1 & (d2 > 1e-7 * s22)
    c2 = jnp.where(ok2, s2 / jnp.where(ok2, d2, 1.0), 0.0)
    c1 = jnp.where(ok1, s1 / d1 - l21 * c2, 0.0)
    c0 = s0 / s00 - l10 * c1 - l20 * c2
    return c0, c1, c2


def couple_kernel(
    stage, slot_rows, after_ref, where_ref, inside_ref, edge_ref, slabs_ref, plan_ref, lane_ref, blocks_ref,
    value_ref, buf_ref,
):
    nx, nz = inside_ref.shape[0], inside_ref.shape[2]
    ny = inside_ref.shape[1] - 2 * SUB
    rows = nx * ny
    gz = lax.axis_index("gz")

    def get(x, row):
        if stage <= x < nx - stage:
            return inside_ref[x, row : row + SUB]
        return edge_ref[x - (stage - 3) if x < stage else x - (nx - stage) + 3, row : row + SUB]

    for tile in range(ny // SUB):
        row = SUB + SUB * tile
        slab = slabs_ref[stage, row : row + SUB, :nz]
        v_low, v_mid = get(-1, row), get(0, row)
        for x in range(nx):
            v_high = get(x + 1, row)
            beside = get(x, row - 1) + get(x, row + 1)
            at = ny * x + SUB * tile
            value_ref[at : at + SUB] = (
                along_z(v_mid, slab, PACK * x, gz) + beside + (v_low + v_high) - 6.0 * v_mid
            )
            v_low, v_mid = v_mid, v_high
    value = jnp.take_along_axis(value_ref[...], lane_ref[...], axis=1)
    plan = plan_ref[...]
    step = 1
    while step < rows:
        value = jnp.where((plan & step) != 0, shift_up(value, step), value)
        step *= 2
    offset = jnp.max(where_ref[0:1]).astype(jnp.int32)
    count = jnp.max(where_ref[1:2]).astype(jnp.int32)
    shape = (slot_rows, LANES)
    slots = jnp.where(subs_of(shape) * LANES + lanes_of(shape) < count, value[:slot_rows], 0.0)
    slots = jnp.concatenate([slots, jnp.zeros((SUB, LANES), F32)], axis=0)
    inner = lax.rem(offset, LANES)
    turned = pltpu.roll(slots, inner, 1)
    moved = jnp.where(lanes_of((slot_rows + SUB, LANES)) >= inner, turned, pltpu.roll(turned, 1, 0))
    buf_ref[...] = jnp.zeros_like(buf_ref)
    buf_ref[pl.ds(offset // LANES, slot_rows + SUB), :] = moved
    gx = lax.axis_index("gx")
    n_gx = lax.axis_size("gx")
    size = blocks_ref.shape[0] // n_gx
    for block in range(n_gx):
        begin = pl.multiple_of((gx ^ block) * size, SUB)
        blocks_ref[block * size : block * size + size] = buf_ref[pl.ds(begin, size), :]


def add_kernel(a_ref, b_ref, after_ref, out_ref):
    out_ref[...] = a_ref[...] + b_ref[...]


def pack_kernel(total_ref, *refs):
    list_refs, out_refs = refs[:3], refs[3:]
    size = (out_refs[0].shape[0] - SUB) // 3
    for block, out_ref in enumerate(out_refs):
        for k, list_ref in enumerate(list_refs):
            out_ref[k * size : k * size + size] = list_ref[block * size : block * size + size]
        out_ref[3 * size :] = total_ref[...]


ROUND = (1, 3, 0, 2)
BACK = (2, 0, 3, 1)


def pack_round_kernel(total_ref, *refs):
    list_refs, (own_ref, round_ref, middle_ref, back_ref, rest_ref) = refs[:3], refs[3:]
    size = (own_ref.shape[0] - SUB) // 3
    half = size // 2
    gx = lax.axis_index("gx")
    inside = (gx == 1) | (gx == 2)
    ahead, behind = jnp.where(inside, 2, 1), jnp.where(inside, 1, 2)
    upper = jnp.where(gx >= 2, half, 0)
    for k, list_ref in enumerate(list_refs):
        for out_ref, begin, rows in (
            (own_ref, 0, size), (round_ref, ahead * size, size), (middle_ref, 3 * size, size),
            (back_ref, behind * size + upper, half), (rest_ref, behind * size + (half - upper), half),
        ):
            if not isinstance(begin, int):
                begin = pl.multiple_of(begin, SUB)
            out_ref[k * rows : k * rows + rows] = list_ref[pl.ds(begin, rows), :]
    for out_ref in (own_ref, round_ref, middle_ref, back_ref):
        out_ref[out_ref.shape[0] - SUB :] = total_ref[...]


def edge_kernel(total_ref, other_ref, after_ref, out_ref):
    gx = lax.axis_index("gx")
    out_ref[...] = total_ref[...] + jnp.where((gx == 1) | (gx == 2), 0.0, other_ref[...])


def land_round(own_ref, round_ref, middle_ref, back_ref, rest_ref, edge_ref):
    size = (own_ref.shape[0] - SUB) // 3
    half = size // 2
    gx = lax.axis_index("gx")
    inside = (gx == 1) | (gx == 2)
    last = lambda ref: ref[ref.shape[0] - SUB :]
    total = edge_ref[...] + last(round_ref) + last(back_ref) + jnp.where(inside, last(middle_ref), 0.0)
    parts = []
    for k in range(3):
        whole = slice(k * size, k * size + size)
        back, rest = [ref[k * half : k * half + half] for ref in (back_ref, rest_ref)]
        odd = lax.rem(gx, 2) == 1
        low = jnp.where(odd, jnp.where(gx == 3, rest, 0.0), back)
        high = jnp.where(odd, back, jnp.where(gx == 0, rest, 0.0))
        part = own_ref[whole] + round_ref[whole] + jnp.where(inside, middle_ref[whole], 0.0)
        parts.append(part + jnp.concatenate([low, high], axis=0))
    return total, parts


def land_pairs(alone, own_ref, *refs):
    small_refs, large_refs = refs[: len(alone[0])], refs[len(alone[0]) :]
    size = (own_ref.shape[0] - SUB) // 3
    gx = lax.axis_index("gx")

    def is_one(flags):
        found = gx < 0
        for place, flag in enumerate(flags):
            if flag:
                found = found | (gx == place)
        return found

    total = own_ref[3 * size :]
    for flags, ref in zip(alone[0], small_refs):
        total = total + jnp.where(is_one(flags), ref[...], 0.0)
    for flags, ref in zip(alone[1], large_refs):
        total = total + jnp.where(is_one(flags), 0.0, ref[3 * size :])
    parts = []
    for k in range(3):
        part = own_ref[k * size : k * size + size]
        for ref in large_refs:
            part = part + ref[k * size : k * size + size]
        parts.append(part)
    return total, parts


def membrane_kernel(
    half_ref, slope_ref, tau_ref, cond_ref, rev_ref, after_ref, v_ref, gates_ref, cot_ref,
    base_ref, sum_ref, factor_ref, coef_ref,
):
    n_states, rows = gates_ref.shape[:2]
    v = v_ref[...]

    def state(g, carry):
        total, current = carry
        inv_slope = 1.0 / slope_ref[g]
        tau_base = tau_ref[g]
        scaled = (v - half_ref[g]) * inv_slope
        gate = gates_ref[g]
        cot = cot_ref[g]
        steady = 1.0 / (1.0 + jnp.exp(-scaled))
        bell = jnp.exp(-scaled * scaled)
        rate = TIME_STEP / (tau_base * (0.5 + bell))
        decay = jnp.exp(-rate)
        steady_slope = steady * (1.0 - steady)
        decay_slope = decay * rate * rate * ((tau_base / TIME_STEP) * bell * (-2.0 * scaled))
        change = (steady_slope * (1.0 - decay) + (gate - steady) * decay_slope) * inv_slope
        base_ref[g] = cot * decay
        coef_ref[0, pl.ds(g, 1)] = jnp.full((1, LANES), TIME_STEP * cond_ref[g])
        coef_ref[1, pl.ds(g, 1)] = jnp.full((1, LANES), rev_ref[g])
        return total + cot * change, current + cond_ref[g] * gate

    zero = jnp.zeros((rows, LANES), F32)
    total, current = lax.fori_loop(0, n_states, state, (zero, zero), unroll=2)
    sum_ref[...] = total
    factor_ref[...] = 1.0 - TIME_STEP * current


def finish_kernel(
    land, coef_ref, vcot_ref, v_ref, sum_ref, factor_ref, base_ref, a_ref, b_ref, c_ref, eb_ref, ec_ref, *refs
):
    x_ref, volt_ref, gate_ref = refs[-3:]
    total, parts = land(*refs[:-3])
    c0, c1, c2 = galerkin(total)
    landed = c0 * parts[0] + c1 * parts[1] + c2 * parts[2]
    cot = vcot_ref[...] + landed
    v = v_ref[...]
    volt_ref[...] = cot * factor_ref[...] + sum_ref[...]
    for g in range(base_ref.shape[0]):
        gate_ref[g] = base_ref[g] - (coef_ref[0, g : g + 1] * cot) * (v - coef_ref[1, g : g + 1])
    nx, ny, nz = x_ref.shape
    own = slice(SUB, SUB + ny)
    for x in range(nx):
        w1 = b_ref[x, own] if 1 <= x < nx - 1 else eb_ref[2 if x == 0 else 3, own]
        w2 = c_ref[x, own] if 2 <= x < nx - 2 else ec_ref[x + 1 if x < 2 else x - (nx - 2) + 3, own]
        x_ref[x] = c0 * a_ref[x, own] + c1 * w1 + c2 * w2


def partners(axis, step):
    count = lax.axis_size(axis)
    if step == 0:
        return [i ^ 1 for i in range(count)]
    return [0] + [i + 1 if i % 2 else i - 1 for i in range(1, count - 1)] + [count - 1]


def swap(value, x_to=None, y_to=None):
    n_x, n_y, n_z = [lax.axis_size(axis) for axis in ("gx", "gy", "gz")]
    pairs = []
    for x in range(n_x):
        for y in range(n_y):
            to_x, to_y = x_to[x] if x_to else x, y_to[y] if y_to else y
            alone = (x_to and to_x == x) or (y_to and to_y == y)
            for z in range(n_z):
                to = (x, y, z ^ 1) if alone else (to_x, to_y, z)
                pairs.append(((x * n_y + y) * n_z + z, (to[0] * n_y + to[1]) * n_z + to[2]))
    return lax.ppermute(value, ("gx", "gy", "gz"), pairs)


def never_meet(count, k, slots, block):
    def apart(tile, owner):
        return owner * block >= (tile + 1) * slots or (owner + 1) * block <= count * block - (count - tile) * slots

    return [apart(i, i ^ k) and apart(i ^ k, i) for i in range(count)]


def local(
    potential_cot, damping, tissue_label, heart_index, voltage, gates, voltage_cot, gates_cot,
    half_voltage, gate_slope, tau_base, conductance, reversal,
):
    nx, ny, nz = potential_cot.shape
    rows = nx * ny
    ring = ny + SUB
    n_gx, n_gy = lax.axis_size("gx"), lax.axis_size("gy")
    n_states = gates.shape[0]
    block_rows = voltage.shape[1] // LANES
    slot_rows = heart_index.shape[3] // LANES
    block = shape_of(nx, ny, nz)
    flat = lambda a: a.reshape(rows, LANES)
    cells = lambda a: a.reshape(block_rows, LANES)
    states = lambda a: a.reshape(n_states, block_rows, LANES)

    w0, inv, packed, stat = call(
        start_kernel, (block, block, shape_of(2, ny, nz), shape_of(2, SUB, nz)), 3,
    )(in_hbm(potential_cot), in_hbm(damping), in_hbm(tissue_label))

    got = lax.ppermute(packed, "gz", [(0, 1), (1, 0)])
    cells_shape = jax.ShapeDtypeStruct((rows, LANES), jnp.int32)
    plan, lanes = call(plan_kernel, (cells_shape, cells_shape), 3, cost=6_000_000)(
        stat, flat(tissue_label), heart_index.reshape(slot_rows, LANES)
    )

    n_y = steps_of("gy")
    shapes = (
        (shape_of(2, ny, nz),) + (shape_of(nx + 1, SUB, nz),) * n_y + (shape_of(6, ny, nz),) * 2
        + (shape_of(4, SUB, nz),) * (2 * n_y)
    )
    slab, *faces = call(functools.partial(faces_kernel, n_y), shapes, 5)(w0, inv, packed, got, stat)
    along_y, along_x, across = faces[:n_y], faces[n_y : n_y + 2], faces[n_y + 2 :]
    y_to = [partners("gy", step) for step in range(n_y)]
    x_to = [partners("gx", step) for step in range(2)]
    along_y = [swap(face, y_to=y_to[j]) for j, face in enumerate(along_y)]
    along_x = [swap(face, x_to=x_to[i]) for i, face in enumerate(along_x)]
    across = [swap(face, x_to=x_to[k // n_y], y_to=y_to[k % n_y]) for k, face in enumerate(across)]

    tall = ring + SUB
    planes = shape_of(nx, tall, nz)
    edges = shape_of(6, tall, nz)
    in0, in_inv, in1, in2, in_sums, own_slab, passed = call(
        functools.partial(inner_kernel, n_y),
        (planes,) * 4 + (shape_of(len(ORDER) - 1, SUB, nz), shape_of(2, tall, nz), shape_of(4, tall, nz)),
        4 + n_y,
        scratch=[pltpu.VMEM((4, tall, nz), F32)] + [pltpu.VMEM((nx, tall, nz), F32)] * 3,
        cost=6_000_000,
    )(potential_cot, w0, inv, slab, *along_y)
    ends0, ends1, ends2, slabs, sums, where = call(
        functools.partial(outer_kernel, n_y, float(n_gx * voltage.shape[1])),
        (edges,) * 3 + (shape_of(3, tall, 2 * nz), shape_of(SUB, nz), shape_of(SUB, nz)),
        12 + 2 * n_y,
        scratch=[
            pltpu.VMEM((4, tall, nz), F32), pltpu.VMEM((1, tall, 2 * nz), F32),
            pltpu.VMEM((2, tall, nz), F32), pltpu.VMEM((2, tall, nz), F32), pltpu.VMEM((4, tall, nz), F32),
        ],
    )(plan, potential_cot, in0, in_inv, in1, in2, own_slab, in_sums, passed, stat, *along_x, *across)

    if n_gx > 4:
        counts = lax.all_gather(jnp.sum(stat[1, 0]), "gx")
        begin = jnp.sum(jnp.where(jnp.arange(n_gx) < lax.axis_index("gx"), counts, 0.0))
        where = where.at[0].set(begin)

    def couple(stage, after, inside, ends):
        return call(
            functools.partial(couple_kernel, stage, slot_rows),
            shape_of(n_gx * block_rows, LANES),
            7,
            scratch=[
                pltpu.VMEM((rows, LANES), F32), pltpu.VMEM((n_gx * block_rows + slot_rows + SUB, LANES), F32),
            ],
            cost=6_000_000,
        )(after, where, inside, ends, slabs, plan, lanes)

    def add(value, axis, step, after):
        got = lax.ppermute(value, axis, [(i, i ^ step) for i in range(lax.axis_size(axis))])
        return call(add_kernel, shape_of(SUB, nz), 3)(value, got, after)

    list0 = couple(0, sums, in0, ends0)
    sums = add(sums, "gz", 1, list0)
    list1 = couple(1, sums, in1, ends1)
    list2 = couple(2, list1, in2, ends2)
    for step in [2**k for k in range(n_gy.bit_length() - 1)]:
        sums = add(sums, "gy", step, list2)
    if n_gx == 4 and 2 * slot_rows == 5 * block_rows:
        own, ahead, middle, back, rest = call(
            pack_round_kernel,
            (shape_of(3 * block_rows + SUB, LANES),) * 3
            + (shape_of(3 * block_rows // 2 + SUB, LANES), shape_of(3 * block_rows // 2, LANES)),
            4,
        )(sums, list0, list1, list2)
        arrived = [
            own,
            swap(ahead, x_to=ROUND),
            swap(middle, x_to=partners("gx", 1)),
            swap(back, x_to=BACK),
            swap(rest, x_to=partners("gx", 0)),
        ]
        other = swap(sums, x_to=[3, 1, 2, 0])
        land = land_round
    else:
        blocks = call(pack_kernel, (shape_of(3 * block_rows + SUB, LANES),) * n_gx, 4)(sums, list0, list1, list2)
        apart = {k: never_meet(n_gx, k, slot_rows, block_rows) for k in range(1, n_gx)}
        few = [k for k in apart if any(apart[k])]
        many = [k for k in [2, 3, 1] + list(range(4, n_gx)) if k < n_gx and not all(apart[k])]
        arrived = [blocks[0]]
        arrived += [swap(sums, x_to=[i ^ k if apart[k][i] else i for i in range(n_gx)]) for k in few]
        arrived += [swap(blocks[k], x_to=[i if apart[k][i] else i ^ k for i in range(n_gx)]) for k in many]
        land = functools.partial(land_pairs, [[apart[k] for k in few], [apart[k] for k in many]])

    base, total_change, factor, state_coefs = call(
        membrane_kernel,
        (
            shape_of(n_states, block_rows, LANES), shape_of(block_rows, LANES), shape_of(block_rows, LANES),
            shape_of(2, n_states, LANES),
        ),
        9,
        specs=[SMEM] * 5 + [VMEM] * 4,
        cost=6_000_000,
    )(
        half_voltage, gate_slope, tau_base, conductance, reversal,
        arrived[0], cells(voltage), states(gates), states(gates_cot),
    )
    if land is land_round:
        arrived.append(call(edge_kernel, shape_of(SUB, nz), 3, cost=EDGE_COST)(sums, other, factor))
    solution, volt_grad, gate_grad = call(
        functools.partial(finish_kernel, land),
        (block, shape_of(block_rows, LANES), shape_of(n_states, block_rows, LANES)),
        11 + len(arrived),
    )(
        state_coefs, cells(voltage_cot), cells(voltage), total_change, factor, base,
        in0, in1, in2, ends1, ends2, *arrived,
    )
    return solution, volt_grad.reshape(voltage.shape), gate_grad.reshape(gates.shape)


def solution(mesh):
    grid = P(("groups", "gx"), "gy", "gz")
    cells = P(("groups", "gy", "gz"), "gx")
    states = P(None, ("groups", "gy", "gz"), "gx")
    in_specs = (
        grid, grid, grid, P(("groups", "gx"), "gy", "gz", None), cells, states, cells, states,
        P(), P(), P(), P(), P(),
    )
    return jax.shard_map(
        local, mesh=mesh, in_specs=in_specs, out_specs=(grid, cells, states), check_vma=False
    )
```

```python
import functools

import jax
import jax.numpy as jnp
from jax import lax
from jax.experimental import pallas as pl
from jax.experimental.pallas import tpu as pltpu
from jax.sharding import PartitionSpec as P

TIME_STEP = 0.5
LANES = 128
SUB = 8
PACK = 8
EDGE_COST = 500_000_000
COUNT_LANE = 4 * PACK
F32 = jnp.float32

VMEM = pl.BlockSpec(memory_space=pltpu.VMEM)
SMEM = pl.BlockSpec(memory_space=pltpu.SMEM)


def shape_of(*dims):
    return jax.ShapeDtypeStruct(dims, F32)


def call(kernel, out_shape, n_in, specs=None, outs=None, scratch=(), cost=2_000_000, limit=32):
    return pl.pallas_call(
        kernel,
        out_shape=out_shape,
        in_specs=specs if specs is not None else [VMEM] * n_in,
        out_specs=outs if outs is not None else jax.tree.map(lambda _: VMEM, out_shape),
        scratch_shapes=list(scratch),
        compiler_params=pltpu.CompilerParams(vmem_limit_bytes=limit * 1024 * 1024),
        cost_estimate=pl.CostEstimate(flops=cost, bytes_accessed=cost, transcendentals=0),
    )


def in_hbm(array):
    return pltpu.with_memory_space_constraint(array, pltpu.HBM)


def lanes_of(shape):
    return lax.broadcasted_iota(jnp.int32, shape, len(shape) - 1)


def subs_of(shape):
    return lax.broadcasted_iota(jnp.int32, shape, len(shape) - 2)


def start_kernel(right_ref, damping_ref, label_ref, w0_ref, inv_ref, pack_ref, stat_ref):
    nx, ny, nz = right_ref.shape
    gz = lax.axis_index("gz")
    lane = lanes_of((ny, nz))
    packed_w = jnp.zeros((ny, nz), F32)
    packed_i = jnp.zeros((ny, nz), F32)
    energy = jnp.zeros((ny, nz), F32)
    cells = jnp.zeros((ny, nz), F32)
    for x in range(nx):
        label = label_ref[x].astype(F32)
        right = right_ref[x]
        inv = 1.0 / (12.0 + damping_ref[x] * (1.0 + 3.0 * label))
        w0 = right * inv
        w0_ref[x] = w0
        inv_ref[x] = inv
        energy = energy + right * w0
        cells = cells + label
        turn = (PACK * x + 3) % nz
        begin = PACK * x + 3 * gz
        chosen = (lane >= begin) & (lane < begin + 3)
        packed_w = jnp.where(chosen, pltpu.roll(w0, turn, 1), packed_w)
        packed_i = jnp.where(chosen, pltpu.roll(inv, turn, 1), packed_i)
    pack_ref[0] = packed_w
    pack_ref[1] = packed_i
    stat_ref[0] = jnp.broadcast_to(jnp.sum(energy, axis=0, keepdims=True), (SUB, nz))
    stat_ref[1] = jnp.broadcast_to(jnp.sum(cells, axis=0, keepdims=True), (SUB, nz))


def steps_of(axis):
    return 1 if lax.axis_size(axis) == 2 else 2


def upper_in(axis, step):
    return lax.rem(lax.axis_index(axis), 2) == step


def has_partner(axis, step):
    here = lax.axis_index(axis)
    return jnp.where(upper_in(axis, step), here < lax.axis_size(axis) - 1, here > 0)


def unpack_rows(tile, step):
    sub = subs_of(tile.shape)
    up, there = upper_in("gy", step), has_partner("gy", step)
    depth = jnp.where(there, jnp.where(up, SUB - 1 - sub, sub), -1)
    return jnp.where(depth >= 5, tile, 0.0), jnp.where(depth >= 6, pltpu.roll(tile, 4, 0), 0.0)


def halo_rows(tiles):
    w_tile, i_tile = unpack_rows(tiles[0], 0)
    for step, tile in enumerate(tiles[1:], 1):
        w_more, i_more = unpack_rows(tile, step)
        w_tile, i_tile = w_tile + w_more, i_tile + i_more
    return w_tile, i_tile


def faces_kernel(n_y, w0_ref, inv_ref, own_ref, got_ref, stat_ref, slab_ref, *refs):
    y_refs, x_refs, edge_refs = refs[:n_y], refs[n_y : n_y + 2], refs[n_y + 2 :]
    nx, ny, nz = w0_ref.shape
    sub = subs_of((SUB, nz))
    lane = lanes_of((ny, nz))
    slab_ref[...] = own_ref[...] + got_ref[...]
    for step, face_ref in enumerate(y_refs):
        up = upper_in("gy", step)
        keep_w = jnp.where(up, sub, SUB - 1 - sub) >= 5
        for x in range(nx + 1):
            w_rows, i_rows = (w0_ref.at[x], inv_ref.at[x]) if x < nx else (slab_ref.at[0], slab_ref.at[1])
            w_face = jnp.where(up, w_rows[ny - SUB :], w_rows[:SUB])
            i_face = jnp.where(up, i_rows[ny - SUB :], i_rows[:SUB])
            face_ref[x] = jnp.where(keep_w, w_face, pltpu.roll(i_face, 4, 0))
    cells = jnp.sum(stat_ref[1, 0:1], axis=1, keepdims=True)
    slab_w = slab_ref[0]
    half = pltpu.roll(slab_ref[1], nz // 2, 1)
    up_slab = jnp.where(lane >= nz - 3 * PACK, slab_w, half)
    down_slab = jnp.where(lane < 3 * PACK, slab_w, half)
    for step, face_ref in enumerate(x_refs):
        up = upper_in("gx", step)
        first = jnp.where(up, nx - 3, 0)
        for k in range(3):
            face_ref[k] = w0_ref[first + k]
        for k in range(2):
            face_ref[3 + k] = inv_ref[jnp.where(up, nx - 2, 0) + k]
        face_ref[5] = jnp.where(lane == COUNT_LANE, cells, jnp.where(up, up_slab, down_slab))
        for y_step, y_ref in enumerate(y_refs):
            edge_ref = edge_refs[step * n_y + y_step]
            for k in range(3):
                edge_ref[k] = y_ref[first + k]
            edge_ref[3] = y_ref[nx]


SUMS = (("w0 k0", "w1 k0"), ("w1 n1", "w1 k1", "w2 k1", "w0 n1"), ("w2 k2",))
ORDER = ("w0 r", "w0 k0", "w1 k0", "w1 n1", "w1 k1", "w2 k1", "w2 k2", "w0 n1")


def slab_step(stage, v, s, inv):
    width = v.shape[1]
    across = pltpu.roll(v, PACK, 1) + pltpu.roll(v, width - PACK, 1)
    q = v + 0.5 * (s + across)
    if stage == 2:
        return q, None
    total = (
        pltpu.roll(q, 1, 1) + pltpu.roll(q, width - 1, 1) + s + across
        + 0.5 * (pltpu.roll(s, PACK, 1) + pltpu.roll(s, width - PACK, 1))
    )
    return q, next_vector(stage, v, total, inv)


def next_vector(stage, v, total, inv):
    return v - total * inv if stage == 0 else total * inv


def along_z(q, half, column, gz):
    nz = q.shape[1]
    lane = lanes_of(q.shape)
    entry = (nz - 1) * (1 - gz)
    turn = lax.rem(entry - (column + 3 - gz) + 2 * nz, nz)
    up = jnp.where(lane == nz - 1, 0.0, pltpu.roll(q, nz - 1, 1))
    down = jnp.where(lane == 0, 0.0, pltpu.roll(q, 1, 1))
    return up + down + jnp.where(lane == entry, pltpu.roll(half, turn, 1), 0.0)


def sweep(stage, spans, nx, ny, nz, gz, get, get_inv, put, slab_q, sums, get_right, get_w0, held):
    margin = 2 - stage
    start = SUB - margin
    tiles = ny // SUB + (margin > 0)
    own = subs_of((SUB, nz)) >= margin
    names = SUMS[stage]
    parts = {name: [] for name in names}
    for tile in range(tiles):
        row = start + SUB * tile
        q_rows = slab_q[SUB * tile : SUB * tile + SUB]
        acc = {name: jnp.zeros((SUB, nz), F32) for name in names}

        def beside(x):
            return get(x, row - 1) + get(x, row + 1)

        def rows(name, x):
            ref, at = held[name, x]
            return ref.at[at, row : row + SUB]

        for first, last in spans:
            s_low, s_mid = beside(first - 1), beside(first)
            v_low, v_mid = get(first - 1, row), get(first, row)
            for x in range(first, last):
                v_high, s_high = get(x + 1, row), beside(x + 1)
                across = v_low + v_high
                column = (PACK * x) % (2 * nz)
                half = q_rows[:, column // nz * nz : column // nz * nz + nz]
                rest = s_mid + across
                total = along_z(v_mid + 0.5 * rest, half, column % nz, gz) + rest + 0.5 * (s_low + s_high)
                if stage < 2:
                    after = next_vector(stage, v_mid, total, get_inv(x, row))
                    put(x, row, after)
                if 0 <= x < nx:
                    if stage == 0:
                        k0 = get_right(x, row) - total
                        rows("k0", x)[...] = k0
                        terms = (v_mid * k0, after * k0)
                    elif stage == 1:
                        rows("n1", x)[...] = total
                        k1 = rows("k0", x)[...] - total
                        terms = (v_mid * total, v_mid * k1, after * k1, get_w0(x, row) * total)
                    else:
                        terms = (v_mid * (rows("n1", x)[...] - total),)
                    for name, term in zip(names, terms):
                        acc[name] = acc[name] + term
                v_low, v_mid, s_low, s_mid = v_mid, v_high, s_mid, s_high
        for name in names:
            parts[name].append(acc[name])
    for name in names:
        part = parts[name]
        total = part[1]
        for other in part[2 : ny // SUB]:
            total = total + other
        sums[name] = total + (jnp.where(own, part[0], part[-1]) if margin else part[0])


def inner_kernel(n_y, right_ref, w0_ref, inv_ref, slab_ref, *refs):
    y_refs, refs = refs[:n_y], refs[n_y:]
    a_ref, i_ref, b_ref, c_ref, sum_ref, own_slab_ref, pass_ref, slabs_ref, r_ref, k_ref, n_ref = refs
    nx, ny, nz = w0_ref.shape
    gz = lax.axis_index("gz")
    for x in range(nx + 1):
        halos = halo_rows([ref[x] for ref in y_refs])
        for k in range(2):
            if x < nx:
                ref, own = (a_ref, i_ref)[k].at[x], (w0_ref, inv_ref)[k][x]
            else:
                ref, own = own_slab_ref.at[k], slab_ref[k]
            ref[:SUB] = halos[k]
            ref[SUB : SUB + ny] = own
            ref[SUB + ny :] = halos[k]
    for k in range(2):
        slabs_ref[3 * k] = own_slab_ref[k]
    for x in range(nx):
        r_ref[x, SUB : SUB + ny] = right_ref[x]
    held = {("k0", x): (k_ref, x) for x in range(nx)} | {("n1", x): (n_ref, x) for x in range(nx)}
    held |= {("k0", 1): (pass_ref, 0), ("k0", nx - 2): (pass_ref, 1)}
    held |= {("n1", 2): (pass_ref, 2), ("n1", nx - 3): (pass_ref, 3)}
    sums = {}
    for stage in range(3):
        source, target = (a_ref, b_ref, c_ref)[stage], (b_ref, c_ref, None)[stage]
        start, size = SUB - 2 + stage, ny if stage == 2 else ny + SUB
        v = slabs_ref[stage, start : start + size]
        s = slabs_ref[stage, start - 1 : start - 1 + size] + slabs_ref[stage, start + 1 : start + 1 + size]
        q, after = slab_step(stage, v, s, slabs_ref[3, start : start + size])
        if stage < 2:
            slabs_ref[stage + 1, start : start + size] = after

        def put(x, row, value):
            target[x, row : row + SUB] = value

        sweep(
            stage, [(1 + stage, nx - 1 - stage)], nx, ny, nz, gz,
            lambda x, row: source[x, row : row + SUB], lambda x, row: i_ref[x, row : row + SUB],
            put, q, sums,
            lambda x, row: r_ref[x, row : row + SUB], lambda x, row: a_ref[x, row : row + SUB], held,
        )
    for k, name in enumerate(ORDER[1:]):
        sum_ref[k] = sums[name]


def outer_kernel(
    n_y, column_total, after_ref, right_ref, a_ref, i_ref, b_ref, c_ref, slab_ref, sum_ref, pass_ref, stat_ref, *refs
):
    x_refs, corner_refs = refs[:2], refs[2 : 2 + 2 * n_y]
    ea_ref, eb_ref, ec_ref, slabs_ref, total_ref, where_ref, ei_ref, si_ref, r_ref, k_ref, n_ref = refs[2 + 2 * n_y :]
    nx, ny, nz = a_ref.shape[0], a_ref.shape[1] - 2 * SUB, a_ref.shape[2]
    ring = ny + SUB
    gz = lax.axis_index("gz")
    odd = lax.rem(lax.axis_index("gx"), 2) == 1

    def beyond(upper, read):
        there = has_partner("gx", 0) if upper else has_partner("gx", 1)
        swapped = has_partner("gx", 1) if upper else has_partner("gx", 0)
        first, second = read(0), read(1)
        if upper:
            return jnp.where(jnp.where(odd, swapped, there), jnp.where(odd, second, first), 0.0)
        return jnp.where(jnp.where(odd, swapped, there), jnp.where(odd, first, second), 0.0)

    def write(ref, at, own, halo):
        ref[at, :SUB] = halo
        ref[at, SUB : SUB + ny] = own
        ref[at, SUB + ny :] = halo

    lane_tile, lane = lanes_of((SUB, nz)), lanes_of((ny, nz))
    slab_parts = []
    for side, upper in enumerate((False, True)):
        tiles = [
            halo_rows([beyond(upper, lambda step: corner_refs[step * n_y + j][k]) for j in range(n_y)])
            for k in range(4)
        ]
        for k in range(3):
            write(ea_ref, 3 * side + k, beyond(upper, lambda step: x_refs[step][k]), tiles[k][0])
        for k in range(2):
            own = beyond(upper, lambda step: x_refs[step][3 + k])
            write(ei_ref, 2 * side + k, own, tiles[k if upper else k + 1][1])
        own = beyond(upper, lambda step: x_refs[step][5])

        def near(value, lanes, planes):
            return jnp.where(lanes < planes * PACK if upper else lanes >= nz - planes * PACK, value, 0.0)

        slab_parts.append((
            near(own, lane, 3), near(tiles[3][0], lane_tile, 3),
            near(pltpu.roll(own, nz // 2, 1), lane, 2), near(tiles[3][1], lane_tile, 2),
            own[0:1, COUNT_LANE : COUNT_LANE + 1],
        ))

    low, high = slab_parts
    for ref, k in ((slabs_ref, 0), (si_ref, 1)):
        ref[0, :, :nz] = slab_ref[k]
        ref[0, SUB : SUB + ny, nz:] = low[2 * k] + high[2 * k]
        ref[0, :SUB, nz:] = low[2 * k + 1] + high[2 * k + 1]
        ref[0, SUB + ny :, nz:] = low[2 * k + 1] + high[2 * k + 1]

    def reader(inside_ref, edge_ref, first, count):
        def get(x, row):
            if first <= x < nx - first:
                return inside_ref[x, row : row + SUB]
            at = x - (first - count) if x < first else x - (nx - first) + count
            return edge_ref[at, row : row + SUB]

        return get

    r_ref[0, SUB : SUB + ny] = right_ref[0]
    r_ref[1, SUB : SUB + ny] = right_ref[nx - 1]
    held = {("k0", 0): (k_ref, 0), ("k0", nx - 1): (k_ref, 1), ("k0", 1): (pass_ref, 0), ("k0", nx - 2): (pass_ref, 1)}
    for at, x in enumerate((0, 1, nx - 2, nx - 1)):
        held["n1", x] = (n_ref, at)
    held |= {("n1", 2): (pass_ref, 2), ("n1", nx - 3): (pass_ref, 3)}
    sums = {}
    for stage in range(3):
        get = reader((a_ref, b_ref, c_ref)[stage], (ea_ref, eb_ref, ec_ref)[stage], stage, 3)
        start, size = SUB - 2 + stage, ny if stage == 2 else ring
        v = slabs_ref[stage, start : start + size]
        s = slabs_ref[stage, start - 1 : start - 1 + size] + slabs_ref[stage, start + 1 : start + 1 + size]
        q, after = slab_step(stage, v, s, si_ref[0, start : start + size])
        if stage < 2:
            slabs_ref[stage + 1, start : start + size] = after

        def put(x, row, value):
            edge_ref = (eb_ref, ec_ref)[stage]
            at = x - (stage - 2) if x < nx // 2 else x - (nx - 1 - stage) + 3
            edge_ref[at, row : row + SUB] = value

        sweep(
            stage, [(stage - 2, stage + 1), (nx - 1 - stage, nx + 2 - stage)], nx, ny, nz, gz,
            get, reader(i_ref, ei_ref, 0, 2), put, q, sums,
            lambda x, row: r_ref[0 if x == 0 else 1, row : row + SUB],
            lambda x, row: a_ref[x, row : row + SUB], held,
        )

    total_ref[0:1] = stat_ref[0, 0:1]
    for k, name in enumerate(ORDER[1:]):
        total_ref[k + 1 : k + 2] = jnp.sum(sums[name] + sum_ref[k], axis=0, keepdims=True)
    gx, n_x = lax.axis_index("gx"), lax.axis_size("gx")
    count = jnp.sum(stat_ref[1, 0:1], axis=1, keepdims=True)
    below, above = [part[4] for part in slab_parts]
    begin = jnp.where(
        gx == 0, 0.0,
        jnp.where(gx == 1, below, jnp.where(gx == n_x - 1, column_total - count, column_total - count - above)),
    )
    where_ref[0:1] = jnp.broadcast_to(begin, (1, nz))
    where_ref[1:2] = jnp.broadcast_to(count, (1, nz))
    where_ref[2:8] = jnp.zeros((6, nz), F32)


def shift_up(v, amount):
    if amount < SUB:
        return pltpu.roll(v, v.shape[0] - amount, 0)
    return jnp.concatenate([v[amount:], v[:amount]], axis=0)


def plan_kernel(after_ref, label_ref, index_ref, plan_ref, lane_ref):
    rows, slot_rows = label_ref.shape[0], index_ref.shape[0]
    wide = -(-(slot_rows + 1) // LANES) * LANES
    shape = (rows, LANES)
    lane, row = lanes_of(shape), subs_of(shape)
    ones = (label_ref[...] == 1).astype(jnp.bfloat16)
    totals = jnp.dot(ones, jnp.ones((LANES, LANES), jnp.bfloat16), preferred_element_type=F32)
    lower = (subs_of((rows, rows)) > lanes_of((rows, rows))).astype(jnp.bfloat16)
    before = jnp.dot(lower, totals.astype(jnp.bfloat16), preferred_element_type=F32).astype(jnp.int32)
    target, first = lax.div(before, LANES), lax.rem(before, LANES)
    listed = jnp.concatenate(
        [lax.rem(index_ref[...], LANES).astype(F32), jnp.zeros((wide - slot_rows, LANES), F32)], axis=0
    ).astype(jnp.bfloat16)
    spread = jnp.concatenate([target] * (wide // LANES), axis=1)
    place = lanes_of((rows, wide))
    here = jnp.dot((spread == place).astype(jnp.bfloat16), listed, preferred_element_type=F32)
    after = jnp.dot((spread + 1 == place).astype(jnp.bfloat16), listed, preferred_element_type=F32)
    lane_ref[...] = jnp.where(lane >= first, here, after).astype(jnp.int32)
    wrapped = (lane < first).astype(jnp.int32)
    filled = lane - first + LANES * wrapped < totals.astype(jnp.int32)
    way = jnp.where(filled, row - target - wrapped, 0)
    plan = jnp.zeros(shape, jnp.int32)
    step = 1
    while step < rows:
        moving = jnp.where((way & step) != 0, way, 0)
        arriving = shift_up(moving, step)
        plan = plan | (arriving & step)
        way = (way - moving) | arriving
        step *= 2
    plan_ref[...] = plan


def galerkin(total):
    def add_up(*rows):
        return [jnp.broadcast_to(jnp.sum(row, axis=1, keepdims=True), row.shape) for row in rows]

    row = {name: total[k : k + 1] for k, name in enumerate(ORDER)}
    b0, b2 = row["w0 r"], row["w0 n1"]
    g00, g01, g02 = row["w0 k0"], row["w1 k0"], row["w1 n1"]
    g11, g12, g22 = row["w1 k1"], row["w2 k1"], row["w2 k2"]
    s00, s01, s02, s0, s11, s22 = add_up(g00, g01, g02, b0, g11, g22)
    l10, l20 = s01 / s00, s02 / s00
    h11 = g11 - l10 * (2.0 * g01 - l10 * g00)
    h12 = g12 - l10 * g02 - l20 * (g01 - l10 * g00)
    h22 = g22 - l20 * (2.0 * g02 - l20 * g00)
    y1, y2 = g00 - l10 * b0, b2 - l20 * b0
    d1, s12, s1 = add_up(h11, h12, y1)
    ok1 = d1 > 1e-7 * s11
    d1 = jnp.where(ok1, d1, 1.0)
    l21 = jnp.where(ok1, s12 / d1, 0.0)
    d2, s2 = add_up(h22 - l21 * (2.0 * h12 - l21 * h11), y2 - l21 * y1)
    ok2 = ok1 & (d2 > 1e-7 * s22)
    c2 = jnp.where(ok2, s2 / jnp.where(ok2, d2, 1.0), 0.0)
    c1 = jnp.where(ok1, s1 / d1 - l21 * c2, 0.0)
    c0 = s0 / s00 - l10 * c1 - l20 * c2
    return c0, c1, c2


def couple_kernel(
    stage, slot_rows, after_ref, where_ref, inside_ref, edge_ref, slabs_ref, plan_ref, lane_ref, blocks_ref,
    value_ref, buf_ref,
):
    nx, nz = inside_ref.shape[0], inside_ref.shape[2]
    ny = inside_ref.shape[1] - 2 * SUB
    rows = nx * ny
    gz = lax.axis_index("gz")

    def get(x, row):
        if stage <= x < nx - stage:
            return inside_ref[x, row : row + SUB]
        return edge_ref[x - (stage - 3) if x < stage else x - (nx - stage) + 3, row : row + SUB]

    for tile in range(ny // SUB):
        row = SUB + SUB * tile
        slab = slabs_ref[stage, row : row + SUB, :nz]
        v_low, v_mid = get(-1, row), get(0, row)
        for x in range(nx):
            v_high = get(x + 1, row)
            beside = get(x, row - 1) + get(x, row + 1)
            at = ny * x + SUB * tile
            value_ref[at : at + SUB] = (
                along_z(v_mid, slab, PACK * x, gz) + beside + (v_low + v_high) - 6.0 * v_mid
            )
            v_low, v_mid = v_mid, v_high
    value = jnp.take_along_axis(value_ref[...], lane_ref[...], axis=1)
    plan = plan_ref[...]
    step = 1
    while step < rows:
        value = jnp.where((plan & step) != 0, shift_up(value, step), value)
        step *= 2
    offset = jnp.max(where_ref[0:1]).astype(jnp.int32)
    count = jnp.max(where_ref[1:2]).astype(jnp.int32)
    shape = (slot_rows, LANES)
    slots = jnp.where(subs_of(shape) * LANES + lanes_of(shape) < count, value[:slot_rows], 0.0)
    slots = jnp.concatenate([slots, jnp.zeros((SUB, LANES), F32)], axis=0)
    inner = lax.rem(offset, LANES)
    turned = pltpu.roll(slots, inner, 1)
    moved = jnp.where(lanes_of((slot_rows + SUB, LANES)) >= inner, turned, pltpu.roll(turned, 1, 0))
    buf_ref[...] = jnp.zeros_like(buf_ref)
    buf_ref[pl.ds(offset // LANES, slot_rows + SUB), :] = moved
    gx = lax.axis_index("gx")
    n_gx = lax.axis_size("gx")
    size = blocks_ref.shape[0] // n_gx
    for block in range(n_gx):
        begin = pl.multiple_of((gx ^ block) * size, SUB)
        blocks_ref[block * size : block * size + size] = buf_ref[pl.ds(begin, size), :]


def add_kernel(a_ref, b_ref, after_ref, out_ref):
    out_ref[...] = a_ref[...] + b_ref[...]


def pack_kernel(total_ref, *refs):
    list_refs, out_refs = refs[:3], refs[3:]
    size = (out_refs[0].shape[0] - SUB) // 3
    for block, out_ref in enumerate(out_refs):
        for k, list_ref in enumerate(list_refs):
            out_ref[k * size : k * size + size] = list_ref[block * size : block * size + size]
        out_ref[3 * size :] = total_ref[...]


ROUND = (1, 3, 0, 2)
BACK = (2, 0, 3, 1)


def pack_round_kernel(total_ref, *refs):
    list_refs, (own_ref, round_ref, middle_ref, back_ref, rest_ref) = refs[:3], refs[3:]
    size = (own_ref.shape[0] - SUB) // 3
    half = size // 2
    gx = lax.axis_index("gx")
    inside = (gx == 1) | (gx == 2)
    ahead, behind = jnp.where(inside, 2, 1), jnp.where(inside, 1, 2)
    upper = jnp.where(gx >= 2, half, 0)
    for k, list_ref in enumerate(list_refs):
        for out_ref, begin, rows in (
            (own_ref, 0, size), (round_ref, ahead * size, size), (middle_ref, 3 * size, size),
            (back_ref, behind * size + upper, half), (rest_ref, behind * size + (half - upper), half),
        ):
            if not isinstance(begin, int):
                begin = pl.multiple_of(begin, SUB)
            out_ref[k * rows : k * rows + rows] = list_ref[pl.ds(begin, rows), :]
    for out_ref in (own_ref, round_ref, middle_ref, back_ref):
        out_ref[out_ref.shape[0] - SUB :] = total_ref[...]


def edge_kernel(total_ref, other_ref, after_ref, out_ref):
    gx = lax.axis_index("gx")
    out_ref[...] = total_ref[...] + jnp.where((gx == 1) | (gx == 2), 0.0, other_ref[...])


def land_round(own_ref, round_ref, middle_ref, back_ref, rest_ref, edge_ref):
    size = (own_ref.shape[0] - SUB) // 3
    half = size // 2
    gx = lax.axis_index("gx")
    inside = (gx == 1) | (gx == 2)
    last = lambda ref: ref[ref.shape[0] - SUB :]
    total = edge_ref[...] + last(round_ref) + last(back_ref) + jnp.where(inside, last(middle_ref), 0.0)
    parts = []
    for k in range(3):
        whole = slice(k * size, k * size + size)
        back, rest = [ref[k * half : k * half + half] for ref in (back_ref, rest_ref)]
        odd = lax.rem(gx, 2) == 1
        low = jnp.where(odd, jnp.where(gx == 3, rest, 0.0), back)
        high = jnp.where(odd, back, jnp.where(gx == 0, rest, 0.0))
        part = own_ref[whole] + round_ref[whole] + jnp.where(inside, middle_ref[whole], 0.0)
        parts.append(part + jnp.concatenate([low, high], axis=0))
    return total, parts


def land_pairs(alone, own_ref, *refs):
    small_refs, large_refs = refs[: len(alone[0])], refs[len(alone[0]) :]
    size = (own_ref.shape[0] - SUB) // 3
    gx = lax.axis_index("gx")

    def is_one(flags):
        found = gx < 0
        for place, flag in enumerate(flags):
            if flag:
                found = found | (gx == place)
        return found

    total = own_ref[3 * size :]
    for flags, ref in zip(alone[0], small_refs):
        total = total + jnp.where(is_one(flags), ref[...], 0.0)
    for flags, ref in zip(alone[1], large_refs):
        total = total + jnp.where(is_one(flags), 0.0, ref[3 * size :])
    parts = []
    for k in range(3):
        part = own_ref[k * size : k * size + size]
        for ref in large_refs:
            part = part + ref[k * size : k * size + size]
        parts.append(part)
    return total, parts


def membrane_kernel(
    half_ref, slope_ref, tau_ref, cond_ref, rev_ref, after_ref, vcot_ref, v_ref, gates_ref, cot_ref,
    base_ref, sum_ref, factor_ref, coef_ref, kept_ref,
):
    n_states, rows = gates_ref.shape[:2]
    v = v_ref[...]

    def state(g, carry):
        total, current = carry
        inv_slope = 1.0 / slope_ref[g]
        tau_base = tau_ref[g]
        scaled = (v - half_ref[g]) * inv_slope
        gate = gates_ref[g]
        cot = cot_ref[g]
        steady = 1.0 / (1.0 + jnp.exp(-scaled))
        bell = jnp.exp(-scaled * scaled)
        rate = TIME_STEP / (tau_base * (0.5 + bell))
        decay = jnp.exp(-rate)
        steady_slope = steady * (1.0 - steady)
        decay_slope = decay * rate * rate * ((tau_base / TIME_STEP) * bell * (-2.0 * scaled))
        change = (steady_slope * (1.0 - decay) + (gate - steady) * decay_slope) * inv_slope
        base_ref[g] = cot * decay
        coef_ref[0, pl.ds(g, 1)] = jnp.full((1, LANES), TIME_STEP * cond_ref[g])
        coef_ref[1, pl.ds(g, 1)] = jnp.full((1, LANES), rev_ref[g])
        return total + cot * change, current + cond_ref[g] * gate

    zero = jnp.zeros((rows, LANES), F32)
    total, current = lax.fori_loop(0, n_states, state, (zero, zero), unroll=2)
    sum_ref[...] = total
    factor_ref[...] = 1.0 - TIME_STEP * current
    kept_ref[...] = vcot_ref[...]


def finish_kernel(
    land, coef_ref, vcot_ref, v_ref, sum_ref, factor_ref, base_ref, a_ref, b_ref, c_ref, eb_ref, ec_ref, *refs
):
    x_ref, volt_ref, gate_ref = refs[-3:]
    total, parts = land(*refs[:-3])
    c0, c1, c2 = galerkin(total)
    landed = c0 * parts[0] + c1 * parts[1] + c2 * parts[2]
    cot = vcot_ref[...] + landed
    v = v_ref[...]
    volt_ref[...] = cot * factor_ref[...] + sum_ref[...]
    for g in range(base_ref.shape[0]):
        gate_ref[g] = base_ref[g] - (coef_ref[0, g : g + 1] * cot) * (v - coef_ref[1, g : g + 1])
    nx, ny, nz = x_ref.shape
    own = slice(SUB, SUB + ny)
    for x in range(nx):
        w1 = b_ref[x, own] if 1 <= x < nx - 1 else eb_ref[2 if x == 0 else 3, own]
        w2 = c_ref[x, own] if 2 <= x < nx - 2 else ec_ref[x + 1 if x < 2 else x - (nx - 2) + 3, own]
        x_ref[x] = c0 * a_ref[x, own] + c1 * w1 + c2 * w2


def partners(axis, step):
    count = lax.axis_size(axis)
    if step == 0:
        return [i ^ 1 for i in range(count)]
    return [0] + [i + 1 if i % 2 else i - 1 for i in range(1, count - 1)] + [count - 1]


def swap(value, x_to=None, y_to=None):
    n_x, n_y, n_z = [lax.axis_size(axis) for axis in ("gx", "gy", "gz")]
    pairs = []
    for x in range(n_x):
        for y in range(n_y):
            to_x, to_y = x_to[x] if x_to else x, y_to[y] if y_to else y
            alone = (x_to and to_x == x) or (y_to and to_y == y)
            for z in range(n_z):
                to = (x, y, z ^ 1) if alone else (to_x, to_y, z)
                pairs.append(((x * n_y + y) * n_z + z, (to[0] * n_y + to[1]) * n_z + to[2]))
    return lax.ppermute(value, ("gx", "gy", "gz"), pairs)


def never_meet(count, k, slots, block):
    def apart(tile, owner):
        return owner * block >= (tile + 1) * slots or (owner + 1) * block <= count * block - (count - tile) * slots

    return [apart(i, i ^ k) and apart(i ^ k, i) for i in range(count)]


def local(
    potential_cot, damping, tissue_label, heart_index, voltage, gates, voltage_cot, gates_cot,
    half_voltage, gate_slope, tau_base, conductance, reversal,
):
    nx, ny, nz = potential_cot.shape
    rows = nx * ny
    ring = ny + SUB
    n_gx, n_gy = lax.axis_size("gx"), lax.axis_size("gy")
    n_states = gates.shape[0]
    block_rows = voltage.shape[1] // LANES
    slot_rows = heart_index.shape[3] // LANES
    block = shape_of(nx, ny, nz)
    flat = lambda a: a.reshape(rows, LANES)
    cells = lambda a: a.reshape(block_rows, LANES)
    states = lambda a: a.reshape(n_states, block_rows, LANES)

    w0, inv, packed, stat = call(
        start_kernel, (block, block, shape_of(2, ny, nz), shape_of(2, SUB, nz)), 3,
    )(in_hbm(potential_cot), in_hbm(damping), in_hbm(tissue_label))

    got = lax.ppermute(packed, "gz", [(0, 1), (1, 0)])
    cells_shape = jax.ShapeDtypeStruct((rows, LANES), jnp.int32)
    plan, lanes = call(plan_kernel, (cells_shape, cells_shape), 3, cost=6_000_000)(
        stat, flat(tissue_label), heart_index.reshape(slot_rows, LANES)
    )

    n_y = steps_of("gy")
    shapes = (
        (shape_of(2, ny, nz),) + (shape_of(nx + 1, SUB, nz),) * n_y + (shape_of(6, ny, nz),) * 2
        + (shape_of(4, SUB, nz),) * (2 * n_y)
    )
    slab, *faces = call(functools.partial(faces_kernel, n_y), shapes, 5)(w0, inv, packed, got, stat)
    along_y, along_x, across = faces[:n_y], faces[n_y : n_y + 2], faces[n_y + 2 :]
    y_to = [partners("gy", step) for step in range(n_y)]
    x_to = [partners("gx", step) for step in range(2)]
    along_y = [swap(face, y_to=y_to[j]) for j, face in enumerate(along_y)]
    along_x = [swap(face, x_to=x_to[i]) for i, face in enumerate(along_x)]
    across = [swap(face, x_to=x_to[k // n_y], y_to=y_to[k % n_y]) for k, face in enumerate(across)]

    tall = ring + SUB
    planes = shape_of(nx, tall, nz)
    edges = shape_of(6, tall, nz)
    in0, in_inv, in1, in2, in_sums, own_slab, passed = call(
        functools.partial(inner_kernel, n_y),
        (planes,) * 4 + (shape_of(len(ORDER) - 1, SUB, nz), shape_of(2, tall, nz), shape_of(4, tall, nz)),
        4 + n_y,
        scratch=[pltpu.VMEM((4, tall, nz), F32)] + [pltpu.VMEM((nx, tall, nz), F32)] * 3,
        cost=6_000_000,
    )(potential_cot, w0, inv, slab, *along_y)
    ends0, ends1, ends2, slabs, sums, where = call(
        functools.partial(outer_kernel, n_y, float(n_gx * voltage.shape[1])),
        (edges,) * 3 + (shape_of(3, tall, 2 * nz), shape_of(SUB, nz), shape_of(SUB, nz)),
        12 + 2 * n_y,
        scratch=[
            pltpu.VMEM((4, tall, nz), F32), pltpu.VMEM((1, tall, 2 * nz), F32),
            pltpu.VMEM((2, tall, nz), F32), pltpu.VMEM((2, tall, nz), F32), pltpu.VMEM((4, tall, nz), F32),
        ],
    )(plan, potential_cot, in0, in_inv, in1, in2, own_slab, in_sums, passed, stat, *along_x, *across)

    if n_gx > 4:
        counts = lax.all_gather(jnp.sum(stat[1, 0]), "gx")
        begin = jnp.sum(jnp.where(jnp.arange(n_gx) < lax.axis_index("gx"), counts, 0.0))
        where = where.at[0].set(begin)

    def couple(stage, after, inside, ends):
        return call(
            functools.partial(couple_kernel, stage, slot_rows),
            shape_of(n_gx * block_rows, LANES),
            7,
            scratch=[
                pltpu.VMEM((rows, LANES), F32), pltpu.VMEM((n_gx * block_rows + slot_rows + SUB, LANES), F32),
            ],
            cost=6_000_000,
        )(after, where, inside, ends, slabs, plan, lanes)

    def add(value, axis, step, after):
        got = lax.ppermute(value, axis, [(i, i ^ step) for i in range(lax.axis_size(axis))])
        return call(add_kernel, shape_of(SUB, nz), 3)(value, got, after)

    list0 = couple(0, sums, in0, ends0)
    sums = add(sums, "gz", 1, list0)
    list1 = couple(1, sums, in1, ends1)
    list2 = couple(2, list1, in2, ends2)
    for step in [2**k for k in range(n_gy.bit_length() - 1)]:
        sums = add(sums, "gy", step, list2)
    if n_gx == 4 and 2 * slot_rows == 5 * block_rows:
        own, ahead, middle, back, rest = call(
            pack_round_kernel,
            (shape_of(3 * block_rows + SUB, LANES),) * 3
            + (shape_of(3 * block_rows // 2 + SUB, LANES), shape_of(3 * block_rows // 2, LANES)),
            4,
        )(sums, list0, list1, list2)
        arrived = [
            own,
            swap(ahead, x_to=ROUND),
            swap(middle, x_to=partners("gx", 1)),
            swap(back, x_to=BACK),
            swap(rest, x_to=partners("gx", 0)),
        ]
        other = swap(sums, x_to=[3, 1, 2, 0])
        land = land_round
    else:
        blocks = call(pack_kernel, (shape_of(3 * block_rows + SUB, LANES),) * n_gx, 4)(sums, list0, list1, list2)
        apart = {k: never_meet(n_gx, k, slot_rows, block_rows) for k in range(1, n_gx)}
        few = [k for k in apart if any(apart[k])]
        many = [k for k in [2, 3, 1] + list(range(4, n_gx)) if k < n_gx and not all(apart[k])]
        arrived = [blocks[0]]
        arrived += [swap(sums, x_to=[i ^ k if apart[k][i] else i for i in range(n_gx)]) for k in few]
        arrived += [swap(blocks[k], x_to=[i if apart[k][i] else i ^ k for i in range(n_gx)]) for k in many]
        land = functools.partial(land_pairs, [[apart[k] for k in few], [apart[k] for k in many]])

    base, total_change, factor, state_coefs, vcot = call(
        membrane_kernel,
        (
            shape_of(n_states, block_rows, LANES), shape_of(block_rows, LANES), shape_of(block_rows, LANES),
            shape_of(2, n_states, LANES), shape_of(block_rows, LANES),
        ),
        10,
        specs=[SMEM] * 5 + [VMEM] * 5,
        cost=6_000_000,
    )(
        half_voltage, gate_slope, tau_base, conductance, reversal,
        arrived[0], cells(voltage_cot), cells(voltage), states(gates), states(gates_cot),
    )
    if land is land_round:
        arrived.append(call(edge_kernel, shape_of(SUB, nz), 3, cost=EDGE_COST)(sums, other, factor))
    solution, volt_grad, gate_grad = call(
        functools.partial(finish_kernel, land),
        (block, shape_of(block_rows, LANES), shape_of(n_states, block_rows, LANES)),
        11 + len(arrived),
    )(
        state_coefs, vcot, cells(voltage), total_change, factor, base,
        in0, in1, in2, ends1, ends2, *arrived,
    )
    return solution, volt_grad.reshape(voltage.shape), gate_grad.reshape(gates.shape)


def solution(mesh):
    grid = P(("groups", "gx"), "gy", "gz")
    cells = P(("groups", "gy", "gz"), "gx")
    states = P(None, ("groups", "gy", "gz"), "gx")
    in_specs = (
        grid, grid, grid, P(("groups", "gx"), "gy", "gz", None), cells, states, cells, states,
        P(), P(), P(), P(), P(),
    )
    return jax.shard_map(
        local, mesh=mesh, in_specs=in_specs, out_specs=(grid, cells, states), check_vma=False
    )
```

```python
import functools

import jax
import jax.numpy as jnp
from jax import lax
from jax.experimental import pallas as pl
from jax.experimental.pallas import tpu as pltpu
from jax.sharding import PartitionSpec as P

TIME_STEP = 0.5
LANES = 128
SUB = 8
PACK = 8
COUNT_LANE = 4 * PACK
F32 = jnp.float32

VMEM = pl.BlockSpec(memory_space=pltpu.VMEM)
SMEM = pl.BlockSpec(memory_space=pltpu.SMEM)
HBM = pl.BlockSpec(memory_space=pltpu.HBM)


def shape_of(*dims):
    return jax.ShapeDtypeStruct(dims, F32)


def call(kernel, out_shape, n_in, specs=None, outs=None, scratch=(), cost=2_000_000, limit=32):
    return pl.pallas_call(
        kernel,
        out_shape=out_shape,
        in_specs=specs if specs is not None else [VMEM] * n_in,
        out_specs=outs if outs is not None else jax.tree.map(lambda _: VMEM, out_shape),
        scratch_shapes=list(scratch),
        compiler_params=pltpu.CompilerParams(vmem_limit_bytes=limit * 1024 * 1024),
        cost_estimate=pl.CostEstimate(flops=cost, bytes_accessed=cost, transcendentals=0),
    )


def in_hbm(array):
    return pltpu.with_memory_space_constraint(array, pltpu.HBM)


def lanes_of(shape):
    return lax.broadcasted_iota(jnp.int32, shape, len(shape) - 1)


def subs_of(shape):
    return lax.broadcasted_iota(jnp.int32, shape, len(shape) - 2)


def start_kernel(right_ref, damping_ref, label_ref, w0_ref, inv_ref, pack_ref, stat_ref):
    nx, ny, nz = right_ref.shape
    gz = lax.axis_index("gz")
    lane = lanes_of((ny, nz))
    packed_w = jnp.zeros((ny, nz), F32)
    packed_i = jnp.zeros((ny, nz), F32)
    energy = jnp.zeros((ny, nz), F32)
    cells = jnp.zeros((ny, nz), F32)
    for x in range(nx):
        label = label_ref[x].astype(F32)
        right = right_ref[x]
        inv = 1.0 / (12.0 + damping_ref[x] * (1.0 + 3.0 * label))
        w0 = right * inv
        w0_ref[x] = w0
        inv_ref[x] = inv
        energy = energy + right * w0
        cells = cells + label
        turn = (PACK * x + 3) % nz
        begin = PACK * x + 3 * gz
        chosen = (lane >= begin) & (lane < begin + 3)
        packed_w = jnp.where(chosen, pltpu.roll(w0, turn, 1), packed_w)
        packed_i = jnp.where(chosen, pltpu.roll(inv, turn, 1), packed_i)
    pack_ref[0] = packed_w
    pack_ref[1] = packed_i
    stat_ref[0] = jnp.broadcast_to(jnp.sum(energy, axis=0, keepdims=True), (SUB, nz))
    stat_ref[1] = jnp.broadcast_to(jnp.sum(cells, axis=0, keepdims=True), (SUB, nz))


def steps_of(axis):
    return 1 if lax.axis_size(axis) == 2 else 2


def upper_in(axis, step):
    return lax.rem(lax.axis_index(axis), 2) == step


def has_partner(axis, step):
    here = lax.axis_index(axis)
    return jnp.where(upper_in(axis, step), here < lax.axis_size(axis) - 1, here > 0)


def unpack_rows(tile, step):
    sub = subs_of(tile.shape)
    up, there = upper_in("gy", step), has_partner("gy", step)
    depth = jnp.where(there, jnp.where(up, SUB - 1 - sub, sub), -1)
    return jnp.where(depth >= 5, tile, 0.0), jnp.where(depth >= 6, pltpu.roll(tile, 4, 0), 0.0)


def halo_rows(tiles):
    w_tile, i_tile = unpack_rows(tiles[0], 0)
    for step, tile in enumerate(tiles[1:], 1):
        w_more, i_more = unpack_rows(tile, step)
        w_tile, i_tile = w_tile + w_more, i_tile + i_more
    return w_tile, i_tile


def faces_kernel(n_y, w0_ref, inv_ref, own_ref, got_ref, stat_ref, slab_ref, *refs):
    y_refs, x_refs, edge_refs = refs[:n_y], refs[n_y : n_y + 2], refs[n_y + 2 :]
    nx, ny, nz = w0_ref.shape
    sub = subs_of((SUB, nz))
    lane = lanes_of((ny, nz))
    slab_ref[...] = own_ref[...] + got_ref[...]
    for step, face_ref in enumerate(y_refs):
        up = upper_in("gy", step)
        keep_w = jnp.where(up, sub, SUB - 1 - sub) >= 5
        for x in range(nx + 1):
            w_rows, i_rows = (w0_ref.at[x], inv_ref.at[x]) if x < nx else (slab_ref.at[0], slab_ref.at[1])
            w_face = jnp.where(up, w_rows[ny - SUB :], w_rows[:SUB])
            i_face = jnp.where(up, i_rows[ny - SUB :], i_rows[:SUB])
            face_ref[x] = jnp.where(keep_w, w_face, pltpu.roll(i_face, 4, 0))
    cells = jnp.sum(stat_ref[1, 0:1], axis=1, keepdims=True)
    slab_w = slab_ref[0]
    half = pltpu.roll(slab_ref[1], nz // 2, 1)
    up_slab = jnp.where(lane >= nz - 3 * PACK, slab_w, half)
    down_slab = jnp.where(lane < 3 * PACK, slab_w, half)
    for step, face_ref in enumerate(x_refs):
        up = upper_in("gx", step)
        first = jnp.where(up, nx - 3, 0)
        for k in range(3):
            face_ref[k] = w0_ref[first + k]
        for k in range(2):
            face_ref[3 + k] = inv_ref[jnp.where(up, nx - 2, 0) + k]
        face_ref[5] = jnp.where(lane == COUNT_LANE, cells, jnp.where(up, up_slab, down_slab))
        for y_step, y_ref in enumerate(y_refs):
            edge_ref = edge_refs[step * n_y + y_step]
            for k in range(3):
                edge_ref[k] = y_ref[first + k]
            edge_ref[3] = y_ref[nx]


SUMS = (("w0 k0", "w1 k0"), ("w1 n1", "w1 k1", "w2 k1", "w0 n1"), ("w2 k2",))
ORDER = ("w0 r", "w0 k0", "w1 k0", "w1 n1", "w1 k1", "w2 k1", "w2 k2", "w0 n1")


def slab_step(stage, v, s, inv):
    width = v.shape[1]
    across = pltpu.roll(v, PACK, 1) + pltpu.roll(v, width - PACK, 1)
    q = v + 0.5 * (s + across)
    if stage == 2:
        return q, None
    total = (
        pltpu.roll(q, 1, 1) + pltpu.roll(q, width - 1, 1) + s + across
        + 0.5 * (pltpu.roll(s, PACK, 1) + pltpu.roll(s, width - PACK, 1))
    )
    return q, next_vector(stage, v, total, inv)


def next_vector(stage, v, total, inv):
    return v - total * inv if stage == 0 else total * inv


def along_z(q, half, column, gz):
    nz = q.shape[1]
    lane = lanes_of(q.shape)
    entry = (nz - 1) * (1 - gz)
    turn = lax.rem(entry - (column + 3 - gz) + 2 * nz, nz)
    up = jnp.where(lane == nz - 1, 0.0, pltpu.roll(q, nz - 1, 1))
    down = jnp.where(lane == 0, 0.0, pltpu.roll(q, 1, 1))
    return up + down + jnp.where(lane == entry, pltpu.roll(half, turn, 1), 0.0)


def sweep(stage, spans, nx, ny, nz, gz, get, get_inv, put, slab_q, sums, get_right, get_w0, held):
    margin = 2 - stage
    start = SUB - margin
    tiles = ny // SUB + (margin > 0)
    own = subs_of((SUB, nz)) >= margin
    names = SUMS[stage]
    parts = {name: [] for name in names}
    for tile in range(tiles):
        row = start + SUB * tile
        q_rows = slab_q[SUB * tile : SUB * tile + SUB]
        acc = {name: jnp.zeros((SUB, nz), F32) for name in names}

        def beside(x):
            return get(x, row - 1) + get(x, row + 1)

        def rows(name, x):
            ref, at = held[name, x]
            return ref.at[at, row : row + SUB]

        for first, last in spans:
            s_low, s_mid = beside(first - 1), beside(first)
            v_low, v_mid = get(first - 1, row), get(first, row)
            for x in range(first, last):
                v_high, s_high = get(x + 1, row), beside(x + 1)
                across = v_low + v_high
                column = (PACK * x) % (2 * nz)
                half = q_rows[:, column // nz * nz : column // nz * nz + nz]
                rest = s_mid + across
                total = along_z(v_mid + 0.5 * rest, half, column % nz, gz) + rest + 0.5 * (s_low + s_high)
                if stage < 2:
                    after = next_vector(stage, v_mid, total, get_inv(x, row))
                    put(x, row, after)
                if 0 <= x < nx:
                    if stage == 0:
                        k0 = get_right(x, row) - total
                        rows("k0", x)[...] = k0
                        terms = (v_mid * k0, after * k0)
                    elif stage == 1:
                        rows("n1", x)[...] = total
                        k1 = rows("k0", x)[...] - total
                        terms = (v_mid * total, v_mid * k1, after * k1, get_w0(x, row) * total)
                    else:
                        terms = (v_mid * (rows("n1", x)[...] - total),)
                    for name, term in zip(names, terms):
                        acc[name] = acc[name] + term
                v_low, v_mid, s_low, s_mid = v_mid, v_high, s_mid, s_high
        for name in names:
            parts[name].append(acc[name])
    for name in names:
        part = parts[name]
        total = part[1]
        for other in part[2 : ny // SUB]:
            total = total + other
        sums[name] = total + (jnp.where(own, part[0], part[-1]) if margin else part[0])


def inner_kernel(n_y, right_ref, w0_ref, inv_ref, slab_ref, *refs):
    y_refs, refs = refs[:n_y], refs[n_y:]
    a_ref, i_ref, b_ref, c_ref, sum_ref, own_slab_ref, pass_ref, slabs_ref, r_ref, k_ref, n_ref = refs
    nx, ny, nz = w0_ref.shape
    gz = lax.axis_index("gz")
    for x in range(nx + 1):
        halos = halo_rows([ref[x] for ref in y_refs])
        for k in range(2):
            if x < nx:
                ref, own = (a_ref, i_ref)[k].at[x], (w0_ref, inv_ref)[k][x]
            else:
                ref, own = own_slab_ref.at[k], slab_ref[k]
            ref[:SUB] = halos[k]
            ref[SUB : SUB + ny] = own
            ref[SUB + ny :] = halos[k]
    for k in range(2):
        slabs_ref[3 * k] = own_slab_ref[k]
    for x in range(nx):
        r_ref[x, SUB : SUB + ny] = right_ref[x]
    held = {("k0", x): (k_ref, x) for x in range(nx)} | {("n1", x): (n_ref, x) for x in range(nx)}
    held |= {("k0", 1): (pass_ref, 0), ("k0", nx - 2): (pass_ref, 1)}
    held |= {("n1", 2): (pass_ref, 2), ("n1", nx - 3): (pass_ref, 3)}
    sums = {}
    for stage in range(3):
        source, target = (a_ref, b_ref, c_ref)[stage], (b_ref, c_ref, None)[stage]
        start, size = SUB - 2 + stage, ny if stage == 2 else ny + SUB
        v = slabs_ref[stage, start : start + size]
        s = slabs_ref[stage, start - 1 : start - 1 + size] + slabs_ref[stage, start + 1 : start + 1 + size]
        q, after = slab_step(stage, v, s, slabs_ref[3, start : start + size])
        if stage < 2:
            slabs_ref[stage + 1, start : start + size] = after

        def put(x, row, value):
            target[x, row : row + SUB] = value

        sweep(
            stage, [(1 + stage, nx - 1 - stage)], nx, ny, nz, gz,
            lambda x, row: source[x, row : row + SUB], lambda x, row: i_ref[x, row : row + SUB],
            put, q, sums,
            lambda x, row: r_ref[x, row : row + SUB], lambda x, row: a_ref[x, row : row + SUB], held,
        )
    for k, name in enumerate(ORDER[1:]):
        sum_ref[k] = sums[name]


def outer_kernel(
    n_y, column_total, after_ref, right_ref, a_ref, i_ref, b_ref, c_ref, slab_ref, sum_ref, pass_ref, stat_ref, *refs
):
    x_refs, corner_refs = refs[:2], refs[2 : 2 + 2 * n_y]
    ea_ref, eb_ref, ec_ref, slabs_ref, total_ref, where_ref, ei_ref, si_ref, r_ref, k_ref, n_ref = refs[2 + 2 * n_y :]
    nx, ny, nz = a_ref.shape[0], a_ref.shape[1] - 2 * SUB, a_ref.shape[2]
    ring = ny + SUB
    gz = lax.axis_index("gz")
    odd = lax.rem(lax.axis_index("gx"), 2) == 1

    def beyond(upper, read):
        there = has_partner("gx", 0) if upper else has_partner("gx", 1)
        swapped = has_partner("gx", 1) if upper else has_partner("gx", 0)
        first, second = read(0), read(1)
        if upper:
            return jnp.where(jnp.where(odd, swapped, there), jnp.where(odd, second, first), 0.0)
        return jnp.where(jnp.where(odd, swapped, there), jnp.where(odd, first, second), 0.0)

    def write(ref, at, own, halo):
        ref[at, :SUB] = halo
        ref[at, SUB : SUB + ny] = own
        ref[at, SUB + ny :] = halo

    lane_tile, lane = lanes_of((SUB, nz)), lanes_of((ny, nz))
    slab_parts = []
    for side, upper in enumerate((False, True)):
        tiles = [
            halo_rows([beyond(upper, lambda step: corner_refs[step * n_y + j][k]) for j in range(n_y)])
            for k in range(4)
        ]
        for k in range(3):
            write(ea_ref, 3 * side + k, beyond(upper, lambda step: x_refs[step][k]), tiles[k][0])
        for k in range(2):
            own = beyond(upper, lambda step: x_refs[step][3 + k])
            write(ei_ref, 2 * side + k, own, tiles[k if upper else k + 1][1])
        own = beyond(upper, lambda step: x_refs[step][5])

        def near(value, lanes, planes):
            return jnp.where(lanes < planes * PACK if upper else lanes >= nz - planes * PACK, value, 0.0)

        slab_parts.append((
            near(own, lane, 3), near(tiles[3][0], lane_tile, 3),
            near(pltpu.roll(own, nz // 2, 1), lane, 2), near(tiles[3][1], lane_tile, 2),
            own[0:1, COUNT_LANE : COUNT_LANE + 1],
        ))

    low, high = slab_parts
    for ref, k in ((slabs_ref, 0), (si_ref, 1)):
        ref[0, :, :nz] = slab_ref[k]
        ref[0, SUB : SUB + ny, nz:] = low[2 * k] + high[2 * k]
        ref[0, :SUB, nz:] = low[2 * k + 1] + high[2 * k + 1]
        ref[0, SUB + ny :, nz:] = low[2 * k + 1] + high[2 * k + 1]

    def reader(inside_ref, edge_ref, first, count):
        def get(x, row):
            if first <= x < nx - first:
                return inside_ref[x, row : row + SUB]
            at = x - (first - count) if x < first else x - (nx - first) + count
            return edge_ref[at, row : row + SUB]

        return get

    r_ref[0, SUB : SUB + ny] = right_ref[0]
    r_ref[1, SUB : SUB + ny] = right_ref[nx - 1]
    held = {("k0", 0): (k_ref, 0), ("k0", nx - 1): (k_ref, 1), ("k0", 1): (pass_ref, 0), ("k0", nx - 2): (pass_ref, 1)}
    for at, x in enumerate((0, 1, nx - 2, nx - 1)):
        held["n1", x] = (n_ref, at)
    held |= {("n1", 2): (pass_ref, 2), ("n1", nx - 3): (pass_ref, 3)}
    sums = {}
    for stage in range(3):
        get = reader((a_ref, b_ref, c_ref)[stage], (ea_ref, eb_ref, ec_ref)[stage], stage, 3)
        start, size = SUB - 2 + stage, ny if stage == 2 else ring
        v = slabs_ref[stage, start : start + size]
        s = slabs_ref[stage, start - 1 : start - 1 + size] + slabs_ref[stage, start + 1 : start + 1 + size]
        q, after = slab_step(stage, v, s, si_ref[0, start : start + size])
        if stage < 2:
            slabs_ref[stage + 1, start : start + size] = after

        def put(x, row, value):
            edge_ref = (eb_ref, ec_ref)[stage]
            at = x - (stage - 2) if x < nx // 2 else x - (nx - 1 - stage) + 3
            edge_ref[at, row : row + SUB] = value

        sweep(
            stage, [(stage - 2, stage + 1), (nx - 1 - stage, nx + 2 - stage)], nx, ny, nz, gz,
            get, reader(i_ref, ei_ref, 0, 2), put, q, sums,
            lambda x, row: r_ref[0 if x == 0 else 1, row : row + SUB],
            lambda x, row: a_ref[x, row : row + SUB], held,
        )

    total_ref[0:1] = stat_ref[0, 0:1]
    for k, name in enumerate(ORDER[1:]):
        total_ref[k + 1 : k + 2] = jnp.sum(sums[name] + sum_ref[k], axis=0, keepdims=True)
    gx, n_x = lax.axis_index("gx"), lax.axis_size("gx")
    count = jnp.sum(stat_ref[1, 0:1], axis=1, keepdims=True)
    below, above = [part[4] for part in slab_parts]
    begin = jnp.where(
        gx == 0, 0.0,
        jnp.where(gx == 1, below, jnp.where(gx == n_x - 1, column_total - count, column_total - count - above)),
    )
    where_ref[0:1] = jnp.broadcast_to(begin, (1, nz))
    where_ref[1:2] = jnp.broadcast_to(count, (1, nz))
    where_ref[2:8] = jnp.zeros((6, nz), F32)


def shift_up(v, amount):
    if amount < SUB:
        return pltpu.roll(v, v.shape[0] - amount, 0)
    return jnp.concatenate([v[amount:], v[:amount]], axis=0)


def plan_kernel(after_ref, label_ref, index_ref, plan_ref, lane_ref):
    rows, slot_rows = label_ref.shape[0], index_ref.shape[0]
    wide = -(-(slot_rows + 1) // LANES) * LANES
    shape = (rows, LANES)
    lane, row = lanes_of(shape), subs_of(shape)
    ones = (label_ref[...] == 1).astype(jnp.bfloat16)
    totals = jnp.dot(ones, jnp.ones((LANES, LANES), jnp.bfloat16), preferred_element_type=F32)
    lower = (subs_of((rows, rows)) > lanes_of((rows, rows))).astype(jnp.bfloat16)
    before = jnp.dot(lower, totals.astype(jnp.bfloat16), preferred_element_type=F32).astype(jnp.int32)
    target, first = lax.div(before, LANES), lax.rem(before, LANES)
    listed = jnp.concatenate(
        [lax.rem(index_ref[...], LANES).astype(F32), jnp.zeros((wide - slot_rows, LANES), F32)], axis=0
    ).astype(jnp.bfloat16)
    spread = jnp.concatenate([target] * (wide // LANES), axis=1)
    place = lanes_of((rows, wide))
    here = jnp.dot((spread == place).astype(jnp.bfloat16), listed, preferred_element_type=F32)
    after = jnp.dot((spread + 1 == place).astype(jnp.bfloat16), listed, preferred_element_type=F32)
    lane_ref[...] = jnp.where(lane >= first, here, after).astype(jnp.int32)
    wrapped = (lane < first).astype(jnp.int32)
    filled = lane - first + LANES * wrapped < totals.astype(jnp.int32)
    way = jnp.where(filled, row - target - wrapped, 0)
    plan = jnp.zeros(shape, jnp.int32)
    step = 1
    while step < rows:
        moving = jnp.where((way & step) != 0, way, 0)
        arriving = shift_up(moving, step)
        plan = plan | (arriving & step)
        way = (way - moving) | arriving
        step *= 2
    plan_ref[...] = plan


def galerkin(total):
    def add_up(*rows):
        sums = jnp.sum(jnp.concatenate(rows, axis=0), axis=1, keepdims=True)
        return [jnp.broadcast_to(sums[k : k + 1], row.shape) for k, row in enumerate(rows)]

    row = {name: total[k : k + 1] for k, name in enumerate(ORDER)}
    b0, b2 = row["w0 r"], row["w0 n1"]
    g00, g01, g02 = row["w0 k0"], row["w1 k0"], row["w1 n1"]
    g11, g12, g22 = row["w1 k1"], row["w2 k1"], row["w2 k2"]
    sums = jnp.sum(total, axis=1, keepdims=True)
    s00, s01, s02, s0, s11, s22 = [
        jnp.broadcast_to(sums[k : k + 1], b0.shape)
        for k in map(ORDER.index, ("w0 k0", "w1 k0", "w1 n1", "w0 r", "w1 k1", "w2 k2"))
    ]
    l10, l20 = s01 / s00, s02 / s00
    h11 = g11 - l10 * (2.0 * g01 - l10 * g00)
    h12 = g12 - l10 * g02 - l20 * (g01 - l10 * g00)
    h22 = g22 - l20 * (2.0 * g02 - l20 * g00)
    y1, y2 = g00 - l10 * b0, b2 - l20 * b0
    d1, s12, s1 = add_up(h11, h12, y1)
    ok1 = d1 > 1e-7 * s11
    d1 = jnp.where(ok1, d1, 1.0)
    l21 = jnp.where(ok1, s12 / d1, 0.0)
    d2, s2 = add_up(h22 - l21 * (2.0 * h12 - l21 * h11), y2 - l21 * y1)
    ok2 = ok1 & (d2 > 1e-7 * s22)
    c2 = jnp.where(ok2, s2 / jnp.where(ok2, d2, 1.0), 0.0)
    c1 = jnp.where(ok1, s1 / d1 - l21 * c2, 0.0)
    c0 = s0 / s00 - l10 * c1 - l20 * c2
    return c0, c1, c2


def couple_kernel(
    stage, slot_rows, after_ref, where_ref, inside_ref, edge_ref, slabs_ref, plan_ref, lane_ref, blocks_ref,
    value_ref, buf_ref,
):
    nx, nz = inside_ref.shape[0], inside_ref.shape[2]
    ny = inside_ref.shape[1] - 2 * SUB
    rows = nx * ny
    gz = lax.axis_index("gz")

    def get(x, row):
        if stage <= x < nx - stage:
            return inside_ref[x, row : row + SUB]
        return edge_ref[x - (stage - 3) if x < stage else x - (nx - stage) + 3, row : row + SUB]

    for tile in range(ny // SUB):
        row = SUB + SUB * tile
        slab = slabs_ref[stage, row : row + SUB, :nz]
        v_low, v_mid = get(-1, row), get(0, row)
        for x in range(nx):
            v_high = get(x + 1, row)
            beside = get(x, row - 1) + get(x, row + 1)
            at = ny * x + SUB * tile
            value_ref[at : at + SUB] = (
                along_z(v_mid, slab, PACK * x, gz) + beside + (v_low + v_high) - 6.0 * v_mid
            )
            v_low, v_mid = v_mid, v_high
    value = jnp.take_along_axis(value_ref[...], lane_ref[...], axis=1)
    plan = plan_ref[...]
    step = 1
    while step < rows:
        value = jnp.where((plan & step) != 0, shift_up(value, step), value)
        step *= 2
    offset = jnp.max(where_ref[0:1]).astype(jnp.int32)
    count = jnp.max(where_ref[1:2]).astype(jnp.int32)
    shape = (slot_rows, LANES)
    slots = jnp.where(subs_of(shape) * LANES + lanes_of(shape) < count, value[:slot_rows], 0.0)
    slots = jnp.concatenate([slots, jnp.zeros((SUB, LANES), F32)], axis=0)
    inner = lax.rem(offset, LANES)
    turned = pltpu.roll(slots, inner, 1)
    moved = jnp.where(lanes_of((slot_rows + SUB, LANES)) >= inner, turned, pltpu.roll(turned, 1, 0))
    buf_ref[...] = jnp.zeros_like(buf_ref)
    buf_ref[pl.ds(offset // LANES, slot_rows + SUB), :] = moved
    gx = lax.axis_index("gx")
    n_gx = lax.axis_size("gx")
    size = blocks_ref.shape[0] // n_gx
    for block in range(n_gx):
        begin = pl.multiple_of((gx ^ block) * size, SUB)
        blocks_ref[block * size : block * size + size] = buf_ref[pl.ds(begin, size), :]


def add_kernel(a_ref, b_ref, after_ref, out_ref):
    out_ref[...] = a_ref[...] + b_ref[...]


def pack_kernel(total_ref, *refs):
    list_refs, out_refs = refs[:3], refs[3:]
    size = (out_refs[0].shape[0] - SUB) // 3
    for block, out_ref in enumerate(out_refs):
        for k, list_ref in enumerate(list_refs):
            out_ref[k * size : k * size + size] = list_ref[block * size : block * size + size]
        out_ref[3 * size :] = total_ref[...]


def membrane_kernel(
    half_ref, slope_ref, tau_ref, cond_ref, rev_ref, after_ref, v_ref, gates_ref, cot_ref,
    base_ref, sum_ref, factor_ref, coef_ref,
):
    n_states, rows = gates_ref.shape[:2]
    v = v_ref[...]

    def state(g, carry):
        total, current = carry
        inv_slope = 1.0 / slope_ref[g]
        tau_base = tau_ref[g]
        scaled = (v - half_ref[g]) * inv_slope
        gate = gates_ref[g]
        cot = cot_ref[g]
        steady = 1.0 / (1.0 + jnp.exp(-scaled))
        bell = jnp.exp(-scaled * scaled)
        rate = TIME_STEP / (tau_base * (0.5 + bell))
        decay = jnp.exp(-rate)
        steady_slope = steady * (1.0 - steady)
        decay_slope = decay * rate * rate * ((tau_base / TIME_STEP) * bell * (-2.0 * scaled))
        change = (steady_slope * (1.0 - decay) + (gate - steady) * decay_slope) * inv_slope
        base_ref[g] = cot * decay
        coef_ref[0, pl.ds(g, 1)] = jnp.full((1, LANES), TIME_STEP * cond_ref[g])
        coef_ref[1, pl.ds(g, 1)] = jnp.full((1, LANES), rev_ref[g])
        return total + cot * change, current + cond_ref[g] * gate

    zero = jnp.zeros((rows, LANES), F32)
    total, current = lax.fori_loop(0, n_states, state, (zero, zero), unroll=2)
    sum_ref[...] = total
    factor_ref[...] = 1.0 - TIME_STEP * current


def finish_kernel(
    alone, coef_ref, vcot_ref, v_ref, sum_ref, factor_ref, base_ref, a_ref, b_ref, c_ref, eb_ref, ec_ref, *refs
):
    n_small, n_large = len(alone[0]), len(alone[1])
    own_ref, small_refs, large_refs = refs[0], refs[1 : 1 + n_small], refs[1 + n_small : 1 + n_small + n_large]
    x_ref, volt_ref, gate_ref = refs[1 + n_small + n_large :]
    size = (own_ref.shape[0] - SUB) // 3
    gx = lax.axis_index("gx")

    def is_one(flags):
        found = gx < 0
        for place, flag in enumerate(flags):
            if flag:
                found = found | (gx == place)
        return found

    total = own_ref[3 * size :]
    for flags, ref in zip(alone[0], small_refs):
        total = total + jnp.where(is_one(flags), ref[...], 0.0)
    for flags, ref in zip(alone[1], large_refs):
        total = total + jnp.where(is_one(flags), 0.0, ref[3 * size :])
    c0, c1, c2 = galerkin(total)
    landed = jnp.zeros((size, LANES), F32)
    for k, c in enumerate((c0, c1, c2)):
        part = own_ref[k * size : k * size + size]
        for ref in large_refs:
            part = part + ref[k * size : k * size + size]
        landed = landed + c * part
    cot = vcot_ref[...] + landed
    v = v_ref[...]
    volt_ref[...] = cot * factor_ref[...] + sum_ref[...]
    for g in range(base_ref.shape[0]):
        gate_ref[g] = base_ref[g] - (coef_ref[0, g : g + 1] * cot) * (v - coef_ref[1, g : g + 1])
    nx, ny, nz = x_ref.shape
    own = slice(SUB, SUB + ny)
    for x in range(nx):
        w1 = b_ref[x, own] if 1 <= x < nx - 1 else eb_ref[2 if x == 0 else 3, own]
        w2 = c_ref[x, own] if 2 <= x < nx - 2 else ec_ref[x + 1 if x < 2 else x - (nx - 2) + 3, own]
        x_ref[x] = c0 * a_ref[x, own] + c1 * w1 + c2 * w2


def partners(axis, step):
    count = lax.axis_size(axis)
    if step == 0:
        return [i ^ 1 for i in range(count)]
    return [0] + [i + 1 if i % 2 else i - 1 for i in range(1, count - 1)] + [count - 1]


def swap(value, x_to=None, y_to=None):
    n_x, n_y, n_z = [lax.axis_size(axis) for axis in ("gx", "gy", "gz")]
    pairs = []
    for x in range(n_x):
        for y in range(n_y):
            to_x, to_y = x_to[x] if x_to else x, y_to[y] if y_to else y
            alone = (x_to and to_x == x) or (y_to and to_y == y)
            for z in range(n_z):
                to = (x, y, z ^ 1) if alone else (to_x, to_y, z)
                pairs.append(((x * n_y + y) * n_z + z, (to[0] * n_y + to[1]) * n_z + to[2]))
    return lax.ppermute(value, ("gx", "gy", "gz"), pairs)


def never_meet(count, k, slots, block):
    def apart(tile, owner):
        return owner * block >= (tile + 1) * slots or (owner + 1) * block <= count * block - (count - tile) * slots

    return [apart(i, i ^ k) and apart(i ^ k, i) for i in range(count)]


def local(
    potential_cot, damping, tissue_label, heart_index, voltage, gates, voltage_cot, gates_cot,
    half_voltage, gate_slope, tau_base, conductance, reversal,
):
    nx, ny, nz = potential_cot.shape
    rows = nx * ny
    ring = ny + SUB
    n_gx, n_gy = lax.axis_size("gx"), lax.axis_size("gy")
    n_states = gates.shape[0]
    block_rows = voltage.shape[1] // LANES
    slot_rows = heart_index.shape[3] // LANES
    block = shape_of(nx, ny, nz)
    flat = lambda a: a.reshape(rows, LANES)
    cells = lambda a: a.reshape(block_rows, LANES)
    states = lambda a: a.reshape(n_states, block_rows, LANES)

    w0, inv, packed, stat = call(
        start_kernel, (block, block, shape_of(2, ny, nz), shape_of(2, SUB, nz)), 3,
    )(in_hbm(potential_cot), in_hbm(damping), in_hbm(tissue_label))

    got = lax.ppermute(packed, "gz", [(0, 1), (1, 0)])
    cells_shape = jax.ShapeDtypeStruct((rows, LANES), jnp.int32)
    plan, lanes = call(plan_kernel, (cells_shape, cells_shape), 3, cost=6_000_000)(
        stat, flat(tissue_label), heart_index.reshape(slot_rows, LANES)
    )

    n_y = steps_of("gy")
    shapes = (
        (shape_of(2, ny, nz),) + (shape_of(nx + 1, SUB, nz),) * n_y + (shape_of(6, ny, nz),) * 2
        + (shape_of(4, SUB, nz),) * (2 * n_y)
    )
    slab, *faces = call(functools.partial(faces_kernel, n_y), shapes, 5)(w0, inv, packed, got, stat)
    along_y, along_x, across = faces[:n_y], faces[n_y : n_y + 2], faces[n_y + 2 :]
    y_to = [partners("gy", step) for step in range(n_y)]
    x_to = [partners("gx", step) for step in range(2)]
    along_y = [swap(face, y_to=y_to[j]) for j, face in enumerate(along_y)]
    along_x = [swap(face, x_to=x_to[i]) for i, face in enumerate(along_x)]
    across = [swap(face, x_to=x_to[k // n_y], y_to=y_to[k % n_y]) for k, face in enumerate(across)]

    tall = ring + SUB
    planes = shape_of(nx, tall, nz)
    edges = shape_of(6, tall, nz)
    in0, in_inv, in1, in2, in_sums, own_slab, passed = call(
        functools.partial(inner_kernel, n_y),
        (planes,) * 4 + (shape_of(len(ORDER) - 1, SUB, nz), shape_of(2, tall, nz), shape_of(4, tall, nz)),
        4 + n_y,
        scratch=[pltpu.VMEM((4, tall, nz), F32)] + [pltpu.VMEM((nx, tall, nz), F32)] * 3,
        cost=6_000_000,
    )(potential_cot, w0, inv, slab, *along_y)
    ends0, ends1, ends2, slabs, sums, where = call(
        functools.partial(outer_kernel, n_y, float(n_gx * voltage.shape[1])),
        (edges,) * 3 + (shape_of(3, tall, 2 * nz), shape_of(SUB, nz), shape_of(SUB, nz)),
        12 + 2 * n_y,
        scratch=[
            pltpu.VMEM((4, tall, nz), F32), pltpu.VMEM((1, tall, 2 * nz), F32),
            pltpu.VMEM((2, tall, nz), F32), pltpu.VMEM((2, tall, nz), F32), pltpu.VMEM((4, tall, nz), F32),
        ],
    )(plan, potential_cot, in0, in_inv, in1, in2, own_slab, in_sums, passed, stat, *along_x, *across)

    if n_gx > 4:
        counts = lax.all_gather(jnp.sum(stat[1, 0]), "gx")
        begin = jnp.sum(jnp.where(jnp.arange(n_gx) < lax.axis_index("gx"), counts, 0.0))
        where = where.at[0].set(begin)

    def couple(stage, after, inside, ends):
        return call(
            functools.partial(couple_kernel, stage, slot_rows),
            shape_of(n_gx * block_rows, LANES),
            7,
            scratch=[
                pltpu.VMEM((rows, LANES), F32), pltpu.VMEM((n_gx * block_rows + slot_rows + SUB, LANES), F32),
            ],
            cost=6_000_000,
        )(after, where, inside, ends, slabs, plan, lanes)

    def add(value, axis, step, after):
        got = lax.ppermute(value, axis, [(i, i ^ step) for i in range(lax.axis_size(axis))])
        return call(add_kernel, shape_of(SUB, nz), 3)(value, got, after)

    list0 = couple(0, sums, in0, ends0)
    sums = add(sums, "gz", 1, list0)
    list1 = couple(1, sums, in1, ends1)
    list2 = couple(2, list1, in2, ends2)
    for step in [2**k for k in range(n_gy.bit_length() - 1)]:
        sums = add(sums, "gy", step, list2)
    blocks = call(pack_kernel, (shape_of(3 * block_rows + SUB, LANES),) * n_gx, 4)(sums, list0, list1, list2)
    apart = {k: never_meet(n_gx, k, slot_rows, block_rows) for k in range(1, n_gx)}
    small, meets = [], []
    for k in range(1, n_gx):
        if any(apart[k]):
            small.append(swap(sums, x_to=[i ^ k if apart[k][i] else i for i in range(n_gx)]))
        meets.append(not all(apart[k]))
    order = [k for k in [2, 3, 1] + list(range(4, n_gx)) if k < n_gx and meets[k - 1]]
    large = [swap(blocks[k], x_to=[i if apart[k][i] else i ^ k for i in range(n_gx)]) for k in order]
    alone = [[apart[k] for k in range(1, n_gx) if any(apart[k])], [apart[k] for k in order]]

    base, total_change, factor, state_coefs = call(
        membrane_kernel,
        (
            shape_of(n_states, block_rows, LANES), shape_of(block_rows, LANES), shape_of(block_rows, LANES),
            shape_of(2, n_states, LANES),
        ),
        9,
        specs=[SMEM] * 5 + [VMEM] * 4,
        cost=6_000_000,
    )(
        half_voltage, gate_slope, tau_base, conductance, reversal,
        blocks[0], cells(voltage), states(gates), states(gates_cot),
    )
    solution, volt_grad, gate_grad = call(
        functools.partial(finish_kernel, alone),
        (block, shape_of(block_rows, LANES), shape_of(n_states, block_rows, LANES)),
        12 + len(small) + len(large),
    )(
        state_coefs, cells(voltage_cot), cells(voltage), total_change, factor, base,
        in0, in1, in2, ends1, ends2, blocks[0], *small, *large,
    )
    return solution, volt_grad.reshape(voltage.shape), gate_grad.reshape(gates.shape)


def solution(mesh):
    grid = P(("groups", "gx"), "gy", "gz")
    cells = P(("groups", "gy", "gz"), "gx")
    states = P(None, ("groups", "gy", "gz"), "gx")
    in_specs = (
        grid, grid, grid, P(("groups", "gx"), "gy", "gz", None), cells, states, cells, states,
        P(), P(), P(), P(), P(),
    )
    return jax.shard_map(
        local, mesh=mesh, in_specs=in_specs, out_specs=(grid, cells, states), check_vma=False
    )
```

```python
import functools

import jax
import jax.numpy as jnp
from jax import lax
from jax.experimental import pallas as pl
from jax.experimental.pallas import tpu as pltpu
from jax.sharding import PartitionSpec as P

TIME_STEP = 0.5
LANES = 128
SUB = 8
PACK = 8
COUNT_LANE = 4 * PACK
F32 = jnp.float32

VMEM = pl.BlockSpec(memory_space=pltpu.VMEM)
SMEM = pl.BlockSpec(memory_space=pltpu.SMEM)
HBM = pl.BlockSpec(memory_space=pltpu.HBM)


def shape_of(*dims):
    return jax.ShapeDtypeStruct(dims, F32)


def call(kernel, out_shape, n_in, specs=None, outs=None, scratch=(), cost=2_000_000, limit=32):
    return pl.pallas_call(
        kernel,
        out_shape=out_shape,
        in_specs=specs if specs is not None else [VMEM] * n_in,
        out_specs=outs if outs is not None else jax.tree.map(lambda _: VMEM, out_shape),
        scratch_shapes=list(scratch),
        compiler_params=pltpu.CompilerParams(vmem_limit_bytes=limit * 1024 * 1024),
        cost_estimate=pl.CostEstimate(flops=cost, bytes_accessed=cost, transcendentals=0),
    )


def in_hbm(array):
    return pltpu.with_memory_space_constraint(array, pltpu.HBM)


def lanes_of(shape):
    return lax.broadcasted_iota(jnp.int32, shape, len(shape) - 1)


def subs_of(shape):
    return lax.broadcasted_iota(jnp.int32, shape, len(shape) - 2)


def start_kernel(right_ref, damping_ref, label_ref, w0_ref, inv_ref, pack_ref, stat_ref):
    nx, ny, nz = right_ref.shape
    gz = lax.axis_index("gz")
    lane = lanes_of((ny, nz))
    packed_w = jnp.zeros((ny, nz), F32)
    packed_i = jnp.zeros((ny, nz), F32)
    energy = jnp.zeros((ny, nz), F32)
    cells = jnp.zeros((ny, nz), F32)
    for x in range(nx):
        label = label_ref[x].astype(F32)
        right = right_ref[x]
        inv = 1.0 / (12.0 + damping_ref[x] * (1.0 + 3.0 * label))
        w0 = right * inv
        w0_ref[x] = w0
        inv_ref[x] = inv
        energy = energy + right * w0
        cells = cells + label
        turn = (PACK * x + 3) % nz
        begin = PACK * x + 3 * gz
        chosen = (lane >= begin) & (lane < begin + 3)
        packed_w = jnp.where(chosen, pltpu.roll(w0, turn, 1), packed_w)
        packed_i = jnp.where(chosen, pltpu.roll(inv, turn, 1), packed_i)
    pack_ref[0] = packed_w
    pack_ref[1] = packed_i
    stat_ref[0] = jnp.broadcast_to(jnp.sum(energy, axis=0, keepdims=True), (SUB, nz))
    stat_ref[1] = jnp.broadcast_to(jnp.sum(cells, axis=0, keepdims=True), (SUB, nz))


def steps_of(axis):
    return 1 if lax.axis_size(axis) == 2 else 2


def upper_in(axis, step):
    return lax.rem(lax.axis_index(axis), 2) == step


def has_partner(axis, step):
    here = lax.axis_index(axis)
    return jnp.where(upper_in(axis, step), here < lax.axis_size(axis) - 1, here > 0)


def unpack_rows(tile, step):
    sub = subs_of(tile.shape)
    up, there = upper_in("gy", step), has_partner("gy", step)
    depth = jnp.where(there, jnp.where(up, SUB - 1 - sub, sub), -1)
    return jnp.where(depth >= 5, tile, 0.0), jnp.where(depth >= 6, pltpu.roll(tile, 4, 0), 0.0)


def halo_rows(tiles):
    w_tile, i_tile = unpack_rows(tiles[0], 0)
    for step, tile in enumerate(tiles[1:], 1):
        w_more, i_more = unpack_rows(tile, step)
        w_tile, i_tile = w_tile + w_more, i_tile + i_more
    return w_tile, i_tile


def faces_kernel(n_y, w0_ref, inv_ref, own_ref, got_ref, stat_ref, slab_ref, *refs):
    y_refs, x_refs, edge_refs = refs[:n_y], refs[n_y : n_y + 2], refs[n_y + 2 :]
    nx, ny, nz = w0_ref.shape
    sub = subs_of((SUB, nz))
    lane = lanes_of((ny, nz))
    slab_ref[...] = own_ref[...] + got_ref[...]
    for step, face_ref in enumerate(y_refs):
        up = upper_in("gy", step)
        keep_w = jnp.where(up, sub, SUB - 1 - sub) >= 5
        for x in range(nx + 1):
            w_rows, i_rows = (w0_ref.at[x], inv_ref.at[x]) if x < nx else (slab_ref.at[0], slab_ref.at[1])
            w_face = jnp.where(up, w_rows[ny - SUB :], w_rows[:SUB])
            i_face = jnp.where(up, i_rows[ny - SUB :], i_rows[:SUB])
            face_ref[x] = jnp.where(keep_w, w_face, pltpu.roll(i_face, 4, 0))
    cells = jnp.sum(stat_ref[1, 0:1], axis=1, keepdims=True)
    slab_w = slab_ref[0]
    half = pltpu.roll(slab_ref[1], nz // 2, 1)
    up_slab = jnp.where(lane >= nz - 3 * PACK, slab_w, half)
    down_slab = jnp.where(lane < 3 * PACK, slab_w, half)
    for step, face_ref in enumerate(x_refs):
        up = upper_in("gx", step)
        first = jnp.where(up, nx - 3, 0)
        for k in range(3):
            face_ref[k] = w0_ref[first + k]
        for k in range(2):
            face_ref[3 + k] = inv_ref[jnp.where(up, nx - 2, 0) + k]
        face_ref[5] = jnp.where(lane == COUNT_LANE, cells, jnp.where(up, up_slab, down_slab))
        for y_step, y_ref in enumerate(y_refs):
            edge_ref = edge_refs[step * n_y + y_step]
            for k in range(3):
                edge_ref[k] = y_ref[first + k]
            edge_ref[3] = y_ref[nx]


SUMS = (("w0 k0", "w1 k0"), ("w1 n1", "w1 k1", "w2 k1", "w0 n1"), ("w2 k2",))
ORDER = ("w0 r", "w0 k0", "w1 k0", "w1 n1", "w1 k1", "w2 k1", "w2 k2", "w0 n1")


def slab_step(stage, v, s, inv):
    width = v.shape[1]
    across = pltpu.roll(v, PACK, 1) + pltpu.roll(v, width - PACK, 1)
    q = v + 0.5 * (s + across)
    if stage == 2:
        return q, None
    total = (
        pltpu.roll(q, 1, 1) + pltpu.roll(q, width - 1, 1) + s + across
        + 0.5 * (pltpu.roll(s, PACK, 1) + pltpu.roll(s, width - PACK, 1))
    )
    return q, next_vector(stage, v, total, inv)


def next_vector(stage, v, total, inv):
    return v - total * inv if stage == 0 else total * inv


def along_z(q, half, column, gz):
    nz = q.shape[1]
    lane = lanes_of(q.shape)
    entry = (nz - 1) * (1 - gz)
    turn = lax.rem(entry - (column + 3 - gz) + 2 * nz, nz)
    up = jnp.where(lane == nz - 1, 0.0, pltpu.roll(q, nz - 1, 1))
    down = jnp.where(lane == 0, 0.0, pltpu.roll(q, 1, 1))
    return up + down + jnp.where(lane == entry, pltpu.roll(half, turn, 1), 0.0)


def sweep(stage, spans, nx, ny, nz, gz, get, get_inv, put, slab_q, sums, get_right, get_w0, held):
    margin = 2 - stage
    start = SUB - margin
    tiles = ny // SUB + (margin > 0)
    own = subs_of((SUB, nz)) >= margin
    names = SUMS[stage]
    parts = {name: [] for name in names}
    for tile in range(tiles):
        row = start + SUB * tile
        q_rows = slab_q[SUB * tile : SUB * tile + SUB]
        acc = {name: jnp.zeros((SUB, nz), F32) for name in names}

        def beside(x):
            return get(x, row - 1) + get(x, row + 1)

        def rows(name, x):
            ref, at = held[name, x]
            return ref.at[at, row : row + SUB]

        for first, last in spans:
            s_low, s_mid = beside(first - 1), beside(first)
            v_low, v_mid = get(first - 1, row), get(first, row)
            for x in range(first, last):
                v_high, s_high = get(x + 1, row), beside(x + 1)
                across = v_low + v_high
                column = (PACK * x) % (2 * nz)
                half = q_rows[:, column // nz * nz : column // nz * nz + nz]
                rest = s_mid + across
                total = along_z(v_mid + 0.5 * rest, half, column % nz, gz) + rest + 0.5 * (s_low + s_high)
                if stage < 2:
                    after = next_vector(stage, v_mid, total, get_inv(x, row))
                    put(x, row, after)
                if 0 <= x < nx:
                    if stage == 0:
                        k0 = get_right(x, row) - total
                        rows("k0", x)[...] = k0
                        terms = (v_mid * k0, after * k0)
                    elif stage == 1:
                        rows("n1", x)[...] = total
                        k1 = rows("k0", x)[...] - total
                        terms = (v_mid * total, v_mid * k1, after * k1, get_w0(x, row) * total)
                    else:
                        terms = (v_mid * (rows("n1", x)[...] - total),)
                    for name, term in zip(names, terms):
                        acc[name] = acc[name] + term
                v_low, v_mid, s_low, s_mid = v_mid, v_high, s_mid, s_high
        for name in names:
            parts[name].append(acc[name])
    for name in names:
        part = parts[name]
        total = part[1]
        for other in part[2 : ny // SUB]:
            total = total + other
        sums[name] = total + (jnp.where(own, part[0], part[-1]) if margin else part[0])


def inner_kernel(n_y, right_ref, w0_ref, inv_ref, slab_ref, *refs):
    y_refs, refs = refs[:n_y], refs[n_y:]
    a_ref, i_ref, b_ref, c_ref, sum_ref, own_slab_ref, pass_ref, slabs_ref, r_ref, k_ref, n_ref = refs
    nx, ny, nz = w0_ref.shape
    gz = lax.axis_index("gz")
    for x in range(nx + 1):
        halos = halo_rows([ref[x] for ref in y_refs])
        for k in range(2):
            if x < nx:
                ref, own = (a_ref, i_ref)[k].at[x], (w0_ref, inv_ref)[k][x]
            else:
                ref, own = own_slab_ref.at[k], slab_ref[k]
            ref[:SUB] = halos[k]
            ref[SUB : SUB + ny] = own
            ref[SUB + ny :] = halos[k]
    for k in range(2):
        slabs_ref[3 * k] = own_slab_ref[k]
    for x in range(nx):
        r_ref[x, SUB : SUB + ny] = right_ref[x]
    held = {("k0", x): (k_ref, x) for x in range(nx)} | {("n1", x): (n_ref, x) for x in range(nx)}
    held |= {("k0", 1): (pass_ref, 0), ("k0", nx - 2): (pass_ref, 1)}
    held |= {("n1", 2): (pass_ref, 2), ("n1", nx - 3): (pass_ref, 3)}
    sums = {}
    for stage in range(3):
        source, target = (a_ref, b_ref, c_ref)[stage], (b_ref, c_ref, None)[stage]
        start, size = SUB - 2 + stage, ny if stage == 2 else ny + SUB
        v = slabs_ref[stage, start : start + size]
        s = slabs_ref[stage, start - 1 : start - 1 + size] + slabs_ref[stage, start + 1 : start + 1 + size]
        q, after = slab_step(stage, v, s, slabs_ref[3, start : start + size])
        if stage < 2:
            slabs_ref[stage + 1, start : start + size] = after

        def put(x, row, value):
            target[x, row : row + SUB] = value

        sweep(
            stage, [(1 + stage, nx - 1 - stage)], nx, ny, nz, gz,
            lambda x, row: source[x, row : row + SUB], lambda x, row: i_ref[x, row : row + SUB],
            put, q, sums,
            lambda x, row: r_ref[x, row : row + SUB], lambda x, row: a_ref[x, row : row + SUB], held,
        )
    for k, name in enumerate(ORDER[1:]):
        sum_ref[k] = sums[name]


def outer_kernel(
    n_y, column_total, after_ref, right_ref, a_ref, i_ref, b_ref, c_ref, slab_ref, sum_ref, pass_ref, stat_ref, *refs
):
    x_refs, corner_refs = refs[:2], refs[2 : 2 + 2 * n_y]
    ea_ref, eb_ref, ec_ref, slabs_ref, total_ref, where_ref, ei_ref, si_ref, r_ref, k_ref, n_ref = refs[2 + 2 * n_y :]
    nx, ny, nz = a_ref.shape[0], a_ref.shape[1] - 2 * SUB, a_ref.shape[2]
    ring = ny + SUB
    gz = lax.axis_index("gz")
    odd = lax.rem(lax.axis_index("gx"), 2) == 1

    def beyond(upper, read):
        there = has_partner("gx", 0) if upper else has_partner("gx", 1)
        swapped = has_partner("gx", 1) if upper else has_partner("gx", 0)
        first, second = read(0), read(1)
        if upper:
            return jnp.where(jnp.where(odd, swapped, there), jnp.where(odd, second, first), 0.0)
        return jnp.where(jnp.where(odd, swapped, there), jnp.where(odd, first, second), 0.0)

    def write(ref, at, own, halo):
        ref[at, :SUB] = halo
        ref[at, SUB : SUB + ny] = own
        ref[at, SUB + ny :] = halo

    lane_tile, lane = lanes_of((SUB, nz)), lanes_of((ny, nz))
    slab_parts = []
    for side, upper in enumerate((False, True)):
        tiles = [
            halo_rows([beyond(upper, lambda step: corner_refs[step * n_y + j][k]) for j in range(n_y)])
            for k in range(4)
        ]
        for k in range(3):
            write(ea_ref, 3 * side + k, beyond(upper, lambda step: x_refs[step][k]), tiles[k][0])
        for k in range(2):
            own = beyond(upper, lambda step: x_refs[step][3 + k])
            write(ei_ref, 2 * side + k, own, tiles[k if upper else k + 1][1])
        own = beyond(upper, lambda step: x_refs[step][5])

        def near(value, lanes, planes):
            return jnp.where(lanes < planes * PACK if upper else lanes >= nz - planes * PACK, value, 0.0)

        slab_parts.append((
            near(own, lane, 3), near(tiles[3][0], lane_tile, 3),
            near(pltpu.roll(own, nz // 2, 1), lane, 2), near(tiles[3][1], lane_tile, 2),
            own[0:1, COUNT_LANE : COUNT_LANE + 1],
        ))

    low, high = slab_parts
    for ref, k in ((slabs_ref, 0), (si_ref, 1)):
        ref[0, :, :nz] = slab_ref[k]
        ref[0, SUB : SUB + ny, nz:] = low[2 * k] + high[2 * k]
        ref[0, :SUB, nz:] = low[2 * k + 1] + high[2 * k + 1]
        ref[0, SUB + ny :, nz:] = low[2 * k + 1] + high[2 * k + 1]

    def reader(inside_ref, edge_ref, first, count):
        def get(x, row):
            if first <= x < nx - first:
                return inside_ref[x, row : row + SUB]
            at = x - (first - count) if x < first else x - (nx - first) + count
            return edge_ref[at, row : row + SUB]

        return get

    r_ref[0, SUB : SUB + ny] = right_ref[0]
    r_ref[1, SUB : SUB + ny] = right_ref[nx - 1]
    held = {("k0", 0): (k_ref, 0), ("k0", nx - 1): (k_ref, 1), ("k0", 1): (pass_ref, 0), ("k0", nx - 2): (pass_ref, 1)}
    for at, x in enumerate((0, 1, nx - 2, nx - 1)):
        held["n1", x] = (n_ref, at)
    held |= {("n1", 2): (pass_ref, 2), ("n1", nx - 3): (pass_ref, 3)}
    sums = {}
    for stage in range(3):
        get = reader((a_ref, b_ref, c_ref)[stage], (ea_ref, eb_ref, ec_ref)[stage], stage, 3)
        start, size = SUB - 2 + stage, ny if stage == 2 else ring
        v = slabs_ref[stage, start : start + size]
        s = slabs_ref[stage, start - 1 : start - 1 + size] + slabs_ref[stage, start + 1 : start + 1 + size]
        q, after = slab_step(stage, v, s, si_ref[0, start : start + size])
        if stage < 2:
            slabs_ref[stage + 1, start : start + size] = after

        def put(x, row, value):
            edge_ref = (eb_ref, ec_ref)[stage]
            at = x - (stage - 2) if x < nx // 2 else x - (nx - 1 - stage) + 3
            edge_ref[at, row : row + SUB] = value

        sweep(
            stage, [(stage - 2, stage + 1), (nx - 1 - stage, nx + 2 - stage)], nx, ny, nz, gz,
            get, reader(i_ref, ei_ref, 0, 2), put, q, sums,
            lambda x, row: r_ref[0 if x == 0 else 1, row : row + SUB],
            lambda x, row: a_ref[x, row : row + SUB], held,
        )

    total_ref[0:1] = stat_ref[0, 0:1]
    for k, name in enumerate(ORDER[1:]):
        total_ref[k + 1 : k + 2] = jnp.sum(sums[name] + sum_ref[k], axis=0, keepdims=True)
    gx, n_x = lax.axis_index("gx"), lax.axis_size("gx")
    count = jnp.sum(stat_ref[1, 0:1], axis=1, keepdims=True)
    below, above = [part[4] for part in slab_parts]
    begin = jnp.where(
        gx == 0, 0.0,
        jnp.where(gx == 1, below, jnp.where(gx == n_x - 1, column_total - count, column_total - count - above)),
    )
    where_ref[0:1] = jnp.broadcast_to(begin, (1, nz))
    where_ref[1:2] = jnp.broadcast_to(count, (1, nz))
    where_ref[2:8] = jnp.zeros((6, nz), F32)


def shift_up(v, amount):
    if amount < SUB:
        return pltpu.roll(v, v.shape[0] - amount, 0)
    return jnp.concatenate([v[amount:], v[:amount]], axis=0)


def plan_kernel(after_ref, label_ref, index_ref, plan_ref, lane_ref):
    rows, slot_rows = label_ref.shape[0], index_ref.shape[0]
    wide = -(-(slot_rows + 1) // LANES) * LANES
    shape = (rows, LANES)
    lane, row = lanes_of(shape), subs_of(shape)
    ones = (label_ref[...] == 1).astype(jnp.bfloat16)
    totals = jnp.dot(ones, jnp.ones((LANES, LANES), jnp.bfloat16), preferred_element_type=F32)
    lower = (subs_of((rows, rows)) > lanes_of((rows, rows))).astype(jnp.bfloat16)
    before = jnp.dot(lower, totals.astype(jnp.bfloat16), preferred_element_type=F32).astype(jnp.int32)
    target, first = lax.div(before, LANES), lax.rem(before, LANES)
    listed = jnp.concatenate(
        [lax.rem(index_ref[...], LANES).astype(F32), jnp.zeros((wide - slot_rows, LANES), F32)], axis=0
    ).astype(jnp.bfloat16)
    spread = jnp.concatenate([target] * (wide // LANES), axis=1)
    place = lanes_of((rows, wide))
    here = jnp.dot((spread == place).astype(jnp.bfloat16), listed, preferred_element_type=F32)
    after = jnp.dot((spread + 1 == place).astype(jnp.bfloat16), listed, preferred_element_type=F32)
    lane_ref[...] = jnp.where(lane >= first, here, after).astype(jnp.int32)
    wrapped = (lane < first).astype(jnp.int32)
    filled = lane - first + LANES * wrapped < totals.astype(jnp.int32)
    way = jnp.where(filled, row - target - wrapped, 0)
    plan = jnp.zeros(shape, jnp.int32)
    step = 1
    while step < rows:
        moving = jnp.where((way & step) != 0, way, 0)
        arriving = shift_up(moving, step)
        plan = plan | (arriving & step)
        way = (way - moving) | arriving
        step *= 2
    plan_ref[...] = plan


def galerkin(total):
    def add_up(*rows):
        return [jnp.broadcast_to(jnp.sum(row, axis=1, keepdims=True), row.shape) for row in rows]

    row = {name: total[k : k + 1] for k, name in enumerate(ORDER)}
    b0, b2 = row["w0 r"], row["w0 n1"]
    g00, g01, g02 = row["w0 k0"], row["w1 k0"], row["w1 n1"]
    g11, g12, g22 = row["w1 k1"], row["w2 k1"], row["w2 k2"]
    s00, s01, s02, s0, s11, s22 = add_up(g00, g01, g02, b0, g11, g22)
    l10, l20 = s01 / s00, s02 / s00
    h11 = g11 - l10 * (2.0 * g01 - l10 * g00)
    h12 = g12 - l10 * g02 - l20 * (g01 - l10 * g00)
    h22 = g22 - l20 * (2.0 * g02 - l20 * g00)
    y1, y2 = g00 - l10 * b0, b2 - l20 * b0
    d1, s12, s1 = add_up(h11, h12, y1)
    ok1 = d1 > 1e-7 * s11
    d1 = jnp.where(ok1, d1, 1.0)
    l21 = jnp.where(ok1, s12 / d1, 0.0)
    d2, s2 = add_up(h22 - l21 * (2.0 * h12 - l21 * h11), y2 - l21 * y1)
    ok2 = ok1 & (d2 > 1e-7 * s22)
    c2 = jnp.where(ok2, s2 / jnp.where(ok2, d2, 1.0), 0.0)
    c1 = jnp.where(ok1, s1 / d1 - l21 * c2, 0.0)
    c0 = s0 / s00 - l10 * c1 - l20 * c2
    return c0, c1, c2


def couple_kernel(
    stage, slot_rows, after_ref, where_ref, inside_ref, edge_ref, slabs_ref, plan_ref, lane_ref, blocks_ref,
    value_ref, buf_ref,
):
    nx, nz = inside_ref.shape[0], inside_ref.shape[2]
    ny = inside_ref.shape[1] - 2 * SUB
    rows = nx * ny
    gz = lax.axis_index("gz")

    def get(x, row):
        if stage <= x < nx - stage:
            return inside_ref[x, row : row + SUB]
        return edge_ref[x - (stage - 3) if x < stage else x - (nx - stage) + 3, row : row + SUB]

    for tile in range(ny // SUB):
        row = SUB + SUB * tile
        slab = slabs_ref[stage, row : row + SUB, :nz]
        v_low, v_mid = get(-1, row), get(0, row)
        for x in range(nx):
            v_high = get(x + 1, row)
            beside = get(x, row - 1) + get(x, row + 1)
            at = ny * x + SUB * tile
            value_ref[at : at + SUB] = (
                along_z(v_mid, slab, PACK * x, gz) + beside + (v_low + v_high) - 6.0 * v_mid
            )
            v_low, v_mid = v_mid, v_high
    value = jnp.take_along_axis(value_ref[...], lane_ref[...], axis=1)
    plan = plan_ref[...]
    step = 1
    while step < rows:
        value = jnp.where((plan & step) != 0, shift_up(value, step), value)
        step *= 2
    offset = jnp.max(where_ref[0:1]).astype(jnp.int32)
    count = jnp.max(where_ref[1:2]).astype(jnp.int32)
    shape = (slot_rows, LANES)
    slots = jnp.where(subs_of(shape) * LANES + lanes_of(shape) < count, value[:slot_rows], 0.0)
    slots = jnp.concatenate([slots, jnp.zeros((SUB, LANES), F32)], axis=0)
    inner = lax.rem(offset, LANES)
    turned = pltpu.roll(slots, inner, 1)
    moved = jnp.where(lanes_of((slot_rows + SUB, LANES)) >= inner, turned, pltpu.roll(turned, 1, 0))
    buf_ref[...] = jnp.zeros_like(buf_ref)
    buf_ref[pl.ds(offset // LANES, slot_rows + SUB), :] = moved
    gx = lax.axis_index("gx")
    n_gx = lax.axis_size("gx")
    size = blocks_ref.shape[0] // n_gx
    for block in range(n_gx):
        begin = pl.multiple_of((gx ^ block) * size, SUB)
        blocks_ref[block * size : block * size + size] = buf_ref[pl.ds(begin, size), :]


def add_kernel(a_ref, b_ref, after_ref, out_ref):
    out_ref[...] = a_ref[...] + b_ref[...]


def pack_kernel(total_ref, *refs):
    list_refs, out_refs = refs[:3], refs[3:]
    size = (out_refs[0].shape[0] - SUB) // 3
    for block, out_ref in enumerate(out_refs):
        for k, list_ref in enumerate(list_refs):
            out_ref[k * size : k * size + size] = list_ref[block * size : block * size + size]
        out_ref[3 * size :] = total_ref[...]


def membrane_kernel(
    half_ref, slope_ref, tau_ref, cond_ref, rev_ref, after_ref, v_ref, gates_ref, cot_ref,
    base_ref, sum_ref, factor_ref, coef_ref,
):
    n_states, rows = gates_ref.shape[:2]
    v = v_ref[...]

    def state(g, carry):
        total, current = carry
        inv_slope = 1.0 / slope_ref[g]
        tau_base = tau_ref[g]
        scaled = (v - half_ref[g]) * inv_slope
        gate = gates_ref[g]
        cot = cot_ref[g]
        steady = 1.0 / (1.0 + jnp.exp(-scaled))
        bell = jnp.exp(-scaled * scaled)
        rate = TIME_STEP / (tau_base * (0.5 + bell))
        decay = jnp.exp(-rate)
        steady_slope = steady * (1.0 - steady)
        decay_slope = decay * rate * rate * ((tau_base / TIME_STEP) * bell * (-2.0 * scaled))
        change = (steady_slope * (1.0 - decay) + (gate - steady) * decay_slope) * inv_slope
        base_ref[g] = cot * decay
        coef_ref[0, pl.ds(g, 1)] = jnp.full((1, LANES), TIME_STEP * cond_ref[g])
        coef_ref[1, pl.ds(g, 1)] = jnp.full((1, LANES), rev_ref[g])
        return total + cot * change, current + cond_ref[g] * gate

    zero = jnp.zeros((rows, LANES), F32)
    total, current = lax.fori_loop(0, n_states, state, (zero, zero), unroll=2)
    sum_ref[...] = total
    factor_ref[...] = 1.0 - TIME_STEP * current


def finish_kernel(
    alone, coef_ref, vcot_ref, v_ref, sum_ref, factor_ref, base_ref, a_ref, b_ref, c_ref, eb_ref, ec_ref, *refs
):
    n_small, n_large = len(alone[0]), len(alone[1])
    own_ref, small_refs, large_refs = refs[0], refs[1 : 1 + n_small], refs[1 + n_small : 1 + n_small + n_large]
    x_ref, volt_ref, gate_ref = refs[1 + n_small + n_large :]
    size = (own_ref.shape[0] - SUB) // 3
    gx = lax.axis_index("gx")

    def is_one(flags):
        found = gx < 0
        for place, flag in enumerate(flags):
            if flag:
                found = found | (gx == place)
        return found

    total = own_ref[3 * size :]
    for flags, ref in zip(alone[0], small_refs):
        total = total + jnp.where(is_one(flags), ref[...], 0.0)
    for flags, ref in zip(alone[1], large_refs):
        total = total + jnp.where(is_one(flags), 0.0, ref[3 * size :])
    c0, c1, c2 = galerkin(total)
    landed = jnp.zeros((size, LANES), F32)
    for k, c in enumerate((c0, c1, c2)):
        part = own_ref[k * size : k * size + size]
        for ref in large_refs:
            part = part + ref[k * size : k * size + size]
        landed = landed + c * part
    cot = vcot_ref[...] + landed
    v = v_ref[...]
    volt_ref[...] = cot * factor_ref[...] + sum_ref[...]
    for g in range(base_ref.shape[0]):
        gate_ref[g] = base_ref[g] - (coef_ref[0, g : g + 1] * cot) * (v - coef_ref[1, g : g + 1])
    nx, ny, nz = x_ref.shape
    own = slice(SUB, SUB + ny)
    for x in range(nx):
        w1 = b_ref[x, own] if 1 <= x < nx - 1 else eb_ref[2 if x == 0 else 3, own]
        w2 = c_ref[x, own] if 2 <= x < nx - 2 else ec_ref[x + 1 if x < 2 else x - (nx - 2) + 3, own]
        x_ref[x] = c0 * a_ref[x, own] + c1 * w1 + c2 * w2


def partners(axis, step):
    count = lax.axis_size(axis)
    if step == 0:
        return [i ^ 1 for i in range(count)]
    return [0] + [i + 1 if i % 2 else i - 1 for i in range(1, count - 1)] + [count - 1]


def swap(value, x_to=None, y_to=None):
    n_x, n_y, n_z = [lax.axis_size(axis) for axis in ("gx", "gy", "gz")]
    pairs = []
    for x in range(n_x):
        for y in range(n_y):
            to_x, to_y = x_to[x] if x_to else x, y_to[y] if y_to else y
            alone = (x_to and to_x == x) or (y_to and to_y == y)
            for z in range(n_z):
                to = (x, y, z ^ 1) if alone else (to_x, to_y, z)
                pairs.append(((x * n_y + y) * n_z + z, (to[0] * n_y + to[1]) * n_z + to[2]))
    return lax.ppermute(value, ("gx", "gy", "gz"), pairs)


def never_meet(count, k, slots, block):
    def apart(tile, owner):
        return owner * block >= (tile + 1) * slots or (owner + 1) * block <= count * block - (count - tile) * slots

    return [apart(i, i ^ k) and apart(i ^ k, i) for i in range(count)]


def local(
    potential_cot, damping, tissue_label, heart_index, voltage, gates, voltage_cot, gates_cot,
    half_voltage, gate_slope, tau_base, conductance, reversal,
):
    nx, ny, nz = potential_cot.shape
    rows = nx * ny
    ring = ny + SUB
    n_gx, n_gy = lax.axis_size("gx"), lax.axis_size("gy")
    n_states = gates.shape[0]
    block_rows = voltage.shape[1] // LANES
    slot_rows = heart_index.shape[3] // LANES
    block = shape_of(nx, ny, nz)
    flat = lambda a: a.reshape(rows, LANES)
    cells = lambda a: a.reshape(block_rows, LANES)
    states = lambda a: a.reshape(n_states, block_rows, LANES)

    w0, inv, packed, stat = call(
        start_kernel, (block, block, shape_of(2, ny, nz), shape_of(2, SUB, nz)), 3,
    )(in_hbm(potential_cot), in_hbm(damping), in_hbm(tissue_label))

    got = lax.ppermute(packed, "gz", [(0, 1), (1, 0)])
    cells_shape = jax.ShapeDtypeStruct((rows, LANES), jnp.int32)
    plan, lanes = call(plan_kernel, (cells_shape, cells_shape), 3, cost=6_000_000)(
        stat, flat(tissue_label), heart_index.reshape(slot_rows, LANES)
    )

    n_y = steps_of("gy")
    shapes = (
        (shape_of(2, ny, nz),) + (shape_of(nx + 1, SUB, nz),) * n_y + (shape_of(6, ny, nz),) * 2
        + (shape_of(4, SUB, nz),) * (2 * n_y)
    )
    slab, *faces = call(functools.partial(faces_kernel, n_y), shapes, 5)(w0, inv, packed, got, stat)
    along_y, along_x, across = faces[:n_y], faces[n_y : n_y + 2], faces[n_y + 2 :]
    y_to = [partners("gy", step) for step in range(n_y)]
    x_to = [partners("gx", step) for step in range(2)]
    along_y = [swap(face, y_to=y_to[j]) for j, face in enumerate(along_y)]
    along_x = [swap(face, x_to=x_to[i]) for i, face in enumerate(along_x)]
    across = [swap(face, x_to=x_to[k // n_y], y_to=y_to[k % n_y]) for k, face in enumerate(across)]

    tall = ring + SUB
    planes = shape_of(nx, tall, nz)
    edges = shape_of(6, tall, nz)
    in0, in_inv, in1, in2, in_sums, own_slab, passed = call(
        functools.partial(inner_kernel, n_y),
        (planes,) * 4 + (shape_of(len(ORDER) - 1, SUB, nz), shape_of(2, tall, nz), shape_of(4, tall, nz)),
        4 + n_y,
        scratch=[pltpu.VMEM((4, tall, nz), F32)] + [pltpu.VMEM((nx, tall, nz), F32)] * 3,
        cost=6_000_000,
    )(potential_cot, w0, inv, slab, *along_y)
    ends0, ends1, ends2, slabs, sums, where = call(
        functools.partial(outer_kernel, n_y, float(n_gx * voltage.shape[1])),
        (edges,) * 3 + (shape_of(3, tall, 2 * nz), shape_of(SUB, nz), shape_of(SUB, nz)),
        12 + 2 * n_y,
        scratch=[
            pltpu.VMEM((4, tall, nz), F32), pltpu.VMEM((1, tall, 2 * nz), F32),
            pltpu.VMEM((2, tall, nz), F32), pltpu.VMEM((2, tall, nz), F32), pltpu.VMEM((4, tall, nz), F32),
        ],
    )(plan, potential_cot, in0, in_inv, in1, in2, own_slab, in_sums, passed, stat, *along_x, *across)

    if n_gx > 4:
        counts = lax.all_gather(jnp.sum(stat[1, 0]), "gx")
        begin = jnp.sum(jnp.where(jnp.arange(n_gx) < lax.axis_index("gx"), counts, 0.0))
        where = where.at[0].set(begin)

    def couple(stage, after, inside, ends):
        return call(
            functools.partial(couple_kernel, stage, slot_rows),
            shape_of(n_gx * block_rows, LANES),
            7,
            scratch=[
                pltpu.VMEM((rows, LANES), F32), pltpu.VMEM((n_gx * block_rows + slot_rows + SUB, LANES), F32),
            ],
            cost=6_000_000,
        )(after, where, inside, ends, slabs, plan, lanes)

    def add(value, axis, step, after):
        got = lax.ppermute(value, axis, [(i, i ^ step) for i in range(lax.axis_size(axis))])
        return call(add_kernel, shape_of(SUB, nz), 3)(value, got, after)

    list0 = couple(0, sums, in0, ends0)
    sums = add(sums, "gz", 1, list0)
    list1 = couple(1, sums, in1, ends1)
    list2 = couple(2, list1, in2, ends2)
    for step in [2**k for k in range(n_gy.bit_length() - 1)]:
        sums = add(sums, "gy", step, list2)
    blocks = call(pack_kernel, (shape_of(3 * block_rows + SUB, LANES),) * n_gx, 4)(sums, list0, list1, list2)
    apart = {k: never_meet(n_gx, k, slot_rows, block_rows) for k in range(1, n_gx)}
    small, meets = [], []
    for k in range(1, n_gx):
        if any(apart[k]):
            small.append(swap(sums, x_to=[i ^ k if apart[k][i] else i for i in range(n_gx)]))
        meets.append(not all(apart[k]))
    order = [k for k in [3, 2, 1] + list(range(4, n_gx)) if k < n_gx and meets[k - 1]]
    large = [swap(blocks[k], x_to=[i if apart[k][i] else i ^ k for i in range(n_gx)]) for k in order]
    alone = [[apart[k] for k in range(1, n_gx) if any(apart[k])], [apart[k] for k in order]]

    base, total_change, factor, state_coefs = call(
        membrane_kernel,
        (
            shape_of(n_states, block_rows, LANES), shape_of(block_rows, LANES), shape_of(block_rows, LANES),
            shape_of(2, n_states, LANES),
        ),
        9,
        specs=[SMEM] * 5 + [VMEM] * 4,
        cost=6_000_000,
    )(
        half_voltage, gate_slope, tau_base, conductance, reversal,
        blocks[0], cells(voltage), states(gates), states(gates_cot),
    )
    solution, volt_grad, gate_grad = call(
        functools.partial(finish_kernel, alone),
        (block, shape_of(block_rows, LANES), shape_of(n_states, block_rows, LANES)),
        12 + len(small) + len(large),
    )(
        state_coefs, cells(voltage_cot), cells(voltage), total_change, factor, base,
        in0, in1, in2, ends1, ends2, blocks[0], *small, *large,
    )
    return solution, volt_grad.reshape(voltage.shape), gate_grad.reshape(gates.shape)


def solution(mesh):
    grid = P(("groups", "gx"), "gy", "gz")
    cells = P(("groups", "gy", "gz"), "gx")
    states = P(None, ("groups", "gy", "gz"), "gx")
    in_specs = (
        grid, grid, grid, P(("groups", "gx"), "gy", "gz", None), cells, states, cells, states,
        P(), P(), P(), P(), P(),
    )
    return jax.shard_map(
        local, mesh=mesh, in_specs=in_specs, out_specs=(grid, cells, states), check_vma=False
    )
```
